32 devices in a mesh: dp: 4 (over x, core), ctx: 8 (over z, y).
Axes of the slice: x: 2, y: 2, z: 4, core: 2. Of those that a mesh axis runs over, the one named last changes fastest.
Arguments:
- tokens: bfloat16 [8, 1024, 1152], P('dp', 'ctx'), may hold values from -6 to 6
- lengths: int32 [8], P('dp'), may hold values from 256 to 1024, as said below
- w_qkv: float32 [1536, 1152], P('ctx', 'dp'), may hold values from -0.1875 to 0.1875
- w_out: float32 [1024, 1152], P('ctx', 'dp'), may hold values from -0.1875 to 0.1875
- w_gate_up: float32 [13824, 1152], P('ctx', 'dp'), may hold values from -0.1875 to 0.1875
- w_down: float32 [6912, 1152], P('ctx', 'dp'), may hold values from -0.078125 to 0.078125
- gains: float32 [5120], P(('dp', 'ctx')), may hold values from -0.5 to 0.5
- cotangent: bfloat16 [8, 1024, 1152], P('dp', 'ctx'), may hold values from -6 to 6
Outputs:
- result: bfloat16 [8, 1024, 1152], P('dp', 'ctx')
- grad_input: float32 [8, 1024, 1152], P('dp', 'ctx')
- grad_qkv: float32 [1536, 1152], P('ctx', 'dp')
- grad_out: float32 [1024, 1152], P('ctx', 'dp')
- grad_gate_up: float32 [13824, 1152], P('ctx', 'dp')
- grad_down: float32 [6912, 1152], P('ctx', 'dp')
- grad_gains: float32 [5120], P(('dp', 'ctx'))
The draws below stay inside these ranges and needn't reach their ends.
Inputs may be any that keep to these rules, and one draw needn't show every extreme that they name: `lengths`: in every group of 2 sequences held by one index of dp, one sequence has length 1024.
All inputs are finite; a program needn't handle non-finite values.
Results may differ from the reference program's by a relative error of at most 0.02.
Values may be sent and summed in bfloat16 or wider, within the bound.
A program may use at most 256 MiB of HBM per device.

```python
import math
import jax
import jax.numpy as jnp
from jax import lax

D = 1152
HEADS = 4
HD = 256
FF = 6912
WINDOW = 512
SEQ_DEV = 2
LEN = 1024
SEQS = 8


def draw_lengths(key, part):
    key = jax.random.fold_in(key, 17)
    key_base, key_full, key_short = jax.random.split(key, 3)
    groups = SEQS // SEQ_DEV
    drawn_base = jax.random.randint(key_base, (SEQS,), LEN // 4, LEN + 1)
    full_slot = jax.random.randint(key_full, (groups,), 0, SEQ_DEV)
    sequence_index = jnp.arange(SEQS, dtype=jnp.int32)
    slot_index = sequence_index % SEQ_DEV
    owner_group = sequence_index // SEQ_DEV
    chosen = full_slot[owner_group]
    short_group = jax.random.randint(key_short, (), 0, groups)
    is_full = slot_index == chosen
    is_short = (owner_group == short_group) & (slot_index == (chosen + 1) % SEQ_DEV)
    return jnp.where(is_full, LEN, jnp.where(is_short, LEN // 4, drawn_base)).astype(jnp.int32)


def levels(stream_key, dims, shards, smallest, high):
    factor_of = 1.0
    for dim, shards_of in shards:
        heights = jax.random.uniform(jax.random.fold_in(jax.random.fold_in(stream_key, 6), dim), (shards_of,), jnp.float32, smallest / len(shards), high / len(shards))
        factor_of = factor_of * jnp.repeat(jnp.exp(heights), dims[dim] // shards_of).reshape((-1,) + (1,) * (len(dims) - 1 - dim))
    return factor_of


def gaussian(stream_key, shape, deviation, limit, shards=(), kind=jnp.bfloat16):
    loudness = levels(stream_key, shape, shards, -0.22, 0.18) if shards else 1.0
    values = jax.random.normal(stream_key, shape, jnp.float32) * deviation * loudness
    return jnp.minimum(jnp.maximum(values, -limit), limit).astype(kind)


def setup_inputs(seed: int = 0) -> dict:
    keys = jax.random.split(jax.random.key(seed), 9)
    tokens = gaussian(keys[0], (SEQS, LEN, D), 1.0, 6.0, ((0, 4), (1, 8)))
    lengths = draw_lengths(jax.random.fold_in(keys[8], 71), 0)
    w_qkv = gaussian(keys[2], ((HEADS + 2) * HD, D), D ** -0.5, 0.1875, ((0, 8), (1, 4)), jnp.float32)
    w_out = gaussian(keys[3], (HEADS * HD, D), (HEADS * HD) ** -0.5, 0.1875, ((0, 8), (1, 4)), jnp.float32)
    w_gate_up = gaussian(keys[4], (2 * FF, D), D ** -0.5, 0.1875, ((0, 8), (1, 4)), jnp.float32)
    w_down = gaussian(keys[5], (FF, D), FF ** -0.5, 0.078125, ((0, 8), (1, 4)), jnp.float32)
    gains = jnp.clip(jax.random.uniform(keys[6], (4 * D + 2 * HD,), jnp.float32, -0.5, 0.5) * levels(keys[6], (4 * D + 2 * HD,), ((0, 32),), -0.4, 0.0), -0.5, 0.5)
    cotangent = gaussian(keys[7], (SEQS, LEN, D), 1.0, 6.0, ((0, 4), (1, 8)))
    return dict(tokens=tokens, lengths=lengths, w_qkv=w_qkv, w_out=w_out, w_gate_up=w_gate_up, w_down=w_down, gains=gains, cotangent=cotangent)


@jax.custom_vjp
def low(v):
    return lax.optimization_barrier(v.astype(jnp.bfloat16)).astype(jnp.float32)

@jax.custom_vjp
def low_back(v):
    return v

def low_keep(v):
    return (low(v), None)

def low_pass(kept, grad):
    return (grad,)

def back_keep(v):
    return (v, None)

def back_low(kept, grad):
    return (low(grad),)
low.defvjp(low_keep, low_pass)
low_back.defvjp(back_keep, back_low)
EPS = 1e-06
BIG = 1e+30
HIGH = lax.Precision.HIGHEST

def norm_scaled(v, gain):
    return v * lax.rsqrt(lax.optimization_barrier(jnp.mean(v * v, axis=-1, keepdims=True)) + EPS) * (1.0 + gain)

def rotate(v, angle):
    half = v.shape[-1] // 2
    cosine = jnp.cos(angle)
    sine = jnp.sin(angle)
    first = v[..., :half]
    second = v[..., half:]
    return jnp.concatenate([first * cosine - second * sine, second * cosine + first * sine], axis=-1)

def angles_of(positions):
    inverse = 1.0 / 10000.0 ** (jnp.arange(HD // 2, dtype=jnp.float32) * (2.0 / HD))
    return positions.astype(jnp.float32)[:, None] * inverse[None, :]

def attend(query, key_rows, value_rows, length):
    block = math.gcd(LEN, 512)
    scale = 1.0 / math.sqrt(HD)
    key_pad = jnp.concatenate([jnp.zeros((WINDOW, HD), key_rows.dtype), key_rows], axis=0)
    value_pad = jnp.concatenate([jnp.zeros((WINDOW, HD), value_rows.dtype), value_rows], axis=0)

    def one_block(number):
        first = number * block
        query_block = lax.dynamic_slice_in_dim(query, first, block, 0)
        key_block = lax.dynamic_slice_in_dim(key_pad, first, block + WINDOW, 0)
        value_block = lax.dynamic_slice_in_dim(value_pad, first, block + WINDOW, 0)
        query_pos = first + jnp.arange(block, dtype=jnp.int32)
        key_pos = first - WINDOW + jnp.arange(block + WINDOW, dtype=jnp.int32)
        allowed = (key_pos[None, :] >= 0) & (key_pos[None, :] <= query_pos[:, None]) & (query_pos[:, None] - key_pos[None, :] < WINDOW) & ((key_pos[None, :] < length) | (key_pos[None, :] == query_pos[:, None]))
        raw = low_back(jnp.einsum('qhd,kd->hqk', query_block, key_block, precision=HIGH))
        scores = jnp.where(allowed[None], raw * scale, -BIG)
        top = lax.optimization_barrier(jnp.max(scores, axis=-1, keepdims=True))
        expo = jnp.exp(scores - top)
        probs = low(expo / lax.optimization_barrier(jnp.sum(expo, axis=-1, keepdims=True)))
        mixed = jnp.einsum('hqk,kd->qhd', probs, value_block, precision=HIGH)
        return mixed.reshape(block, HEADS * HD)
    blocks = lax.map(jax.checkpoint(one_block), jnp.arange(LEN // block, dtype=jnp.int32))
    return blocks.reshape(LEN, HEADS * HD)

def sequence_layer(inputs, length, w_qkv, w_out, w_gate_up, w_down, gains):
    positions = jnp.arange(LEN, dtype=jnp.int32)
    angle = angles_of(positions)
    gain_in = gains[:D]
    gain_attn = gains[D:2 * D]
    gain_pre = gains[2 * D:3 * D]
    gain_post = gains[3 * D:4 * D]
    gain_query = gains[4 * D:4 * D + HD]
    gain_key = gains[4 * D + HD:]
    normed_in = low(norm_scaled(inputs, gain_in))
    projected = low_back(jnp.dot(normed_in, w_qkv.T, precision=HIGH))
    query = projected[:, :HEADS * HD].reshape(LEN, HEADS, HD)
    key_rows = projected[:, HEADS * HD:(HEADS + 1) * HD]
    value_rows = low(projected[:, (HEADS + 1) * HD:])
    query = low(rotate(norm_scaled(query, gain_query), angle[:, None, :]))
    key_rows = low(rotate(norm_scaled(key_rows, gain_key), angle))
    attended = low(low_back(attend(query, key_rows, value_rows, length)))
    out_proj = low_back(jnp.dot(attended, w_out, precision=HIGH))
    mixed = inputs + norm_scaled(out_proj, gain_attn)
    normed_mid = low(norm_scaled(mixed, gain_pre))
    gate_up = low_back(jnp.dot(normed_mid, w_gate_up.T, precision=HIGH))
    paired = gate_up.reshape(LEN, FF, 2)
    hidden = low(jax.nn.gelu(paired[..., 0], approximate=True) * paired[..., 1])
    down = low_back(jnp.dot(hidden, w_down, precision=HIGH))
    valid = (positions < length)[:, None]
    return jnp.where(valid, mixed + norm_scaled(down, gain_post), 0.0)

def reference(tokens, lengths, w_qkv, w_out, w_gate_up, w_down, gains, cotangent):

    def forward(inputs, weight_qkv, weight_out, weight_gate_up, weight_down, gain_all):
        weight_qkv = low(weight_qkv)
        weight_out = low(weight_out)
        weight_gate_up = low(weight_gate_up)
        weight_down = low(weight_down)
        gain_all = low(gain_all)

        def one_sequence(pair):
            return sequence_layer(pair[0], pair[1], weight_qkv, weight_out, weight_gate_up, weight_down, gain_all)
        return lax.map(jax.checkpoint(one_sequence), (inputs, lengths))
    output, pull = jax.vjp(forward, tokens.astype(jnp.float32), w_qkv, w_out, w_gate_up, w_down, gains)
    grads = pull(cotangent.astype(jnp.float32))
    return (output.astype(jnp.bfloat16), grads[0], grads[1], grads[2], grads[3], grads[4], grads[5])
```

```python
from functools import partial
import math

import jax
import jax.numpy as jnp
from jax import lax
from jax.experimental import pallas as pl
from jax.experimental.pallas import tpu as pltpu
from jax.sharding import PartitionSpec as P

D = 1152
HEADS = 4
HD = 256
WINDOW = 512
GROUP = 8

EPS = 1e-06
BIG = 1e30
MESH = pl.DeviceIdType.MESH
VMEM_LIMIT = 56 * 2**20


class Layout:
    def __init__(self, mesh):
        self.dp = mesh.shape["dp"]
        self.ctx = mesh.shape["ctx"]
        self.lo = max(1, GROUP // self.dp)
        self.hi = self.ctx // self.lo
        self.wide = self.dp // 2
        self.chips = self.wide * self.lo
        self.group = self.dp * self.lo
        self.hi_groups = [
            [h * self.lo + low for h in range(self.hi)] for low in range(self.lo)
        ]

    def place(self):
        dp = lax.axis_index("dp")
        ctx = lax.axis_index("ctx")
        chip = lax.rem(ctx, self.lo) * self.wide + dp // 2
        return chip, lax.rem(dp, 2), ctx // self.lo

    def device(self, chip, core, high):
        return (lax.rem(chip, self.wide) * 2 + core, high * self.lo + chip // self.wide)


def remote(src, dst, send, recv, device):
    return pltpu.make_async_remote_copy(
        src_ref=src, dst_ref=dst, send_sem=send, recv_sem=recv, device_id=device, device_id_type=MESH
    )


def greet(devices):
    barrier = pltpu.get_barrier_semaphore()
    for device in devices:
        pl.semaphore_signal(barrier, inc=1, device_id=device, device_id_type=MESH)
    pl.semaphore_wait(barrier, len(devices))


def gather_tokens_kernel(lay, own, out, local_sem, send, recv, core_send, core_recv):
    chip, core, high = lay.place()
    n = lay.chips
    peers = [lay.device(lax.rem(chip + k, n), core, high) for k in range(1, n)]
    partner = lay.device(chip, 1 - core, high)
    greet(peers + [partner])
    mine = chip * 2 + core
    pushes = [
        remote(own, out.at[mine], send.at[k], recv.at[k], peers[k]) for k in range(n - 1)
    ]
    for push in pushes:
        push.start()
    shares = [remote(own, out.at[mine], core_send.at[0], core_recv.at[0], partner)]
    shares[0].start()
    keep = pltpu.make_async_copy(own, out.at[mine], local_sem)
    keep.start()
    for k in range(1, n):
        source = lax.rem(chip + n - k, n) * 2 + core
        pushes[k - 1].wait_recv()
        share = remote(out.at[source], out.at[source], core_send.at[k], core_recv.at[k], partner)
        share.start()
        shares.append(share)
    keep.wait()
    for push in pushes:
        push.wait_send()
    for share in shares:
        share.wait()


def gather_tokens(lay, value, collective_id):
    n = lay.chips
    return pl.pallas_call(
        partial(gather_tokens_kernel, lay),
        out_shape=jax.ShapeDtypeStruct((lay.group,) + value.shape, value.dtype),
        in_specs=[pl.BlockSpec(memory_space=pl.ANY)],
        out_specs=pl.BlockSpec(memory_space=pl.ANY),
        scratch_shapes=[
            pltpu.SemaphoreType.DMA,
            pltpu.SemaphoreType.DMA((n - 1,)),
            pltpu.SemaphoreType.DMA((n - 1,)),
            pltpu.SemaphoreType.DMA((n,)),
            pltpu.SemaphoreType.DMA((n,)),
        ],
        compiler_params=pltpu.CompilerParams(
            collective_id=collective_id, has_side_effects=True, vmem_limit_bytes=VMEM_LIMIT
        ),
    )(value)


def scatter_tokens_kernel(lay, parts, out, from_core, sums, landed, send, recv, core_send, core_recv):
    chip, core, high = lay.place()
    n = lay.chips
    peers = [lay.device(lax.rem(chip + k, n), core, high) for k in range(1, n)]
    partner = lay.device(chip, 1 - core, high)
    greet(peers + [partner])
    shares = []
    for k in list(range(1, n)) + [0]:
        target = lax.rem(chip + k, n)
        share = remote(
            parts.at[target * 2 + 1 - core],
            from_core.at[k],
            core_send.at[k],
            core_recv.at[k],
            partner,
        )
        share.start()
        shares.append((k, share))
    pushes = []
    for k, share in shares:
        share.wait_recv()
        target = lax.rem(chip + k, n)
        total = parts[target * 2 + core].astype(jnp.float32) + from_core[k].astype(jnp.float32)
        if k:
            sums[k - 1] = total.astype(sums.dtype)
            push = remote(
                sums.at[k - 1], landed.at[k - 1], send.at[k - 1], recv.at[k - 1], peers[k - 1]
            )
            push.start()
            pushes.append(push)
        else:
            out[...] = total
    for push in pushes:
        push.wait_recv()
    total = out[...]
    for k in range(n - 1):
        total = total + landed[k].astype(jnp.float32)
    out[...] = total
    for push in pushes:
        push.wait_send()
    for _, share in shares:
        share.wait_send()


def scatter_tokens(lay, parts, collective_id):
    n = lay.chips
    rows, cols = parts.shape[1:]
    return pl.pallas_call(
        partial(scatter_tokens_kernel, lay),
        out_shape=jax.ShapeDtypeStruct((rows, cols), jnp.float32),
        in_specs=[pl.BlockSpec(memory_space=pltpu.VMEM)],
        out_specs=pl.BlockSpec(memory_space=pltpu.VMEM),
        scratch_shapes=[
            pltpu.VMEM((n, rows, cols), jnp.bfloat16),
            pltpu.VMEM((n - 1, rows, cols), jnp.bfloat16),
            pltpu.VMEM((n - 1, rows, cols), jnp.bfloat16),
            pltpu.SemaphoreType.DMA((n - 1,)),
            pltpu.SemaphoreType.DMA((n - 1,)),
            pltpu.SemaphoreType.DMA((n,)),
            pltpu.SemaphoreType.DMA((n,)),
        ],
        compiler_params=pltpu.CompilerParams(
            collective_id=collective_id, has_side_effects=True, vmem_limit_bytes=VMEM_LIMIT
        ),
    )(parts)


def shifted(value, axis, steps):
    count = lax.axis_size(axis)
    leading, last = (max(0, -steps), min(count, count - steps))
    return lax.ppermute(value, axis, [(source, source + steps) for source in range(leading, last)])


def norm_scaled(v, gain):
    return v * lax.rsqrt(jnp.mean(v * v, axis=-1, keepdims=True) + EPS) * (1.0 + gain)


def rotate(v, angle):
    half = v.shape[-1] // 2
    cosine = jnp.cos(angle)
    sine = jnp.sin(angle)
    first = v[..., :half]
    second = v[..., half:]
    return jnp.concatenate(
        [first * cosine - second * sine, second * cosine + first * sine], axis=-1
    )


def angles_of(positions):
    inverse = 1.0 / 10000.0 ** (jnp.arange(HD // 2, dtype=jnp.float32) * (2.0 / HD))
    return positions.astype(jnp.float32)[:, None] * inverse[None, :]


def head_inputs(projected, gain_query, gain_key, angle):
    query = projected[..., : HEADS * HD].reshape(projected.shape[:-1] + (HEADS, HD))
    key_rows = projected[..., HEADS * HD : (HEADS + 1) * HD]
    value_rows = projected[..., (HEADS + 1) * HD :]
    query = rotate(norm_scaled(query, gain_query), angle[:, None, :])
    key_rows = rotate(norm_scaled(key_rows, gain_key), angle)
    return (query, key_rows, value_rows)


def gate_times_up(gate, up):
    return jax.nn.gelu(gate, approximate=True) * up


def to_group(lay, quarters):
    rows, cols = quarters.shape
    per = rows // lay.dp
    padded = -(-per // 16) * 16
    value = quarters.astype(jnp.bfloat16).reshape(lay.dp, per, cols)
    return jnp.pad(value, ((0, 0), (0, padded - per), (0, 0)))


def across(lay, stacked):
    return lax.all_to_all(stacked, "dp", split_axis=0, concat_axis=2, tiled=True)[0]


def back_across(lay, rows):
    return lax.all_to_all(rows[None], "dp", split_axis=2, concat_axis=0, tiled=True)


def contract(left, right, dims_left, dims_right):
    return lax.dot_general(
        left, right, ((dims_left, dims_right), ((), ())), preferred_element_type=jnp.float32
    )


def per_device(lay, tokens, lengths, w_qkv, w_out, w_gate_up, w_down, gains, cotangent):
    seq_count = tokens.shape[0]
    local_len = tokens.shape[1]
    reach = (WINDOW - 1) // local_len + 1
    scale = 1.0 / math.sqrt(HD)
    attn_masters = (
        w_qkv.astype(jnp.bfloat16),
        w_out.astype(jnp.bfloat16),
        gains.astype(jnp.bfloat16),
    )
    row_qkv, row_out, row_gain = (
        lax.all_gather(attn_masters[0], "ctx", axis=0, tiled=True),
        lax.all_gather(attn_masters[1], "ctx", axis=0, tiled=True),
        lax.all_gather(attn_masters[2], "ctx", axis=0, tiled=True),
    )
    full_qkv, full_out, gain_low = (
        lax.all_gather(row_qkv, "dp", axis=1, tiled=True),
        lax.all_gather(row_out, "dp", axis=1, tiled=True),
        lax.all_gather(row_gain, "dp", axis=0, tiled=True),
    )
    pairs = w_gate_up.reshape(w_gate_up.shape[0] // 2, 2, w_gate_up.shape[1])
    per = pairs.shape[0] // lay.dp
    stacked = jnp.concatenate(
        [to_group(lay, pairs[:, 0]), to_group(lay, pairs[:, 1]), to_group(lay, w_down)], axis=1
    )
    padded = stacked.shape[1] // 3
    moved = across(lay, stacked)
    w_gate, w_up, w_low = (
        lax.all_gather(
            moved[i * padded : (i + 1) * padded],
            "ctx",
            axis=0,
            tiled=True,
            axis_index_groups=lay.hi_groups,
        )
        for i in range(3)
    )
    gain_all = gain_low.astype(jnp.float32)
    gain_in = gain_all[:D]
    gain_attn = gain_all[D : 2 * D]
    gain_pre = gain_all[2 * D : 3 * D]
    gain_post = gain_all[3 * D : 4 * D]
    gain_query = gain_all[4 * D : 4 * D + HD]
    gain_key = gain_all[4 * D + HD :]
    offset = lax.axis_index("ctx") * local_len
    positions = offset + jnp.arange(local_len, dtype=jnp.int32)
    angle = angles_of(positions)
    valid = positions[None, :] < lengths[:, None]
    inputs = tokens.astype(jnp.float32)
    normed_in, pull_in = jax.vjp(norm_scaled, inputs, gain_in)
    normed_low = normed_in.astype(jnp.bfloat16)
    projected = contract(normed_low, full_qkv, (2,), (1,))
    (query, key_rot, value_rows), pull_heads = jax.vjp(
        partial(head_inputs, angle=angle), projected, gain_query, gain_key
    )
    query_low = query.astype(jnp.bfloat16)
    own_pair = jnp.concatenate(
        [key_rot.astype(jnp.bfloat16), value_rows.astype(jnp.bfloat16)], axis=-1
    )
    earlier = []
    for distance in range(reach, 0, -1):
        earlier.append(shifted(own_pair, "ctx", distance))
    key_pairs = jnp.concatenate(earlier + [own_pair], axis=1)
    keys_low = key_pairs[..., :HD]
    values_low = key_pairs[..., HD:]
    key_pos = offset - reach * local_len + jnp.arange((reach + 1) * local_len, dtype=jnp.int32)
    key_grid = key_pos[None, None, :]
    query_grid = positions[None, :, None]
    allowed = (
        (key_grid >= 0)
        & (key_grid <= query_grid)
        & (query_grid - key_grid < WINDOW)
        & ((key_grid < lengths[:, None, None]) | (key_grid == query_grid))
    )

    def scores_of():
        raw = jnp.einsum("schd,skd->shck", query_low, keys_low, preferred_element_type=jnp.float32)
        return jnp.where(allowed[:, None], raw * scale, -BIG)

    scores = scores_of()
    top = jnp.max(scores, axis=-1, keepdims=True)
    expo = jnp.exp(scores - top)
    total = jnp.sum(expo, axis=-1, keepdims=True)
    probs = expo / total
    log_total = top + jnp.log(total)
    probs_low = probs.astype(jnp.bfloat16)
    attended = jnp.einsum(
        "shck,skd->schd", probs_low, values_low, preferred_element_type=jnp.float32
    )
    attended_low = attended.reshape(seq_count, local_len, HEADS * HD).astype(jnp.bfloat16)
    out_proj = contract(attended_low, full_out, (2,), (0,))
    normed_out, pull_out = jax.vjp(norm_scaled, out_proj, gain_attn)
    mixed = inputs + normed_out
    normed_mid, pull_mid = jax.vjp(norm_scaled, mixed, gain_pre)
    mid_low = normed_mid.astype(jnp.bfloat16)
    token_count = seq_count * local_len
    mid_all = gather_tokens(lay, mid_low.reshape(token_count, D), 1)
    gate = contract(mid_all, w_gate, (2,), (1,))
    up = contract(mid_all, w_up, (2,), (1,))
    hidden, pull_act = jax.vjp(gate_times_up, gate, up)
    hidden_low = hidden.astype(jnp.bfloat16)
    down_parts = contract(hidden_low, w_low, (2,), (0,)).astype(jnp.bfloat16)
    down = scatter_tokens(lay, down_parts, 2).reshape(seq_count, local_len, D)
    normed_down, pull_down = jax.vjp(norm_scaled, down, gain_post)
    result = jnp.where(valid[..., None], mixed + normed_down, 0.0).astype(jnp.bfloat16)
    upstream = jnp.where(valid[..., None], cotangent.astype(jnp.float32), 0.0)
    grad_down_in, grad_gain_post = pull_down(upstream)
    down_low = grad_down_in.astype(jnp.bfloat16)
    down_all = gather_tokens(lay, down_low.reshape(token_count, D), 3)
    grad_hidden = contract(down_all, w_low, (2,), (1,))
    grad_low = contract(hidden_low, down_all, (0, 1), (0, 1)).astype(jnp.bfloat16)
    grad_gate, grad_up = pull_act(grad_hidden)
    gate_low = grad_gate.astype(jnp.bfloat16)
    up_low = grad_up.astype(jnp.bfloat16)
    mid_parts = contract(gate_low, w_gate, (2,), (0,)) + contract(up_low, w_up, (2,), (0,))
    grad_mid = scatter_tokens(lay, mid_parts.astype(jnp.bfloat16), 4).reshape(mixed.shape)
    grad_w_gate = contract(gate_low, mid_all, (0, 1), (0, 1)).astype(jnp.bfloat16)
    grad_w_up = contract(up_low, mid_all, (0, 1), (0, 1)).astype(jnp.bfloat16)
    grad_mixed_in, grad_gain_pre = pull_mid(grad_mid)
    grad_mixed = upstream + grad_mixed_in
    grad_proj, grad_gain_attn = pull_out(grad_mixed)
    proj_low = grad_proj.astype(jnp.bfloat16)
    grad_attended = contract(proj_low, full_out, (2,), (1,))
    grad_w_out = contract(attended_low, proj_low, (0, 1), (0, 1))
    attn_low = grad_attended.astype(jnp.bfloat16).reshape(seq_count, local_len, HEADS, HD)
    again_probs = jnp.exp(scores_of() - log_total)
    again_low = again_probs.astype(jnp.bfloat16)
    grad_values = jnp.einsum(
        "shck,schd->skd", again_low, attn_low, preferred_element_type=jnp.float32
    )
    grad_probs = jnp.einsum(
        "schd,skd->shck", attn_low, values_low, preferred_element_type=jnp.float32
    )
    row_dot = jnp.sum(again_probs * grad_probs, axis=-1, keepdims=True)
    grad_scores = (scale * again_probs * (grad_probs - row_dot)).astype(jnp.bfloat16)
    grad_query = jnp.einsum(
        "shck,skd->schd", grad_scores, keys_low, preferred_element_type=jnp.float32
    )
    grad_keys = jnp.einsum(
        "shck,schd->skd", grad_scores, query_low, preferred_element_type=jnp.float32
    )
    grad_pairs = jnp.concatenate([grad_keys, grad_values], axis=-1)
    own_grad = grad_pairs[:, reach * local_len :]
    for distance in range(1, reach + 1):
        piece = grad_pairs[:, (reach - distance) * local_len : (reach - distance + 1) * local_len]
        own_grad = own_grad + shifted(piece.astype(jnp.bfloat16), "ctx", -distance).astype(
            piece.dtype
        )
    grad_projected, grad_gain_query, grad_gain_key = pull_heads(
        (grad_query, own_grad[..., :HD], own_grad[..., HD:])
    )
    qkv_low = grad_projected.astype(jnp.bfloat16)
    grad_w_qkv = contract(qkv_low, normed_low, (0, 1), (0, 1))
    grad_normed = contract(qkv_low, full_qkv, (2,), (0,))
    grad_in_norm, grad_gain_in = pull_in(grad_normed)
    grad_input = grad_mixed + grad_in_norm
    grad_gain_all = jnp.concatenate(
        [
            grad_gain_in,
            grad_gain_attn,
            grad_gain_pre,
            grad_gain_post,
            grad_gain_query,
            grad_gain_key,
        ]
    )
    col_qkv, col_out, col_gains = (
        lax.psum_scatter(
            grad_w_qkv.astype(jnp.bfloat16), "dp", scatter_dimension=1, tiled=True
        ).astype(jnp.float32),
        lax.psum_scatter(
            grad_w_out.astype(jnp.bfloat16), "dp", scatter_dimension=1, tiled=True
        ).astype(jnp.float32),
        lax.psum_scatter(
            grad_gain_all.astype(jnp.bfloat16), "dp", scatter_dimension=0, tiled=True
        ).astype(jnp.float32),
    )
    part_qkv, part_out, part_gains = (
        lax.psum_scatter(
            col_qkv.astype(jnp.bfloat16), "ctx", scatter_dimension=0, tiled=True
        ).astype(jnp.float32),
        lax.psum_scatter(
            col_out.astype(jnp.bfloat16), "ctx", scatter_dimension=0, tiled=True
        ).astype(jnp.float32),
        lax.psum_scatter(
            col_gains.astype(jnp.bfloat16), "ctx", scatter_dimension=0, tiled=True
        ).astype(jnp.float32),
    )
    owned = [
        lax.psum_scatter(
            piece, "ctx", scatter_dimension=0, tiled=True, axis_index_groups=lay.hi_groups
        )
        for piece in (grad_low, grad_w_gate, grad_w_up)
    ]
    returned = back_across(lay, jnp.concatenate(owned, axis=0)).astype(jnp.float32)
    part_down = returned[:, :per].reshape(w_down.shape)
    part_gate_up = jnp.stack(
        [returned[:, padded : padded + per], returned[:, 2 * padded : 2 * padded + per]], axis=2
    ).reshape(w_gate_up.shape)
    return (result, grad_input, part_qkv, part_out, part_gate_up, part_down, part_gains)


def solution(mesh):
    placed = (
        P("dp", "ctx", None),
        P("dp"),
        P("ctx", "dp"),
        P("ctx", "dp"),
        P("ctx", "dp"),
        P("ctx", "dp"),
        P(("dp", "ctx")),
        P("dp", "ctx", None),
    )
    return jax.shard_map(
        partial(per_device, Layout(mesh)),
        mesh=mesh,
        in_specs=placed,
        out_specs=(
            P("dp", "ctx", None),
            P("dp", "ctx", None),
            P("ctx", "dp"),
            P("ctx", "dp"),
            P("ctx", "dp"),
            P("ctx", "dp"),
            P(("dp", "ctx")),
        ),
        check_vma=False,
    )
```

```python
from functools import partial
import math

import jax
import jax.numpy as jnp
from jax import lax
from jax.experimental import pallas as pl
from jax.experimental.pallas import tpu as pltpu
from jax.sharding import PartitionSpec as P

D = 1152
HEADS = 4
HD = 256
WINDOW = 512
GROUP = 8

EPS = 1e-06
BIG = 1e30
MESH = pl.DeviceIdType.MESH
VMEM_LIMIT = 56 * 2**20


class Layout:
    def __init__(self, mesh):
        self.dp = mesh.shape["dp"]
        self.ctx = mesh.shape["ctx"]
        self.lo = max(1, GROUP // self.dp)
        self.hi = self.ctx // self.lo
        self.wide = self.dp // 2
        self.chips = self.wide * self.lo
        self.group = self.dp * self.lo
        self.hi_groups = [
            [h * self.lo + low for h in range(self.hi)] for low in range(self.lo)
        ]

    def place(self):
        dp = lax.axis_index("dp")
        ctx = lax.axis_index("ctx")
        chip = lax.rem(ctx, self.lo) * self.wide + dp // 2
        return chip, lax.rem(dp, 2), ctx // self.lo

    def device(self, chip, core, high):
        return (lax.rem(chip, self.wide) * 2 + core, high * self.lo + chip // self.wide)


def remote(src, dst, send, recv, device):
    return pltpu.make_async_remote_copy(
        src_ref=src, dst_ref=dst, send_sem=send, recv_sem=recv, device_id=device, device_id_type=MESH
    )


def greet(devices):
    barrier = pltpu.get_barrier_semaphore()
    for device in devices:
        pl.semaphore_signal(barrier, inc=1, device_id=device, device_id_type=MESH)
    pl.semaphore_wait(barrier, len(devices))


def gather_tokens_kernel(lay, own, out, local_sem, send, recv, core_send, core_recv):
    chip, core, high = lay.place()
    n = lay.chips
    peers = [lay.device(lax.rem(chip + k, n), core, high) for k in range(1, n)]
    partner = lay.device(chip, 1 - core, high)
    greet(peers + [partner])
    mine = chip * 2 + core
    pushes = [
        remote(own, out.at[mine], send.at[k], recv.at[k], peers[k]) for k in range(n - 1)
    ]
    for push in pushes:
        push.start()
    shares = [remote(own, out.at[mine], core_send.at[0], core_recv.at[0], partner)]
    shares[0].start()
    keep = pltpu.make_async_copy(own, out.at[mine], local_sem)
    keep.start()
    for k in range(1, n):
        source = lax.rem(chip + n - k, n) * 2 + core
        pushes[k - 1].wait_recv()
        share = remote(out.at[source], out.at[source], core_send.at[k], core_recv.at[k], partner)
        share.start()
        shares.append(share)
    keep.wait()
    for push in pushes:
        push.wait_send()
    for share in shares:
        share.wait()


def gather_tokens(lay, value, collective_id):
    n = lay.chips
    return pl.pallas_call(
        partial(gather_tokens_kernel, lay),
        out_shape=jax.ShapeDtypeStruct((lay.group,) + value.shape, value.dtype),
        in_specs=[pl.BlockSpec(memory_space=pl.ANY)],
        out_specs=pl.BlockSpec(memory_space=pl.ANY),
        scratch_shapes=[
            pltpu.SemaphoreType.DMA,
            pltpu.SemaphoreType.DMA((n - 1,)),
            pltpu.SemaphoreType.DMA((n - 1,)),
            pltpu.SemaphoreType.DMA((n,)),
            pltpu.SemaphoreType.DMA((n,)),
        ],
        compiler_params=pltpu.CompilerParams(
            collective_id=collective_id, has_side_effects=True, vmem_limit_bytes=VMEM_LIMIT
        ),
    )(value)


def scatter_tokens_kernel(lay, parts, out, from_core, sums, landed, send, recv, core_send, core_recv):
    chip, core, high = lay.place()
    n = lay.chips
    peers = [lay.device(lax.rem(chip + k, n), core, high) for k in range(1, n)]
    partner = lay.device(chip, 1 - core, high)
    greet(peers + [partner])
    shares = []
    for k in list(range(1, n)) + [0]:
        target = lax.rem(chip + k, n)
        share = remote(
            parts.at[target * 2 + 1 - core],
            from_core.at[k],
            core_send.at[k],
            core_recv.at[k],
            partner,
        )
        share.start()
        shares.append((k, share))
    pushes = []
    for k, share in shares:
        share.wait_recv()
        target = lax.rem(chip + k, n)
        total = parts[target * 2 + core].astype(jnp.float32) + from_core[k].astype(jnp.float32)
        if k:
            sums[k - 1] = total.astype(sums.dtype)
            push = remote(
                sums.at[k - 1], landed.at[k - 1], send.at[k - 1], recv.at[k - 1], peers[k - 1]
            )
            push.start()
            pushes.append(push)
        else:
            out[...] = total
    for push in pushes:
        push.wait_recv()
    total = out[...]
    for k in range(n - 1):
        total = total + landed[k].astype(jnp.float32)
    out[...] = total
    for push in pushes:
        push.wait_send()
    for _, share in shares:
        share.wait_send()


def scatter_tokens(lay, parts, collective_id):
    n = lay.chips
    rows, cols = parts.shape[1:]
    return pl.pallas_call(
        partial(scatter_tokens_kernel, lay),
        out_shape=jax.ShapeDtypeStruct((rows, cols), jnp.float32),
        in_specs=[pl.BlockSpec(memory_space=pltpu.VMEM)],
        out_specs=pl.BlockSpec(memory_space=pltpu.VMEM),
        scratch_shapes=[
            pltpu.VMEM((n, rows, cols), jnp.bfloat16),
            pltpu.VMEM((n - 1, rows, cols), jnp.bfloat16),
            pltpu.VMEM((n - 1, rows, cols), jnp.bfloat16),
            pltpu.SemaphoreType.DMA((n - 1,)),
            pltpu.SemaphoreType.DMA((n - 1,)),
            pltpu.SemaphoreType.DMA((n,)),
            pltpu.SemaphoreType.DMA((n,)),
        ],
        compiler_params=pltpu.CompilerParams(
            collective_id=collective_id, has_side_effects=True, vmem_limit_bytes=VMEM_LIMIT
        ),
    )(parts)


def lane_tiles(cols):
    return [(first, min(128, cols - first)) for first in range(0, cols, 128)]


def exchange_in_kernel(
    lay, pack, pairs, lows, attn_out, gate_out, up_out, low_out,
    attn_land, stack, land, lanes, attn_send, attn_recv, send, recv,
):
    n = lay.dp
    dp = lax.axis_index("dp")
    ctx = lax.axis_index("ctx")
    per = lows.shape[1]
    padded = gate_out.shape[0]
    cols = lows.shape[2]
    targets = [lax.rem(dp + k, n) for k in range(n)]
    greet([(target, ctx) for target in targets[1:]])
    attn_pushes = []
    for k in range(1, n):
        push = remote(
            pack.at[targets[k]], attn_land.at[dp], attn_send.at[k], attn_recv.at[k], (targets[k], ctx)
        )
        push.start()
        attn_pushes.append(push)
    attn_land[dp] = pack[dp]
    pushes = []
    blank = jnp.zeros((padded - per, cols), jnp.bfloat16)
    for k in list(range(2, n)) + [1, 0]:
        target = targets[k]
        for j, (first, width) in enumerate(lane_tiles(cols)):
            lanes[j, :, :width] = pairs[target, :, first : first + width]
        for i in range(3):
            for j, (first, width) in enumerate(lane_tiles(cols)):
                if i == 2:
                    piece = lows[target, :, first : first + width]
                else:
                    piece = lanes[j, pl.ds(i, per, stride=2), :][:, :width]
                if k:
                    stack[k - 1, i, :per, first : first + width] = piece.astype(jnp.bfloat16)
                else:
                    land[dp, i, :per, first : first + width] = piece.astype(jnp.bfloat16)
            if k:
                stack[k - 1, i, per:] = blank
            else:
                land[dp, i, per:] = blank
        if k:
            push = remote(stack.at[k - 1], land.at[dp], send.at[k], recv.at[k], (target, ctx))
            push.start()
            pushes.append(push)
    for push in attn_pushes:
        push.wait_recv()
    for q in range(n):
        attn_out[:, q * cols : (q + 1) * cols] = attn_land[q]
    for push in pushes:
        push.wait_recv()
    for q in range(n):
        for i, out in enumerate((gate_out, up_out, low_out)):
            out[:, q * cols : (q + 1) * cols] = land[q, i]
    for push in attn_pushes + pushes:
        push.wait_send()


def exchange_in(lay, pack, pairs, lows, collective_id):
    n, per, cols = lows.shape
    rows = pack.shape[1]
    padded = -(-per // 16) * 16
    wide = jax.ShapeDtypeStruct((padded, n * cols), jnp.bfloat16)
    vmem = pl.BlockSpec(memory_space=pltpu.VMEM)
    return pl.pallas_call(
        partial(exchange_in_kernel, lay),
        out_shape=(jax.ShapeDtypeStruct((rows, n * cols), jnp.bfloat16), wide, wide, wide),
        in_specs=[vmem] * 3,
        out_specs=(vmem,) * 4,
        scratch_shapes=[
            pltpu.VMEM((n, rows, cols), jnp.bfloat16),
            pltpu.VMEM((n - 1, 3, padded, cols), jnp.bfloat16),
            pltpu.VMEM((n, 3, padded, cols), jnp.bfloat16),
            pltpu.VMEM((len(lane_tiles(cols)), 2 * per, 128), jnp.float32),
        ]
        + [pltpu.SemaphoreType.DMA((n,))] * 4,
        compiler_params=pltpu.CompilerParams(
            collective_id=collective_id, has_side_effects=True, vmem_limit_bytes=VMEM_LIMIT
        ),
    )(pack, pairs, lows)


def gather_attn_kernel(lay, own, out, local_sem, chain_send, chain_recv, low_send, low_recv,
                       wide_send, wide_recv, core_send, core_recv):
    dp = lax.axis_index("dp")
    ctx = lax.axis_index("ctx")
    hi, lo, wide = lay.hi, lay.lo, lay.wide
    high, low = ctx // lo, lax.rem(ctx, lo)
    across, core = dp // 2, lax.rem(dp, 2)
    partner = (across * 2 + 1 - core, ctx)
    low_peers = [(dp, high * lo + lax.rem(low + k, lo)) for k in range(1, lo)]
    wide_peers = [(lax.rem(across + k, wide) * 2 + core, ctx) for k in range(1, wide)]
    right, left = (dp, ctx + lo), (dp, ctx - lo)
    has_right, has_left = high < hi - 1, high > 0
    barrier = pltpu.get_barrier_semaphore()
    for device in low_peers + wide_peers + [partner]:
        pl.semaphore_signal(barrier, inc=1, device_id=device, device_id_type=MESH)
    for there, device in ((has_right, right), (has_left, left)):
        @pl.when(there)
        def _():
            pl.semaphore_signal(barrier, inc=1, device_id=device, device_id_type=MESH)
    sides = jnp.where(has_right, 1, 0) + jnp.where(has_left, 1, 0)
    pl.semaphore_wait(barrier, len(low_peers) + len(wide_peers) + 1 + sides)

    def to_core(source, c, d, slot):
        return remote(source, out.at[c, d], core_send.at[slot], core_recv.at[slot], partner)

    def to_wide(source, c, d, slot):
        return [
            remote(source, out.at[c, d], wide_send.at[slot, k], wide_recv.at[slot, k], wide_peers[k])
            for k in range(wide - 1)
        ]

    def to_low(source, c, d, slot):
        return [
            remote(source, out.at[c, d], low_send.at[slot, k], low_recv.at[slot, k], low_peers[k])
            for k in range(lo - 1)
        ]

    def chain(source, c, side, step):
        return remote(
            source, out.at[c, dp], chain_send.at[side, step], chain_recv.at[side, step],
            right if side == 0 else left,
        )

    def blocks():
        yield 0, 0, jnp.bool_(True), high
        for step in range(1, hi):
            yield 0, step, high - step >= 0, high - step
            yield 1, step, high + step < hi, high + step

    everything = list(blocks())
    number = {(side, step): i for i, (side, step, _, _) in enumerate(everything)}
    per_low = lo
    per_wide = lo * wide

    def core_slot(i, a, b):
        return (i * per_low + a) * wide + b

    def stage_low_arrivals(i, where):
        for k in range(lo - 1):
            c = where * lo + lax.rem(low + lo - 1 - k, lo)
            low_copy = remote(own, out.at[c, dp], low_send.at[i, k], low_recv.at[i, k], low_peers[k])
            low_copy.wait_recv()
            for push in to_wide(out.at[c, dp], c, dp, i * per_low + k + 1):
                push.start()
            to_core(out.at[c, dp], c, dp, core_slot(i, k + 1, 0)).start()

    def stage_wide_arrivals(i, where):
        for a in range(lo):
            c = where * lo + (low if a == 0 else lax.rem(low + lo - a, lo))
            for k in range(wide - 1):
                d = lax.rem(across + wide - 1 - k, wide) * 2 + core
                copy = remote(
                    own, out.at[c, d], wide_send.at[i * per_low + a, k],
                    wide_recv.at[i * per_low + a, k], wide_peers[k],
                )
                copy.wait_recv()
                to_core(out.at[c, d], c, d, core_slot(i, a, k + 1)).start()

    def stage_own(i, side, step, where):
        c = where * lo + low
        source = own if step == 0 else out.at[c, dp]
        if step:
            chain(own, c, side, step - 1).wait_recv()
        for go_side, there in ((0, has_right), (1, has_left)):
            if step and go_side != side:
                continue
            if step < hi - 1:
                @pl.when(there)
                def _():
                    chain(source, c, go_side, step).start()
        for push in to_low(source, c, dp, i):
            push.start()
        for push in to_wide(source, c, dp, i * per_low):
            push.start()
        to_core(source, c, dp, core_slot(i, 0, 0)).start()

    def finish(i, side, step, where):
        c = where * lo + low
        for go_side, there in ((0, has_right), (1, has_left)):
            if step and go_side != side:
                continue
            if step < hi - 1:
                @pl.when(there)
                def _():
                    chain(own, c, go_side, step).wait_send()
        for push in to_low(own, c, dp, i):
            push.wait_send()
        for a in range(lo):
            for push in to_wide(own, c, dp, i * per_low + a):
                push.wait_send()
            for b in range(wide):
                to_core(own, c, dp, core_slot(i, a, b)).wait()

    keep = pltpu.make_async_copy(own, out.at[ctx, dp], local_sem)
    keep.start()
    previous = []
    for step in range(hi + 2):
        for stage, age in ((stage_own, 0), (stage_low_arrivals, 1), (stage_wide_arrivals, 2)):
            for i, (side, s, there, where) in enumerate(everything):
                if s != step - age:
                    continue
                if stage is stage_own:
                    call = partial(stage_own, i, side, s, where)
                else:
                    call = partial(stage, i, where)
                if s == 0:
                    call()
                else:
                    pl.when(there)(call)
    keep.wait()
    for i, (side, s, there, where) in enumerate(everything):
        call = partial(finish, i, side, s, where)
        if s == 0:
            call()
        else:
            pl.when(there)(call)


def gather_attn(lay, own, collective_id):
    count = 2 * lay.hi - 1
    lows, wides = max(1, lay.lo - 1), max(1, lay.wide - 1)
    return pl.pallas_call(
        partial(gather_attn_kernel, lay),
        out_shape=jax.ShapeDtypeStruct((lay.ctx, lay.dp) + own.shape, own.dtype),
        in_specs=[pl.BlockSpec(memory_space=pl.ANY)],
        out_specs=pl.BlockSpec(memory_space=pl.ANY),
        scratch_shapes=[pltpu.SemaphoreType.DMA]
        + [pltpu.SemaphoreType.DMA((2, lay.hi))] * 2
        + [pltpu.SemaphoreType.DMA((count, lows))] * 2
        + [pltpu.SemaphoreType.DMA((count * lay.lo, wides))] * 2
        + [pltpu.SemaphoreType.DMA((count * lay.lo * lay.wide,))] * 2,
        compiler_params=pltpu.CompilerParams(
            collective_id=collective_id, has_side_effects=True, vmem_limit_bytes=VMEM_LIMIT
        ),
    )(own)


def flip(index, bit):
    return index + bit * (1 - 2 * lax.rem(index // bit, 2))


def scatter_attn_kernel(lay, with_gains, *refs):
    refs = list(refs)
    parts = refs.pop(0)
    gains = refs.pop(0) if with_gains else None
    out = refs.pop(0)
    gains_out = refs.pop(0) if with_gains else None
    core_land, wide_sum, wide_land, keep, low_sum, low_land, hi_sum, hi_land, last, last_land = refs[:10]
    (core_send, core_recv, wide_send, wide_recv, low_send, low_recv, hi_send, hi_recv,
     last_send, last_recv) = refs[10:20]
    if with_gains:
        gains_sum, gains_land, gains_send, gains_recv = refs[20:]
    dp = lax.axis_index("dp")
    ctx = lax.axis_index("ctx")
    hi, lo, wide, n = lay.hi, lay.lo, lay.wide, lay.dp
    high, low = ctx // lo, lax.rem(ctx, lo)
    across, core = dp // 2, lax.rem(dp, 2)
    cols = out.shape[1]
    rows = parts.shape[2]
    partner = (across * 2 + 1 - core, ctx)
    low_peers = [(dp, high * lo + lax.rem(low + k, lo)) for k in range(1, lo)]
    wide_peers = [(lax.rem(across + k, wide) * 2 + core, ctx) for k in range(1, wide)]
    hi_peers = [(dp, lax.rem(high + k, hi) * lo + low) for k in range(1, hi)]
    last_peers = [(lax.rem(dp + k, n), ctx) for k in range(1, n)]
    steps = [1 << i for i in range((n - 1).bit_length())]
    gain_peers = [(flip(dp, bit), ctx) for bit in steps]
    gain_peers += [(dp, flip(ctx, 1 << i)) for i in range((lay.ctx - 1).bit_length())]
    greet(
        low_peers + hi_peers + last_peers + (gain_peers if with_gains else [])
    )

    order = [(k, a) for k in list(range(1, hi)) + [0] for a in list(range(1, lo)) + [0]]

    def block(k, a):
        return lax.rem(high + k, hi) * lo + lax.rem(low + a, lo)

    def slot(k, a):
        return k * lo + a

    sends = []
    core_copies = {}
    for k, a in order:
        for b in list(range(1, wide)) + [0]:
            there = lax.rem(across + b, wide)
            copy = remote(
                parts.at[block(k, a), there * 2 + 1 - core],
                core_land.at[slot(k, a), b],
                core_send.at[slot(k, a), b],
                core_recv.at[slot(k, a), b],
                partner,
            )
            copy.start()
            core_copies[k, a, b] = copy
            sends.append(copy)
    gain_copies = []

    def gains_step(i):
        if not with_gains or i > len(gain_peers):
            return
        if i == 0:
            gains_sum[0] = gains[...]
        else:
            gain_copies[i - 1].wait_recv()
            gains_sum[i] = gains_sum[i - 1] + gains_land[i - 1]
        if i < len(gain_peers):
            copy = remote(
                gains_sum.at[i], gains_land.at[i], gains_send.at[i], gains_recv.at[i], gain_peers[i]
            )
            copy.start()
            gain_copies.append(copy)
            sends.append(copy)
        else:
            gains_out[...] = gains_sum[i]

    wide_copies, low_copies, hi_copies = {}, {}, {}

    def sum_cores(k, a):
        s = slot(k, a)
        for b in list(range(1, wide)) + [0]:
            there = lax.rem(across + b, wide)
            core_copies[k, a, b].wait_recv()
            total = parts[block(k, a), there * 2 + core].astype(jnp.float32) + core_land[
                s, b
            ].astype(jnp.float32)
            if b:
                wide_sum[s, b - 1] = total.astype(jnp.bfloat16)
                copy = remote(
                    wide_sum.at[s, b - 1], wide_land.at[s, b - 1], wide_send.at[s, b - 1],
                    wide_recv.at[s, b - 1], wide_peers[b - 1],
                )
                copy.start()
                wide_copies[k, a, b] = copy
                sends.append(copy)
            else:
                keep[s] = total

    def sum_wide(k, a):
        s = slot(k, a)
        total = keep[s]
        for b in range(1, wide):
            wide_copies[k, a, b].wait_recv()
            total = total + wide_land[s, b - 1].astype(jnp.float32)
        if a:
            low_sum[k, a - 1] = total.astype(jnp.bfloat16)
            copy = remote(
                low_sum.at[k, a - 1], low_land.at[k, a - 1], low_send.at[k, a - 1],
                low_recv.at[k, a - 1], low_peers[a - 1],
            )
            copy.start()
            low_copies[k, a] = copy
            sends.append(copy)
        else:
            keep[s] = total

    def sum_low(k):
        total = keep[slot(k, 0)]
        for a in range(1, lo):
            low_copies[k, a].wait_recv()
            total = total + low_land[k, a - 1].astype(jnp.float32)
        if k:
            hi_sum[k - 1] = total.astype(jnp.bfloat16)
            copy = remote(
                hi_sum.at[k - 1], hi_land.at[k - 1], hi_send.at[k - 1], hi_recv.at[k - 1], hi_peers[k - 1]
            )
            copy.start()
            hi_copies[k] = copy
            sends.append(copy)
        else:
            keep[slot(0, 0)] = total

    gains_step(0)
    ks = list(range(1, hi)) + [0]
    offsets = list(range(1, lo)) + [0]
    for i in range(hi + 2):
        if i < hi:
            for a in offsets:
                sum_cores(ks[i], a)
        gains_step(i + 1)
        if 1 <= i <= hi:
            for a in offsets:
                sum_wide(ks[i - 1], a)
        if 2 <= i:
            sum_low(ks[i - 2])
    for i in range(hi + 3, len(gain_peers) + 1):
        gains_step(i)
    total = keep[slot(0, 0)]
    for k in range(1, hi):
        hi_copies[k].wait_recv()
        total = total + hi_land[k - 1].astype(jnp.float32)
    keep[slot(0, 0)] = total
    for q in range(n):
        last[q] = keep[slot(0, 0), :, q * cols : (q + 1) * cols].astype(jnp.bfloat16)
    last_copies = []
    for k in range(1, n):
        copy = remote(
            last.at[lax.rem(dp + k, n)], last_land.at[dp], last_send.at[k], last_recv.at[k], last_peers[k - 1]
        )
        copy.start()
        last_copies.append(copy)
        sends.append(copy)
    last_land[dp] = last[dp]
    for copy in last_copies:
        copy.wait_recv()
    for q in range(n):
        out[q * rows : (q + 1) * rows] = last_land[q].astype(jnp.float32)
    for copy in sends:
        copy.wait_send()


def scatter_attn(lay, parts, gains, collective_id):
    rows = parts.shape[2]
    cols = D // lay.dp
    with_gains = gains is not None
    lows, wides, his = max(1, lay.lo - 1), max(1, lay.wide - 1), max(1, lay.hi - 1)
    vmem = pl.BlockSpec(memory_space=pltpu.VMEM)
    dma = pltpu.SemaphoreType.DMA
    out_shape = [jax.ShapeDtypeStruct((lay.dp * rows, cols), jnp.float32)]
    scratch = [
        pltpu.VMEM((lay.ctx, lay.wide, rows, D), jnp.bfloat16),
        pltpu.VMEM((lay.ctx, wides, rows, D), jnp.bfloat16),
        pltpu.VMEM((lay.ctx, wides, rows, D), jnp.bfloat16),
        pltpu.VMEM((lay.ctx, rows, D), jnp.float32),
        pltpu.VMEM((lay.hi, lows, rows, D), jnp.bfloat16),
        pltpu.VMEM((lay.hi, lows, rows, D), jnp.bfloat16),
        pltpu.VMEM((his, rows, D), jnp.bfloat16),
        pltpu.VMEM((his, rows, D), jnp.bfloat16),
        pltpu.VMEM((lay.dp, rows, cols), jnp.bfloat16),
        pltpu.VMEM((lay.dp, rows, cols), jnp.bfloat16),
    ]
    for shape in ((lay.ctx, lay.wide), (lay.ctx, wides), (lay.hi, lows), (his,), (lay.dp,)):
        scratch += [dma(shape), dma(shape)]
    if with_gains:
        count = (lay.dp - 1).bit_length() + (lay.ctx - 1).bit_length()
        out_shape.append(jax.ShapeDtypeStruct(gains.shape, jnp.float32))
        scratch += [
            pltpu.VMEM((count + 1,) + gains.shape, jnp.float32),
            pltpu.VMEM((count,) + gains.shape, jnp.float32),
            dma((count,)),
            dma((count,)),
        ]
    return pl.pallas_call(
        partial(scatter_attn_kernel, lay, with_gains),
        out_shape=tuple(out_shape),
        in_specs=[vmem] * (2 if with_gains else 1),
        out_specs=(vmem,) * len(out_shape),
        scratch_shapes=scratch,
        compiler_params=pltpu.CompilerParams(
            collective_id=collective_id, has_side_effects=True, vmem_limit_bytes=VMEM_LIMIT
        ),
    )(*([parts, gains] if with_gains else [parts]))


def exchange_out_kernel(lay, gate, up, down, pairs_out, lows_out, stack, land, lanes, send, recv):
    n = lay.dp
    dp = lax.axis_index("dp")
    ctx = lax.axis_index("ctx")
    cols = lows_out.shape[2]
    per = lows_out.shape[1]
    greet([(lax.rem(dp + k, n), ctx) for k in range(1, n)])
    for q in range(n):
        for i, piece in enumerate((gate, up, down)):
            stack[q, i] = piece[:, q * cols : (q + 1) * cols]
    pushes = []
    for k in range(1, n):
        target = lax.rem(dp + k, n)
        push = remote(stack.at[target], land.at[dp], send.at[k], recv.at[k], (target, ctx))
        push.start()
        pushes.append(push)
    land[dp] = stack[dp]
    for push in pushes:
        push.wait_recv()
    for q in range(n):
        for j, (first, width) in enumerate(lane_tiles(cols)):
            for i in range(2):
                piece = land[q, i, :per, first : first + width].astype(jnp.float32)
                if width < 128:
                    piece = jnp.concatenate(
                        [piece, jnp.zeros((per, 128 - width), jnp.float32)], axis=1
                    )
                lanes[j, pl.ds(i, per, stride=2), :] = piece
            pairs_out[q, :, first : first + width] = lanes[j, :, :width]
        lows_out[q] = land[q, 2, :per].astype(jnp.float32)
    for push in pushes:
        push.wait_send()


def exchange_out(lay, gate, up, down, per, collective_id):
    padded = gate.shape[0]
    n, cols = lay.dp, gate.shape[1] // lay.dp
    vmem = pl.BlockSpec(memory_space=pltpu.VMEM)
    return pl.pallas_call(
        partial(exchange_out_kernel, lay),
        out_shape=(
            jax.ShapeDtypeStruct((n, 2 * per, cols), jnp.float32),
            jax.ShapeDtypeStruct((n, per, cols), jnp.float32),
        ),
        in_specs=[vmem] * 3,
        out_specs=(vmem,) * 2,
        scratch_shapes=[
            pltpu.VMEM((n, 3, padded, cols), jnp.bfloat16),
            pltpu.VMEM((n, 3, padded, cols), jnp.bfloat16),
            pltpu.VMEM((len(lane_tiles(cols)), 2 * per, 128), jnp.float32),
            pltpu.SemaphoreType.DMA((n,)),
            pltpu.SemaphoreType.DMA((n,)),
        ],
        compiler_params=pltpu.CompilerParams(
            collective_id=collective_id, has_side_effects=True, vmem_limit_bytes=VMEM_LIMIT
        ),
    )(gate, up, down)


def shifted(value, axis, steps):
    count = lax.axis_size(axis)
    leading, last = (max(0, -steps), min(count, count - steps))
    return lax.ppermute(value, axis, [(source, source + steps) for source in range(leading, last)])


def norm_scaled(v, gain):
    return v * lax.rsqrt(jnp.mean(v * v, axis=-1, keepdims=True) + EPS) * (1.0 + gain)


def rotate(v, angle):
    half = v.shape[-1] // 2
    cosine = jnp.cos(angle)
    sine = jnp.sin(angle)
    first = v[..., :half]
    second = v[..., half:]
    return jnp.concatenate(
        [first * cosine - second * sine, second * cosine + first * sine], axis=-1
    )


def angles_of(positions):
    inverse = 1.0 / 10000.0 ** (jnp.arange(HD // 2, dtype=jnp.float32) * (2.0 / HD))
    return positions.astype(jnp.float32)[:, None] * inverse[None, :]


def head_inputs(projected, gain_query, gain_key, angle):
    query = projected[..., : HEADS * HD].reshape(projected.shape[:-1] + (HEADS, HD))
    key_rows = projected[..., HEADS * HD : (HEADS + 1) * HD]
    value_rows = projected[..., (HEADS + 1) * HD :]
    query = rotate(norm_scaled(query, gain_query), angle[:, None, :])
    key_rows = rotate(norm_scaled(key_rows, gain_key), angle)
    return (query, key_rows, value_rows)


def gate_times_up(gate, up):
    return jax.nn.gelu(gate, approximate=True) * up


def contract(left, right, dims_left, dims_right):
    return lax.dot_general(
        left, right, ((dims_left, dims_right), ((), ())), preferred_element_type=jnp.float32
    )


def per_device(lay, tokens, lengths, w_qkv, w_out, w_gate_up, w_down, gains, cotangent):
    seq_count = tokens.shape[0]
    local_len = tokens.shape[1]
    reach = (WINDOW - 1) // local_len + 1
    scale = 1.0 / math.sqrt(HD)
    units = w_down.shape[0]
    per = units // lay.dp
    qkv_rows, out_rows = w_qkv.shape[0], w_out.shape[0]
    cols = w_qkv.shape[1]
    used = qkv_rows + out_rows + 1
    block = 16 * lay.dp
    pack_rows = -(-used // block) * block
    gain_row = jnp.pad(gains, (0, cols - gains.shape[0]))[None]
    pack = jnp.concatenate(
        [w_qkv, w_out, gain_row, jnp.zeros((pack_rows - used, cols), jnp.float32)], axis=0
    ).astype(jnp.bfloat16)
    own_attn, gate_rows, up_rows, low_rows = exchange_in(
        lay,
        pack.reshape(lay.dp, pack_rows // lay.dp, cols),
        w_gate_up.reshape(lay.dp, 2 * per, cols),
        w_down.reshape(lay.dp, per, cols),
        5,
    )
    w_gate, w_up, w_low = (
        lax.all_gather(rows, "ctx", axis=0, tiled=True, axis_index_groups=lay.hi_groups)
        for rows in (gate_rows, up_rows, low_rows)
    )
    attn_all = gather_attn(lay, own_attn, 6).reshape(lay.ctx, pack_rows, D)
    full_qkv = attn_all[:, :qkv_rows].reshape(lay.ctx * qkv_rows, D)
    full_out = attn_all[:, qkv_rows : qkv_rows + out_rows].reshape(lay.ctx * out_rows, D)
    gain_all = (
        attn_all[:, used - 1]
        .reshape(lay.ctx, lay.dp, cols)[:, :, : gains.shape[0]]
        .transpose(1, 0, 2)
        .reshape(-1)
        .astype(jnp.float32)
    )
    gain_in = gain_all[:D]
    gain_attn = gain_all[D : 2 * D]
    gain_pre = gain_all[2 * D : 3 * D]
    gain_post = gain_all[3 * D : 4 * D]
    gain_query = gain_all[4 * D : 4 * D + HD]
    gain_key = gain_all[4 * D + HD :]
    offset = lax.axis_index("ctx") * local_len
    positions = offset + jnp.arange(local_len, dtype=jnp.int32)
    angle = angles_of(positions)
    valid = positions[None, :] < lengths[:, None]
    inputs = tokens.astype(jnp.float32)
    normed_in, pull_in = jax.vjp(norm_scaled, inputs, gain_in)
    normed_low = normed_in.astype(jnp.bfloat16)
    projected = contract(normed_low, full_qkv, (2,), (1,))
    (query, key_rot, value_rows), pull_heads = jax.vjp(
        partial(head_inputs, angle=angle), projected, gain_query, gain_key
    )
    query_low = query.astype(jnp.bfloat16)
    own_pair = jnp.concatenate(
        [key_rot.astype(jnp.bfloat16), value_rows.astype(jnp.bfloat16)], axis=-1
    )
    earlier = []
    for distance in range(reach, 0, -1):
        earlier.append(shifted(own_pair, "ctx", distance))
    key_pairs = jnp.concatenate(earlier + [own_pair], axis=1)
    keys_low = key_pairs[..., :HD]
    values_low = key_pairs[..., HD:]
    key_pos = offset - reach * local_len + jnp.arange((reach + 1) * local_len, dtype=jnp.int32)
    key_grid = key_pos[None, None, :]
    query_grid = positions[None, :, None]
    allowed = (
        (key_grid >= 0)
        & (key_grid <= query_grid)
        & (query_grid - key_grid < WINDOW)
        & ((key_grid < lengths[:, None, None]) | (key_grid == query_grid))
    )

    def scores_of():
        raw = jnp.einsum("schd,skd->shck", query_low, keys_low, preferred_element_type=jnp.float32)
        return jnp.where(allowed[:, None], raw * scale, -BIG)

    scores = scores_of()
    top = jnp.max(scores, axis=-1, keepdims=True)
    expo = jnp.exp(scores - top)
    total = jnp.sum(expo, axis=-1, keepdims=True)
    probs = expo / total
    log_total = top + jnp.log(total)
    probs_low = probs.astype(jnp.bfloat16)
    attended = jnp.einsum(
        "shck,skd->schd", probs_low, values_low, preferred_element_type=jnp.float32
    )
    attended_low = attended.reshape(seq_count, local_len, HEADS * HD).astype(jnp.bfloat16)
    out_proj = contract(attended_low, full_out, (2,), (0,))
    normed_out, pull_out = jax.vjp(norm_scaled, out_proj, gain_attn)
    mixed = inputs + normed_out
    normed_mid, pull_mid = jax.vjp(norm_scaled, mixed, gain_pre)
    mid_low = normed_mid.astype(jnp.bfloat16)
    token_count = seq_count * local_len
    mid_all = gather_tokens(lay, mid_low.reshape(token_count, D), 1)
    gate = contract(mid_all, w_gate, (2,), (1,))
    up = contract(mid_all, w_up, (2,), (1,))
    hidden, pull_act = jax.vjp(gate_times_up, gate, up)
    hidden_low = hidden.astype(jnp.bfloat16)
    down_parts = contract(hidden_low, w_low, (2,), (0,)).astype(jnp.bfloat16)
    down = scatter_tokens(lay, down_parts, 2).reshape(seq_count, local_len, D)
    normed_down, pull_down = jax.vjp(norm_scaled, down, gain_post)
    result = jnp.where(valid[..., None], mixed + normed_down, 0.0).astype(jnp.bfloat16)
    upstream = jnp.where(valid[..., None], cotangent.astype(jnp.float32), 0.0)
    grad_down_in, grad_gain_post = pull_down(upstream)
    down_low = grad_down_in.astype(jnp.bfloat16)
    down_all = gather_tokens(lay, down_low.reshape(token_count, D), 3)
    grad_hidden = contract(down_all, w_low, (2,), (1,))
    grad_low = contract(hidden_low, down_all, (0, 1), (0, 1)).astype(jnp.bfloat16)
    grad_gate, grad_up = pull_act(grad_hidden)
    gate_low = grad_gate.astype(jnp.bfloat16)
    up_low = grad_up.astype(jnp.bfloat16)
    mid_parts = contract(gate_low, w_gate, (2,), (0,)) + contract(up_low, w_up, (2,), (0,))
    grad_mid = scatter_tokens(lay, mid_parts.astype(jnp.bfloat16), 4).reshape(mixed.shape)
    grad_w_gate = contract(gate_low, mid_all, (0, 1), (0, 1)).astype(jnp.bfloat16)
    grad_w_up = contract(up_low, mid_all, (0, 1), (0, 1)).astype(jnp.bfloat16)
    grad_mixed_in, grad_gain_pre = pull_mid(grad_mid)
    grad_mixed = upstream + grad_mixed_in
    grad_proj, grad_gain_attn = pull_out(grad_mixed)
    proj_low = grad_proj.astype(jnp.bfloat16)
    grad_attended = contract(proj_low, full_out, (2,), (1,))
    grad_w_out = contract(attended_low, proj_low, (0, 1), (0, 1))
    attn_low = grad_attended.astype(jnp.bfloat16).reshape(seq_count, local_len, HEADS, HD)
    again_probs = jnp.exp(scores_of() - log_total)
    again_low = again_probs.astype(jnp.bfloat16)
    grad_values = jnp.einsum(
        "shck,schd->skd", again_low, attn_low, preferred_element_type=jnp.float32
    )
    grad_probs = jnp.einsum(
        "schd,skd->shck", attn_low, values_low, preferred_element_type=jnp.float32
    )
    row_dot = jnp.sum(again_probs * grad_probs, axis=-1, keepdims=True)
    grad_scores = (scale * again_probs * (grad_probs - row_dot)).astype(jnp.bfloat16)
    grad_query = jnp.einsum(
        "shck,skd->schd", grad_scores, keys_low, preferred_element_type=jnp.float32
    )
    grad_keys = jnp.einsum(
        "shck,schd->skd", grad_scores, query_low, preferred_element_type=jnp.float32
    )
    grad_pairs = jnp.concatenate([grad_keys, grad_values], axis=-1)
    own_grad = grad_pairs[:, reach * local_len :]
    for distance in range(1, reach + 1):
        piece = grad_pairs[:, (reach - distance) * local_len : (reach - distance + 1) * local_len]
        own_grad = own_grad + shifted(piece.astype(jnp.bfloat16), "ctx", -distance).astype(
            piece.dtype
        )
    grad_projected, grad_gain_query, grad_gain_key = pull_heads(
        (grad_query, own_grad[..., :HD], own_grad[..., HD:])
    )
    qkv_low = grad_projected.astype(jnp.bfloat16)
    grad_w_qkv = contract(qkv_low, normed_low, (0, 1), (0, 1))
    grad_normed = contract(qkv_low, full_qkv, (2,), (0,))
    grad_in_norm, grad_gain_in = pull_in(grad_normed)
    grad_input = grad_mixed + grad_in_norm
    grad_gain_all = jnp.concatenate(
        [
            grad_gain_in,
            grad_gain_attn,
            grad_gain_pre,
            grad_gain_post,
            grad_gain_query,
            grad_gain_key,
        ]
    )
    def own_blocks(grad, rows):
        whole = grad.astype(jnp.bfloat16).reshape(lay.ctx, rows, D)
        padded = -(-rows // block) * block
        whole = jnp.pad(whole, ((0, 0), (0, padded - rows), (0, 0)))
        return whole.reshape(lay.ctx, lay.dp, padded // lay.dp, D)

    (part_out,) = scatter_attn(lay, own_blocks(grad_w_out, out_rows), None, 7)
    part_qkv, gains_sum = scatter_attn(
        lay, own_blocks(grad_w_qkv, qkv_rows), grad_gain_all.reshape(-1, 128), 8
    )
    part_out = part_out[:out_rows]
    part_qkv = part_qkv[:qkv_rows]
    place = (lax.axis_index("dp") * lay.ctx + lax.axis_index("ctx")) * gains.shape[0]
    part_gains = lax.dynamic_slice_in_dim(gains_sum.reshape(-1), place, gains.shape[0])
    owned = [
        lax.psum_scatter(
            piece, "ctx", scatter_dimension=0, tiled=True, axis_index_groups=lay.hi_groups
        )
        for piece in (grad_low, grad_w_gate, grad_w_up)
    ]
    part_gate_up, part_down = exchange_out(lay, owned[1], owned[2], owned[0], per, 9)
    part_gate_up = part_gate_up.reshape(w_gate_up.shape)
    part_down = part_down.reshape(w_down.shape)
    return (result, grad_input, part_qkv, part_out, part_gate_up, part_down, part_gains)


def solution(mesh):
    placed = (
        P("dp", "ctx", None),
        P("dp"),
        P("ctx", "dp"),
        P("ctx", "dp"),
        P("ctx", "dp"),
        P("ctx", "dp"),
        P(("dp", "ctx")),
        P("dp", "ctx", None),
    )
    return jax.shard_map(
        partial(per_device, Layout(mesh)),
        mesh=mesh,
        in_specs=placed,
        out_specs=(
            P("dp", "ctx", None),
            P("dp", "ctx", None),
            P("ctx", "dp"),
            P("ctx", "dp"),
            P("ctx", "dp"),
            P("ctx", "dp"),
            P(("dp", "ctx")),
        ),
        check_vma=False,
    )
```

```python
from functools import partial
import math

import jax
import jax.numpy as jnp
from jax import lax
from jax.experimental import pallas as pl
from jax.experimental.pallas import tpu as pltpu
from jax.sharding import PartitionSpec as P

D = 1152
HEADS = 4
HD = 256
WINDOW = 512
GROUP = 8

EPS = 1e-06
BIG = 1e30
MESH = pl.DeviceIdType.MESH
VMEM_LIMIT = 56 * 2**20


class Layout:
    def __init__(self, mesh):
        self.dp = mesh.shape["dp"]
        self.ctx = mesh.shape["ctx"]
        self.lo = max(1, GROUP // self.dp)
        self.hi = self.ctx // self.lo
        self.wide = self.dp // 2
        self.chips = self.wide * self.lo
        self.group = self.dp * self.lo
        self.hi_groups = [
            [h * self.lo + low for h in range(self.hi)] for low in range(self.lo)
        ]

    def place(self):
        dp = lax.axis_index("dp")
        ctx = lax.axis_index("ctx")
        chip = lax.rem(ctx, self.lo) * self.wide + dp // 2
        return chip, lax.rem(dp, 2), ctx // self.lo

    def offset(self, chip, k, sign=1):
        across = lax.rem(chip, self.wide) + self.wide + sign * (k % self.wide)
        low = chip // self.wide + self.lo + sign * (k // self.wide)
        return lax.rem(low, self.lo) * self.wide + lax.rem(across, self.wide)

    def back(self, k):
        return (-(k // self.wide)) % self.lo * self.wide + (-(k % self.wide)) % self.wide

    def device(self, chip, core, high):
        return (lax.rem(chip, self.wide) * 2 + core, high * self.lo + chip // self.wide)


def remote(src, dst, send, recv, device):
    return pltpu.make_async_remote_copy(
        src_ref=src, dst_ref=dst, send_sem=send, recv_sem=recv, device_id=device, device_id_type=MESH
    )


def greet(devices):
    barrier = pltpu.get_barrier_semaphore()
    for device in devices:
        pl.semaphore_signal(barrier, inc=1, device_id=device, device_id_type=MESH)
    pl.semaphore_wait(barrier, len(devices))


def gather_tokens_kernel(lay, own, out, local_sem, send, recv, core_send, core_recv):
    chip, core, high = lay.place()
    n = lay.chips
    peers = [lay.device(lay.offset(chip, k), core, high) for k in range(1, n)]
    partner = lay.device(chip, 1 - core, high)
    greet(peers + [partner])
    mine = chip * 2 + core
    pushes = [
        remote(own, out.at[mine], send.at[k], recv.at[k], peers[k]) for k in range(n - 1)
    ]
    for push in pushes:
        push.start()
    shares = [remote(own, out.at[mine], core_send.at[0], core_recv.at[0], partner)]
    shares[0].start()
    keep = pltpu.make_async_copy(own, out.at[mine], local_sem)
    keep.start()
    for k in range(1, n):
        source = lay.offset(chip, k, -1) * 2 + core
        pushes[k - 1].wait_recv()
        share = remote(out.at[source], out.at[source], core_send.at[k], core_recv.at[k], partner)
        share.start()
        shares.append(share)
    keep.wait()
    for push in pushes:
        push.wait_send()
    for share in shares:
        share.wait()


def gather_tokens(lay, value, collective_id):
    n = lay.chips
    return pl.pallas_call(
        partial(gather_tokens_kernel, lay),
        out_shape=jax.ShapeDtypeStruct((lay.group,) + value.shape, value.dtype),
        in_specs=[pl.BlockSpec(memory_space=pl.ANY)],
        out_specs=pl.BlockSpec(memory_space=pl.ANY),
        scratch_shapes=[
            pltpu.SemaphoreType.DMA,
            pltpu.SemaphoreType.DMA((n - 1,)),
            pltpu.SemaphoreType.DMA((n - 1,)),
            pltpu.SemaphoreType.DMA((n,)),
            pltpu.SemaphoreType.DMA((n,)),
        ],
        compiler_params=pltpu.CompilerParams(
            collective_id=collective_id, has_side_effects=True, vmem_limit_bytes=VMEM_LIMIT
        ),
    )(value)


def lane_tiles(cols):
    return [(first, min(128, cols - first)) for first in range(0, cols, 128)]


def weights_in_kernel(
    lay, pack, pairs, lows, attn_out, gate_out, up_out, low_out,
    attn_land, own, stack, land, lanes, keep_sem, attn_send, attn_recv, send, recv,
    chain_send, chain_recv, low_send, low_recv, core_send, core_recv,
):
    n = lay.dp
    hi, lo = lay.hi, lay.lo
    dp = lax.axis_index("dp")
    ctx = lax.axis_index("ctx")
    high, low = ctx // lo, lax.rem(ctx, lo)
    core = lax.rem(dp, 2)
    per, cols = lows.shape[1:]
    padded = gate_out.shape[0]
    targets = [lax.rem(dp + k, n) for k in range(n)]
    partner = (dp + 1 - 2 * core, ctx)
    low_peers = [(dp, high * lo + lax.rem(low + k, lo)) for k in range(1, lo)]
    right, left = (dp, ctx + lo), (dp, ctx - lo)
    has_right, has_left = high < hi - 1, high > 0
    barrier = pltpu.get_barrier_semaphore()
    for device in [(target, ctx) for target in targets[1:]] + low_peers:
        pl.semaphore_signal(barrier, inc=1, device_id=device, device_id_type=MESH)
    for there, device in ((has_right, right), (has_left, left)):
        @pl.when(there)
        def _():
            pl.semaphore_signal(barrier, inc=1, device_id=device, device_id_type=MESH)
    sides = jnp.where(has_right, 1, 0) + jnp.where(has_left, 1, 0)
    pl.semaphore_wait(barrier, n - 1 + len(low_peers) + sides)

    attn_pushes = []
    for k in range(1, n):
        push = remote(
            pack.at[lax.rem(targets[k], 2)], attn_land.at[dp], attn_send.at[k], attn_recv.at[k],
            (targets[k], ctx),
        )
        push.start()
        attn_pushes.append(push)
    attn_land[dp] = pack[core]
    blank = jnp.zeros((padded - per, cols), jnp.bfloat16)
    pushes = []

    def feed_forward(k):
        target = targets[k]
        for j, (first, width) in enumerate(lane_tiles(cols)):
            lanes[j, :, :width] = pairs[target, :, first : first + width]
        for i in range(3):
            for j, (first, width) in enumerate(lane_tiles(cols)):
                if i == 2:
                    piece = lows[target, :, first : first + width]
                else:
                    piece = lanes[j, pl.ds(i, per, stride=2), :][:, :width]
                if k:
                    stack[k - 1, i, :per, first : first + width] = piece.astype(jnp.bfloat16)
                else:
                    land[dp, i, :per, first : first + width] = piece.astype(jnp.bfloat16)
            if k:
                stack[k - 1, i, per:] = blank
            else:
                land[dp, i, per:] = blank
        if k:
            push = remote(stack.at[k - 1], land.at[dp], send.at[k], recv.at[k], (target, ctx))
            push.start()
            pushes.append(push)

    everything = [(0, 0, None, high)]
    for step in range(1, hi):
        everything.append((0, step, high - step >= 0, high - step))
        everything.append((1, step, high + step < hi, high + step))

    def to_core(source, c, slot):
        return remote(source, attn_out.at[c, core], core_send.at[slot], core_recv.at[slot], partner)

    def to_low(source, c, i):
        return [
            remote(source, attn_out.at[c, core], low_send.at[i, k], low_recv.at[i, k], low_peers[k])
            for k in range(lo - 1)
        ]

    def chain(source, c, side, step):
        return remote(
            source, attn_out.at[c, core], chain_send.at[side, step], chain_recv.at[side, step],
            right if side == 0 else left,
        )

    def sides_of(side, step):
        if step == hi - 1:
            return []
        return [s for s in ((0, has_right), (1, has_left)) if step == 0 or s[0] == side]

    def pass_own(i, side, step, where):
        c = where * lo + low
        source = attn_out.at[c, core] if step else own
        if step:
            chain(own, c, side, step - 1).wait_recv()
        for go, there in sides_of(side, step):
            @pl.when(there)
            def _():
                chain(source, c, go, step).start()
        for push in to_low(source, c, i):
            push.start()
        to_core(source, c, i * lo).start()

    def pass_low(i, side, step, where):
        for k in range(lo - 1):
            c = where * lo + lax.rem(low + lo - 1 - k, lo)
            to_low(own, c, i)[k].wait_recv()
            to_core(attn_out.at[c, core], c, i * lo + k + 1).start()

    def finish(i, side, step, where):
        c = where * lo + low
        for go, there in sides_of(side, step):
            @pl.when(there)
            def _():
                chain(own, c, go, step).wait_send()
        for push in to_low(own, c, i):
            push.wait_send()
        for k in range(lo):
            to_core(own, c, i * lo + k).wait()

    def each(stage, step):
        for i, (side, s, there, where) in enumerate(everything):
            if s == step:
                call = partial(stage, i, side, s, where)
                if s:
                    pl.when(there)(call)
                else:
                    call()

    order = list(range(2, n)) + [1, 0]
    feed_forward(order[0])
    for push in attn_pushes:
        push.wait_recv()
    for q in range(n):
        own[:, q * cols : (q + 1) * cols] = attn_land[q]
    keep = pltpu.make_async_copy(own, attn_out.at[ctx, core], keep_sem)
    keep.start()
    each(pass_own, 0)
    for k in order[1:]:
        feed_forward(k)
    for step in range(1, hi + 1):
        each(pass_own, step)
        each(pass_low, step - 1)
    for push in pushes:
        push.wait_recv()
    for q in range(n):
        for i, out in enumerate((gate_out, up_out, low_out)):
            out[:, q * cols : (q + 1) * cols] = land[q, i]
    keep.wait()
    for step in range(hi):
        each(finish, step)
    for push in attn_pushes + pushes:
        push.wait_send()


def weights_in(lay, pack, pairs, lows, collective_id):
    n, per, cols = lows.shape
    rows = pack.shape[1]
    padded = -(-per // 16) * 16
    count = 2 * lay.hi - 1
    wide = jax.ShapeDtypeStruct((padded, n * cols), jnp.bfloat16)
    vmem = pl.BlockSpec(memory_space=pltpu.VMEM)
    dma = pltpu.SemaphoreType.DMA
    scratch = [
        pltpu.VMEM((n, rows, cols), jnp.bfloat16),
        pltpu.VMEM((rows, n * cols), jnp.bfloat16),
        pltpu.VMEM((n - 1, 3, padded, cols), jnp.bfloat16),
        pltpu.VMEM((n, 3, padded, cols), jnp.bfloat16),
        pltpu.VMEM((len(lane_tiles(cols)), 2 * per, 128), jnp.float32),
        dma,
    ]
    for shape in ((n,), (n,), (2, lay.hi), (count, max(1, lay.lo - 1)), (count * lay.lo,)):
        scratch += [dma(shape), dma(shape)]
    return pl.pallas_call(
        partial(weights_in_kernel, lay),
        out_shape=(jax.ShapeDtypeStruct((lay.ctx, 2, rows, n * cols), jnp.bfloat16), wide, wide, wide),
        in_specs=[vmem] * 3,
        out_specs=(pl.BlockSpec(memory_space=pl.ANY),) + (vmem,) * 3,
        scratch_shapes=scratch,
        compiler_params=pltpu.CompilerParams(
            collective_id=collective_id, has_side_effects=True, vmem_limit_bytes=VMEM_LIMIT
        ),
    )(pack, pairs, lows)


def flip(index, bit):
    return index + bit * (1 - 2 * lax.rem(index // bit, 2))


def scatter_attn_kernel(lay, with_gains, *refs):
    refs = list(refs)
    parts = refs.pop(0)
    gains = refs.pop(0) if with_gains else None
    out = refs.pop(0)
    gains_out = refs.pop(0) if with_gains else None
    core_land, wide_sum, wide_land, keep, low_sum, low_land, hi_sum, hi_land, last, last_land = refs[:10]
    (core_send, core_recv, wide_send, wide_recv, low_send, low_recv, hi_send, hi_recv,
     last_send, last_recv) = refs[10:20]
    if with_gains:
        gains_sum, gains_land, gains_send, gains_recv = refs[20:]
    dp = lax.axis_index("dp")
    ctx = lax.axis_index("ctx")
    hi, lo, wide, n = lay.hi, lay.lo, lay.wide, lay.dp
    high, low = ctx // lo, lax.rem(ctx, lo)
    across, core = dp // 2, lax.rem(dp, 2)
    cols = out.shape[1]
    rows = parts.shape[2]
    partner = (across * 2 + 1 - core, ctx)
    low_peers = [(dp, high * lo + lax.rem(low + k, lo)) for k in range(1, lo)]
    wide_peers = [(lax.rem(across + k, wide) * 2 + core, ctx) for k in range(1, wide)]
    hi_peers = [(dp, lax.rem(high + k, hi) * lo + low) for k in range(1, hi)]
    last_peers = [(lax.rem(dp + k, n), ctx) for k in range(1, n)]
    steps = [1 << i for i in range((n - 1).bit_length())]
    gain_peers = [(flip(dp, bit), ctx) for bit in steps]
    gain_peers += [(dp, flip(ctx, 1 << i)) for i in range((lay.ctx - 1).bit_length())]
    greet(
        low_peers + hi_peers + last_peers + (gain_peers if with_gains else [])
    )

    order = [(k, a) for k in list(range(1, hi)) + [0] for a in list(range(1, lo)) + [0]]

    def block(k, a):
        return lax.rem(high + k, hi) * lo + lax.rem(low + a, lo)

    def slot(k, a):
        return k * lo + a

    sends = []
    core_copies = {}
    for k, a in order:
        for b in list(range(1, wide)) + [0]:
            there = lax.rem(across + b, wide)
            copy = remote(
                parts.at[block(k, a), there * 2 + 1 - core],
                core_land.at[slot(k, a), b],
                core_send.at[slot(k, a), b],
                core_recv.at[slot(k, a), b],
                partner,
            )
            copy.start()
            core_copies[k, a, b] = copy
            sends.append(copy)
    gain_copies = []

    def gains_step(i):
        if not with_gains or i > len(gain_peers):
            return
        if i == 0:
            gains_sum[0] = gains[...]
        else:
            gain_copies[i - 1].wait_recv()
            gains_sum[i] = gains_sum[i - 1] + gains_land[i - 1]
        if i < len(gain_peers):
            copy = remote(
                gains_sum.at[i], gains_land.at[i], gains_send.at[i], gains_recv.at[i], gain_peers[i]
            )
            copy.start()
            gain_copies.append(copy)
            sends.append(copy)
        else:
            gains_out[...] = gains_sum[i]

    wide_copies, low_copies, hi_copies = {}, {}, {}

    def sum_cores(k, a):
        s = slot(k, a)
        for b in list(range(1, wide)) + [0]:
            there = lax.rem(across + b, wide)
            core_copies[k, a, b].wait_recv()
            total = parts[block(k, a), there * 2 + core].astype(jnp.float32) + core_land[
                s, b
            ].astype(jnp.float32)
            if b:
                wide_sum[s, b - 1] = total.astype(jnp.bfloat16)
                copy = remote(
                    wide_sum.at[s, b - 1], wide_land.at[s, b - 1], wide_send.at[s, b - 1],
                    wide_recv.at[s, b - 1], wide_peers[b - 1],
                )
                copy.start()
                wide_copies[k, a, b] = copy
                sends.append(copy)
            else:
                keep[s] = total

    def sum_wide(k, a):
        s = slot(k, a)
        total = keep[s]
        for b in range(1, wide):
            wide_copies[k, a, b].wait_recv()
            total = total + wide_land[s, b - 1].astype(jnp.float32)
        if a:
            low_sum[k, a - 1] = total.astype(jnp.bfloat16)
            copy = remote(
                low_sum.at[k, a - 1], low_land.at[k, a - 1], low_send.at[k, a - 1],
                low_recv.at[k, a - 1], low_peers[a - 1],
            )
            copy.start()
            low_copies[k, a] = copy
            sends.append(copy)
        else:
            keep[s] = total

    def sum_low(k):
        total = keep[slot(k, 0)]
        for a in range(1, lo):
            low_copies[k, a].wait_recv()
            total = total + low_land[k, a - 1].astype(jnp.float32)
        if k:
            hi_sum[k - 1] = total.astype(jnp.bfloat16)
            copy = remote(
                hi_sum.at[k - 1], hi_land.at[k - 1], hi_send.at[k - 1], hi_recv.at[k - 1], hi_peers[k - 1]
            )
            copy.start()
            hi_copies[k] = copy
            sends.append(copy)
        else:
            keep[slot(0, 0)] = total

    gains_step(0)
    ks = list(range(1, hi)) + [0]
    offsets = list(range(1, lo)) + [0]
    for i in range(hi + 2):
        if i < hi:
            for a in offsets:
                sum_cores(ks[i], a)
        gains_step(i + 1)
        if 1 <= i <= hi:
            for a in offsets:
                sum_wide(ks[i - 1], a)
        if 2 <= i:
            sum_low(ks[i - 2])
    for i in range(hi + 3, len(gain_peers) + 1):
        gains_step(i)
    total = keep[slot(0, 0)]
    for k in range(1, hi):
        hi_copies[k].wait_recv()
        total = total + hi_land[k - 1].astype(jnp.float32)
    keep[slot(0, 0)] = total
    for q in range(n):
        last[q] = keep[slot(0, 0), :, q * cols : (q + 1) * cols].astype(jnp.bfloat16)
    last_copies = []
    for k in range(1, n):
        copy = remote(
            last.at[lax.rem(dp + k, n)], last_land.at[dp], last_send.at[k], last_recv.at[k], last_peers[k - 1]
        )
        copy.start()
        last_copies.append(copy)
        sends.append(copy)
    last_land[dp] = last[dp]
    for copy in last_copies:
        copy.wait_recv()
    for q in range(n):
        out[q * rows : (q + 1) * rows] = last_land[q].astype(jnp.float32)
    for copy in sends:
        copy.wait_send()


def scatter_attn(lay, parts, gains, collective_id):
    rows = parts.shape[2]
    cols = D // lay.dp
    with_gains = gains is not None
    lows, wides, his = max(1, lay.lo - 1), max(1, lay.wide - 1), max(1, lay.hi - 1)
    vmem = pl.BlockSpec(memory_space=pltpu.VMEM)
    dma = pltpu.SemaphoreType.DMA
    out_shape = [jax.ShapeDtypeStruct((lay.dp * rows, cols), jnp.float32)]
    scratch = [
        pltpu.VMEM((lay.ctx, lay.wide, rows, D), jnp.bfloat16),
        pltpu.VMEM((lay.ctx, wides, rows, D), jnp.bfloat16),
        pltpu.VMEM((lay.ctx, wides, rows, D), jnp.bfloat16),
        pltpu.VMEM((lay.ctx, rows, D), jnp.float32),
        pltpu.VMEM((lay.hi, lows, rows, D), jnp.bfloat16),
        pltpu.VMEM((lay.hi, lows, rows, D), jnp.bfloat16),
        pltpu.VMEM((his, rows, D), jnp.bfloat16),
        pltpu.VMEM((his, rows, D), jnp.bfloat16),
        pltpu.VMEM((lay.dp, rows, cols), jnp.bfloat16),
        pltpu.VMEM((lay.dp, rows, cols), jnp.bfloat16),
    ]
    for shape in ((lay.ctx, lay.wide), (lay.ctx, wides), (lay.hi, lows), (his,), (lay.dp,)):
        scratch += [dma(shape), dma(shape)]
    if with_gains:
        count = (lay.dp - 1).bit_length() + (lay.ctx - 1).bit_length()
        out_shape.append(jax.ShapeDtypeStruct(gains.shape, jnp.float32))
        scratch += [
            pltpu.VMEM((count + 1,) + gains.shape, jnp.float32),
            pltpu.VMEM((count,) + gains.shape, jnp.float32),
            dma((count,)),
            dma((count,)),
        ]
    return pl.pallas_call(
        partial(scatter_attn_kernel, lay, with_gains),
        out_shape=tuple(out_shape),
        in_specs=[vmem] * (2 if with_gains else 1),
        out_specs=(vmem,) * len(out_shape),
        scratch_shapes=scratch,
        compiler_params=pltpu.CompilerParams(
            collective_id=collective_id, has_side_effects=True, vmem_limit_bytes=VMEM_LIMIT
        ),
    )(*([parts, gains] if with_gains else [parts]))


def exchange_out_kernel(lay, gate, up, down, pairs_out, lows_out, stack, land, lanes, send, recv):
    n = lay.dp
    dp = lax.axis_index("dp")
    ctx = lax.axis_index("ctx")
    cols = lows_out.shape[2]
    per = lows_out.shape[1]
    greet([(lax.rem(dp + k, n), ctx) for k in range(1, n)])
    for q in range(n):
        for i, piece in enumerate((gate, up, down)):
            stack[q, i] = piece[:, q * cols : (q + 1) * cols]
    pushes = []
    for k in range(1, n):
        target = lax.rem(dp + k, n)
        push = remote(stack.at[target], land.at[dp], send.at[k], recv.at[k], (target, ctx))
        push.start()
        pushes.append(push)
    land[dp] = stack[dp]
    for push in pushes:
        push.wait_recv()
    for q in range(n):
        for j, (first, width) in enumerate(lane_tiles(cols)):
            for i in range(2):
                piece = land[q, i, :per, first : first + width].astype(jnp.float32)
                if width < 128:
                    piece = jnp.concatenate(
                        [piece, jnp.zeros((per, 128 - width), jnp.float32)], axis=1
                    )
                lanes[j, pl.ds(i, per, stride=2), :] = piece
            pairs_out[q, :, first : first + width] = lanes[j, :, :width]
        lows_out[q] = land[q, 2, :per].astype(jnp.float32)
    for push in pushes:
        push.wait_send()


def exchange_out(lay, gate, up, down, per, collective_id):
    padded = gate.shape[0]
    n, cols = lay.dp, gate.shape[1] // lay.dp
    vmem = pl.BlockSpec(memory_space=pltpu.VMEM)
    return pl.pallas_call(
        partial(exchange_out_kernel, lay),
        out_shape=(
            jax.ShapeDtypeStruct((n, 2 * per, cols), jnp.float32),
            jax.ShapeDtypeStruct((n, per, cols), jnp.float32),
        ),
        in_specs=[vmem] * 3,
        out_specs=(vmem,) * 2,
        scratch_shapes=[
            pltpu.VMEM((n, 3, padded, cols), jnp.bfloat16),
            pltpu.VMEM((n, 3, padded, cols), jnp.bfloat16),
            pltpu.VMEM((len(lane_tiles(cols)), 2 * per, 128), jnp.float32),
            pltpu.SemaphoreType.DMA((n,)),
            pltpu.SemaphoreType.DMA((n,)),
        ],
        compiler_params=pltpu.CompilerParams(
            collective_id=collective_id, has_side_effects=True, vmem_limit_bytes=VMEM_LIMIT
        ),
    )(gate, up, down)


def in_tiles(total, size, body):
    whole = total // size

    def step(i, carry):
        body(pl.multiple_of(i * size, size), size)
        return carry

    if whole:
        lax.fori_loop(0, whole, step, 0)
    if total % size:
        body(whole * size, total % size)


def dot_nt(left, right):
    return lax.dot_general(left, right, (((1,), (1,)), ((), ())), preferred_element_type=jnp.float32)


def dot_nn(left, right):
    return lax.dot_general(left, right, (((1,), (0,)), ((), ())), preferred_element_type=jnp.float32)


ROOT = math.sqrt(2.0 / math.pi)


def feed_forward_kernel(
    lay, mid, w_gate, w_up, w_down, mixed, cotangent, valid, gain,
    result, grad_mid, gate_t, up_t, grad_gain, dw_gate, dw_up, dw_down,
    act, slope, hidden, hidden_t, grads, parts, core_land, sums, landed, total, dy, sem,
    core_send, core_recv, send, recv, share_send, share_recv, dy_send, dy_recv,
):
    chip, core, high = lay.place()
    n = lay.chips
    tokens = mixed.shape[0]
    units = w_gate.shape[0]
    places = [lay.offset(chip, k) for k in range(n)]
    sources = [lay.offset(chip, k, -1) for k in range(n)]
    peers = [lay.device(place, core, high) for place in places]
    partner = lay.device(chip, 1 - core, high)
    mine = pl.ds(pl.multiple_of(core * tokens, tokens), tokens)
    theirs = pl.ds(pl.multiple_of((1 - core) * tokens, tokens), tokens)
    greet(peers[1:] + [partner])

    def to_partner(phase, k):
        return remote(
            parts.at[places[k], theirs], core_land.at[k], core_send.at[phase, k], core_recv.at[phase, k], partner
        )

    def to_owner(phase, k):
        return remote(
            sums.at[k - 1], landed.at[k - 1], send.at[phase, k], recv.at[phase, k], peers[k]
        )

    def add_core(phase, k):
        to_partner(phase, k).wait_recv()

        def chunk(first, rows):
            span = pl.ds(first, rows)
            here = pl.ds(pl.multiple_of(core * tokens + first, rows), rows)
            both = parts[places[k], here].astype(jnp.float32) + core_land[k, span].astype(jnp.float32)
            if k:
                sums[k - 1, span] = both.astype(jnp.bfloat16)
            else:
                total[span] = both

        in_tiles(tokens, 32, chunk)
        if k:
            to_owner(phase, k).start()

    def add_owners(phase):
        for k in range(1, n):
            to_owner(phase, k).wait_recv()

        def chunk(first, rows):
            span = pl.ds(first, rows)
            value = total[span]
            for k in range(1, n):
                value = value + landed[k - 1, span].astype(jnp.float32)
            total[span] = value

        in_tiles(tokens, 32, chunk)

    def settle(phase):
        for k in range(n):
            to_partner(phase, k).wait_send()
            if k:
                to_owner(phase, k).wait_send()

    def forward(c):
        def tile(first, width):
            rows = pl.ds(first, width)
            weights = jnp.concatenate([w_gate[rows], w_up[rows]], axis=0)
            both = dot_nt(mid[c], weights)
            gate, up = both[:, :width], both[:, width:]
            square = gate * gate
            tanh = jnp.tanh(ROOT * gate * (1.0 + 0.044715 * square))
            half = 0.5 * (1.0 + tanh)
            active = gate * half
            slant = half + 0.5 * gate * (1.0 - tanh * tanh) * (ROOT * (1.0 + 3.0 * 0.044715 * square))
            product = (active * up).astype(jnp.bfloat16)
            act[c, :, rows] = active.astype(jnp.bfloat16)
            slope[c, :, rows] = (slant * up).astype(jnp.bfloat16)
            hidden[:, rows] = product
            hidden_t[c, rows] = product.T

        in_tiles(units, 128, tile)

        def out_tile(first, width):
            lanes = pl.ds(first, width)
            parts[c, :, lanes] = dot_nn(hidden[...], w_down[:, lanes]).astype(jnp.bfloat16)

        in_tiles(D, 256, out_tile)

    def backward(c):
        def tile(first, width):
            rows = pl.ds(first, width)
            grad = dot_nt(dy[c], w_down[rows])
            up_grad = (grad * act[c, :, rows].astype(jnp.float32)).astype(jnp.bfloat16)
            gate_grad = (grad * slope[c, :, rows].astype(jnp.float32)).astype(jnp.bfloat16)
            grads[0, :, rows] = gate_grad
            grads[1, :, rows] = up_grad
            gate_t[c, rows] = gate_grad.T
            up_t[c, rows] = up_grad.T

        in_tiles(units, 256, tile)

        def out_tile(first, width):
            lanes = pl.ds(first, width)
            both = dot_nn(grads[0], w_gate[:, lanes]) + dot_nn(grads[1], w_up[:, lanes])
            parts[c, :, lanes] = both.astype(jnp.bfloat16)

        in_tiles(D, 256, out_tile)

    order = list(range(n - 1, 0, -1)) + [0]
    for i, k in enumerate(order):
        forward(places[k])
        to_partner(0, k).start()
        if i:
            add_core(0, order[i - 1])
    add_core(0, order[-1])
    add_owners(0)

    grad_gain[...] = jnp.zeros_like(grad_gain)
    scale = 1.0 + gain[...]

    def finish(first, rows):
        span = pl.ds(first, rows)
        here = pl.ds(pl.multiple_of(core * tokens + first, rows), rows)
        y = total[span]
        ok = valid[span]
        rate = lax.rsqrt(jnp.mean(y * y, axis=-1, keepdims=True) + EPS)
        unit = y * rate
        result[span] = ((mixed[span] + unit * scale) * ok).astype(jnp.bfloat16)
        upstream = cotangent[span].astype(jnp.float32) * ok
        down = upstream * unit
        for r in range(0, rows, 8):
            grad_gain[...] += down[r : r + 8]
        scaled = upstream * scale
        inner = jnp.mean(scaled * unit, axis=-1, keepdims=True)
        dy[chip, here] = (rate * (scaled - unit * inner)).astype(jnp.bfloat16)

    in_tiles(tokens, 32, finish)

    pushes = [None] + [
        remote(dy.at[chip, mine], dy.at[chip, mine], dy_send.at[k], dy_recv.at[k], peers[k])
        for k in range(1, n)
    ]
    shares = [
        remote(dy.at[sources[k], mine], dy.at[sources[k], mine], share_send.at[k], share_recv.at[k], partner)
        for k in range(n)
    ]
    for push in pushes[1:]:
        push.start()
    shares[0].start()
    settle(0)
    for i in range(n):
        k = lay.back(i)
        if i:
            pushes[i].wait_recv()
            shares[i].start()
        shares[i].wait_recv()
        backward(sources[i])
        to_partner(1, k).start()
        if i:
            add_core(1, lay.back(i - 1))
    add_core(1, lay.back(n - 1))

    def weight_grad(left_ref, right, out):
        def tile(first, width):
            lanes = pl.ds(first, width)
            value = dot_nn(left_ref[0], right[0, :, lanes])
            for c in range(1, n):
                value = value + dot_nn(left_ref[c], right[c, :, lanes])
            out[:, lanes] = value.astype(jnp.bfloat16)

        in_tiles(D, 256, tile)

    weight_grad(hidden_t, dy, dw_down)
    weight_grad(gate_t, mid, dw_gate)
    weight_grad(up_t, mid, dw_up)
    add_owners(1)
    grad_mid[...] = total[...]
    settle(1)
    for k in range(n):
        if k:
            pushes[k].wait_send()
        shares[k].wait_send()


def feed_forward(lay, mid, w_gate, w_up, w_down, mixed, cotangent, valid, gain, collective_id):
    n = lay.chips
    tokens = mixed.shape[0]
    units = w_gate.shape[0]
    low, high = jnp.bfloat16, jnp.float32
    vmem = pl.BlockSpec(memory_space=pltpu.VMEM)
    dma = pltpu.SemaphoreType.DMA
    dw = jax.ShapeDtypeStruct((units, D), low)
    out_shape = (
        jax.ShapeDtypeStruct((tokens, D), low),
        jax.ShapeDtypeStruct((tokens, D), high),
        jax.ShapeDtypeStruct((8, D), high),
        dw,
        dw,
        dw,
    )

    def kernel(*refs):
        ins, outs, scratch = refs[:8], refs[8:14], list(refs[14:])
        gate_t, up_t = scratch.pop(0), scratch.pop(0)
        feed_forward_kernel(
            lay, *ins, outs[0], outs[1], gate_t, up_t, *outs[2:], *scratch[:11], None, *scratch[11:]
        )

    return pl.pallas_call(
        kernel,
        out_shape=out_shape,
        in_specs=[vmem] * 8,
        out_specs=(vmem,) * 6,
        scratch_shapes=[
            pltpu.VMEM((n, units, 2 * tokens), low),
            pltpu.VMEM((n, units, 2 * tokens), low),
            pltpu.VMEM((n, 2 * tokens, units), low),
            pltpu.VMEM((n, 2 * tokens, units), low),
            pltpu.VMEM((2 * tokens, units), low),
            pltpu.VMEM((n, units, 2 * tokens), low),
            pltpu.VMEM((2, 2 * tokens, units), low),
            pltpu.VMEM((n, 2 * tokens, D), low),
            pltpu.VMEM((n, tokens, D), low),
            pltpu.VMEM((max(1, n - 1), tokens, D), low),
            pltpu.VMEM((max(1, n - 1), tokens, D), low),
            pltpu.VMEM((tokens, D), high),
            pltpu.VMEM((n, 2 * tokens, D), low),
        ]
        + [dma((2, n))] * 4
        + [dma((n,))] * 4,
        compiler_params=pltpu.CompilerParams(
            collective_id=collective_id, has_side_effects=True, vmem_limit_bytes=63 * 2**20
        ),
    )(
        mid.reshape(n, 2 * tokens, D), w_gate, w_up, w_down, mixed, cotangent, valid, gain
    )


def shifted(value, axis, steps):
    count = lax.axis_size(axis)
    leading, last = (max(0, -steps), min(count, count - steps))
    return lax.ppermute(value, axis, [(source, source + steps) for source in range(leading, last)])


def norm_scaled(v, gain):
    return v * lax.rsqrt(jnp.mean(v * v, axis=-1, keepdims=True) + EPS) * (1.0 + gain)


def rotate(v, angle):
    half = v.shape[-1] // 2
    cosine = jnp.cos(angle)
    sine = jnp.sin(angle)
    first = v[..., :half]
    second = v[..., half:]
    return jnp.concatenate(
        [first * cosine - second * sine, second * cosine + first * sine], axis=-1
    )


def angles_of(positions):
    inverse = 1.0 / 10000.0 ** (jnp.arange(HD // 2, dtype=jnp.float32) * (2.0 / HD))
    return positions.astype(jnp.float32)[:, None] * inverse[None, :]


def head_inputs(projected, gain_query, gain_key, angle):
    query = projected[..., : HEADS * HD].reshape(projected.shape[:-1] + (HEADS, HD))
    key_rows = projected[..., HEADS * HD : (HEADS + 1) * HD]
    value_rows = projected[..., (HEADS + 1) * HD :]
    query = rotate(norm_scaled(query, gain_query), angle[:, None, :])
    key_rows = rotate(norm_scaled(key_rows, gain_key), angle)
    return (query, key_rows, value_rows)


def contract(left, right, dims_left, dims_right):
    return lax.dot_general(
        left, right, ((dims_left, dims_right), ((), ())), preferred_element_type=jnp.float32
    )


def per_device(lay, tokens, lengths, w_qkv, w_out, w_gate_up, w_down, gains, cotangent):
    seq_count = tokens.shape[0]
    local_len = tokens.shape[1]
    reach = (WINDOW - 1) // local_len + 1
    scale = 1.0 / math.sqrt(HD)
    units = w_down.shape[0]
    per = units // lay.dp
    qkv_rows, out_rows = w_qkv.shape[0], w_out.shape[0]
    cols = w_qkv.shape[1]
    used = qkv_rows + out_rows + 1
    pack_rows = -(-used // 32) * 32
    gain_row = jnp.pad(gains, (0, cols - gains.shape[0]))[None]
    pack = jnp.concatenate(
        [w_qkv, w_out, gain_row, jnp.zeros((pack_rows - used, cols), jnp.float32)], axis=0
    ).astype(jnp.bfloat16)
    attn_all, gate_rows, up_rows, low_rows = weights_in(
        lay,
        pack.reshape(2, pack_rows // 2, cols),
        w_gate_up.reshape(lay.dp, 2 * per, cols),
        w_down.reshape(lay.dp, per, cols),
        5,
    )
    w_gate, w_up, w_low = (
        lax.all_gather(rows, "ctx", axis=0, tiled=True, axis_index_groups=lay.hi_groups)
        for rows in (gate_rows, up_rows, low_rows)
    )
    attn_all = attn_all.reshape(lay.ctx, pack_rows, D)
    full_qkv = attn_all[:, :qkv_rows].reshape(lay.ctx * qkv_rows, D)
    full_out = attn_all[:, qkv_rows : qkv_rows + out_rows].reshape(lay.ctx * out_rows, D)
    gain_all = (
        attn_all[:, used - 1]
        .reshape(lay.ctx, lay.dp, cols)[:, :, : gains.shape[0]]
        .transpose(1, 0, 2)
        .reshape(-1)
        .astype(jnp.float32)
    )
    gain_in = gain_all[:D]
    gain_attn = gain_all[D : 2 * D]
    gain_pre = gain_all[2 * D : 3 * D]
    gain_post = gain_all[3 * D : 4 * D]
    gain_query = gain_all[4 * D : 4 * D + HD]
    gain_key = gain_all[4 * D + HD :]
    offset = lax.axis_index("ctx") * local_len
    positions = offset + jnp.arange(local_len, dtype=jnp.int32)
    angle = angles_of(positions)
    valid = positions[None, :] < lengths[:, None]
    inputs = tokens.astype(jnp.float32)
    normed_in, pull_in = jax.vjp(norm_scaled, inputs, gain_in)
    normed_low = normed_in.astype(jnp.bfloat16)
    projected = contract(normed_low, full_qkv, (2,), (1,))
    (query, key_rot, value_rows), pull_heads = jax.vjp(
        partial(head_inputs, angle=angle), projected, gain_query, gain_key
    )
    query_low = query.astype(jnp.bfloat16)
    own_pair = jnp.concatenate(
        [key_rot.astype(jnp.bfloat16), value_rows.astype(jnp.bfloat16)], axis=-1
    )
    earlier = []
    for distance in range(reach, 0, -1):
        earlier.append(shifted(own_pair, "ctx", distance))
    key_pairs = jnp.concatenate(earlier + [own_pair], axis=1)
    keys_low = key_pairs[..., :HD]
    values_low = key_pairs[..., HD:]
    key_pos = offset - reach * local_len + jnp.arange((reach + 1) * local_len, dtype=jnp.int32)
    key_grid = key_pos[None, None, :]
    query_grid = positions[None, :, None]
    allowed = (
        (key_grid >= 0)
        & (key_grid <= query_grid)
        & (query_grid - key_grid < WINDOW)
        & ((key_grid < lengths[:, None, None]) | (key_grid == query_grid))
    )

    def scores_of():
        raw = jnp.einsum("schd,skd->shck", query_low, keys_low, preferred_element_type=jnp.float32)
        return jnp.where(allowed[:, None], raw * scale, -BIG)

    scores = scores_of()
    top = jnp.max(scores, axis=-1, keepdims=True)
    expo = jnp.exp(scores - top)
    total = jnp.sum(expo, axis=-1, keepdims=True)
    probs = expo / total
    log_total = top + jnp.log(total)
    probs_low = probs.astype(jnp.bfloat16)
    attended = jnp.einsum(
        "shck,skd->schd", probs_low, values_low, preferred_element_type=jnp.float32
    )
    attended_low = attended.reshape(seq_count, local_len, HEADS * HD).astype(jnp.bfloat16)
    out_proj = contract(attended_low, full_out, (2,), (0,))
    normed_out, pull_out = jax.vjp(norm_scaled, out_proj, gain_attn)
    mixed = inputs + normed_out
    normed_mid, pull_mid = jax.vjp(norm_scaled, mixed, gain_pre)
    mid_low = normed_mid.astype(jnp.bfloat16)
    token_count = seq_count * local_len
    mid_all = gather_tokens(lay, mid_low.reshape(token_count, D), 1)
    result, grad_mid, grad_gain_post, grad_w_gate, grad_w_up, grad_low = feed_forward(
        lay,
        mid_all,
        w_gate,
        w_up,
        w_low,
        mixed.reshape(token_count, D),
        cotangent.reshape(token_count, D),
        valid.reshape(token_count, 1).astype(jnp.float32),
        gain_post[None],
        2,
    )
    result = result.reshape(mixed.shape)
    grad_mid = grad_mid.reshape(mixed.shape)
    grad_gain_post = jnp.sum(grad_gain_post, axis=0)
    upstream = jnp.where(valid[..., None], cotangent.astype(jnp.float32), 0.0)
    grad_mixed_in, grad_gain_pre = pull_mid(grad_mid)
    grad_mixed = upstream + grad_mixed_in
    grad_proj, grad_gain_attn = pull_out(grad_mixed)
    proj_low = grad_proj.astype(jnp.bfloat16)
    grad_attended = contract(proj_low, full_out, (2,), (1,))
    grad_w_out = contract(attended_low, proj_low, (0, 1), (0, 1))
    attn_low = grad_attended.astype(jnp.bfloat16).reshape(seq_count, local_len, HEADS, HD)
    again_probs = jnp.exp(scores_of() - log_total)
    again_low = again_probs.astype(jnp.bfloat16)
    grad_values = jnp.einsum(
        "shck,schd->skd", again_low, attn_low, preferred_element_type=jnp.float32
    )
    grad_probs = jnp.einsum(
        "schd,skd->shck", attn_low, values_low, preferred_element_type=jnp.float32
    )
    row_dot = jnp.sum(again_probs * grad_probs, axis=-1, keepdims=True)
    grad_scores = (scale * again_probs * (grad_probs - row_dot)).astype(jnp.bfloat16)
    grad_query = jnp.einsum(
        "shck,skd->schd", grad_scores, keys_low, preferred_element_type=jnp.float32
    )
    grad_keys = jnp.einsum(
        "shck,schd->skd", grad_scores, query_low, preferred_element_type=jnp.float32
    )
    grad_pairs = jnp.concatenate([grad_keys, grad_values], axis=-1)
    own_grad = grad_pairs[:, reach * local_len :]
    for distance in range(1, reach + 1):
        piece = grad_pairs[:, (reach - distance) * local_len : (reach - distance + 1) * local_len]
        own_grad = own_grad + shifted(piece.astype(jnp.bfloat16), "ctx", -distance).astype(
            piece.dtype
        )
    grad_projected, grad_gain_query, grad_gain_key = pull_heads(
        (grad_query, own_grad[..., :HD], own_grad[..., HD:])
    )
    qkv_low = grad_projected.astype(jnp.bfloat16)
    grad_w_qkv = contract(qkv_low, normed_low, (0, 1), (0, 1))
    grad_normed = contract(qkv_low, full_qkv, (2,), (0,))
    grad_in_norm, grad_gain_in = pull_in(grad_normed)
    grad_input = grad_mixed + grad_in_norm
    grad_gain_all = jnp.concatenate(
        [
            grad_gain_in,
            grad_gain_attn,
            grad_gain_pre,
            grad_gain_post,
            grad_gain_query,
            grad_gain_key,
        ]
    )
    block = 16 * lay.dp
    sum_rows = -(-(qkv_rows + out_rows) // block) * block
    partial_sums = jnp.concatenate(
        [
            grad_w_qkv.astype(jnp.bfloat16).reshape(lay.ctx, qkv_rows, D),
            grad_w_out.astype(jnp.bfloat16).reshape(lay.ctx, out_rows, D),
            jnp.zeros((lay.ctx, sum_rows - qkv_rows - out_rows, D), jnp.bfloat16),
        ],
        axis=1,
    ).reshape(lay.ctx, lay.dp, sum_rows // lay.dp, D)
    part_attn, gains_sum = scatter_attn(lay, partial_sums, grad_gain_all.reshape(-1, 128), 8)
    part_qkv = part_attn[:qkv_rows]
    part_out = part_attn[qkv_rows : qkv_rows + out_rows]
    place = (lax.axis_index("dp") * lay.ctx + lax.axis_index("ctx")) * gains.shape[0]
    part_gains = lax.dynamic_slice_in_dim(gains_sum.reshape(-1), place, gains.shape[0])
    owned = [
        lax.psum_scatter(
            piece, "ctx", scatter_dimension=0, tiled=True, axis_index_groups=lay.hi_groups
        )
        for piece in (grad_low, grad_w_gate, grad_w_up)
    ]
    part_gate_up, part_down = exchange_out(lay, owned[1], owned[2], owned[0], per, 9)
    part_gate_up = part_gate_up.reshape(w_gate_up.shape)
    part_down = part_down.reshape(w_down.shape)
    return (result, grad_input, part_qkv, part_out, part_gate_up, part_down, part_gains)


def solution(mesh):
    placed = (
        P("dp", "ctx", None),
        P("dp"),
        P("ctx", "dp"),
        P("ctx", "dp"),
        P("ctx", "dp"),
        P("ctx", "dp"),
        P(("dp", "ctx")),
        P("dp", "ctx", None),
    )
    return jax.shard_map(
        partial(per_device, Layout(mesh)),
        mesh=mesh,
        in_specs=placed,
        out_specs=(
            P("dp", "ctx", None),
            P("dp", "ctx", None),
            P("ctx", "dp"),
            P("ctx", "dp"),
            P("ctx", "dp"),
            P("ctx", "dp"),
            P(("dp", "ctx")),
        ),
        check_vma=False,
    )
```

```python
from functools import partial
import math

import jax
import jax.numpy as jnp
from jax import lax
from jax.experimental import pallas as pl
from jax.experimental.pallas import tpu as pltpu
from jax.sharding import PartitionSpec as P

D = 1152
HEADS = 4
HD = 256
WINDOW = 512
GROUP = 8

EPS = 1e-06
BIG = 1e30
MESH = pl.DeviceIdType.MESH
VMEM_LIMIT = 56 * 2**20


class Layout:
    def __init__(self, mesh):
        self.dp = mesh.shape["dp"]
        self.ctx = mesh.shape["ctx"]
        self.lo = max(1, GROUP // self.dp)
        self.hi = self.ctx // self.lo
        self.wide = self.dp // 2
        self.chips = self.wide * self.lo
        self.group = self.dp * self.lo
        self.hi_groups = [
            [h * self.lo + low for h in range(self.hi)] for low in range(self.lo)
        ]

    def place(self):
        dp = lax.axis_index("dp")
        ctx = lax.axis_index("ctx")
        chip = lax.rem(ctx, self.lo) * self.wide + dp // 2
        return chip, lax.rem(dp, 2), ctx // self.lo

    def offset(self, chip, k, sign=1):
        across = lax.rem(chip, self.wide) + self.wide + sign * (k % self.wide)
        low = chip // self.wide + self.lo + sign * (k // self.wide)
        return lax.rem(low, self.lo) * self.wide + lax.rem(across, self.wide)

    def straight(self):
        return list(range(1, self.wide)) + [low * self.wide for low in range(1, self.lo)]

    def bent(self):
        return [k for k in range(1, self.chips) if k not in self.straight()]

    def position(self, k):
        return (self.bent() + self.straight() + [0]).index(k)

    def device(self, chip, core, high):
        return (lax.rem(chip, self.wide) * 2 + core, high * self.lo + chip // self.wide)


def remote(src, dst, send, recv, device):
    return pltpu.make_async_remote_copy(
        src_ref=src, dst_ref=dst, send_sem=send, recv_sem=recv, device_id=device, device_id_type=MESH
    )


def greet(devices):
    barrier = pltpu.get_barrier_semaphore()
    for device in devices:
        pl.semaphore_signal(barrier, inc=1, device_id=device, device_id_type=MESH)
    pl.semaphore_wait(barrier, len(devices))


def gather_group_kernel(lay, slot, own, out, local_sem, send, recv, pass_send, core_send, core_recv):
    chip, core, high = lay.place()
    n = lay.chips
    half = own.shape[0] // 2
    halves = (pl.ds(0, half), pl.ds(half, half))
    peers = [lay.device(lay.offset(chip, k), core, high) for k in range(n)]
    sources = [lay.offset(chip, k, -1) for k in range(n)]
    partner = lay.device(chip, 1 - core, high)
    greet(peers[1:] + [partner])
    mine = [slot(out, k, chip, core) for k in range(n)]
    straight, bent = lay.straight(), lay.bent()
    keep = pltpu.make_async_copy(own, mine[0], local_sem)
    keep.start()
    pushes = []

    def push(k, h, source, target, sem):
        copy = remote(source.at[halves[h]], target.at[halves[h]], sem, recv.at[k, h], peers[k])
        return copy

    ordered = [(k, i if k < lay.wide else 1 - i) for i in range(2) for k in straight]
    for k, h in ordered:
        copy = push(k, h, own, mine[k], send.at[k, h])
        copy.start()
        pushes.append(copy)
    shares = [remote(own, mine[0], core_send.at[0], core_recv.at[0], partner)]
    shares[0].start()

    def arrived(k, h):
        copy = remote(own.at[halves[h]], mine[k].at[halves[h]], send.at[k, h], recv.at[k, h], peers[k])
        copy.wait_recv()

    for k, h in ordered:
        arrived(k, h)
        block = slot(out, k, sources[k], core)
        if k < lay.wide and h == 0:
            onward = [b * lay.wide for b in range(1, lay.lo)]
        elif k >= lay.wide and h == 1:
            onward = list(range(1, lay.wide))
        else:
            onward = []
        for step in onward:
            total = k + step
            there = slot(out, total, sources[k], core)
            copy = remote(
                block.at[halves[h]], there.at[halves[h]], pass_send.at[total, h], recv.at[total, h], peers[step]
            )
            copy.start()
            pushes.append(copy)
    for k in straight + bent:
        if k in bent:
            for h in range(2):
                arrived(k, h)
        block = slot(out, k, sources[k], core)
        share = remote(block, block, core_send.at[k], core_recv.at[k], partner)
        share.start()
        shares.append(share)
    keep.wait()
    for copy in pushes:
        copy.wait_send()
    for share in shares:
        share.wait()


def gather_group(lay, value, out_shape, slot, collective_id):
    n = lay.chips
    dma = pltpu.SemaphoreType.DMA
    return pl.pallas_call(
        partial(gather_group_kernel, lay, slot),
        out_shape=jax.ShapeDtypeStruct(out_shape, value.dtype),
        in_specs=[pl.BlockSpec(memory_space=pl.ANY)],
        out_specs=pl.BlockSpec(memory_space=pl.ANY),
        scratch_shapes=[dma, dma((n, 2)), dma((n, 2)), dma((n, 2)), dma((n,)), dma((n,))],
        compiler_params=pltpu.CompilerParams(
            collective_id=collective_id, has_side_effects=True, vmem_limit_bytes=VMEM_LIMIT
        ),
    )(value)


def lane_tiles(cols):
    return [(first, min(128, cols - first)) for first in range(0, cols, 128)]


def weights_in_kernel(
    lay, reach, tokens, pack, pairs, lows, attn_out, ffn_out, earlier_out,
    hops_land, attn_land, own, stack, land, lanes, keep_sem, token_sem, hop_send, hop_recv, low_send, low_recv, attn_send, attn_recv, send, recv, chain_send, chain_recv,
):
    n, hi, lo = lay.dp, lay.hi, lay.lo
    dp = lax.axis_index("dp")
    ctx = lax.axis_index("ctx")
    high = ctx // lo
    per, cols = lows.shape[1:]
    padded = ffn_out.shape[0] // 3
    targets = [lax.rem(dp + k, n) for k in range(n)]
    right, left = (dp, ctx + lo), (dp, ctx - lo)
    has_right, has_left = high < hi - 1, high > 0
    low = lax.rem(ctx, lo)
    low_peers = [(dp, high * lo + other) for other in range(lo)]
    hops = hops_land.shape[0] - 1
    barrier = pltpu.get_barrier_semaphore()
    for target in targets[1:]:
        pl.semaphore_signal(barrier, inc=1, device_id=(target, ctx), device_id_type=MESH)
    for other in range(lo):
        if lo > 1:
            @pl.when(low != other)
            def _():
                pl.semaphore_signal(barrier, inc=1, device_id=low_peers[other], device_id_type=MESH)
    for there, device in ((has_right, right), (has_left, left)):
        @pl.when(there)
        def _():
            pl.semaphore_signal(barrier, inc=1, device_id=device, device_id_type=MESH)
    sides = jnp.where(has_right, 1, 0) + jnp.where(has_left, 1, 0)
    pl.semaphore_wait(barrier, n - 1 + sides + lo - 1)

    attn_pushes = []
    for k in range(1, n):
        push = remote(
            pack.at[targets[k]], attn_land.at[dp], attn_send.at[k], attn_recv.at[k], (targets[k], ctx)
        )
        push.start()
        attn_pushes.append(push)
    attn_land[dp] = pack[dp]
    blank = jnp.zeros((padded - per, cols), jnp.bfloat16)
    pushes = []

    def feed_forward_rows(k):
        target = targets[k]
        for j, (first, width) in enumerate(lane_tiles(cols)):
            lanes[j, :, :width] = pairs[target, :, first : first + width]
        for i in range(3):
            for j, (first, width) in enumerate(lane_tiles(cols)):
                if i == 2:
                    piece = lows[target, :, first : first + width]
                else:
                    piece = lanes[j, pl.ds(i, per, stride=2), :][:, :width]
                if k:
                    stack[k - 1, i, :per, first : first + width] = piece.astype(jnp.bfloat16)
                else:
                    land[dp, i, :per, first : first + width] = piece.astype(jnp.bfloat16)
            if padded > per and k:
                stack[k - 1, i, per:] = blank
            elif padded > per:
                land[dp, i, per:] = blank
        if k:
            push = remote(stack.at[k - 1], land.at[dp], send.at[k], recv.at[k], (target, ctx))
            push.start()
            pushes.append(push)

    def chain(source, where, side, step):
        return remote(
            source, attn_out.at[where], chain_send.at[side, step], chain_recv.at[side, step],
            right if side == 0 else left,
        )

    def pass_on(step):
        if step == 0:
            for side, there in ((0, has_right), (1, has_left)):
                @pl.when(there)
                def _():
                    chain(own, high, side, 0).start()
            return
        for side, here, there in (
            (0, high - step >= 0, has_right),
            (1, high + step < hi, has_left),
        ):
            where = high - step if side == 0 else high + step

            @pl.when(here)
            def _():
                chain(own, where, side, step - 1).wait_recv()
                if step < hi - 1:
                    @pl.when(there)
                    def _():
                        chain(attn_out.at[where], where, side, step).start()

    def finish(step):
        for side, here, there in (
            (0, high - step >= 0, has_right),
            (1, high + step < hi, has_left),
        ):
            @pl.when(here & there)
            def _():
                chain(own, high, side, step).wait_send()

    def hop(h):
        return remote(hops_land.at[h], hops_land.at[h + 1], hop_send.at[h], hop_recv.at[h], right)

    def wanted(h, source, target):
        distance = h * lo + target - source
        return (distance >= 1) & (distance <= reach) & (high >= h)

    def aside(h, source, target, device):
        return remote(
            hops_land.at[h], earlier_out.at[reach - (h * lo + target - source)], low_send.at[h, target],
            low_recv.at[h, source], device,
        )

    def pass_tokens(h):
        if h:
            @pl.when(high >= h)
            def _():
                hop(h - 1).wait_recv()
        if h < hops:
            @pl.when((high >= h) & has_right)
            def _():
                hop(h).start()
        for other in range(lo):
            if lo > 1:
                @pl.when((low != other) & wanted(h, low, other))
                def _():
                    aside(h, low, other, low_peers[other]).start()
        if h and h * lo <= reach:
            @pl.when(high >= h)
            def _():
                earlier_out[reach - h * lo] = hops_land[h]

    def finish_tokens(h):
        if h < hops:
            @pl.when((high >= h) & has_right)
            def _():
                hop(h).wait_send()
        for other in range(lo):
            if lo > 1:
                @pl.when((low != other) & wanted(h, other, low))
                def _():
                    aside(h, other, low, low_peers[other]).wait_recv()

                @pl.when((low != other) & wanted(h, low, other))
                def _():
                    aside(h, low, other, low_peers[other]).wait_send()

    take = pltpu.make_async_copy(tokens, hops_land.at[0], token_sem)
    take.start()
    for d in range(1, reach + 1):
        @pl.when(ctx < d)
        def _():
            earlier_out[reach - d] = jnp.zeros(earlier_out.shape[1:], earlier_out.dtype)
    order = list(range(2, n)) + [1, 0]
    feed_forward_rows(order[0])
    for push in attn_pushes:
        push.wait_recv()
    for q in range(n):
        own[:, q * cols : (q + 1) * cols] = attn_land[q]
    keep = pltpu.make_async_copy(own, attn_out.at[high], keep_sem)
    keep.start()
    pass_on(0)
    take.wait()
    pass_tokens(0)
    for k in order[1:]:
        feed_forward_rows(k)
    for step in range(1, max(hi, hops + 1)):
        if step < hi:
            pass_on(step)
        if step <= hops:
            pass_tokens(step)
    for push in pushes:
        push.wait_recv()
    for q in range(n):
        for i in range(3):
            ffn_out[i * padded : (i + 1) * padded, q * cols : (q + 1) * cols] = land[q, i]
    keep.wait()
    for step in range(hi - 1):
        finish(step)
    for h in range(hops + 1):
        finish_tokens(h)
    for push in attn_pushes + pushes:
        push.wait_send()


def weights_in(lay, reach, tokens, pack, pairs, lows, collective_id):
    n, per, cols = lows.shape
    rows = pack.shape[1]
    padded = -(-per // 16) * 16
    vmem = pl.BlockSpec(memory_space=pltpu.VMEM)
    dma = pltpu.SemaphoreType.DMA
    hops = min(lay.hi - 1, (reach + lay.lo - 1) // lay.lo)
    scratch = [
        pltpu.VMEM((hops + 1,) + tokens.shape, tokens.dtype),
        pltpu.VMEM((n, rows, cols), jnp.bfloat16),
        pltpu.VMEM((rows, n * cols), jnp.bfloat16),
        pltpu.VMEM((n - 1, 3, padded, cols), jnp.bfloat16),
        pltpu.VMEM((n, 3, padded, cols), jnp.bfloat16),
        pltpu.VMEM((len(lane_tiles(cols)), 2 * per, 128), jnp.float32),
        dma,
        dma,
    ]
    for shape in ((hops + 1,), (hops + 1, lay.lo), (n,), (n,), (2, lay.hi)):
        scratch += [dma(shape), dma(shape)]
    return pl.pallas_call(
        partial(weights_in_kernel, lay, reach),
        out_shape=(
            jax.ShapeDtypeStruct((lay.hi, rows, n * cols), jnp.bfloat16),
            jax.ShapeDtypeStruct((3 * padded, n * cols), jnp.bfloat16),
            jax.ShapeDtypeStruct((reach,) + tokens.shape, tokens.dtype),
        ),
        in_specs=[vmem] * 4,
        out_specs=(pl.BlockSpec(memory_space=pl.ANY), vmem, vmem),
        scratch_shapes=scratch,
        compiler_params=pltpu.CompilerParams(
            collective_id=collective_id, has_side_effects=True, vmem_limit_bytes=VMEM_LIMIT
        ),
    )(tokens, pack, pairs, lows)


def later_kernel(lay, reach, pieces, out, low_land, moved, arrived, chain_send, chain_recv, low_send, low_recv):
    hi, lo = lay.hi, lay.lo
    dp = lax.axis_index("dp")
    ctx = lax.axis_index("ctx")
    high, low = ctx // lo, lax.rem(ctx, lo)
    hops = min(hi - 1, (reach + lo - 1) // lo)
    right, left = (dp, ctx + lo), (dp, ctx - lo)
    has_right, has_left = high < hi - 1, high > 0
    low_peers = [(dp, high * lo + other) for other in range(lo)]
    barrier = pltpu.get_barrier_semaphore()
    for there, device in [(has_right, right), (has_left, left)] + [
        (low != other, low_peers[other]) for other in range(lo) if lo > 1
    ]:
        @pl.when(there)
        def _():
            pl.semaphore_signal(barrier, inc=1, device_id=device, device_id_type=MESH)
    sides = jnp.where(has_right, 1, 0) + jnp.where(has_left, 1, 0)
    pl.semaphore_wait(barrier, sides + lo - 1)

    def wanted(h, owner, reader):
        distance = h * lo + reader - owner
        return (distance >= 1) & (distance <= reach) & (high >= h)

    def across(h, other):
        return remote(
            pieces.at[reach - (h * lo + low - other)], low_land.at[h, low], low_send.at[h, other],
            low_recv.at[h, low], low_peers[other],
        )

    def from_low(h, other):
        return remote(
            pieces.at[0], low_land.at[h, other], low_send.at[h, other], low_recv.at[h, other], low_peers[other]
        )

    def hop(h):
        return remote(moved.at[h], arrived.at[h - 1], chain_send.at[h], chain_recv.at[h - 1], left)

    for h in range(hops, -1, -1):
        for other in range(lo):
            if lo > 1:
                @pl.when((low != other) & wanted(h, other, low))
                def _():
                    across(h, other).start()
    for h in range(hops, -1, -1):
        out[...] = jnp.zeros_like(out)
        if h and h * lo <= reach:
            out[...] += pieces[reach - h * lo].astype(jnp.float32)
        for other in range(lo):
            if lo > 1:
                @pl.when((low != other) & wanted(h, low, other))
                def _():
                    from_low(h, other).wait_recv()
                    out[...] += low_land[h, other].astype(jnp.float32)
        if h < hops:
            @pl.when(has_right & (high >= h))
            def _():
                hop(h + 1).wait_recv()
                out[...] += arrived[h].astype(jnp.float32)
        if h:
            @pl.when(high >= h)
            def _():
                moved[h] = out[...].astype(moved.dtype)
                hop(h).start()
    for h in range(hops + 1):
        if h:
            @pl.when(high >= h)
            def _():
                hop(h).wait_send()
        for other in range(lo):
            if lo > 1:
                @pl.when((low != other) & wanted(h, other, low))
                def _():
                    across(h, other).wait_send()


def later_sum(lay, reach, pieces, collective_id):
    hops = min(lay.hi - 1, (reach + lay.lo - 1) // lay.lo)
    shape = pieces.shape[1:]
    vmem = pl.BlockSpec(memory_space=pltpu.VMEM)
    dma = pltpu.SemaphoreType.DMA
    return pl.pallas_call(
        partial(later_kernel, lay, reach),
        out_shape=jax.ShapeDtypeStruct(shape, jnp.float32),
        in_specs=[vmem],
        out_specs=vmem,
        scratch_shapes=[
            pltpu.VMEM((hops + 1, lay.lo) + shape, pieces.dtype),
            pltpu.VMEM((hops + 1,) + shape, pieces.dtype),
            pltpu.VMEM((hops + 1,) + shape, pieces.dtype),
        ]
        + [dma((hops + 1,))] * 2
        + [dma((hops + 1, lay.lo))] * 2,
        compiler_params=pltpu.CompilerParams(
            collective_id=collective_id, has_side_effects=True, vmem_limit_bytes=VMEM_LIMIT
        ),
    )(pieces)


def flip(index, bit):
    return index + bit * (1 - 2 * lax.rem(index // bit, 2))


def scatter_attn_kernel(lay, with_gains, *refs):
    refs = list(refs)
    parts = refs.pop(0)
    gains = refs.pop(0) if with_gains else None
    out = refs.pop(0)
    gains_out = refs.pop(0) if with_gains else None
    core_land, wide_sum, wide_land, keep, low_sum, low_land, hi_sum, hi_land, last, last_land = refs[:10]
    (core_send, core_recv, wide_send, wide_recv, low_send, low_recv, hi_send, hi_recv,
     last_send, last_recv) = refs[10:20]
    if with_gains:
        gains_sum, gains_land, gains_send, gains_recv = refs[20:]
    dp = lax.axis_index("dp")
    ctx = lax.axis_index("ctx")
    hi, lo, wide, n = lay.hi, lay.lo, lay.wide, lay.dp
    high, low = ctx // lo, lax.rem(ctx, lo)
    across, core = dp // 2, lax.rem(dp, 2)
    cols = out.shape[1]
    rows = parts.shape[2]
    partner = (across * 2 + 1 - core, ctx)
    low_peers = [(dp, high * lo + lax.rem(low + k, lo)) for k in range(1, lo)]
    wide_peers = [(lax.rem(across + k, wide) * 2 + core, ctx) for k in range(1, wide)]
    hi_peers = [(dp, lax.rem(high + k, hi) * lo + low) for k in range(1, hi)]
    last_peers = [(lax.rem(dp + k, n), ctx) for k in range(1, n)]
    steps = [1 << i for i in range((n - 1).bit_length())]
    gain_peers = [(flip(dp, bit), ctx) for bit in steps]
    gain_peers += [(dp, flip(ctx, 1 << i)) for i in range((lay.ctx - 1).bit_length())]
    greet(
        low_peers + hi_peers + last_peers + (gain_peers if with_gains else [])
    )

    order = [(k, a) for k in list(range(1, hi)) + [0] for a in list(range(1, lo)) + [0]]

    def block(k, a):
        return lax.rem(high + k, hi) * lo + lax.rem(low + a, lo)

    def slot(k, a):
        return k * lo + a

    sends = []
    core_copies = {}
    for k, a in order:
        for b in list(range(1, wide)) + [0]:
            there = lax.rem(across + b, wide)
            copy = remote(
                parts.at[block(k, a), there * 2 + 1 - core],
                core_land.at[slot(k, a), b],
                core_send.at[slot(k, a), b],
                core_recv.at[slot(k, a), b],
                partner,
            )
            copy.start()
            core_copies[k, a, b] = copy
            sends.append(copy)
    gain_copies = []

    def gains_step(i):
        if not with_gains or i > len(gain_peers):
            return
        if i == 0:
            gains_sum[0] = gains[...]
        else:
            gain_copies[i - 1].wait_recv()
            gains_sum[i] = gains_sum[i - 1] + gains_land[i - 1]
        if i < len(gain_peers):
            copy = remote(
                gains_sum.at[i], gains_land.at[i], gains_send.at[i], gains_recv.at[i], gain_peers[i]
            )
            copy.start()
            gain_copies.append(copy)
            sends.append(copy)
        else:
            gains_out[...] = gains_sum[i]

    wide_copies, low_copies, hi_copies = {}, {}, {}

    def sum_cores(k, a):
        s = slot(k, a)
        for b in list(range(1, wide)) + [0]:
            there = lax.rem(across + b, wide)
            core_copies[k, a, b].wait_recv()
            total = parts[block(k, a), there * 2 + core].astype(jnp.float32) + core_land[
                s, b
            ].astype(jnp.float32)
            if b:
                wide_sum[s, b - 1] = total.astype(jnp.bfloat16)
                copy = remote(
                    wide_sum.at[s, b - 1], wide_land.at[s, b - 1], wide_send.at[s, b - 1],
                    wide_recv.at[s, b - 1], wide_peers[b - 1],
                )
                copy.start()
                wide_copies[k, a, b] = copy
                sends.append(copy)
            else:
                keep[s] = total

    def sum_wide(k, a):
        s = slot(k, a)
        total = keep[s]
        for b in range(1, wide):
            wide_copies[k, a, b].wait_recv()
            total = total + wide_land[s, b - 1].astype(jnp.float32)
        if a:
            low_sum[k, a - 1] = total.astype(jnp.bfloat16)
            copy = remote(
                low_sum.at[k, a - 1], low_land.at[k, a - 1], low_send.at[k, a - 1],
                low_recv.at[k, a - 1], low_peers[a - 1],
            )
            copy.start()
            low_copies[k, a] = copy
            sends.append(copy)
        else:
            keep[s] = total

    def sum_low(k):
        total = keep[slot(k, 0)]
        for a in range(1, lo):
            low_copies[k, a].wait_recv()
            total = total + low_land[k, a - 1].astype(jnp.float32)
        if k:
            hi_sum[k - 1] = total.astype(jnp.bfloat16)
            copy = remote(
                hi_sum.at[k - 1], hi_land.at[k - 1], hi_send.at[k - 1], hi_recv.at[k - 1], hi_peers[k - 1]
            )
            copy.start()
            hi_copies[k] = copy
            sends.append(copy)
        else:
            keep[slot(0, 0)] = total

    gains_step(0)
    ks = list(range(1, hi)) + [0]
    offsets = list(range(1, lo)) + [0]
    for i in range(hi + 2):
        if i < hi:
            for a in offsets:
                sum_cores(ks[i], a)
        gains_step(i + 1)
        if 1 <= i <= hi:
            for a in offsets:
                sum_wide(ks[i - 1], a)
        if 2 <= i:
            sum_low(ks[i - 2])
    for i in range(hi + 3, len(gain_peers) + 1):
        gains_step(i)
    total = keep[slot(0, 0)]
    for k in range(1, hi):
        hi_copies[k].wait_recv()
        total = total + hi_land[k - 1].astype(jnp.float32)
    keep[slot(0, 0)] = total
    for q in range(n):
        last[q] = keep[slot(0, 0), :, q * cols : (q + 1) * cols].astype(jnp.bfloat16)
    last_copies = []
    for k in range(1, n):
        copy = remote(
            last.at[lax.rem(dp + k, n)], last_land.at[dp], last_send.at[k], last_recv.at[k], last_peers[k - 1]
        )
        copy.start()
        last_copies.append(copy)
        sends.append(copy)
    last_land[dp] = last[dp]
    for copy in last_copies:
        copy.wait_recv()
    for q in range(n):
        out[q * rows : (q + 1) * rows] = last_land[q].astype(jnp.float32)
    for copy in sends:
        copy.wait_send()


def scatter_attn(lay, parts, gains, collective_id):
    rows = parts.shape[2]
    cols = D // lay.dp
    with_gains = gains is not None
    lows, wides, his = max(1, lay.lo - 1), max(1, lay.wide - 1), max(1, lay.hi - 1)
    vmem = pl.BlockSpec(memory_space=pltpu.VMEM)
    dma = pltpu.SemaphoreType.DMA
    out_shape = [jax.ShapeDtypeStruct((lay.dp * rows, cols), jnp.float32)]
    scratch = [
        pltpu.VMEM((lay.ctx, lay.wide, rows, D), jnp.bfloat16),
        pltpu.VMEM((lay.ctx, wides, rows, D), jnp.bfloat16),
        pltpu.VMEM((lay.ctx, wides, rows, D), jnp.bfloat16),
        pltpu.VMEM((lay.ctx, rows, D), jnp.float32),
        pltpu.VMEM((lay.hi, lows, rows, D), jnp.bfloat16),
        pltpu.VMEM((lay.hi, lows, rows, D), jnp.bfloat16),
        pltpu.VMEM((his, rows, D), jnp.bfloat16),
        pltpu.VMEM((his, rows, D), jnp.bfloat16),
        pltpu.VMEM((lay.dp, rows, cols), jnp.bfloat16),
        pltpu.VMEM((lay.dp, rows, cols), jnp.bfloat16),
    ]
    for shape in ((lay.ctx, lay.wide), (lay.ctx, wides), (lay.hi, lows), (his,), (lay.dp,)):
        scratch += [dma(shape), dma(shape)]
    if with_gains:
        count = (lay.dp - 1).bit_length() + (lay.ctx - 1).bit_length()
        out_shape.append(jax.ShapeDtypeStruct(gains.shape, jnp.float32))
        scratch += [
            pltpu.VMEM((count + 1,) + gains.shape, jnp.float32),
            pltpu.VMEM((count,) + gains.shape, jnp.float32),
            dma((count,)),
            dma((count,)),
        ]
    return pl.pallas_call(
        partial(scatter_attn_kernel, lay, with_gains),
        out_shape=tuple(out_shape),
        in_specs=[vmem] * (2 if with_gains else 1),
        out_specs=(vmem,) * len(out_shape),
        scratch_shapes=scratch,
        compiler_params=pltpu.CompilerParams(
            collective_id=collective_id, has_side_effects=True, vmem_limit_bytes=VMEM_LIMIT
        ),
    )(*([parts, gains] if with_gains else [parts]))


def exchange_out_kernel(lay, rows, pairs_out, lows_out, stack, land, lanes, send, recv):
    n = lay.dp
    dp = lax.axis_index("dp")
    ctx = lax.axis_index("ctx")
    cols = lows_out.shape[2]
    per = lows_out.shape[1]
    padded = rows.shape[0] // 3
    greet([(lax.rem(dp + k, n), ctx) for k in range(1, n)])
    for q in range(n):
        for i in range(3):
            stack[q, i] = rows[i * padded : (i + 1) * padded, q * cols : (q + 1) * cols]
    pushes = []
    for k in range(1, n):
        target = lax.rem(dp + k, n)
        push = remote(stack.at[target], land.at[dp], send.at[k], recv.at[k], (target, ctx))
        push.start()
        pushes.append(push)
    land[dp] = stack[dp]
    for push in pushes:
        push.wait_recv()
    for q in range(n):
        for j, (first, width) in enumerate(lane_tiles(cols)):
            for i in range(2):
                piece = land[q, i, :per, first : first + width].astype(jnp.float32)
                if width < 128:
                    piece = jnp.concatenate(
                        [piece, jnp.zeros((per, 128 - width), jnp.float32)], axis=1
                    )
                lanes[j, pl.ds(i, per, stride=2), :] = piece
            pairs_out[q, :, first : first + width] = lanes[j, :, :width]
        lows_out[q] = land[q, 2, :per].astype(jnp.float32)
    for push in pushes:
        push.wait_send()


def exchange_out(lay, rows, per, collective_id):
    padded = rows.shape[0] // 3
    n, cols = lay.dp, rows.shape[1] // lay.dp
    vmem = pl.BlockSpec(memory_space=pltpu.VMEM)
    return pl.pallas_call(
        partial(exchange_out_kernel, lay),
        out_shape=(
            jax.ShapeDtypeStruct((n, 2 * per, cols), jnp.float32),
            jax.ShapeDtypeStruct((n, per, cols), jnp.float32),
        ),
        in_specs=[vmem],
        out_specs=(vmem,) * 2,
        scratch_shapes=[
            pltpu.VMEM((n, 3, padded, cols), jnp.bfloat16),
            pltpu.VMEM((n, 3, padded, cols), jnp.bfloat16),
            pltpu.VMEM((len(lane_tiles(cols)), 2 * per, 128), jnp.float32),
            pltpu.SemaphoreType.DMA((n,)),
            pltpu.SemaphoreType.DMA((n,)),
        ],
        compiler_params=pltpu.CompilerParams(
            collective_id=collective_id, has_side_effects=True, vmem_limit_bytes=VMEM_LIMIT
        ),
    )(rows)


def in_tiles(total, size, body, begin=0):
    whole = total // size

    def step(i, carry):
        body(pl.multiple_of(begin + i * size, math.gcd(begin, size)), size)
        return carry

    if whole:
        lax.fori_loop(0, whole, step, 0)
    if total % size:
        body(begin + whole * size, total % size)


def dot_nt(left, right):
    return lax.dot_general(left, right, (((1,), (1,)), ((), ())), preferred_element_type=jnp.float32)


def dot_nn(left, right):
    return lax.dot_general(left, right, (((1,), (0,)), ((), ())), preferred_element_type=jnp.float32)


ROOT = math.sqrt(2.0 / math.pi)


def feed_forward_kernel(
    lay, mid, weights, mixed, cotangent, valid, gain,
    result, grad_mid, grad_gain, grad_weights,
    w_gate, w_up, w_down, gate_t, up_t, act, slope, hidden, hidden_t, grads, parts, core_land, sums, via, landed,
    total, dy, weight_sem, core_send, core_recv, share_send, share_recv,
    send, recv, via_send, via_recv, dy_send, dy_recv, dy_pass,
):
    chip, core, high = lay.place()
    n, wide = lay.chips, lay.wide
    tokens = mixed.shape[0]
    units = w_gate.shape[0]
    padded = units // lay.hi
    loads = [
        pltpu.make_async_copy(
            weights.at[h, pl.ds(i * padded, padded)], held.at[pl.ds(h * padded, padded)], weight_sem.at[i, h]
        )
        for i, held in enumerate((w_gate, w_up, w_down))
        for h in range(lay.hi)
    ]
    for load in loads:
        load.start()
    peers = [lay.device(lay.offset(chip, k), core, high) for k in range(n)]
    owners = [lay.device(lay.offset(chip, k, -1), core, high) for k in range(n)]
    partner = lay.device(chip, 1 - core, high)
    mine = pl.ds(pl.multiple_of(core * tokens, tokens), tokens)
    theirs = pl.ds(pl.multiple_of((1 - core) * tokens, tokens), tokens)
    half = tokens // 2
    halves = (pl.ds(0, half), pl.ds(half, half))
    straight, bent = lay.straight(), lay.bent()
    place = [lay.position(k) for k in range(n)]
    greet(peers[1:] + [partner])

    def to_partner(phase, k):
        return remote(
            parts.at[place[k], theirs], core_land.at[k], core_send.at[phase, k], core_recv.at[phase, k], partner
        )

    def to_owner(phase, k, h):
        return remote(
            sums.at[k - 1, halves[h]], landed.at[place[k] - len(bent), halves[h]], send.at[phase, k, h],
            recv.at[phase, k, h], owners[k],
        )

    def to_neighbour(phase, k, h):
        step = k % wide if h == 0 else k // wide * wide
        return remote(
            sums.at[k - 1, halves[h]], via.at[place[k], halves[h]], via_send.at[phase, k, h], via_recv.at[phase, k, h],
            owners[step],
        )

    def added(k):
        if k < wide:
            return 1, [k + b * wide for b in range(1, lay.lo)]
        return 0, [k + step for step in range(1, wide)]

    def add_core(phase, k):
        to_partner(phase, k).wait_recv()

        def chunk(first, rows):
            span = pl.ds(first, rows)
            here = pl.ds(pl.multiple_of(core * tokens + first, rows), rows)
            both = parts[place[k], here].astype(jnp.float32) + core_land[k, span].astype(jnp.float32)
            if k:
                sums[k - 1, span] = both.astype(jnp.bfloat16)
            else:
                total[span] = both

        in_tiles(tokens, 32, chunk)
        if k in bent:
            for h in range(2):
                to_neighbour(phase, k, h).start()
        elif k:
            h, others = added(k)
            to_owner(phase, k, 1 - h).start()
            if not others:
                to_owner(phase, k, h).start()

    def add_neighbours(phase, k):
        h, others = added(k)
        if not others:
            return
        for other in others:
            to_neighbour(phase, other, h).wait_recv()

        def chunk(first, rows):
            span = pl.ds(first + h * half, rows)
            value = sums[k - 1, span].astype(jnp.float32)
            for other in others:
                value = value + via[place[other], span].astype(jnp.float32)
            sums[k - 1, span] = value.astype(jnp.bfloat16)

        in_tiles(half, 32, chunk)
        to_owner(phase, k, h).start()

    def add_owners(phase):
        for k in straight:
            for h in range(2):
                to_owner(phase, k, h).wait_recv()

        def chunk(first, rows):
            span = pl.ds(first, rows)
            value = total[span]
            for k in straight:
                value = value + landed[place[k] - len(bent), span].astype(jnp.float32)
            total[span] = value

        in_tiles(tokens, 32, chunk)

    def settle(phase):
        for k in range(n):
            to_partner(phase, k).wait_send()
            for h in range(2):
                if k in bent:
                    to_neighbour(phase, k, h).wait_send()
                elif k:
                    to_owner(phase, k, h).wait_send()

    rows_of = 2 * tokens

    def joined(ref, group, *index):
        value = ref[(pl.ds(*group),) + index]
        return value.reshape((group[1] * rows_of,) + value.shape[2:])

    def forward_units(group, begin, end):
        count = group[1]

        def tile(first, width):
            units_here = pl.ds(first, width)
            weights = jnp.concatenate([w_gate[units_here], w_up[units_here]], axis=0)
            both = dot_nt(joined(mid, group), weights)
            gate, up = both[:, :width], both[:, width:]
            square = gate * gate
            tanh = jnp.tanh(gate * (ROOT + (0.044715 * ROOT) * square))
            half_way = 0.5 + 0.5 * tanh
            active = gate * half_way
            slant = half_way + active * (1.0 - tanh) * (ROOT + (3.0 * 0.044715 * ROOT) * square)
            product = (active * up).astype(jnp.bfloat16)
            shape = (count, rows_of, width)
            act[pl.ds(*group), :, units_here] = active.astype(jnp.bfloat16).reshape(shape)
            slope[pl.ds(*group), :, units_here] = (slant * up).astype(jnp.bfloat16).reshape(shape)
            hidden[: count * rows_of, units_here] = product
            for c in range(count):
                hidden_t[group[0] + c, units_here] = product[c * rows_of : (c + 1) * rows_of].T

        in_tiles(end - begin, 128, tile, begin)

    def forward_down(group):
        count = group[1]

        def tile(first, width):
            lanes = pl.ds(first, width)
            value = dot_nn(hidden[: count * rows_of], w_down[:, lanes]).astype(jnp.bfloat16)
            parts[pl.ds(*group), :, lanes] = value.reshape(count, rows_of, width)

        in_tiles(D, 256, tile)

    def backward_units(group):
        count = group[1]

        def tile(first, width):
            units_here = pl.ds(first, width)
            grad = dot_nt(joined(dy, group), w_down[units_here])
            up_grad = (grad * joined(act, group, slice(None), units_here).astype(jnp.float32)).astype(jnp.bfloat16)
            gate_grad = (grad * joined(slope, group, slice(None), units_here).astype(jnp.float32)).astype(jnp.bfloat16)
            grads[0, : count * rows_of, units_here] = gate_grad
            grads[1, : count * rows_of, units_here] = up_grad
            for c in range(count):
                rows = slice(c * rows_of, (c + 1) * rows_of)
                gate_t[group[0] + c, units_here] = gate_grad[rows].T
                up_t[group[0] + c, units_here] = up_grad[rows].T

        in_tiles(units, 256, tile)

    def backward_in(group):
        count = group[1]

        def tile(first, width):
            lanes = pl.ds(first, width)
            both = dot_nn(grads[0, : count * rows_of], w_gate[:, lanes]) + dot_nn(
                grads[1, : count * rows_of], w_up[:, lanes]
            )
            parts[pl.ds(*group), :, lanes] = both.astype(jnp.bfloat16).reshape(count, rows_of, width)

        in_tiles(D, 256, tile)

    far, near, here = (0, len(bent)), (len(bent), len(straight)), (n - 1, 1)
    most = hidden.shape[0] // rows_of

    def runs(group):
        return [(first, min(most, group[0] + group[1] - first)) for first in range(group[0], sum(group), most)]

    quarter = units // 512 * 128
    for load in loads:
        load.wait()
    for run in runs(far):
        forward_units(run, 0, units)
        forward_down(run)
    for k in bent:
        to_partner(0, k).start()
    for i, run in enumerate(runs(near)):
        forward_units(run, 0, 2 * quarter)
        if i == 0:
            for k in bent:
                add_core(0, k)
        forward_units(run, 2 * quarter, units)
        forward_down(run)
    for k in straight:
        to_partner(0, k).start()
    forward_units(here, 0, 2 * quarter)
    for k in straight:
        add_core(0, k)
    for k in straight:
        add_neighbours(0, k)
    forward_units(here, 2 * quarter, units)
    forward_down(here)
    to_partner(0, 0).start()
    add_core(0, 0)
    add_owners(0)

    grad_gain[...] = jnp.zeros_like(grad_gain)
    scale = 1.0 + gain[...]

    def finish(first, rows):
        span = pl.ds(first, rows)
        spot = pl.ds(pl.multiple_of(core * tokens + first, rows), rows)
        y = total[span]
        ok = valid[span]
        rate = lax.rsqrt(jnp.mean(y * y, axis=-1, keepdims=True) + EPS)
        unit = y * rate
        result[span] = ((mixed[span] + unit * scale) * ok).astype(jnp.bfloat16)
        upstream = cotangent[span].astype(jnp.float32) * ok
        down = upstream * unit
        for r in range(0, rows, 8):
            grad_gain[...] += down[r : r + 8]
        scaled = upstream * scale
        inner = jnp.mean(scaled * unit, axis=-1, keepdims=True)
        dy[n - 1, spot] = (rate * (scaled - unit * inner)).astype(jnp.bfloat16)

    in_tiles(tokens, 32, finish)

    def dy_half(k, h):
        return dy.at[place[k], pl.ds(pl.multiple_of(core * tokens + h * half, half), half)]

    def dy_push(k, h):
        return remote(dy_half(0, h), dy_half(k, h), dy_send.at[k, h], dy_recv.at[k, h], peers[k])

    def dy_onward(k, h, step):
        return remote(
            dy_half(k, h), dy_half(k + step, h), dy_pass.at[k + step, h], dy_recv.at[k + step, h], peers[step]
        )

    shares = [
        remote(dy.at[place[k], mine], dy.at[place[k], mine], share_send.at[k], share_recv.at[k], partner)
        for k in range(n)
    ]
    ordered = [(k, i if k < wide else 1 - i) for i in range(2) for k in straight]
    for k, h in ordered:
        dy_push(k, h).start()
    shares[0].start()
    settle(0)
    shares[0].wait_recv()
    backward_units(here)
    backward_in(here)
    to_partner(1, 0).start()
    onward = []
    for k, h in ordered:
        dy_push(k, h).wait_recv()
        if k < wide and h == 0:
            onward += [(k, h, b * wide) for b in range(1, lay.lo)]
        elif k >= wide and h == 1:
            onward += [(k, h, step) for step in range(1, wide)]
        for go in onward:
            if go[:2] == (k, h):
                dy_onward(*go).start()
    for k in straight:
        shares[k].start()
    add_core(1, 0)
    for k in straight:
        shares[k].wait_recv()
    for i, run in enumerate(runs(near)):
        backward_units(run)
        if i == 0:
            for k in bent:
                for h in range(2):
                    dy_push(k, h).wait_recv()
                shares[k].start()
        backward_in(run)
    for k in straight:
        to_partner(1, k).start()
    for k in bent:
        shares[k].wait_recv()
    for i, run in enumerate(runs(far)):
        backward_units(run)
        if i == 0:
            for k in straight:
                add_core(1, k)
        backward_in(run)
    if not bent:
        for k in straight:
            add_core(1, k)
    for k in bent:
        to_partner(1, k).start()
    for k in bent:
        add_core(1, k)

    def weight_grad(left_ref, right, i):
        def tile(first, width):
            lanes = pl.ds(first, width)
            value = dot_nn(left_ref[0], right[0, :, lanes])
            for c in range(1, n):
                value = value + dot_nn(left_ref[c], right[c, :, lanes])
            value = value.astype(jnp.bfloat16)
            for h in range(lay.hi):
                grad_weights[h, i * padded : (i + 1) * padded, lanes] = value[h * padded : (h + 1) * padded]

        in_tiles(D, 256, tile)

    weight_grad(hidden_t, dy, 2)
    for k in straight:
        add_neighbours(1, k)
    weight_grad(gate_t, mid, 0)
    weight_grad(up_t, mid, 1)
    add_owners(1)
    grad_mid[...] = total[...]
    settle(1)
    for k, h in ordered:
        dy_push(k, h).wait_send()
    for go in onward:
        dy_onward(*go).wait_send()
    for share in shares:
        share.wait_send()


def feed_forward(lay, mid, weights, mixed, cotangent, valid, gain, collective_id):
    n = lay.chips
    tokens = mixed.shape[0]
    units = weights.shape[0] * weights.shape[1] // 3
    most = min(n, max(1, 1920 // units))
    low, high = jnp.bfloat16, jnp.float32
    vmem = pl.BlockSpec(memory_space=pltpu.VMEM)
    dma = pltpu.SemaphoreType.DMA
    return pl.pallas_call(
        partial(feed_forward_kernel, lay),
        out_shape=(
            jax.ShapeDtypeStruct((tokens, D), low),
            jax.ShapeDtypeStruct((tokens, D), high),
            jax.ShapeDtypeStruct((8, D), high),
            jax.ShapeDtypeStruct(weights.shape, low),
        ),
        in_specs=[vmem, pl.BlockSpec(memory_space=pl.ANY)] + [vmem] * 4,
        out_specs=(vmem,) * 4,
        scratch_shapes=[
            pltpu.VMEM((units, D), low),
            pltpu.VMEM((units, D), low),
            pltpu.VMEM((units, D), low),
            pltpu.VMEM((n, units, 2 * tokens), low),
            pltpu.VMEM((n, units, 2 * tokens), low),
            pltpu.VMEM((n, 2 * tokens, units), low),
            pltpu.VMEM((n, 2 * tokens, units), low),
            pltpu.VMEM((most * 2 * tokens, units), low),
            pltpu.VMEM((n, units, 2 * tokens), low),
            pltpu.VMEM((2, most * 2 * tokens, units), low),
            pltpu.VMEM((n, 2 * tokens, D), low),
            pltpu.VMEM((n, tokens, D), low),
            pltpu.VMEM((max(1, n - 1), tokens, D), low),
            pltpu.VMEM((max(1, len(lay.bent())), tokens if lay.bent() else 16, D), low),
            pltpu.VMEM((max(1, len(lay.straight())), tokens, D), low),
            pltpu.VMEM((tokens, D), high),
            pltpu.VMEM((n, 2 * tokens, D), low),
            dma((3, lay.hi)),
        ]
        + [dma((2, n))] * 2
        + [dma((n,))] * 2
        + [dma((2, n, 2))] * 4
        + [dma((n, 2))] * 3,
        compiler_params=pltpu.CompilerParams(
            collective_id=collective_id, has_side_effects=True, vmem_limit_bytes=63 * 2**20
        ),
    )(mid, weights, mixed, cotangent, valid, gain)


def norm_scaled(v, gain):
    return v * lax.rsqrt(jnp.mean(v * v, axis=-1, keepdims=True) + EPS) * (1.0 + gain)


def rotate(v, angle):
    half = v.shape[-1] // 2
    cosine = jnp.cos(angle)
    sine = jnp.sin(angle)
    first = v[..., :half]
    second = v[..., half:]
    return jnp.concatenate(
        [first * cosine - second * sine, second * cosine + first * sine], axis=-1
    )


def angles_of(positions):
    inverse = 1.0 / 10000.0 ** (jnp.arange(HD // 2, dtype=jnp.float32) * (2.0 / HD))
    return positions.astype(jnp.float32)[:, None] * inverse[None, :]


def head_inputs(projected, gain_query, gain_key, angle):
    query = projected[..., : HEADS * HD].reshape(projected.shape[:-1] + (HEADS, HD))
    key_rows = projected[..., HEADS * HD : (HEADS + 1) * HD]
    value_rows = projected[..., (HEADS + 1) * HD :]
    query = rotate(norm_scaled(query, gain_query), angle[:, None, :])
    key_rows = rotate(norm_scaled(key_rows, gain_key), angle)
    return (query, key_rows, value_rows)


def contract(left, right, dims_left, dims_right):
    return lax.dot_general(
        left, right, ((dims_left, dims_right), ((), ())), preferred_element_type=jnp.float32
    )


def per_device(lay, tokens, lengths, w_qkv, w_out, w_gate_up, w_down, gains, cotangent):
    seq_count = tokens.shape[0]
    local_len = tokens.shape[1]
    reach = (WINDOW - 1) // local_len + 1
    scale = 1.0 / math.sqrt(HD)
    units = w_down.shape[0]
    per = units // lay.dp
    qkv_rows, out_rows = w_qkv.shape[0], w_out.shape[0]
    cols = w_qkv.shape[1]
    used = qkv_rows + out_rows + 1
    block = 16 * lay.dp
    pack_rows = -(-used // block) * block
    gain_row = jnp.pad(gains, (0, cols - gains.shape[0]))[None]
    pack = jnp.concatenate(
        [w_qkv, w_out, gain_row, jnp.zeros((pack_rows - used, cols), jnp.float32)], axis=0
    ).astype(jnp.bfloat16)
    plane, ffn_rows, earlier_tokens = weights_in(
        lay,
        reach,
        tokens,
        pack.reshape(lay.dp, pack_rows // lay.dp, cols),
        w_gate_up.reshape(lay.dp, 2 * per, cols),
        w_down.reshape(lay.dp, per, cols),
        5,
    )
    ffn_all = lax.all_gather(ffn_rows, "ctx", axis=0, axis_index_groups=lay.hi_groups)
    attn_all = gather_group(
        lay,
        plane,
        (lay.hi, lay.lo, lay.dp, pack_rows // lay.dp, D),
        lambda out, k, chip, core: out.at[
            :, chip // lay.wide, lax.rem(chip, lay.wide) * 2 + core
        ],
        6,
    ).reshape(lay.ctx, pack_rows, D)
    full_qkv = attn_all[:, :qkv_rows].reshape(lay.ctx * qkv_rows, D)
    full_out = attn_all[:, qkv_rows : qkv_rows + out_rows].reshape(lay.ctx * out_rows, D)
    gain_all = (
        attn_all[:, used - 1]
        .reshape(lay.ctx, lay.dp, cols)[:, :, : gains.shape[0]]
        .transpose(1, 0, 2)
        .reshape(-1)
        .astype(jnp.float32)
    )
    gain_in = gain_all[:D]
    gain_attn = gain_all[D : 2 * D]
    gain_pre = gain_all[2 * D : 3 * D]
    gain_post = gain_all[3 * D : 4 * D]
    gain_query = gain_all[4 * D : 4 * D + HD]
    gain_key = gain_all[4 * D + HD :]
    offset = lax.axis_index("ctx") * local_len
    positions = offset + jnp.arange(local_len, dtype=jnp.int32)
    angle = angles_of(positions)
    valid = positions[None, :] < lengths[:, None]
    inputs = tokens.astype(jnp.float32)
    normed_in, pull_in = jax.vjp(norm_scaled, inputs, gain_in)
    normed_low = normed_in.astype(jnp.bfloat16)
    projected = contract(normed_low, full_qkv, (2,), (1,))
    (query, key_rot, value_rows), pull_heads = jax.vjp(
        partial(head_inputs, angle=angle), projected, gain_query, gain_key
    )
    query_low = query.astype(jnp.bfloat16)
    key_pos = offset - reach * local_len + jnp.arange((reach + 1) * local_len, dtype=jnp.int32)
    earlier = earlier_tokens.transpose(1, 0, 2, 3).reshape(seq_count, reach * local_len, D)
    earlier = norm_scaled(earlier.astype(jnp.float32), gain_in).astype(jnp.bfloat16)
    earlier = contract(earlier, full_qkv[HEADS * HD :], (2,), (1,))
    earlier_keys = rotate(
        norm_scaled(earlier[..., :HD], gain_key), angles_of(key_pos[: reach * local_len])
    )
    key_pairs = jnp.concatenate(
        [
            jnp.concatenate([earlier_keys, earlier[..., HD:]], axis=-1).astype(jnp.bfloat16),
            jnp.concatenate([key_rot, value_rows], axis=-1).astype(jnp.bfloat16),
        ],
        axis=1,
    )
    keys_low = key_pairs[..., :HD]
    values_low = key_pairs[..., HD:]
    key_grid = key_pos[None, None, :]
    query_grid = positions[None, :, None]
    allowed = (
        (key_grid >= 0)
        & (key_grid <= query_grid)
        & (query_grid - key_grid < WINDOW)
        & ((key_grid < lengths[:, None, None]) | (key_grid == query_grid))
    )

    def scores_of():
        raw = jnp.einsum("schd,skd->shck", query_low, keys_low, preferred_element_type=jnp.float32)
        return jnp.where(allowed[:, None], raw * scale, -BIG)

    scores = scores_of()
    top = jnp.max(scores, axis=-1, keepdims=True)
    expo = jnp.exp(scores - top)
    total = jnp.sum(expo, axis=-1, keepdims=True)
    probs = expo / total
    log_total = top + jnp.log(total)
    probs_low = probs.astype(jnp.bfloat16)
    attended = jnp.einsum(
        "shck,skd->schd", probs_low, values_low, preferred_element_type=jnp.float32
    )
    attended_low = attended.reshape(seq_count, local_len, HEADS * HD).astype(jnp.bfloat16)
    out_proj = contract(attended_low, full_out, (2,), (0,))
    normed_out, pull_out = jax.vjp(norm_scaled, out_proj, gain_attn)
    mixed = inputs + normed_out
    normed_mid, pull_mid = jax.vjp(norm_scaled, mixed, gain_pre)
    mid_low = normed_mid.astype(jnp.bfloat16)
    token_count = seq_count * local_len
    mid_all = gather_group(
        lay,
        mid_low.reshape(2, token_count // 2, D),
        (lay.chips, 2, 2, token_count // 2, D),
        lambda out, k, chip, core: out.at[lay.position(k), core],
        1,
    ).reshape(lay.chips, 2 * token_count, D)
    result, grad_mid, grad_gain_post, grad_ffn = feed_forward(
        lay,
        mid_all,
        ffn_all,
        mixed.reshape(token_count, D),
        cotangent.reshape(token_count, D),
        valid.reshape(token_count, 1).astype(jnp.float32),
        gain_post[None],
        2,
    )
    result = result.reshape(mixed.shape)
    grad_mid = grad_mid.reshape(mixed.shape)
    grad_gain_post = jnp.sum(grad_gain_post, axis=0)
    upstream = jnp.where(valid[..., None], cotangent.astype(jnp.float32), 0.0)
    grad_mixed_in, grad_gain_pre = pull_mid(grad_mid)
    grad_mixed = upstream + grad_mixed_in
    grad_proj, grad_gain_attn = pull_out(grad_mixed)
    proj_low = grad_proj.astype(jnp.bfloat16)
    grad_attended = contract(proj_low, full_out, (2,), (1,))
    grad_w_out = contract(attended_low, proj_low, (0, 1), (0, 1))
    attn_low = grad_attended.astype(jnp.bfloat16).reshape(seq_count, local_len, HEADS, HD)
    again_probs = jnp.exp(scores_of() - log_total)
    again_low = again_probs.astype(jnp.bfloat16)
    grad_values = jnp.einsum(
        "shck,schd->skd", again_low, attn_low, preferred_element_type=jnp.float32
    )
    grad_probs = jnp.einsum(
        "schd,skd->shck", attn_low, values_low, preferred_element_type=jnp.float32
    )
    row_dot = jnp.sum(again_probs * grad_probs, axis=-1, keepdims=True)
    grad_scores = (scale * again_probs * (grad_probs - row_dot)).astype(jnp.bfloat16)
    grad_query = jnp.einsum(
        "shck,skd->schd", grad_scores, keys_low, preferred_element_type=jnp.float32
    )
    grad_keys = jnp.einsum(
        "shck,schd->skd", grad_scores, query_low, preferred_element_type=jnp.float32
    )
    grad_pairs = jnp.concatenate([grad_keys, grad_values], axis=-1)
    own_grad = grad_pairs[:, reach * local_len :]
    pieces = grad_pairs[:, : reach * local_len].astype(jnp.bfloat16)
    pieces = pieces.reshape(seq_count, reach, local_len, 2 * HD).transpose(1, 0, 2, 3)
    later = later_sum(lay, reach, pieces, 11)
    own_grad = own_grad + later
    grad_projected, grad_gain_query, grad_gain_key = pull_heads(
        (grad_query, own_grad[..., :HD], own_grad[..., HD:])
    )
    qkv_low = grad_projected.astype(jnp.bfloat16)
    grad_w_qkv = contract(qkv_low, normed_low, (0, 1), (0, 1))
    grad_normed = contract(qkv_low, full_qkv, (2,), (0,))
    grad_in_norm, grad_gain_in = pull_in(grad_normed)
    grad_input = grad_mixed + grad_in_norm
    grad_gain_all = jnp.concatenate(
        [
            grad_gain_in,
            grad_gain_attn,
            grad_gain_pre,
            grad_gain_post,
            grad_gain_query,
            grad_gain_key,
        ]
    )
    sum_rows = -(-(qkv_rows + out_rows) // block) * block
    partial_sums = jnp.concatenate(
        [
            grad_w_qkv.astype(jnp.bfloat16).reshape(lay.ctx, qkv_rows, D),
            grad_w_out.astype(jnp.bfloat16).reshape(lay.ctx, out_rows, D),
            jnp.zeros((lay.ctx, sum_rows - qkv_rows - out_rows, D), jnp.bfloat16),
        ],
        axis=1,
    ).reshape(lay.ctx, lay.dp, sum_rows // lay.dp, D)
    part_attn, gains_sum = scatter_attn(lay, partial_sums, grad_gain_all.reshape(-1, 128), 8)
    owned = lax.psum_scatter(grad_ffn, "ctx", scatter_dimension=0, axis_index_groups=lay.hi_groups)
    part_gate_up, part_down = exchange_out(lay, owned, per, 9)
    part_qkv = part_attn[:qkv_rows]
    part_out = part_attn[qkv_rows : qkv_rows + out_rows]
    place = (lax.axis_index("dp") * lay.ctx + lax.axis_index("ctx")) * gains.shape[0]
    part_gains = lax.dynamic_slice_in_dim(gains_sum.reshape(-1), place, gains.shape[0])
    part_gate_up = part_gate_up.reshape(w_gate_up.shape)
    part_down = part_down.reshape(w_down.shape)
    return (result, grad_input, part_qkv, part_out, part_gate_up, part_down, part_gains)


def solution(mesh):
    placed = (
        P("dp", "ctx", None),
        P("dp"),
        P("ctx", "dp"),
        P("ctx", "dp"),
        P("ctx", "dp"),
        P("ctx", "dp"),
        P(("dp", "ctx")),
        P("dp", "ctx", None),
    )
    return jax.shard_map(
        partial(per_device, Layout(mesh)),
        mesh=mesh,
        in_specs=placed,
        out_specs=(
            P("dp", "ctx", None),
            P("dp", "ctx", None),
            P("ctx", "dp"),
            P("ctx", "dp"),
            P("ctx", "dp"),
            P("ctx", "dp"),
            P(("dp", "ctx")),
        ),
        check_vma=False,
    )
```

```python
from functools import partial
import math

import jax
import jax.numpy as jnp
from jax import lax
from jax.experimental import pallas as pl
from jax.experimental.pallas import tpu as pltpu
from jax.sharding import PartitionSpec as P

D = 1152
HEADS = 4
HD = 256
WINDOW = 512
GROUP = 8

EPS = 1e-06
BIG = 1e30
MESH = pl.DeviceIdType.MESH
VMEM_LIMIT = 56 * 2**20


class Layout:
    def __init__(self, mesh):
        self.dp = mesh.shape["dp"]
        self.ctx = mesh.shape["ctx"]
        self.lo = max(1, GROUP // self.dp)
        self.hi = self.ctx // self.lo
        self.wide = self.dp // 2
        self.chips = self.wide * self.lo
        self.group = self.dp * self.lo
        self.hi_groups = [
            [h * self.lo + low for h in range(self.hi)] for low in range(self.lo)
        ]

    def place(self):
        dp = lax.axis_index("dp")
        ctx = lax.axis_index("ctx")
        chip = lax.rem(ctx, self.lo) * self.wide + dp // 2
        return chip, lax.rem(dp, 2), ctx // self.lo

    def offset(self, chip, k, sign=1):
        across = lax.rem(chip, self.wide) + self.wide + sign * (k % self.wide)
        low = chip // self.wide + self.lo + sign * (k // self.wide)
        return lax.rem(low, self.lo) * self.wide + lax.rem(across, self.wide)

    def straight(self):
        return list(range(1, self.wide)) + [low * self.wide for low in range(1, self.lo)]

    def bent(self):
        return [k for k in range(1, self.chips) if k not in self.straight()]

    def position(self, k):
        return (self.bent() + self.straight() + [0]).index(k)

    def device(self, chip, core, high):
        return (lax.rem(chip, self.wide) * 2 + core, high * self.lo + chip // self.wide)


def remote(src, dst, send, recv, device):
    return pltpu.make_async_remote_copy(
        src_ref=src, dst_ref=dst, send_sem=send, recv_sem=recv, device_id=device, device_id_type=MESH
    )


def greet(devices):
    barrier = pltpu.get_barrier_semaphore()
    for device in devices:
        pl.semaphore_signal(barrier, inc=1, device_id=device, device_id_type=MESH)
    pl.semaphore_wait(barrier, len(devices))


def gather_group_kernel(lay, slot, own, out, local_sem, send, recv, pass_send, core_send, core_recv):
    chip, core, high = lay.place()
    n = lay.chips
    half = own.shape[0] // 2
    halves = (pl.ds(0, half), pl.ds(half, half))
    peers = [lay.device(lay.offset(chip, k), core, high) for k in range(n)]
    sources = [lay.offset(chip, k, -1) for k in range(n)]
    partner = lay.device(chip, 1 - core, high)
    greet(peers[1:] + [partner])
    mine = [slot(out, k, chip, core) for k in range(n)]
    straight, bent = lay.straight(), lay.bent()
    keep = pltpu.make_async_copy(own, mine[0], local_sem)
    keep.start()
    pushes = []

    def push(k, h, source, target, sem):
        copy = remote(source.at[halves[h]], target.at[halves[h]], sem, recv.at[k, h], peers[k])
        return copy

    ordered = [(k, i if k < lay.wide else 1 - i) for i in range(2) for k in straight]
    for k, h in ordered:
        copy = push(k, h, own, mine[k], send.at[k, h])
        copy.start()
        pushes.append(copy)
    shares = [remote(own, mine[0], core_send.at[0], core_recv.at[0], partner)]
    shares[0].start()

    def arrived(k, h):
        copy = remote(own.at[halves[h]], mine[k].at[halves[h]], send.at[k, h], recv.at[k, h], peers[k])
        copy.wait_recv()

    for k, h in ordered:
        arrived(k, h)
        block = slot(out, k, sources[k], core)
        if k < lay.wide and h == 0:
            onward = [b * lay.wide for b in range(1, lay.lo)]
        elif k >= lay.wide and h == 1:
            onward = list(range(1, lay.wide))
        else:
            onward = []
        for step in onward:
            total = k + step
            there = slot(out, total, sources[k], core)
            copy = remote(
                block.at[halves[h]], there.at[halves[h]], pass_send.at[total, h], recv.at[total, h], peers[step]
            )
            copy.start()
            pushes.append(copy)
    for k in straight + bent:
        if k in bent:
            for h in range(2):
                arrived(k, h)
        block = slot(out, k, sources[k], core)
        share = remote(block, block, core_send.at[k], core_recv.at[k], partner)
        share.start()
        shares.append(share)
    keep.wait()
    for copy in pushes:
        copy.wait_send()
    for share in shares:
        share.wait()


def gather_group(lay, value, out_shape, slot, collective_id):
    n = lay.chips
    dma = pltpu.SemaphoreType.DMA
    return pl.pallas_call(
        partial(gather_group_kernel, lay, slot),
        out_shape=jax.ShapeDtypeStruct(out_shape, value.dtype),
        in_specs=[pl.BlockSpec(memory_space=pl.ANY)],
        out_specs=pl.BlockSpec(memory_space=pl.ANY),
        scratch_shapes=[dma, dma((n, 2)), dma((n, 2)), dma((n, 2)), dma((n,)), dma((n,))],
        compiler_params=pltpu.CompilerParams(
            collective_id=collective_id, has_side_effects=True, vmem_limit_bytes=VMEM_LIMIT
        ),
    )(value)


def lane_tiles(cols):
    return [(first, min(128, cols - first)) for first in range(0, cols, 128)]


def weights_in_kernel(
    lay, reach, tokens, pack, pairs, lows, attn_out, ffn_out, earlier_out,
    hops_land, attn_land, own, stack, land, lanes, keep_sem, hop_send, hop_recv, low_send, low_recv, attn_send, attn_recv, send, recv, chain_send, chain_recv,
):
    n, hi, lo = lay.dp, lay.hi, lay.lo
    dp = lax.axis_index("dp")
    ctx = lax.axis_index("ctx")
    high = ctx // lo
    per, cols = lows.shape[1:]
    padded = ffn_out.shape[0] // 3
    targets = [lax.rem(dp + k, n) for k in range(n)]
    right, left = (dp, ctx + lo), (dp, ctx - lo)
    has_right, has_left = high < hi - 1, high > 0
    low = lax.rem(ctx, lo)
    low_peers = [(dp, high * lo + other) for other in range(lo)]
    hops = hops_land.shape[0] - 1
    barrier = pltpu.get_barrier_semaphore()
    for target in targets[1:]:
        pl.semaphore_signal(barrier, inc=1, device_id=(target, ctx), device_id_type=MESH)
    for other in range(lo):
        if lo > 1:
            @pl.when(low != other)
            def _():
                pl.semaphore_signal(barrier, inc=1, device_id=low_peers[other], device_id_type=MESH)
    for there, device in ((has_right, right), (has_left, left)):
        @pl.when(there)
        def _():
            pl.semaphore_signal(barrier, inc=1, device_id=device, device_id_type=MESH)
    sides = jnp.where(has_right, 1, 0) + jnp.where(has_left, 1, 0)
    pl.semaphore_wait(barrier, n - 1 + sides + lo - 1)

    attn_pushes = []
    for k in range(1, n):
        push = remote(
            pack.at[targets[k]], attn_land.at[dp], attn_send.at[k], attn_recv.at[k], (targets[k], ctx)
        )
        push.start()
        attn_pushes.append(push)
    attn_land[dp] = pack[dp]
    blank = jnp.zeros((padded - per, cols), jnp.bfloat16)
    pushes = []

    def feed_forward_rows(k):
        target = targets[k]
        for j, (first, width) in enumerate(lane_tiles(cols)):
            lanes[j, :, :width] = pairs[target, :, first : first + width]
        for i in range(3):
            for j, (first, width) in enumerate(lane_tiles(cols)):
                if i == 2:
                    piece = lows[target, :, first : first + width]
                else:
                    piece = lanes[j, pl.ds(i, per, stride=2), :][:, :width]
                if k:
                    stack[k - 1, i, :per, first : first + width] = piece.astype(jnp.bfloat16)
                else:
                    land[dp, i, :per, first : first + width] = piece.astype(jnp.bfloat16)
            if padded > per and k:
                stack[k - 1, i, per:] = blank
            elif padded > per:
                land[dp, i, per:] = blank
        if k:
            push = remote(stack.at[k - 1], land.at[dp], send.at[k], recv.at[k], (target, ctx))
            push.start()
            pushes.append(push)

    def chain(source, where, side, step):
        return remote(
            source, attn_out.at[where], chain_send.at[side, step], chain_recv.at[side, step],
            right if side == 0 else left,
        )

    def pass_on(step):
        if step == 0:
            for side, there in ((0, has_right), (1, has_left)):
                @pl.when(there)
                def _():
                    chain(own, high, side, 0).start()
            return
        for side, here, there in (
            (0, high - step >= 0, has_right),
            (1, high + step < hi, has_left),
        ):
            where = high - step if side == 0 else high + step

            @pl.when(here)
            def _():
                chain(own, where, side, step - 1).wait_recv()
                if step < hi - 1:
                    @pl.when(there)
                    def _():
                        chain(attn_out.at[where], where, side, step).start()

    def finish(step):
        for side, here, there in (
            (0, high - step >= 0, has_right),
            (1, high + step < hi, has_left),
        ):
            @pl.when(here & there)
            def _():
                chain(own, high, side, step).wait_send()

    parts = 2
    span = tokens.shape[0] // parts

    def part_of(ref, part):
        return ref.at[pl.ds(part * span, span)]

    def hop(h, part):
        source = tokens if h == 0 else hops_land.at[h]
        return remote(
            part_of(source, part), part_of(hops_land.at[h + 1], part), hop_send.at[h, part], hop_recv.at[h, part], right
        )

    def wanted(h, source, target):
        distance = h * lo + target - source
        return (distance >= 1) & (distance <= reach) & (high >= h)

    def aside(h, source, target, device, part):
        block = tokens if h == 0 else hops_land.at[h]
        return remote(
            part_of(block, part), part_of(earlier_out.at[reach - (h * lo + target - source)], part),
            low_send.at[h, target, part], low_recv.at[h, source, part], device,
        )

    def pass_tokens(h, part):
        if h:
            @pl.when(high >= h)
            def _():
                hop(h - 1, part).wait_recv()
        if h < hops:
            @pl.when((high >= h) & has_right)
            def _():
                hop(h, part).start()
        for other in range(lo):
            if lo > 1:
                @pl.when((low != other) & wanted(h, low, other))
                def _():
                    aside(h, low, other, low_peers[other], part).start()
        if h and h * lo <= reach:
            @pl.when(high >= h)
            def _():
                block = pl.ds(part * span, span)
                earlier_out[reach - h * lo, block] = hops_land[h, block]

    def finish_tokens(h, part):
        if h < hops:
            @pl.when((high >= h) & has_right)
            def _():
                hop(h, part).wait_send()
        for other in range(lo):
            if lo > 1:
                @pl.when((low != other) & wanted(h, other, low))
                def _():
                    aside(h, other, low, low_peers[other], part).wait_recv()

                @pl.when((low != other) & wanted(h, low, other))
                def _():
                    aside(h, low, other, low_peers[other], part).wait_send()

    for part in range(parts):
        pass_tokens(0, part)
    for d in range(1, reach + 1):
        @pl.when(ctx < d)
        def _():
            earlier_out[reach - d] = jnp.zeros(earlier_out.shape[1:], earlier_out.dtype)
    order = list(range(2, n)) + [1, 0]
    feed_forward_rows(order[0])
    for push in attn_pushes:
        push.wait_recv()
    for q in range(n):
        own[:, q * cols : (q + 1) * cols] = attn_land[q]
    keep = pltpu.make_async_copy(own, attn_out.at[high], keep_sem)
    keep.start()
    pass_on(0)
    events = [partial(feed_forward_rows, order[1])]
    for step in range(1, max(hi, hops + 1)):
        if step <= hops:
            events += [partial(pass_tokens, step, part) for part in range(parts)]
        if step == 1:
            events.insert(2, partial(feed_forward_rows, order[2]))
        if step < hi:
            events.append(partial(pass_on, step))
        if step == 1:
            events += [partial(feed_forward_rows, k) for k in order[3:]]
    for event in events:
        event()
    for push in pushes:
        push.wait_recv()
    for q in range(n):
        for i in range(3):
            ffn_out[i * padded : (i + 1) * padded, q * cols : (q + 1) * cols] = land[q, i]
    keep.wait()
    for step in range(hi - 1):
        finish(step)
    for h in range(hops + 1):
        for part in range(parts):
            finish_tokens(h, part)
    for push in attn_pushes + pushes:
        push.wait_send()


def weights_in(lay, reach, tokens, pack, pairs, lows, collective_id):
    n, per, cols = lows.shape
    rows = pack.shape[1]
    padded = -(-per // 16) * 16
    vmem = pl.BlockSpec(memory_space=pltpu.VMEM)
    dma = pltpu.SemaphoreType.DMA
    hops = min(lay.hi - 1, (reach + lay.lo - 1) // lay.lo)
    scratch = [
        pltpu.VMEM((hops + 1,) + tokens.shape, tokens.dtype),
        pltpu.VMEM((n, rows, cols), jnp.bfloat16),
        pltpu.VMEM((rows, n * cols), jnp.bfloat16),
        pltpu.VMEM((n - 1, 3, padded, cols), jnp.bfloat16),
        pltpu.VMEM((n, 3, padded, cols), jnp.bfloat16),
        pltpu.VMEM((len(lane_tiles(cols)), 2 * per, 128), jnp.float32),
        dma,
    ]
    for shape in ((hops + 1, 2), (hops + 1, lay.lo, 2), (n,), (n,), (2, lay.hi)):
        scratch += [dma(shape), dma(shape)]
    return pl.pallas_call(
        partial(weights_in_kernel, lay, reach),
        out_shape=(
            jax.ShapeDtypeStruct((lay.hi, rows, n * cols), jnp.bfloat16),
            jax.ShapeDtypeStruct((3 * padded, n * cols), jnp.bfloat16),
            jax.ShapeDtypeStruct((reach,) + tokens.shape, tokens.dtype),
        ),
        in_specs=[vmem] * 4,
        out_specs=(pl.BlockSpec(memory_space=pl.ANY), vmem, vmem),
        scratch_shapes=scratch,
        compiler_params=pltpu.CompilerParams(
            collective_id=collective_id, has_side_effects=True, vmem_limit_bytes=VMEM_LIMIT
        ),
    )(tokens, pack, pairs, lows)


def later_kernel(lay, reach, pieces, out, low_land, moved, arrived, chain_send, chain_recv, low_send, low_recv):
    hi, lo = lay.hi, lay.lo
    dp = lax.axis_index("dp")
    ctx = lax.axis_index("ctx")
    high, low = ctx // lo, lax.rem(ctx, lo)
    hops = min(hi - 1, (reach + lo - 1) // lo)
    right, left = (dp, ctx + lo), (dp, ctx - lo)
    has_right, has_left = high < hi - 1, high > 0
    low_peers = [(dp, high * lo + other) for other in range(lo)]
    barrier = pltpu.get_barrier_semaphore()
    for there, device in [(has_right, right), (has_left, left)] + [
        (low != other, low_peers[other]) for other in range(lo) if lo > 1
    ]:
        @pl.when(there)
        def _():
            pl.semaphore_signal(barrier, inc=1, device_id=device, device_id_type=MESH)
    sides = jnp.where(has_right, 1, 0) + jnp.where(has_left, 1, 0)
    pl.semaphore_wait(barrier, sides + lo - 1)

    def wanted(h, owner, reader):
        distance = h * lo + reader - owner
        return (distance >= 1) & (distance <= reach) & (high >= h)

    def across(h, other):
        return remote(
            pieces.at[reach - (h * lo + low - other)], low_land.at[h, low], low_send.at[h, other],
            low_recv.at[h, low], low_peers[other],
        )

    def from_low(h, other):
        return remote(
            pieces.at[0], low_land.at[h, other], low_send.at[h, other], low_recv.at[h, other], low_peers[other]
        )

    def hop(h):
        return remote(moved.at[h], arrived.at[h - 1], chain_send.at[h], chain_recv.at[h - 1], left)

    for h in range(hops, -1, -1):
        for other in range(lo):
            if lo > 1:
                @pl.when((low != other) & wanted(h, other, low))
                def _():
                    across(h, other).start()
    for h in range(hops, -1, -1):
        out[...] = jnp.zeros_like(out)
        if h and h * lo <= reach:
            out[...] += pieces[reach - h * lo].astype(jnp.float32)
        for other in range(lo):
            if lo > 1:
                @pl.when((low != other) & wanted(h, low, other))
                def _():
                    from_low(h, other).wait_recv()
                    out[...] += low_land[h, other].astype(jnp.float32)
        if h < hops:
            @pl.when(has_right & (high >= h))
            def _():
                hop(h + 1).wait_recv()
                out[...] += arrived[h].astype(jnp.float32)
        if h:
            @pl.when(high >= h)
            def _():
                moved[h] = out[...].astype(moved.dtype)
                hop(h).start()
    for h in range(hops + 1):
        if h:
            @pl.when(high >= h)
            def _():
                hop(h).wait_send()
        for other in range(lo):
            if lo > 1:
                @pl.when((low != other) & wanted(h, other, low))
                def _():
                    across(h, other).wait_send()


def later_sum(lay, reach, pieces, collective_id):
    hops = min(lay.hi - 1, (reach + lay.lo - 1) // lay.lo)
    shape = pieces.shape[1:]
    vmem = pl.BlockSpec(memory_space=pltpu.VMEM)
    dma = pltpu.SemaphoreType.DMA
    return pl.pallas_call(
        partial(later_kernel, lay, reach),
        out_shape=jax.ShapeDtypeStruct(shape, jnp.float32),
        in_specs=[vmem],
        out_specs=vmem,
        scratch_shapes=[
            pltpu.VMEM((hops + 1, lay.lo) + shape, pieces.dtype),
            pltpu.VMEM((hops + 1,) + shape, pieces.dtype),
            pltpu.VMEM((hops + 1,) + shape, pieces.dtype),
        ]
        + [dma((hops + 1,))] * 2
        + [dma((hops + 1, lay.lo))] * 2,
        compiler_params=pltpu.CompilerParams(
            collective_id=collective_id, has_side_effects=True, vmem_limit_bytes=VMEM_LIMIT
        ),
    )(pieces)


def flip(index, bit):
    return index + bit * (1 - 2 * lax.rem(index // bit, 2))


def sum_group_kernel(lay, parts, gains, out, gains_out, core_land, wide_sum, wide_land, keep, low_sum, low_land,
                     gains_sum, gains_land, core_send, core_recv, wide_send, wide_recv, low_send, low_recv,
                     gains_send, gains_recv):
    dp = lax.axis_index("dp")
    ctx = lax.axis_index("ctx")
    hi, lo, wide, n = lay.hi, lay.lo, lay.wide, lay.dp
    high, low = ctx // lo, lax.rem(ctx, lo)
    across, core = dp // 2, lax.rem(dp, 2)
    partner = (across * 2 + 1 - core, ctx)
    low_peers = [(dp, high * lo + lax.rem(low + k, lo)) for k in range(1, lo)]
    wide_peers = [(lax.rem(across + k, wide) * 2 + core, ctx) for k in range(1, wide)]
    gain_peers = [(flip(dp, 1 << i), ctx) for i in range((n - 1).bit_length())]
    gain_peers += [(dp, flip(ctx, 1 << i)) for i in range((lay.ctx - 1).bit_length())]
    greet(low_peers + wide_peers + [partner] + gain_peers)

    def block(h, a):
        return h * lo + lax.rem(low + a, lo)

    def slot(h, a):
        return h * lo + a

    sends = []
    core_copies, wide_copies, low_copies, gain_copies = {}, {}, {}, []
    offsets = list(range(1, lo)) + [0]
    for h in range(hi):
        for a in offsets:
            for b in list(range(1, wide)) + [0]:
                there = lax.rem(across + b, wide)
                copy = remote(
                    parts.at[block(h, a), there * 2 + 1 - core],
                    core_land.at[slot(h, a), b],
                    core_send.at[slot(h, a), b],
                    core_recv.at[slot(h, a), b],
                    partner,
                )
                copy.start()
                core_copies[h, a, b] = copy
                sends.append(copy)

    def gains_step(i):
        if i > len(gain_peers):
            return
        if i == 0:
            gains_sum[0] = gains[...]
        else:
            gain_copies[i - 1].wait_recv()
            gains_sum[i] = gains_sum[i - 1] + gains_land[i - 1]
        if i < len(gain_peers):
            copy = remote(
                gains_sum.at[i], gains_land.at[i], gains_send.at[i], gains_recv.at[i], gain_peers[i]
            )
            copy.start()
            gain_copies.append(copy)
            sends.append(copy)
        else:
            gains_out[...] = gains_sum[i]

    def sum_cores(h, a):
        s = slot(h, a)
        for b in list(range(1, wide)) + [0]:
            there = lax.rem(across + b, wide)
            core_copies[h, a, b].wait_recv()
            total = parts[block(h, a), there * 2 + core].astype(jnp.float32) + core_land[
                s, b
            ].astype(jnp.float32)
            if b:
                wide_sum[s, b - 1] = total.astype(jnp.bfloat16)
                copy = remote(
                    wide_sum.at[s, b - 1], wide_land.at[s, b - 1], wide_send.at[s, b - 1],
                    wide_recv.at[s, b - 1], wide_peers[b - 1],
                )
                copy.start()
                wide_copies[h, a, b] = copy
                sends.append(copy)
            else:
                keep[s] = total

    def sum_wide(h, a):
        s = slot(h, a)
        total = keep[s]
        for b in range(1, wide):
            wide_copies[h, a, b].wait_recv()
            total = total + wide_land[s, b - 1].astype(jnp.float32)
        if a:
            low_sum[h, a - 1] = total.astype(jnp.bfloat16)
            copy = remote(
                low_sum.at[h, a - 1], low_land.at[h, a - 1], low_send.at[h, a - 1],
                low_recv.at[h, a - 1], low_peers[a - 1],
            )
            copy.start()
            low_copies[h, a] = copy
            sends.append(copy)
        else:
            keep[s] = total

    def sum_low(h):
        total = keep[slot(h, 0)]
        for a in range(1, lo):
            low_copies[h, a].wait_recv()
            total = total + low_land[h, a - 1].astype(jnp.float32)
        out[h] = total.astype(jnp.bfloat16)

    gains_step(0)
    for i in range(hi + 2):
        if i < hi:
            for a in offsets:
                sum_cores(i, a)
        gains_step(i + 1)
        if 1 <= i <= hi:
            for a in offsets:
                sum_wide(i - 1, a)
        if 2 <= i:
            sum_low(i - 2)
    for i in range(hi + 3, len(gain_peers) + 1):
        gains_step(i)
    for copy in sends:
        copy.wait_send()


def sum_group(lay, parts, gains, collective_id):
    rows = parts.shape[2]
    lows, wides = max(1, lay.lo - 1), max(1, lay.wide - 1)
    vmem = pl.BlockSpec(memory_space=pltpu.VMEM)
    dma = pltpu.SemaphoreType.DMA
    count = (lay.dp - 1).bit_length() + (lay.ctx - 1).bit_length()
    scratch = [
        pltpu.VMEM((lay.ctx, lay.wide, rows, D), jnp.bfloat16),
        pltpu.VMEM((lay.ctx, wides, rows, D), jnp.bfloat16),
        pltpu.VMEM((lay.ctx, wides, rows, D), jnp.bfloat16),
        pltpu.VMEM((lay.ctx, rows, D), jnp.float32),
        pltpu.VMEM((lay.hi, lows, rows, D), jnp.bfloat16),
        pltpu.VMEM((lay.hi, lows, rows, D), jnp.bfloat16),
        pltpu.VMEM((count + 1,) + gains.shape, jnp.float32),
        pltpu.VMEM((count,) + gains.shape, jnp.float32),
    ]
    for shape in ((lay.ctx, lay.wide), (lay.ctx, wides), (lay.hi, lows), (count,)):
        scratch += [dma(shape), dma(shape)]
    return pl.pallas_call(
        partial(sum_group_kernel, lay),
        out_shape=(
            jax.ShapeDtypeStruct((lay.hi, rows, D), jnp.bfloat16),
            jax.ShapeDtypeStruct(gains.shape, jnp.float32),
        ),
        in_specs=[vmem] * 2,
        out_specs=(vmem,) * 2,
        scratch_shapes=scratch,
        compiler_params=pltpu.CompilerParams(
            collective_id=collective_id, has_side_effects=True, vmem_limit_bytes=VMEM_LIMIT
        ),
    )(parts, gains)


def grads_out_kernel(lay, rows, attn, pairs_out, lows_out, attn_out, stack, land, lanes, hi_land, last, last_land,
                     send, recv, hi_send, hi_recv, last_send, last_recv):
    n, hi, lo = lay.dp, lay.hi, lay.lo
    dp = lax.axis_index("dp")
    ctx = lax.axis_index("ctx")
    high, low = ctx // lo, lax.rem(ctx, lo)
    cols = lows_out.shape[2]
    per = lows_out.shape[1]
    padded = rows.shape[0] // 3
    attn_rows = attn.shape[1]
    hi_peers = [(dp, lax.rem(high + k, hi) * lo + low) for k in range(1, hi)]
    greet([(lax.rem(dp + k, n), ctx) for k in range(1, n)] + hi_peers)
    hi_pushes = []
    for k in range(1, hi):
        push = remote(
            attn.at[lax.rem(high + k, hi)], hi_land.at[k - 1], hi_send.at[k], hi_recv.at[k], hi_peers[k - 1]
        )
        push.start()
        hi_pushes.append(push)
    for q in range(n):
        for i in range(3):
            stack[q, i] = rows[i * padded : (i + 1) * padded, q * cols : (q + 1) * cols]
    pushes = []
    for k in range(1, n):
        target = lax.rem(dp + k, n)
        push = remote(stack.at[target], land.at[dp], send.at[k], recv.at[k], (target, ctx))
        push.start()
        pushes.append(push)
    land[dp] = stack[dp]
    total = attn[high].astype(jnp.float32)
    for k, push in enumerate(hi_pushes):
        push.wait_recv()
        total = total + hi_land[k].astype(jnp.float32)
    for q in range(n):
        last[q] = total[:, q * cols : (q + 1) * cols].astype(jnp.bfloat16)
    last_pushes = []
    for k in range(1, n):
        target = lax.rem(dp + k, n)
        push = remote(last.at[target], last_land.at[dp], last_send.at[k], last_recv.at[k], (target, ctx))
        push.start()
        last_pushes.append(push)
    last_land[dp] = last[dp]

    def place(q):
        for j, (first, width) in enumerate(lane_tiles(cols)):
            for i in range(2):
                piece = land[q, i, :per, first : first + width].astype(jnp.float32)
                if width < 128:
                    piece = jnp.concatenate(
                        [piece, jnp.zeros((per, 128 - width), jnp.float32)], axis=1
                    )
                lanes[j, pl.ds(i, per, stride=2), :] = piece
            pairs_out[q, :, first : first + width] = lanes[j, :, :width]
        lows_out[q] = land[q, 2, :per].astype(jnp.float32)

    for push in pushes:
        push.wait_recv()
    for q in range(n):
        place(q)
    for push in last_pushes:
        push.wait_recv()
    for q in range(n):
        attn_out[q * attn_rows : (q + 1) * attn_rows] = last_land[q].astype(jnp.float32)
    for push in hi_pushes + pushes + last_pushes:
        push.wait_send()


def grads_out(lay, rows, attn, per, collective_id):
    padded = rows.shape[0] // 3
    n, cols = lay.dp, rows.shape[1] // lay.dp
    attn_rows = attn.shape[1]
    vmem = pl.BlockSpec(memory_space=pltpu.VMEM)
    dma = pltpu.SemaphoreType.DMA
    return pl.pallas_call(
        partial(grads_out_kernel, lay),
        out_shape=(
            jax.ShapeDtypeStruct((n, 2 * per, cols), jnp.float32),
            jax.ShapeDtypeStruct((n, per, cols), jnp.float32),
            jax.ShapeDtypeStruct((n * attn_rows, cols), jnp.float32),
        ),
        in_specs=[vmem] * 2,
        out_specs=(vmem,) * 3,
        scratch_shapes=[
            pltpu.VMEM((n, 3, padded, cols), jnp.bfloat16),
            pltpu.VMEM((n, 3, padded, cols), jnp.bfloat16),
            pltpu.VMEM((len(lane_tiles(cols)), 2 * per, 128), jnp.float32),
            pltpu.VMEM((max(1, lay.hi - 1), attn_rows, D), jnp.bfloat16),
            pltpu.VMEM((n, attn_rows, cols), jnp.bfloat16),
            pltpu.VMEM((n, attn_rows, cols), jnp.bfloat16),
        ]
        + [dma((n,))] * 2
        + [dma((lay.hi,))] * 2
        + [dma((n,))] * 2,
        compiler_params=pltpu.CompilerParams(
            collective_id=collective_id, has_side_effects=True, vmem_limit_bytes=VMEM_LIMIT
        ),
    )(rows, attn)


def in_tiles(total, size, body, begin=0):
    whole = total // size

    def step(i, carry):
        body(pl.multiple_of(begin + i * size, math.gcd(begin, size)), size)
        return carry

    if whole:
        lax.fori_loop(0, whole, step, 0)
    if total % size:
        body(begin + whole * size, total % size)


def dot_nt(left, right):
    return lax.dot_general(left, right, (((1,), (1,)), ((), ())), preferred_element_type=jnp.float32)


def dot_nn(left, right):
    return lax.dot_general(left, right, (((1,), (0,)), ((), ())), preferred_element_type=jnp.float32)


ROOT = math.sqrt(2.0 / math.pi)


def feed_forward_kernel(
    lay, mid, weights, mixed, cotangent, valid, gain,
    result, grad_mid, grad_gain, grad_weights,
    w_gate, w_up, w_down, gate_t, up_t, act, slope, hidden, hidden_t, grads, parts, core_land, sums, via, landed,
    total, dy, weight_sem, core_send, core_recv, share_send, share_recv,
    send, recv, via_send, via_recv, dy_send, dy_recv, dy_pass,
):
    chip, core, high = lay.place()
    n, wide = lay.chips, lay.wide
    tokens = mixed.shape[0]
    units = w_gate.shape[0]
    padded = units // lay.hi
    loads = [
        pltpu.make_async_copy(
            weights.at[h, pl.ds(i * padded, padded)], held.at[pl.ds(h * padded, padded)], weight_sem.at[i, h]
        )
        for i, held in enumerate((w_gate, w_up, w_down))
        for h in range(lay.hi)
    ]
    for load in loads:
        load.start()
    peers = [lay.device(lay.offset(chip, k), core, high) for k in range(n)]
    owners = [lay.device(lay.offset(chip, k, -1), core, high) for k in range(n)]
    partner = lay.device(chip, 1 - core, high)
    mine = pl.ds(pl.multiple_of(core * tokens, tokens), tokens)
    theirs = pl.ds(pl.multiple_of((1 - core) * tokens, tokens), tokens)
    half = tokens // 2
    halves = (pl.ds(0, half), pl.ds(half, half))
    straight, bent = lay.straight(), lay.bent()
    place = [lay.position(k) for k in range(n)]
    greet(peers[1:] + [partner])

    def to_partner(phase, k):
        return remote(
            parts.at[place[k], theirs], core_land.at[k], core_send.at[phase, k], core_recv.at[phase, k], partner
        )

    def to_owner(phase, k, h):
        return remote(
            sums.at[k - 1, halves[h]], landed.at[place[k] - len(bent), halves[h]], send.at[phase, k, h],
            recv.at[phase, k, h], owners[k],
        )

    def to_neighbour(phase, k, h):
        step = k % wide if h == 0 else k // wide * wide
        return remote(
            sums.at[k - 1, halves[h]], via.at[place[k], halves[h]], via_send.at[phase, k, h], via_recv.at[phase, k, h],
            owners[step],
        )

    def added(k):
        if k < wide:
            return 1, [k + b * wide for b in range(1, lay.lo)]
        return 0, [k + step for step in range(1, wide)]

    def add_core(phase, k):
        to_partner(phase, k).wait_recv()

        def chunk(first, rows):
            span = pl.ds(first, rows)
            here = pl.ds(pl.multiple_of(core * tokens + first, rows), rows)
            both = parts[place[k], here].astype(jnp.float32) + core_land[k, span].astype(jnp.float32)
            if k:
                sums[k - 1, span] = both.astype(jnp.bfloat16)
            else:
                total[span] = both

        in_tiles(tokens, 32, chunk)
        if k in bent:
            for h in range(2):
                to_neighbour(phase, k, h).start()
        elif k:
            h, others = added(k)
            to_owner(phase, k, 1 - h).start()
            if not others:
                to_owner(phase, k, h).start()

    def add_neighbours(phase, k):
        h, others = added(k)
        if not others:
            return
        for other in others:
            to_neighbour(phase, other, h).wait_recv()

        def chunk(first, rows):
            span = pl.ds(first + h * half, rows)
            value = sums[k - 1, span].astype(jnp.float32)
            for other in others:
                value = value + via[place[other], span].astype(jnp.float32)
            sums[k - 1, span] = value.astype(jnp.bfloat16)

        in_tiles(half, 32, chunk)
        to_owner(phase, k, h).start()

    def add_owners(phase):
        for k in straight:
            for h in range(2):
                to_owner(phase, k, h).wait_recv()

        def chunk(first, rows):
            span = pl.ds(first, rows)
            value = total[span]
            for k in straight:
                value = value + landed[place[k] - len(bent), span].astype(jnp.float32)
            total[span] = value

        in_tiles(tokens, 32, chunk)

    def settle(phase):
        for k in range(n):
            to_partner(phase, k).wait_send()
            for h in range(2):
                if k in bent:
                    to_neighbour(phase, k, h).wait_send()
                elif k:
                    to_owner(phase, k, h).wait_send()

    rows_of = 2 * tokens

    def joined(ref, group, *index):
        value = ref[(pl.ds(*group),) + index]
        return value.reshape((group[1] * rows_of,) + value.shape[2:])

    def forward_units(group, begin, end):
        count = group[1]

        def tile(first, width):
            units_here = pl.ds(first, width)
            weights = jnp.concatenate([w_gate[units_here], w_up[units_here]], axis=0)
            both = dot_nt(joined(mid, group), weights)
            gate, up = both[:, :width], both[:, width:]
            square = gate * gate
            tanh = jnp.tanh(gate * (ROOT + (0.044715 * ROOT) * square))
            half_way = 0.5 + 0.5 * tanh
            active = gate * half_way
            slant = half_way + active * (1.0 - tanh) * (ROOT + (3.0 * 0.044715 * ROOT) * square)
            product = (active * up).astype(jnp.bfloat16)
            shape = (count, rows_of, width)
            act[pl.ds(*group), :, units_here] = active.astype(jnp.bfloat16).reshape(shape)
            slope[pl.ds(*group), :, units_here] = (slant * up).astype(jnp.bfloat16).reshape(shape)
            hidden[: count * rows_of, units_here] = product
            for c in range(count):
                hidden_t[group[0] + c, units_here] = product[c * rows_of : (c + 1) * rows_of].T

        in_tiles(end - begin, 128, tile, begin)

    def forward_down(group):
        count = group[1]

        def tile(first, width):
            lanes = pl.ds(first, width)
            value = dot_nn(hidden[: count * rows_of], w_down[:, lanes]).astype(jnp.bfloat16)
            parts[pl.ds(*group), :, lanes] = value.reshape(count, rows_of, width)

        in_tiles(D, 256, tile)

    def backward_units(group):
        count = group[1]

        def tile(first, width):
            units_here = pl.ds(first, width)
            grad = dot_nt(joined(dy, group), w_down[units_here])
            up_grad = (grad * joined(act, group, slice(None), units_here).astype(jnp.float32)).astype(jnp.bfloat16)
            gate_grad = (grad * joined(slope, group, slice(None), units_here).astype(jnp.float32)).astype(jnp.bfloat16)
            grads[0, : count * rows_of, units_here] = gate_grad
            grads[1, : count * rows_of, units_here] = up_grad
            for c in range(count):
                rows = slice(c * rows_of, (c + 1) * rows_of)
                gate_t[group[0] + c, units_here] = gate_grad[rows].T
                up_t[group[0] + c, units_here] = up_grad[rows].T

        in_tiles(units, 256, tile)

    def backward_in(group):
        count = group[1]

        def tile(first, width):
            lanes = pl.ds(first, width)
            both = dot_nn(grads[0, : count * rows_of], w_gate[:, lanes]) + dot_nn(
                grads[1, : count * rows_of], w_up[:, lanes]
            )
            parts[pl.ds(*group), :, lanes] = both.astype(jnp.bfloat16).reshape(count, rows_of, width)

        in_tiles(D, 256, tile)

    far, near, here = (0, len(bent)), (len(bent), len(straight)), (n - 1, 1)
    most = hidden.shape[0] // rows_of

    def runs(group):
        return [(first, min(most, group[0] + group[1] - first)) for first in range(group[0], sum(group), most)]

    quarter = units // 512 * 128
    for load in loads:
        load.wait()
    for run in runs(far):
        forward_units(run, 0, units)
        forward_down(run)
    for k in bent:
        to_partner(0, k).start()
    for i, run in enumerate(runs(near)):
        forward_units(run, 0, 2 * quarter)
        if i == 0:
            for k in bent:
                add_core(0, k)
        forward_units(run, 2 * quarter, units)
        forward_down(run)
    for k in straight:
        to_partner(0, k).start()
    forward_units(here, 0, 2 * quarter)
    for k in straight:
        add_core(0, k)
    for k in straight:
        add_neighbours(0, k)
    forward_units(here, 2 * quarter, units)
    forward_down(here)
    to_partner(0, 0).start()
    add_core(0, 0)
    add_owners(0)

    grad_gain[...] = jnp.zeros_like(grad_gain)
    scale = 1.0 + gain[...]

    def finish(first, rows):
        span = pl.ds(first, rows)
        spot = pl.ds(pl.multiple_of(core * tokens + first, rows), rows)
        y = total[span]
        ok = valid[span]
        rate = lax.rsqrt(jnp.mean(y * y, axis=-1, keepdims=True) + EPS)
        unit = y * rate
        result[span] = ((mixed[span] + unit * scale) * ok).astype(jnp.bfloat16)
        upstream = cotangent[span].astype(jnp.float32) * ok
        down = upstream * unit
        for r in range(0, rows, 8):
            grad_gain[...] += down[r : r + 8]
        scaled = upstream * scale
        inner = jnp.mean(scaled * unit, axis=-1, keepdims=True)
        dy[n - 1, spot] = (rate * (scaled - unit * inner)).astype(jnp.bfloat16)

    in_tiles(tokens, 32, finish)

    def dy_half(k, h):
        return dy.at[place[k], pl.ds(pl.multiple_of(core * tokens + h * half, half), half)]

    def dy_push(k, h):
        return remote(dy_half(0, h), dy_half(k, h), dy_send.at[k, h], dy_recv.at[k, h], peers[k])

    def dy_onward(k, h, step):
        return remote(
            dy_half(k, h), dy_half(k + step, h), dy_pass.at[k + step, h], dy_recv.at[k + step, h], peers[step]
        )

    shares = [
        remote(dy.at[place[k], mine], dy.at[place[k], mine], share_send.at[k], share_recv.at[k], partner)
        for k in range(n)
    ]
    ordered = [(k, i if k < wide else 1 - i) for i in range(2) for k in straight]
    for k, h in ordered:
        dy_push(k, h).start()
    shares[0].start()
    settle(0)
    shares[0].wait_recv()
    backward_units(here)
    backward_in(here)
    to_partner(1, 0).start()
    onward = []
    for k, h in ordered:
        dy_push(k, h).wait_recv()
        if k < wide and h == 0:
            onward += [(k, h, b * wide) for b in range(1, lay.lo)]
        elif k >= wide and h == 1:
            onward += [(k, h, step) for step in range(1, wide)]
        for go in onward:
            if go[:2] == (k, h):
                dy_onward(*go).start()
    for k in straight:
        shares[k].start()
    add_core(1, 0)
    for k in straight:
        shares[k].wait_recv()
    for i, run in enumerate(runs(near)):
        backward_units(run)
        if i == 0:
            for k in bent:
                for h in range(2):
                    dy_push(k, h).wait_recv()
                shares[k].start()
        backward_in(run)
    for k in straight:
        to_partner(1, k).start()
    for k in bent:
        shares[k].wait_recv()
    for i, run in enumerate(runs(far)):
        backward_units(run)
        if i == 0:
            for k in straight:
                add_core(1, k)
        backward_in(run)
    if not bent:
        for k in straight:
            add_core(1, k)
    for k in bent:
        to_partner(1, k).start()
    for k in bent:
        add_core(1, k)

    def weight_grad(left_ref, right, i):
        def tile(first, width):
            lanes = pl.ds(first, width)
            value = dot_nn(left_ref[0], right[0, :, lanes])
            for c in range(1, n):
                value = value + dot_nn(left_ref[c], right[c, :, lanes])
            value = value.astype(jnp.bfloat16)
            for h in range(lay.hi):
                grad_weights[h, i * padded : (i + 1) * padded, lanes] = value[h * padded : (h + 1) * padded]

        in_tiles(D, 256, tile)

    weight_grad(hidden_t, dy, 2)
    for k in straight:
        add_neighbours(1, k)
    weight_grad(gate_t, mid, 0)
    weight_grad(up_t, mid, 1)
    add_owners(1)
    grad_mid[...] = total[...]
    settle(1)
    for k, h in ordered:
        dy_push(k, h).wait_send()
    for go in onward:
        dy_onward(*go).wait_send()
    for share in shares:
        share.wait_send()


def feed_forward(lay, mid, weights, mixed, cotangent, valid, gain, collective_id):
    n = lay.chips
    tokens = mixed.shape[0]
    units = weights.shape[0] * weights.shape[1] // 3
    most = min(n, max(1, 1920 // units))
    low, high = jnp.bfloat16, jnp.float32
    vmem = pl.BlockSpec(memory_space=pltpu.VMEM)
    dma = pltpu.SemaphoreType.DMA
    return pl.pallas_call(
        partial(feed_forward_kernel, lay),
        out_shape=(
            jax.ShapeDtypeStruct((tokens, D), low),
            jax.ShapeDtypeStruct((tokens, D), high),
            jax.ShapeDtypeStruct((8, D), high),
            jax.ShapeDtypeStruct(weights.shape, low),
        ),
        in_specs=[vmem, pl.BlockSpec(memory_space=pl.ANY)] + [vmem] * 4,
        out_specs=(vmem,) * 4,
        scratch_shapes=[
            pltpu.VMEM((units, D), low),
            pltpu.VMEM((units, D), low),
            pltpu.VMEM((units, D), low),
            pltpu.VMEM((n, units, 2 * tokens), low),
            pltpu.VMEM((n, units, 2 * tokens), low),
            pltpu.VMEM((n, 2 * tokens, units), low),
            pltpu.VMEM((n, 2 * tokens, units), low),
            pltpu.VMEM((most * 2 * tokens, units), low),
            pltpu.VMEM((n, units, 2 * tokens), low),
            pltpu.VMEM((2, most * 2 * tokens, units), low),
            pltpu.VMEM((n, 2 * tokens, D), low),
            pltpu.VMEM((n, tokens, D), low),
            pltpu.VMEM((max(1, n - 1), tokens, D), low),
            pltpu.VMEM((max(1, len(lay.bent())), tokens if lay.bent() else 16, D), low),
            pltpu.VMEM((max(1, len(lay.straight())), tokens, D), low),
            pltpu.VMEM((tokens, D), high),
            pltpu.VMEM((n, 2 * tokens, D), low),
            dma((3, lay.hi)),
        ]
        + [dma((2, n))] * 2
        + [dma((n,))] * 2
        + [dma((2, n, 2))] * 4
        + [dma((n, 2))] * 3,
        compiler_params=pltpu.CompilerParams(
            collective_id=collective_id, has_side_effects=True, vmem_limit_bytes=63 * 2**20
        ),
    )(mid, weights, mixed, cotangent, valid, gain)


def norm_scaled(v, gain):
    return v * lax.rsqrt(jnp.mean(v * v, axis=-1, keepdims=True) + EPS) * (1.0 + gain)


def rotate(v, angle):
    half = v.shape[-1] // 2
    cosine = jnp.cos(angle)
    sine = jnp.sin(angle)
    first = v[..., :half]
    second = v[..., half:]
    return jnp.concatenate(
        [first * cosine - second * sine, second * cosine + first * sine], axis=-1
    )


def angles_of(positions):
    inverse = 1.0 / 10000.0 ** (jnp.arange(HD // 2, dtype=jnp.float32) * (2.0 / HD))
    return positions.astype(jnp.float32)[:, None] * inverse[None, :]


def head_inputs(projected, gain_query, gain_key, angle):
    query = projected[..., : HEADS * HD].reshape(projected.shape[:-1] + (HEADS, HD))
    key_rows = projected[..., HEADS * HD : (HEADS + 1) * HD]
    value_rows = projected[..., (HEADS + 1) * HD :]
    query = rotate(norm_scaled(query, gain_query), angle[:, None, :])
    key_rows = rotate(norm_scaled(key_rows, gain_key), angle)
    return (query, key_rows, value_rows)


def contract(left, right, dims_left, dims_right):
    return lax.dot_general(
        left, right, ((dims_left, dims_right), ((), ())), preferred_element_type=jnp.float32
    )


def per_device(lay, tokens, lengths, w_qkv, w_out, w_gate_up, w_down, gains, cotangent):
    seq_count = tokens.shape[0]
    local_len = tokens.shape[1]
    reach = (WINDOW - 1) // local_len + 1
    scale = 1.0 / math.sqrt(HD)
    units = w_down.shape[0]
    per = units // lay.dp
    qkv_rows, out_rows = w_qkv.shape[0], w_out.shape[0]
    cols = w_qkv.shape[1]
    used = qkv_rows + out_rows + 1
    block = 16 * lay.dp
    pack_rows = -(-used // block) * block
    gain_row = jnp.pad(gains, (0, cols - gains.shape[0]))[None]
    pack = jnp.concatenate(
        [w_qkv, w_out, gain_row, jnp.zeros((pack_rows - used, cols), jnp.float32)], axis=0
    ).astype(jnp.bfloat16)
    plane, ffn_rows, earlier_tokens = weights_in(
        lay,
        reach,
        tokens,
        pack.reshape(lay.dp, pack_rows // lay.dp, cols),
        w_gate_up.reshape(lay.dp, 2 * per, cols),
        w_down.reshape(lay.dp, per, cols),
        5,
    )
    ffn_all = lax.all_gather(ffn_rows, "ctx", axis=0, axis_index_groups=lay.hi_groups)
    attn_all = gather_group(
        lay,
        plane,
        (lay.hi, lay.lo, lay.dp, pack_rows // lay.dp, D),
        lambda out, k, chip, core: out.at[
            :, chip // lay.wide, lax.rem(chip, lay.wide) * 2 + core
        ],
        6,
    ).reshape(lay.ctx, pack_rows, D)
    full_qkv = attn_all[:, :qkv_rows].reshape(lay.ctx * qkv_rows, D)
    full_out = attn_all[:, qkv_rows : qkv_rows + out_rows].reshape(lay.ctx * out_rows, D)
    gain_all = (
        attn_all[:, used - 1]
        .reshape(lay.ctx, lay.dp, cols)[:, :, : gains.shape[0]]
        .transpose(1, 0, 2)
        .reshape(-1)
        .astype(jnp.float32)
    )
    gain_in = gain_all[:D]
    gain_attn = gain_all[D : 2 * D]
    gain_pre = gain_all[2 * D : 3 * D]
    gain_post = gain_all[3 * D : 4 * D]
    gain_query = gain_all[4 * D : 4 * D + HD]
    gain_key = gain_all[4 * D + HD :]
    offset = lax.axis_index("ctx") * local_len
    positions = offset + jnp.arange(local_len, dtype=jnp.int32)
    angle = angles_of(positions)
    valid = positions[None, :] < lengths[:, None]
    inputs = tokens.astype(jnp.float32)
    normed_in, pull_in = jax.vjp(norm_scaled, inputs, gain_in)
    normed_low = normed_in.astype(jnp.bfloat16)
    projected = contract(normed_low, full_qkv, (2,), (1,))
    (query, key_rot, value_rows), pull_heads = jax.vjp(
        partial(head_inputs, angle=angle), projected, gain_query, gain_key
    )
    query_low = query.astype(jnp.bfloat16)
    key_pos = offset - reach * local_len + jnp.arange((reach + 1) * local_len, dtype=jnp.int32)
    earlier = earlier_tokens.transpose(1, 0, 2, 3).reshape(seq_count, reach * local_len, D)
    earlier = norm_scaled(earlier.astype(jnp.float32), gain_in).astype(jnp.bfloat16)
    earlier = contract(earlier, full_qkv[HEADS * HD :], (2,), (1,))
    earlier_keys = rotate(
        norm_scaled(earlier[..., :HD], gain_key), angles_of(key_pos[: reach * local_len])
    )
    key_pairs = jnp.concatenate(
        [
            jnp.concatenate([earlier_keys, earlier[..., HD:]], axis=-1).astype(jnp.bfloat16),
            jnp.concatenate([key_rot, value_rows], axis=-1).astype(jnp.bfloat16),
        ],
        axis=1,
    )
    keys_low = key_pairs[..., :HD]
    values_low = key_pairs[..., HD:]
    key_grid = key_pos[None, None, :]
    query_grid = positions[None, :, None]
    allowed = (
        (key_grid >= 0)
        & (key_grid <= query_grid)
        & (query_grid - key_grid < WINDOW)
        & ((key_grid < lengths[:, None, None]) | (key_grid == query_grid))
    )

    def scores_of():
        raw = jnp.einsum("schd,skd->shck", query_low, keys_low, preferred_element_type=jnp.float32)
        return jnp.where(allowed[:, None], raw * scale, -BIG)

    scores = scores_of()
    top = jnp.max(scores, axis=-1, keepdims=True)
    expo = jnp.exp(scores - top)
    total = jnp.sum(expo, axis=-1, keepdims=True)
    probs = expo / total
    log_total = top + jnp.log(total)
    probs_low = probs.astype(jnp.bfloat16)
    attended = jnp.einsum(
        "shck,skd->schd", probs_low, values_low, preferred_element_type=jnp.float32
    )
    attended_low = attended.reshape(seq_count, local_len, HEADS * HD).astype(jnp.bfloat16)
    out_proj = contract(attended_low, full_out, (2,), (0,))
    normed_out, pull_out = jax.vjp(norm_scaled, out_proj, gain_attn)
    mixed = inputs + normed_out
    normed_mid, pull_mid = jax.vjp(norm_scaled, mixed, gain_pre)
    mid_low = normed_mid.astype(jnp.bfloat16)
    token_count = seq_count * local_len
    mid_all = gather_group(
        lay,
        mid_low.reshape(2, token_count // 2, D),
        (lay.chips, 2, 2, token_count // 2, D),
        lambda out, k, chip, core: out.at[lay.position(k), core],
        1,
    ).reshape(lay.chips, 2 * token_count, D)
    result, grad_mid, grad_gain_post, grad_ffn = feed_forward(
        lay,
        mid_all,
        ffn_all,
        mixed.reshape(token_count, D),
        cotangent.reshape(token_count, D),
        valid.reshape(token_count, 1).astype(jnp.float32),
        gain_post[None],
        2,
    )
    result = result.reshape(mixed.shape)
    grad_mid = grad_mid.reshape(mixed.shape)
    grad_gain_post = jnp.sum(grad_gain_post, axis=0)
    upstream = jnp.where(valid[..., None], cotangent.astype(jnp.float32), 0.0)
    grad_mixed_in, grad_gain_pre = pull_mid(grad_mid)
    grad_mixed = upstream + grad_mixed_in
    grad_proj, grad_gain_attn = pull_out(grad_mixed)
    proj_low = grad_proj.astype(jnp.bfloat16)
    grad_attended = contract(proj_low, full_out, (2,), (1,))
    grad_w_out = contract(attended_low, proj_low, (0, 1), (0, 1))
    attn_low = grad_attended.astype(jnp.bfloat16).reshape(seq_count, local_len, HEADS, HD)
    again_probs = jnp.exp(scores_of() - log_total)
    again_low = again_probs.astype(jnp.bfloat16)
    grad_values = jnp.einsum(
        "shck,schd->skd", again_low, attn_low, preferred_element_type=jnp.float32
    )
    grad_probs = jnp.einsum(
        "schd,skd->shck", attn_low, values_low, preferred_element_type=jnp.float32
    )
    row_dot = jnp.sum(again_probs * grad_probs, axis=-1, keepdims=True)
    grad_scores = (scale * again_probs * (grad_probs - row_dot)).astype(jnp.bfloat16)
    grad_query = jnp.einsum(
        "shck,skd->schd", grad_scores, keys_low, preferred_element_type=jnp.float32
    )
    grad_keys = jnp.einsum(
        "shck,schd->skd", grad_scores, query_low, preferred_element_type=jnp.float32
    )
    grad_pairs = jnp.concatenate([grad_keys, grad_values], axis=-1)
    own_grad = grad_pairs[:, reach * local_len :]
    pieces = grad_pairs[:, : reach * local_len].astype(jnp.bfloat16)
    pieces = pieces.reshape(seq_count, reach, local_len, 2 * HD).transpose(1, 0, 2, 3)
    later = later_sum(lay, reach, pieces, 11)
    own_grad = own_grad + later
    grad_projected, grad_gain_query, grad_gain_key = pull_heads(
        (grad_query, own_grad[..., :HD], own_grad[..., HD:])
    )
    qkv_low = grad_projected.astype(jnp.bfloat16)
    grad_w_qkv = contract(qkv_low, normed_low, (0, 1), (0, 1))
    grad_normed = contract(qkv_low, full_qkv, (2,), (0,))
    grad_in_norm, grad_gain_in = pull_in(grad_normed)
    grad_input = grad_mixed + grad_in_norm
    grad_gain_all = jnp.concatenate(
        [
            grad_gain_in,
            grad_gain_attn,
            grad_gain_pre,
            grad_gain_post,
            grad_gain_query,
            grad_gain_key,
        ]
    )
    sum_rows = -(-(qkv_rows + out_rows) // block) * block
    partial_sums = jnp.concatenate(
        [
            grad_w_qkv.astype(jnp.bfloat16).reshape(lay.ctx, qkv_rows, D),
            grad_w_out.astype(jnp.bfloat16).reshape(lay.ctx, out_rows, D),
            jnp.zeros((lay.ctx, sum_rows - qkv_rows - out_rows, D), jnp.bfloat16),
        ],
        axis=1,
    ).reshape(lay.ctx, lay.dp, sum_rows // lay.dp, D)
    plane_attn, gains_sum = sum_group(lay, partial_sums, grad_gain_all.reshape(-1, 128), 8)
    owned = lax.psum_scatter(grad_ffn, "ctx", scatter_dimension=0, axis_index_groups=lay.hi_groups)
    part_gate_up, part_down, part_attn = grads_out(lay, owned, plane_attn, per, 9)
    part_qkv = part_attn[:qkv_rows]
    part_out = part_attn[qkv_rows : qkv_rows + out_rows]
    place = (lax.axis_index("dp") * lay.ctx + lax.axis_index("ctx")) * gains.shape[0]
    part_gains = lax.dynamic_slice_in_dim(gains_sum.reshape(-1), place, gains.shape[0])
    part_gate_up = part_gate_up.reshape(w_gate_up.shape)
    part_down = part_down.reshape(w_down.shape)
    return (result, grad_input, part_qkv, part_out, part_gate_up, part_down, part_gains)


def solution(mesh):
    placed = (
        P("dp", "ctx", None),
        P("dp"),
        P("ctx", "dp"),
        P("ctx", "dp"),
        P("ctx", "dp"),
        P("ctx", "dp"),
        P(("dp", "ctx")),
        P("dp", "ctx", None),
    )
    return jax.shard_map(
        partial(per_device, Layout(mesh)),
        mesh=mesh,
        in_specs=placed,
        out_specs=(
            P("dp", "ctx", None),
            P("dp", "ctx", None),
            P("ctx", "dp"),
            P("ctx", "dp"),
            P("ctx", "dp"),
            P("ctx", "dp"),
            P(("dp", "ctx")),
        ),
        check_vma=False,
    )
```

```python
from functools import partial
import math

import jax
import jax.numpy as jnp
from jax import lax
from jax.experimental import pallas as pl
from jax.experimental.pallas import tpu as pltpu
from jax.sharding import PartitionSpec as P

D = 1152
HEADS = 4
HD = 256
WINDOW = 512
GROUP = 8

EPS = 1e-06
BIG = 1e30
MESH = pl.DeviceIdType.MESH
VMEM_LIMIT = 56 * 2**20


class Layout:
    def __init__(self, mesh):
        self.dp = mesh.shape["dp"]
        self.ctx = mesh.shape["ctx"]
        self.lo = max(1, GROUP // self.dp)
        self.hi = self.ctx // self.lo
        self.wide = self.dp // 2
        self.chips = self.wide * self.lo
        self.group = self.dp * self.lo
        self.hi_groups = [
            [h * self.lo + low for h in range(self.hi)] for low in range(self.lo)
        ]

    def place(self):
        dp = lax.axis_index("dp")
        ctx = lax.axis_index("ctx")
        chip = lax.rem(ctx, self.lo) * self.wide + dp // 2
        return chip, lax.rem(dp, 2), ctx // self.lo

    def offset(self, chip, k, sign=1):
        across = lax.rem(chip, self.wide) + self.wide + sign * (k % self.wide)
        low = chip // self.wide + self.lo + sign * (k // self.wide)
        return lax.rem(low, self.lo) * self.wide + lax.rem(across, self.wide)

    def straight(self):
        return list(range(1, self.wide)) + [low * self.wide for low in range(1, self.lo)]

    def bent(self):
        return [k for k in range(1, self.chips) if k not in self.straight()]

    def position(self, k):
        return (self.bent() + self.straight() + [0]).index(k)

    def device(self, chip, core, high):
        return (lax.rem(chip, self.wide) * 2 + core, high * self.lo + chip // self.wide)


def remote(src, dst, send, recv, device):
    return pltpu.make_async_remote_copy(
        src_ref=src, dst_ref=dst, send_sem=send, recv_sem=recv, device_id=device, device_id_type=MESH
    )


def greet(devices):
    barrier = pltpu.get_barrier_semaphore()
    for device in devices:
        pl.semaphore_signal(barrier, inc=1, device_id=device, device_id_type=MESH)
    pl.semaphore_wait(barrier, len(devices))


def gather_group_kernel(lay, slot, own, out, local_sem, send, recv, pass_send, core_send, core_recv):
    chip, core, high = lay.place()
    n = lay.chips
    half = own.shape[0] // 2
    halves = (pl.ds(0, half), pl.ds(half, half))
    peers = [lay.device(lay.offset(chip, k), core, high) for k in range(n)]
    sources = [lay.offset(chip, k, -1) for k in range(n)]
    partner = lay.device(chip, 1 - core, high)
    greet(peers[1:] + [partner])
    mine = [slot(out, k, chip, core) for k in range(n)]
    straight, bent = lay.straight(), lay.bent()
    keep = pltpu.make_async_copy(own, mine[0], local_sem)
    keep.start()
    pushes = []

    def push(k, h, source, target, sem):
        copy = remote(source.at[halves[h]], target.at[halves[h]], sem, recv.at[k, h], peers[k])
        return copy

    ordered = [(k, i if k < lay.wide else 1 - i) for i in range(2) for k in straight]
    for k, h in ordered:
        copy = push(k, h, own, mine[k], send.at[k, h])
        copy.start()
        pushes.append(copy)
    shares = [remote(own, mine[0], core_send.at[0], core_recv.at[0], partner)]
    shares[0].start()

    def arrived(k, h):
        copy = remote(own.at[halves[h]], mine[k].at[halves[h]], send.at[k, h], recv.at[k, h], peers[k])
        copy.wait_recv()

    for k, h in ordered:
        arrived(k, h)
        block = slot(out, k, sources[k], core)
        if k < lay.wide and h == 0:
            onward = [b * lay.wide for b in range(1, lay.lo)]
        elif k >= lay.wide and h == 1:
            onward = list(range(1, lay.wide))
        else:
            onward = []
        for step in onward:
            total = k + step
            there = slot(out, total, sources[k], core)
            copy = remote(
                block.at[halves[h]], there.at[halves[h]], pass_send.at[total, h], recv.at[total, h], peers[step]
            )
            copy.start()
            pushes.append(copy)
    for k in straight + bent:
        if k in bent:
            for h in range(2):
                arrived(k, h)
        block = slot(out, k, sources[k], core)
        share = remote(block, block, core_send.at[k], core_recv.at[k], partner)
        share.start()
        shares.append(share)
    keep.wait()
    for copy in pushes:
        copy.wait_send()
    for share in shares:
        share.wait()


def gather_group(lay, value, out_shape, slot, collective_id):
    n = lay.chips
    dma = pltpu.SemaphoreType.DMA
    return pl.pallas_call(
        partial(gather_group_kernel, lay, slot),
        out_shape=jax.ShapeDtypeStruct(out_shape, value.dtype),
        in_specs=[pl.BlockSpec(memory_space=pl.ANY)],
        out_specs=pl.BlockSpec(memory_space=pl.ANY),
        scratch_shapes=[dma, dma((n, 2)), dma((n, 2)), dma((n, 2)), dma((n,)), dma((n,))],
        compiler_params=pltpu.CompilerParams(
            collective_id=collective_id, has_side_effects=True, vmem_limit_bytes=VMEM_LIMIT
        ),
    )(value)


def weights_in_kernel(
    lay, reach, tokens, pack, pairs, lows, attn_out, ffn_out, earlier_out,
    hops_land, attn_land, own, stack, land, keep_sem, hop_send, hop_recv, low_send, low_recv, attn_send, attn_recv, send, recv, chain_send, chain_recv,
):
    n, hi, lo = lay.dp, lay.hi, lay.lo
    dp = lax.axis_index("dp")
    ctx = lax.axis_index("ctx")
    high = ctx // lo
    cols = lows.shape[0]
    per = lows.shape[1] // n
    padded = ffn_out.shape[0] // 3
    targets = [lax.rem(dp + k, n) for k in range(n)]
    right, left = (dp, ctx + lo), (dp, ctx - lo)
    has_right, has_left = high < hi - 1, high > 0
    low = lax.rem(ctx, lo)
    low_peers = [(dp, high * lo + other) for other in range(lo)]
    hops = hops_land.shape[0] - 1
    barrier = pltpu.get_barrier_semaphore()
    for target in targets[1:]:
        pl.semaphore_signal(barrier, inc=1, device_id=(target, ctx), device_id_type=MESH)
    for other in range(lo):
        if lo > 1:
            @pl.when(low != other)
            def _():
                pl.semaphore_signal(barrier, inc=1, device_id=low_peers[other], device_id_type=MESH)
    for there, device in ((has_right, right), (has_left, left)):
        @pl.when(there)
        def _():
            pl.semaphore_signal(barrier, inc=1, device_id=device, device_id_type=MESH)
    sides = jnp.where(has_right, 1, 0) + jnp.where(has_left, 1, 0)
    pl.semaphore_wait(barrier, n - 1 + sides + lo - 1)

    attn_pushes = []
    for k in range(1, n):
        push = remote(
            pack.at[targets[k]], attn_land.at[dp], attn_send.at[k], attn_recv.at[k], (targets[k], ctx)
        )
        push.start()
        attn_pushes.append(push)
    attn_land[dp] = pack[dp]
    wide = land.shape[3]

    def feed_forward_push(q):
        return remote(stack.at[:, q], land.at[:, dp], send.at[q], recv.at[dp], (q, ctx))

    def feed_forward_units(q):
        for i, (ref, first, stride) in enumerate(
            ((pairs, 2 * per * q, 2), (pairs, 2 * per * q + 1, 2), (lows, per * q, 1))
        ):
            begin = first // 128 * 128
            end = min(ref.shape[1], -(-(first + stride * (per - 1) + 1) // 128) * 128)
            column = lax.broadcasted_iota(jnp.int32, (end - begin, wide), 0) + (begin - first)
            unit = lax.broadcasted_iota(jnp.int32, (end - begin, wide), 1)
            pick = jnp.where((column == stride * unit) & (unit < per), 1.0, 0.0).astype(jnp.bfloat16)
            picked = dot_nn(ref[:, begin:end].astype(jnp.bfloat16), pick).astype(jnp.bfloat16)
            stack[i, q] = picked

        @pl.when(dp != q)
        def _():
            feed_forward_push(q).start()

    def chain(source, where, side, step):
        return remote(
            source, attn_out.at[where], chain_send.at[side, step], chain_recv.at[side, step],
            right if side == 0 else left,
        )

    def pass_on(step):
        if step == 0:
            for side, there in ((0, has_right), (1, has_left)):
                @pl.when(there)
                def _():
                    chain(own, high, side, 0).start()
            return
        for side, here, there in (
            (0, high - step >= 0, has_right),
            (1, high + step < hi, has_left),
        ):
            where = high - step if side == 0 else high + step

            @pl.when(here)
            def _():
                chain(own, where, side, step - 1).wait_recv()
                if step < hi - 1:
                    @pl.when(there)
                    def _():
                        chain(attn_out.at[where], where, side, step).start()

    def finish(step):
        for side, here, there in (
            (0, high - step >= 0, has_right),
            (1, high + step < hi, has_left),
        ):
            @pl.when(here & there)
            def _():
                chain(own, high, side, step).wait_send()

    parts = 2
    span = tokens.shape[0] // parts

    def part_of(ref, part):
        return ref.at[pl.ds(part * span, span)]

    def hop(h, part):
        source = tokens if h == 0 else hops_land.at[h]
        return remote(
            part_of(source, part), part_of(hops_land.at[h + 1], part), hop_send.at[h, part], hop_recv.at[h, part], right
        )

    def wanted(h, source, target):
        distance = h * lo + target - source
        return (distance >= 1) & (distance <= reach) & (high >= h)

    def aside(h, source, target, device, part):
        block = tokens if h == 0 else hops_land.at[h]
        return remote(
            part_of(block, part), part_of(earlier_out.at[reach - (h * lo + target - source)], part),
            low_send.at[h, target, part], low_recv.at[h, source, part], device,
        )

    def pass_tokens(h, part):
        if h:
            @pl.when(high >= h)
            def _():
                hop(h - 1, part).wait_recv()
        if h < hops:
            @pl.when((high >= h) & has_right)
            def _():
                hop(h, part).start()
        for other in range(lo):
            if lo > 1:
                @pl.when((low != other) & wanted(h, low, other))
                def _():
                    aside(h, low, other, low_peers[other], part).start()
        if h and h * lo <= reach:
            @pl.when(high >= h)
            def _():
                block = pl.ds(part * span, span)
                earlier_out[reach - h * lo, block] = hops_land[h, block]

    def finish_tokens(h, part):
        if h < hops:
            @pl.when((high >= h) & has_right)
            def _():
                hop(h, part).wait_send()
        for other in range(lo):
            if lo > 1:
                @pl.when((low != other) & wanted(h, other, low))
                def _():
                    aside(h, other, low, low_peers[other], part).wait_recv()

                @pl.when((low != other) & wanted(h, low, other))
                def _():
                    aside(h, low, other, low_peers[other], part).wait_send()

    for part in range(parts):
        pass_tokens(0, part)
    for d in range(1, reach + 1):
        @pl.when(ctx < d)
        def _():
            earlier_out[reach - d] = jnp.zeros(earlier_out.shape[1:], earlier_out.dtype)
    feed_forward_units(0)
    for push in attn_pushes:
        push.wait_recv()
    for q in range(n):
        own[:, q * cols : (q + 1) * cols] = attn_land[q]
    keep = pltpu.make_async_copy(own, attn_out.at[high], keep_sem)
    keep.start()
    pass_on(0)
    events = [partial(feed_forward_units, 1)]
    for step in range(1, max(hi, hops + 1)):
        if step <= hops:
            events += [partial(pass_tokens, step, part) for part in range(parts)]
        if step == 1:
            events.insert(2, partial(feed_forward_units, 2))
        if step < hi:
            events.append(partial(pass_on, step))
        if step == 1:
            events += [partial(feed_forward_units, q) for q in range(3, n)]
    for event in events:
        event()
    for i in range(3):
        land[i, dp] = stack[i, dp]
    for q in range(n):
        @pl.when(dp != q)
        def _():
            remote(stack.at[:, q], land.at[:, q], send.at[q], recv.at[q], (q, ctx)).wait_recv()
    for i in range(3):
        whole = land[i].reshape(n * cols, wide)
        ffn_out[i * padded : (i + 1) * padded] = whole.T[:padded]
    keep.wait()
    for step in range(hi - 1):
        finish(step)
    for h in range(hops + 1):
        for part in range(parts):
            finish_tokens(h, part)
    for push in attn_pushes:
        push.wait_send()
    for q in range(n):
        @pl.when(dp != q)
        def _():
            feed_forward_push(q).wait_send()


def weights_in(lay, reach, tokens, pack, pairs, lows, collective_id):
    n = lay.dp
    cols, per = lows.shape[0], lows.shape[1] // n
    rows = pack.shape[1]
    padded = -(-per // 32) * 32
    vmem = pl.BlockSpec(memory_space=pltpu.VMEM)
    dma = pltpu.SemaphoreType.DMA
    hops = min(lay.hi - 1, (reach + lay.lo - 1) // lay.lo)
    scratch = [
        pltpu.VMEM((hops + 1,) + tokens.shape, tokens.dtype),
        pltpu.VMEM((n, rows, cols), jnp.bfloat16),
        pltpu.VMEM((rows, n * cols), jnp.bfloat16),
        pltpu.VMEM((3, n, cols, -(-padded // 128) * 128), jnp.bfloat16),
        pltpu.VMEM((3, n, cols, -(-padded // 128) * 128), jnp.bfloat16),
        dma,
    ]
    for shape in ((hops + 1, 2), (hops + 1, lay.lo, 2), (n,), (n,), (2, lay.hi)):
        scratch += [dma(shape), dma(shape)]
    return pl.pallas_call(
        partial(weights_in_kernel, lay, reach),
        out_shape=(
            jax.ShapeDtypeStruct((lay.hi, rows, n * cols), jnp.bfloat16),
            jax.ShapeDtypeStruct((3 * padded, n * cols), jnp.bfloat16),
            jax.ShapeDtypeStruct((reach,) + tokens.shape, tokens.dtype),
        ),
        in_specs=[vmem] * 4,
        out_specs=(pl.BlockSpec(memory_space=pl.ANY), vmem, vmem),
        scratch_shapes=scratch,
        compiler_params=pltpu.CompilerParams(
            collective_id=collective_id, has_side_effects=True, vmem_limit_bytes=VMEM_LIMIT
        ),
    )(tokens, pack, pairs, lows)


def later_kernel(
    lay, reach, pieces, parts, out, group_out, low_land, moved, arrived, chain_send, chain_recv, low_send, low_recv, *scratch
):
    group = GroupSum(lay, parts, group_out, *scratch)
    hi, lo = lay.hi, lay.lo
    dp = lax.axis_index("dp")
    ctx = lax.axis_index("ctx")
    high, low = ctx // lo, lax.rem(ctx, lo)
    hops = min(hi - 1, (reach + lo - 1) // lo)
    right, left = (dp, ctx + lo), (dp, ctx - lo)
    has_right, has_left = high < hi - 1, high > 0
    low_peers = [(dp, high * lo + other) for other in range(lo)]
    barrier = pltpu.get_barrier_semaphore()
    for device in group.peers:
        pl.semaphore_signal(barrier, inc=1, device_id=device, device_id_type=MESH)
    for there, device in [(has_right, right), (has_left, left)]:
        @pl.when(there)
        def _():
            pl.semaphore_signal(barrier, inc=1, device_id=device, device_id_type=MESH)
    sides = jnp.where(has_right, 1, 0) + jnp.where(has_left, 1, 0)
    pl.semaphore_wait(barrier, sides + len(group.peers))

    def wanted(h, owner, reader):
        distance = h * lo + reader - owner
        return (distance >= 1) & (distance <= reach) & (high >= h)

    def across(h, other):
        return remote(
            pieces.at[reach - (h * lo + low - other)], low_land.at[h, low], low_send.at[h, other],
            low_recv.at[h, low], low_peers[other],
        )

    def from_low(h, other):
        return remote(
            pieces.at[0], low_land.at[h, other], low_send.at[h, other], low_recv.at[h, other], low_peers[other]
        )

    def hop(h):
        return remote(moved.at[h], arrived.at[h - 1], chain_send.at[h], chain_recv.at[h - 1], left)

    for h in range(hops, -1, -1):
        for other in range(lo):
            if lo > 1:
                @pl.when((low != other) & wanted(h, other, low))
                def _():
                    across(h, other).start()
    group.start()
    stages = group.stages()
    every = -(-len(stages) // (hops + 1))
    for h in range(hops, -1, -1):
        turn = hops - h
        for calls in stages[turn * every : (turn + 1) * every]:
            for call in calls:
                call()
        out[...] = jnp.zeros_like(out)
        if h and h * lo <= reach:
            out[...] += pieces[reach - h * lo].astype(jnp.float32)
        for other in range(lo):
            if lo > 1:
                @pl.when((low != other) & wanted(h, low, other))
                def _():
                    from_low(h, other).wait_recv()
                    out[...] += low_land[h, other].astype(jnp.float32)
        if h < hops:
            @pl.when(has_right & (high >= h))
            def _():
                hop(h + 1).wait_recv()
                out[...] += arrived[h].astype(jnp.float32)
        if h:
            @pl.when(high >= h)
            def _():
                moved[h] = out[...].astype(moved.dtype)
                hop(h).start()
    for h in range(hops + 1):
        if h:
            @pl.when(high >= h)
            def _():
                hop(h).wait_send()
        for other in range(lo):
            if lo > 1:
                @pl.when((low != other) & wanted(h, other, low))
                def _():
                    across(h, other).wait_send()
    group.finish()


def later_sum(lay, reach, pieces, parts, collective_id):
    hops = min(lay.hi - 1, (reach + lay.lo - 1) // lay.lo)
    shape = pieces.shape[1:]
    vmem = pl.BlockSpec(memory_space=pltpu.VMEM)
    dma = pltpu.SemaphoreType.DMA
    return pl.pallas_call(
        partial(later_kernel, lay, reach),
        out_shape=(
            jax.ShapeDtypeStruct(shape, jnp.float32),
            jax.ShapeDtypeStruct((lay.hi, parts.shape[2], D), parts.dtype),
        ),
        in_specs=[vmem] * 2,
        out_specs=(vmem,) * 2,
        scratch_shapes=[
            pltpu.VMEM((hops + 1, lay.lo) + shape, pieces.dtype),
            pltpu.VMEM((hops + 1,) + shape, pieces.dtype),
            pltpu.VMEM((hops + 1,) + shape, pieces.dtype),
        ]
        + [dma((hops + 1,))] * 2
        + [dma((hops + 1, lay.lo))] * 2
        + GroupSum.scratch(lay, parts.shape[2]),
        compiler_params=pltpu.CompilerParams(
            collective_id=collective_id, has_side_effects=True, vmem_limit_bytes=VMEM_LIMIT
        ),
    )(pieces, parts)


def flip(index, bit):
    return index + bit * (1 - 2 * lax.rem(index // bit, 2))


class GroupSum:
    @staticmethod
    def scratch(lay, rows):
        dma = pltpu.SemaphoreType.DMA
        blocks = (lay.hi, lay.lo, lay.wide)
        data = [pltpu.VMEM(blocks + (rows, D), jnp.bfloat16)] * 3
        return data + [dma(blocks)] * 6

    def __init__(self, lay, parts, out, land, sums, second_land, core_send, core_recv, send, recv, second_send, second_recv):
        self.lay, self.parts, self.out = lay, parts, out
        self.land, self.sums, self.second_land = land, sums, second_land
        self.core_sems, self.sems, self.second_sems = (core_send, core_recv), (send, recv), (second_send, second_recv)
        dp = lax.axis_index("dp")
        ctx = lax.axis_index("ctx")
        hi, lo, wide = lay.hi, lay.lo, lay.wide
        high, self.low = ctx // lo, lax.rem(ctx, lo)
        self.across, self.core = dp // 2, lax.rem(dp, 2)
        self.partner = (self.across * 2 + 1 - self.core, ctx)
        self.low_peers = [(dp, high * lo + lax.rem(self.low + k, lo)) for k in range(lo)]
        self.wide_peers = [(lax.rem(self.across + k, wide) * 2 + self.core, ctx) for k in range(wide)]
        self.peers = self.low_peers[1:] + self.wide_peers[1:] + [self.partner]
        self.sends = []

    def at(self, h, a, b):
        lay = self.lay
        return h * lay.lo + lax.rem(self.low + a, lay.lo), lax.rem(self.across + b, lay.wide) * 2

    def turned(self, h):
        return h >= self.lay.hi // 2 and self.lay.lo > 1

    def core_copy(self, h, a, b):
        ctx, there = self.at(h, a, b)
        return remote(
            self.parts.at[ctx, there + 1 - self.core], self.land.at[h, a, b], self.core_sems[0].at[h, a, b],
            self.core_sems[1].at[h, a, b], self.partner,
        )

    def blocks(self):
        lay = self.lay
        return [
            (a, b) for a in list(range(1, lay.lo)) + [0] for b in list(range(1, lay.wide)) + [0]
        ]

    def start(self):
        for h in range(self.lay.hi):
            for a, b in self.blocks():
                self.core_copy(h, a, b).start()

    def first_copy(self, h, a, b):
        where = (h, a, b)
        return remote(
            self.sums.at[where], self.land_first(h, a, b), self.sems[0].at[where], self.sems[1].at[where],
            self.low_peers[a] if self.turned(h) else self.wide_peers[b],
        )

    def land_first(self, h, a, b):
        return self.second_land.at[h, a, b]

    def second_copy(self, h, a, b):
        where = (h, a, b)
        return remote(
            self.sums.at[where], self.second_land.at[where], self.second_sems[0].at[where],
            self.second_sems[1].at[where], self.wide_peers[b] if self.turned(h) else self.low_peers[a],
        )

    def moves_first(self, h, a, b):
        return a > 0 if self.turned(h) else b > 0

    def sum_cores(self, h):
        for a, b in self.blocks():
            self.core_copy(h, a, b).wait_recv()
            ctx, there = self.at(h, a, b)
            total = self.parts[ctx, there + self.core].astype(jnp.float32) + self.land[h, a, b].astype(jnp.float32)
            self.sums[h, a, b] = total.astype(jnp.bfloat16)
            if self.moves_first(h, a, b):
                self.first_copy(h, a, b).start()

    def sum_first(self, h):
        lay = self.lay
        for a, b in self.blocks():
            if self.moves_first(h, a, b):
                continue
            total = self.sums[h, a, b].astype(jnp.float32)
            others = [(k, b) for k in range(1, lay.lo)] if self.turned(h) else [(a, k) for k in range(1, lay.wide)]
            for other in others:
                self.first_copy(h, *other).wait_recv()
                total = total + self.second_land[(h,) + other].astype(jnp.float32)
            self.sums[h, a, b] = total.astype(jnp.bfloat16)
            if a or b:
                self.second_copy(h, a, b).start()

    def sum_second(self, h):
        lay = self.lay
        total = self.sums[h, 0, 0].astype(jnp.float32)
        others = [(0, k) for k in range(1, lay.wide)] if self.turned(h) else [(k, 0) for k in range(1, lay.lo)]
        for other in others:
            self.second_copy(h, *other).wait_recv()
            total = total + self.second_land[(h,) + other].astype(jnp.float32)
        self.out[h] = total.astype(jnp.bfloat16)

    def order(self):
        half = self.lay.hi // 2
        pairs = [h for pair in zip(range(half), range(half, 2 * half)) for h in pair]
        return pairs + list(range(2 * half, self.lay.hi))

    def stages(self):
        order = self.order()
        stages = []
        for i in range(len(order) + 4):
            calls = []
            if i < len(order):
                calls.append(partial(self.sum_cores, order[i]))
            if 2 <= i < len(order) + 2:
                calls.append(partial(self.sum_first, order[i - 2]))
            if 4 <= i:
                calls.append(partial(self.sum_second, order[i - 4]))
            stages.append(calls)
        return stages

    def finish(self):
        for h in range(self.lay.hi):
            for a, b in self.blocks():
                self.core_copy(h, a, b).wait_send()
                if self.moves_first(h, a, b):
                    self.first_copy(h, a, b).wait_send()
                elif a or b:
                    self.second_copy(h, a, b).wait_send()


def sum_group_kernel(lay, parts, gains, out, gains_out, gains_sum, gains_land, gains_send, gains_recv, *scratch):
    dp = lax.axis_index("dp")
    ctx = lax.axis_index("ctx")
    group = GroupSum(lay, parts, out, *scratch)
    gain_peers = [(flip(dp, 1 << i), ctx) for i in range((lay.dp - 1).bit_length())]
    gain_peers += [(dp, flip(ctx, 1 << i)) for i in range((lay.ctx - 1).bit_length())]
    greet(group.peers + gain_peers)

    def gains_copy(i):
        return remote(gains_sum.at[i], gains_land.at[i], gains_send.at[i], gains_recv.at[i], gain_peers[i])

    def gains_step(i):
        if i > len(gain_peers):
            return
        if i == 0:
            gains_sum[0] = gains[...]
        else:
            gains_copy(i - 1).wait_recv()
            gains_sum[i] = gains_sum[i - 1] + gains_land[i - 1]
        if i < len(gain_peers):
            gains_copy(i).start()
        else:
            gains_out[...] = gains_sum[i]

    group.start()
    stages = group.stages()
    for i, calls in enumerate(stages):
        gains_step(i)
        for call in calls:
            call()
    for i in range(len(stages), len(gain_peers) + 1):
        gains_step(i)
    group.finish()
    for i in range(len(gain_peers)):
        gains_copy(i).wait_send()


def sum_group(lay, parts, gains, collective_id):
    rows = parts.shape[2]
    vmem = pl.BlockSpec(memory_space=pltpu.VMEM)
    dma = pltpu.SemaphoreType.DMA
    count = (lay.dp - 1).bit_length() + (lay.ctx - 1).bit_length()
    return pl.pallas_call(
        partial(sum_group_kernel, lay),
        out_shape=(
            jax.ShapeDtypeStruct((lay.hi, rows, D), jnp.bfloat16),
            jax.ShapeDtypeStruct(gains.shape, jnp.float32),
        ),
        in_specs=[vmem] * 2,
        out_specs=(vmem,) * 2,
        scratch_shapes=[
            pltpu.VMEM((count + 1,) + gains.shape, jnp.float32),
            pltpu.VMEM((count,) + gains.shape, jnp.float32),
            dma((count,)),
            dma((count,)),
        ]
        + GroupSum.scratch(lay, rows),
        compiler_params=pltpu.CompilerParams(
            collective_id=collective_id, has_side_effects=True, vmem_limit_bytes=VMEM_LIMIT
        ),
    )(parts, gains)


def grads_out_kernel(lay, rows, early, attn, pairs_out, lows_out, attn_out, stack, land, hi_land, last, last_land,
                     send, recv, hi_send, hi_recv, last_send, last_recv):
    n, hi, lo = lay.dp, lay.hi, lay.lo
    dp = lax.axis_index("dp")
    ctx = lax.axis_index("ctx")
    high, low = ctx // lo, lax.rem(ctx, lo)
    cols = lows_out.shape[0]
    per = lows_out.shape[1] // n
    padded = (rows.shape[0] + early.shape[0]) // 3
    wide = land.shape[3]
    attn_rows = attn.shape[1]
    hi_peers = [(dp, lax.rem(high + k, hi) * lo + low) for k in range(1, hi)]
    greet([(lax.rem(dp + k, n), ctx) for k in range(1, n)] + hi_peers)
    hi_pushes = []
    for k in range(1, hi):
        push = remote(
            attn.at[lax.rem(high + k, hi)], hi_land.at[k - 1], hi_send.at[k], hi_recv.at[k], hi_peers[k - 1]
        )
        push.start()
        hi_pushes.append(push)
    blank = jnp.zeros((wide - padded, n * cols), jnp.bfloat16)
    for i in range(3):
        pieces = [rows[i * padded : (i + 1) * padded if i < 2 else rows.shape[0]]]
        if i == 2:
            pieces.append(early[...])
        if wide > padded:
            pieces.append(blank)
        whole = jnp.concatenate(pieces, axis=0) if len(pieces) > 1 else pieces[0]
        stack[i] = whole.T.reshape(n, cols, wide)
    pushes = []
    for k in range(1, n):
        target = lax.rem(dp + k, n)
        push = remote(stack.at[:, target], land.at[:, dp], send.at[k], recv.at[k], (target, ctx))
        push.start()
        pushes.append(push)
    for i in range(3):
        land[i, dp] = stack[i, dp]
    total = attn[high].astype(jnp.float32)
    for k, push in enumerate(hi_pushes):
        push.wait_recv()
        total = total + hi_land[k].astype(jnp.float32)
    for q in range(n):
        last[q] = total[:, q * cols : (q + 1) * cols].astype(jnp.bfloat16)
    last_pushes = []
    for k in range(1, n):
        target = lax.rem(dp + k, n)
        push = remote(last.at[target], last_land.at[dp], last_send.at[k], last_recv.at[k], (target, ctx))
        push.start()
        last_pushes.append(push)
    last_land[dp] = last[dp]

    unit = lax.broadcasted_iota(jnp.int32, (wide, 2 * per), 0)
    column = lax.broadcasted_iota(jnp.int32, (wide, 2 * per), 1)
    spread = [jnp.where(column == 2 * unit + i, 1.0, 0.0).astype(jnp.bfloat16) for i in range(2)]
    for push in pushes:
        push.wait_recv()
    for q in range(n):
        turns = dot_nn(land[0, q], spread[0]) + dot_nn(land[1, q], spread[1])
        pairs_out[:, 2 * per * q : 2 * per * (q + 1)] = turns.astype(jnp.bfloat16)
        lows_out[:, per * q : per * (q + 1)] = land[2, q, :, :per]
    for push in last_pushes:
        push.wait_recv()
    for q in range(n):
        attn_out[q * attn_rows : (q + 1) * attn_rows] = last_land[q].astype(jnp.float32)
    for push in hi_pushes + pushes + last_pushes:
        push.wait_send()


def grads_out(lay, rows, early, attn, per, collective_id):
    padded = (rows.shape[0] + early.shape[0]) // 3
    n, cols = lay.dp, rows.shape[1] // lay.dp
    attn_rows = attn.shape[1]
    vmem = pl.BlockSpec(memory_space=pltpu.VMEM)
    dma = pltpu.SemaphoreType.DMA
    return pl.pallas_call(
        partial(grads_out_kernel, lay),
        out_shape=(
            jax.ShapeDtypeStruct((cols, n * 2 * per), jnp.bfloat16),
            jax.ShapeDtypeStruct((cols, n * per), jnp.bfloat16),
            jax.ShapeDtypeStruct((n * attn_rows, cols), jnp.float32),
        ),
        in_specs=[vmem] * 3,
        out_specs=(vmem,) * 3,
        scratch_shapes=[
            pltpu.VMEM((3, n, cols, -(-padded // 128) * 128), jnp.bfloat16),
            pltpu.VMEM((3, n, cols, -(-padded // 128) * 128), jnp.bfloat16),
            pltpu.VMEM((max(1, lay.hi - 1), attn_rows, D), jnp.bfloat16),
            pltpu.VMEM((n, attn_rows, cols), jnp.bfloat16),
            pltpu.VMEM((n, attn_rows, cols), jnp.bfloat16),
        ]
        + [dma((n,))] * 2
        + [dma((lay.hi,))] * 2
        + [dma((n,))] * 2,
        compiler_params=pltpu.CompilerParams(
            collective_id=collective_id, has_side_effects=True, vmem_limit_bytes=VMEM_LIMIT
        ),
    )(rows, early, attn)


def in_tiles(total, size, body, begin=0):
    whole = total // size

    def step(i, carry):
        body(pl.multiple_of(begin + i * size, math.gcd(begin, size)), size)
        return carry

    if whole:
        lax.fori_loop(0, whole, step, 0)
    if total % size:
        body(begin + whole * size, total % size)


def dot_nt(left, right):
    return lax.dot_general(left, right, (((1,), (1,)), ((), ())), preferred_element_type=jnp.float32)


def dot_nn(left, right):
    return lax.dot_general(left, right, (((1,), (0,)), ((), ())), preferred_element_type=jnp.float32)


ROOT = math.sqrt(2.0 / math.pi)


def feed_forward_kernel(
    lay, mid, weights, mixed, cotangent, valid, gain, result, grad_mid, grad_gain, grad_weights, early_sum,
    late, late_sem, early, early_land, hi_send, hi_recv, w_gate, w_up, w_down, gate_t, up_t, act, slope, hidden, hidden_t, grads, parts, core_land, sums, via, landed,
    total, dy, weight_sem, core_send, core_recv, share_send, share_recv,
    send, recv, via_send, via_recv, dy_send, dy_recv, dy_pass,
):
    chip, core, high = lay.place()
    n, wide = lay.chips, lay.wide
    tokens = mixed.shape[0]
    units = w_gate.shape[0]
    hi = lay.hi
    padded = units // hi
    part_rows = padded // 2
    loads = [
        pltpu.make_async_copy(
            weights.at[h, pl.ds(i * padded + part * part_rows, part_rows)],
            held.at[pl.ds((part * hi + h) * part_rows, part_rows)],
            weight_sem.at[i, part, h],
        )
        for i, held in enumerate((w_gate, w_up, w_down))
        for part in range(2)
        for h in range(hi)
    ]
    for load in loads:
        load.start()
    peers = [lay.device(lay.offset(chip, k), core, high) for k in range(n)]
    owners = [lay.device(lay.offset(chip, k, -1), core, high) for k in range(n)]
    partner = lay.device(chip, 1 - core, high)
    mine = pl.ds(pl.multiple_of(core * tokens, tokens), tokens)
    theirs = pl.ds(pl.multiple_of((1 - core) * tokens, tokens), tokens)
    half = tokens // 2
    halves = (pl.ds(0, half), pl.ds(half, half))
    straight, bent = lay.straight(), lay.bent()
    place = [lay.position(k) for k in range(n)]
    hi_peers = [lay.device(chip, core, lax.rem(high + k, hi)) for k in range(hi)]
    greet(peers[1:] + [partner] + hi_peers[1:])

    def to_partner(phase, k):
        return remote(
            parts.at[place[k], theirs], core_land.at[k], core_send.at[phase, k], core_recv.at[phase, k], partner
        )

    def to_owner(phase, k, h):
        return remote(
            sums.at[k - 1, halves[h]], landed.at[place[k] - len(bent), halves[h]], send.at[phase, k, h],
            recv.at[phase, k, h], owners[k],
        )

    def to_neighbour(phase, k, h):
        step = k % wide if h == 0 else k // wide * wide
        return remote(
            sums.at[k - 1, halves[h]], via.at[place[k], halves[h]], via_send.at[phase, k, h], via_recv.at[phase, k, h],
            owners[step],
        )

    def added(k):
        if k < wide:
            return 1, [k + b * wide for b in range(1, lay.lo)]
        return 0, [k + step for step in range(1, wide)]

    def add_core(phase, k):
        to_partner(phase, k).wait_recv()

        def chunk(first, rows):
            span = pl.ds(first, rows)
            here = pl.ds(pl.multiple_of(core * tokens + first, rows), rows)
            both = parts[place[k], here].astype(jnp.float32) + core_land[k, span].astype(jnp.float32)
            if k:
                sums[k - 1, span] = both.astype(jnp.bfloat16)
            else:
                total[span] = both

        in_tiles(tokens, 32, chunk)
        if k in bent:
            for h in range(2):
                to_neighbour(phase, k, h).start()
        elif k:
            h, others = added(k)
            to_owner(phase, k, 1 - h).start()
            if not others:
                to_owner(phase, k, h).start()

    def add_neighbours(phase, k):
        h, others = added(k)
        if not others:
            return
        for other in others:
            to_neighbour(phase, other, h).wait_recv()

        def chunk(first, rows):
            span = pl.ds(first + h * half, rows)
            value = sums[k - 1, span].astype(jnp.float32)
            for other in others:
                value = value + via[place[other], span].astype(jnp.float32)
            sums[k - 1, span] = value.astype(jnp.bfloat16)

        in_tiles(half, 32, chunk)
        to_owner(phase, k, h).start()

    def add_owners(phase):
        for k in straight:
            for h in range(2):
                to_owner(phase, k, h).wait_recv()

        def chunk(first, rows):
            span = pl.ds(first, rows)
            value = total[span]
            for k in straight:
                value = value + landed[place[k] - len(bent), span].astype(jnp.float32)
            total[span] = value

        in_tiles(tokens, 32, chunk)

    def settle(phase):
        for k in range(n):
            to_partner(phase, k).wait_send()
            for h in range(2):
                if k in bent:
                    to_neighbour(phase, k, h).wait_send()
                elif k:
                    to_owner(phase, k, h).wait_send()

    rows_of = 2 * tokens

    def joined(ref, group, *index):
        value = ref[(pl.ds(*group),) + index]
        return value.reshape((group[1] * rows_of,) + value.shape[2:])

    def forward_units(group, begin, end):
        count = group[1]

        def tile(first, width):
            units_here = pl.ds(first, width)
            weights = jnp.concatenate([w_gate[units_here], w_up[units_here]], axis=0)
            both = dot_nt(joined(mid, group), weights)
            gate, up = both[:, :width], both[:, width:]
            square = gate * gate
            tanh = jnp.tanh(gate * (ROOT + (0.044715 * ROOT) * square))
            half_way = 0.5 + 0.5 * tanh
            active = gate * half_way
            slant = half_way + active * (1.0 - tanh) * (ROOT + (3.0 * 0.044715 * ROOT) * square)
            product = (active * up).astype(jnp.bfloat16)
            shape = (count, rows_of, width)
            act[pl.ds(*group), :, units_here] = active.astype(jnp.bfloat16).reshape(shape)
            slope[pl.ds(*group), :, units_here] = (slant * up).astype(jnp.bfloat16).reshape(shape)
            hidden[: count * rows_of, units_here] = product
            for c in range(count):
                hidden_t[group[0] + c, units_here] = product[c * rows_of : (c + 1) * rows_of].T

        in_tiles(end - begin, 128, tile, begin)

    def forward_down(group):
        count = group[1]

        def tile(first, width):
            lanes = pl.ds(first, width)
            value = dot_nn(hidden[: count * rows_of], w_down[:, lanes]).astype(jnp.bfloat16)
            parts[pl.ds(*group), :, lanes] = value.reshape(count, rows_of, width)

        in_tiles(D, 256, tile)

    def backward_units(group):
        count = group[1]

        def tile(first, width):
            units_here = pl.ds(first, width)
            grad = dot_nt(joined(dy, group), w_down[units_here])
            up_grad = (grad * joined(act, group, slice(None), units_here).astype(jnp.float32)).astype(jnp.bfloat16)
            gate_grad = (grad * joined(slope, group, slice(None), units_here).astype(jnp.float32)).astype(jnp.bfloat16)
            grads[0, : count * rows_of, units_here] = gate_grad
            grads[1, : count * rows_of, units_here] = up_grad
            for c in range(count):
                rows = slice(c * rows_of, (c + 1) * rows_of)
                gate_t[group[0] + c, units_here] = gate_grad[rows].T
                up_t[group[0] + c, units_here] = up_grad[rows].T

        in_tiles(units, 256, tile)

    def backward_in(group):
        count = group[1]

        def tile(first, width):
            lanes = pl.ds(first, width)
            both = dot_nn(grads[0, : count * rows_of], w_gate[:, lanes]) + dot_nn(
                grads[1, : count * rows_of], w_up[:, lanes]
            )
            parts[pl.ds(*group), :, lanes] = both.astype(jnp.bfloat16).reshape(count, rows_of, width)

        in_tiles(D, 256, tile)

    def product_over_tokens(left, begin, end, right, lanes):
        value = dot_nn(left[0, begin:end], right[0, :, lanes])
        for c in range(1, n):
            value = value + dot_nn(left[c, begin:end], right[c, :, lanes])
        return value.astype(jnp.bfloat16)

    far, near, here = (0, len(bent)), (len(bent), len(straight)), (n - 1, 1)
    most = hidden.shape[0] // rows_of

    def runs(group):
        return [(first, min(most, group[0] + group[1] - first)) for first in range(group[0], sum(group), most)]

    quarter = units // 512 * 128
    for load in loads:
        load.wait()
    for run in runs(far):
        forward_units(run, 0, units)
        forward_down(run)
    for k in bent:
        to_partner(0, k).start()
    for i, run in enumerate(runs(near)):
        forward_units(run, 0, 2 * quarter)
        if i == 0:
            for k in bent:
                add_core(0, k)
        forward_units(run, 2 * quarter, units)
        forward_down(run)
    for k in straight:
        to_partner(0, k).start()
    forward_units(here, 0, 2 * quarter)
    for k in straight:
        add_core(0, k)
    for k in straight:
        add_neighbours(0, k)
    forward_units(here, 2 * quarter, units)
    forward_down(here)
    to_partner(0, 0).start()
    add_core(0, 0)
    add_owners(0)

    grad_gain[...] = jnp.zeros_like(grad_gain)
    scale = 1.0 + gain[...]

    def finish(first, rows):
        span = pl.ds(first, rows)
        spot = pl.ds(pl.multiple_of(core * tokens + first, rows), rows)
        y = total[span]
        ok = valid[span]
        rate = lax.rsqrt(jnp.mean(y * y, axis=-1, keepdims=True) + EPS)
        unit = y * rate
        result[span] = ((mixed[span] + unit * scale) * ok).astype(jnp.bfloat16)
        upstream = cotangent[span].astype(jnp.float32) * ok
        down = upstream * unit
        for r in range(0, rows, 8):
            grad_gain[...] += down[r : r + 8]
        scaled = upstream * scale
        inner = jnp.mean(scaled * unit, axis=-1, keepdims=True)
        dy[n - 1, spot] = (rate * (scaled - unit * inner)).astype(jnp.bfloat16)

    in_tiles(tokens, 32, finish)

    def dy_half(k, h):
        return dy.at[place[k], pl.ds(pl.multiple_of(core * tokens + h * half, half), half)]

    def dy_push(k, h):
        return remote(dy_half(0, h), dy_half(k, h), dy_send.at[k, h], dy_recv.at[k, h], peers[k])

    def dy_onward(k, h, step):
        return remote(
            dy_half(k, h), dy_half(k + step, h), dy_pass.at[k + step, h], dy_recv.at[k + step, h], peers[step]
        )

    shares = [
        remote(dy.at[place[k], mine], dy.at[place[k], mine], share_send.at[k], share_recv.at[k], partner)
        for k in range(n)
    ]
    ordered = [(k, i if k < wide else 1 - i) for i in range(2) for k in straight]
    for k, h in ordered:
        dy_push(k, h).start()
    shares[0].start()
    settle(0)
    shares[0].wait_recv()
    backward_units(here)
    backward_in(here)
    to_partner(1, 0).start()
    onward = []
    for k, h in ordered:
        dy_push(k, h).wait_recv()
        if k < wide and h == 0:
            onward += [(k, h, b * wide) for b in range(1, lay.lo)]
        elif k >= wide and h == 1:
            onward += [(k, h, step) for step in range(1, wide)]
        for go in onward:
            if go[:2] == (k, h):
                dy_onward(*go).start()
    for k in straight:
        shares[k].start()
    add_core(1, 0)
    for k in straight:
        shares[k].wait_recv()
    for i, run in enumerate(runs(near)):
        backward_units(run)
        if i == 0:
            for k in bent:
                for h in range(2):
                    dy_push(k, h).wait_recv()
                shares[k].start()
        backward_in(run)
    for k in straight:
        to_partner(1, k).start()
    for k in bent:
        shares[k].wait_recv()
    split = hi * part_rows

    def early_grad(first, width):
        lanes = pl.ds(first, width)
        value = product_over_tokens(hidden_t, split, units, dy, lanes)
        for h in range(hi):
            early[h, :, lanes] = value[h * part_rows : (h + 1) * part_rows]

    in_tiles(D, 256, early_grad)
    hi_pushes = []
    for k in range(1, hi):
        push = remote(
            early.at[lax.rem(high + k, hi)], early_land.at[k - 1], hi_send.at[k], hi_recv.at[k], hi_peers[k]
        )
        push.start()
        hi_pushes.append(push)
    for i, run in enumerate(runs(far)):
        backward_units(run)
        if i == 0:
            for k in straight:
                add_core(1, k)
        backward_in(run)
    if not bent:
        for k in straight:
            add_core(1, k)
    for k in bent:
        to_partner(1, k).start()
    for k in bent:
        add_core(1, k)

    stores = []

    def weight_grad(left, right, i):
        parts_here = (0,) if i == 2 else (0, 1)

        def tile(first, width):
            lanes = pl.ds(first, width)
            value = product_over_tokens(left, 0, split * len(parts_here), right, lanes)
            for part in parts_here:
                for h in range(hi):
                    row = i * padded + part * part_rows
                    start = (part * hi + h) * part_rows
                    late[h, row : row + part_rows, lanes] = value[start : start + part_rows]

        in_tiles(D, 256, tile)
        rows = pl.ds(i * padded, part_rows * len(parts_here))
        store = pltpu.make_async_copy(late.at[:, rows], grad_weights.at[:, rows], late_sem.at[i])
        store.start()
        stores.append(store)

    weight_grad(hidden_t, dy, 2)
    for k in straight:
        add_neighbours(1, k)
    weight_grad(gate_t, mid, 0)
    weight_grad(up_t, mid, 1)
    add_owners(1)
    grad_mid[...] = total[...]
    for push in hi_pushes:
        push.wait_recv()
    early_total = early[high].astype(jnp.float32)
    for k in range(hi - 1):
        early_total = early_total + early_land[k].astype(jnp.float32)
    early_sum[...] = early_total.astype(jnp.bfloat16)
    for push in hi_pushes:
        push.wait_send()
    for store in stores:
        store.wait()
    settle(1)
    for k, h in ordered:
        dy_push(k, h).wait_send()
    for go in onward:
        dy_onward(*go).wait_send()
    for share in shares:
        share.wait_send()


def feed_forward(lay, mid, weights, mixed, cotangent, valid, gain, collective_id):
    n = lay.chips
    tokens = mixed.shape[0]
    units = weights.shape[0] * weights.shape[1] // 3
    early_rows = weights.shape[1] // 6
    late_rows = weights.shape[1] - early_rows
    most = min(n, max(1, 1920 // units))
    low, high = jnp.bfloat16, jnp.float32
    vmem = pl.BlockSpec(memory_space=pltpu.VMEM)
    dma = pltpu.SemaphoreType.DMA
    return pl.pallas_call(
        partial(feed_forward_kernel, lay),
        out_shape=(
            jax.ShapeDtypeStruct((tokens, D), low),
            jax.ShapeDtypeStruct((tokens, D), high),
            jax.ShapeDtypeStruct((8, D), high),
            jax.ShapeDtypeStruct((lay.hi, late_rows, D), low),
            jax.ShapeDtypeStruct((early_rows, D), low),
        ),
        in_specs=[vmem, pl.BlockSpec(memory_space=pl.ANY)] + [vmem] * 4,
        out_specs=(vmem, vmem, vmem, pl.BlockSpec(memory_space=pl.ANY), vmem),
        scratch_shapes=[
            pltpu.VMEM((lay.hi, late_rows, D), low),
            dma((3,)),
            pltpu.VMEM((lay.hi, early_rows, D), low),
            pltpu.VMEM((max(1, lay.hi - 1), early_rows, D), low),
            dma((lay.hi,)),
            dma((lay.hi,)),
            pltpu.VMEM((units, D), low),
            pltpu.VMEM((units, D), low),
            pltpu.VMEM((units, D), low),
            pltpu.VMEM((n, units, 2 * tokens), low),
            pltpu.VMEM((n, units, 2 * tokens), low),
            pltpu.VMEM((n, 2 * tokens, units), low),
            pltpu.VMEM((n, 2 * tokens, units), low),
            pltpu.VMEM((most * 2 * tokens, units), low),
            pltpu.VMEM((n, units, 2 * tokens), low),
            pltpu.VMEM((2, most * 2 * tokens, units), low),
            pltpu.VMEM((n, 2 * tokens, D), low),
            pltpu.VMEM((n, tokens, D), low),
            pltpu.VMEM((max(1, n - 1), tokens, D), low),
            pltpu.VMEM((max(1, len(lay.bent())), tokens if lay.bent() else 16, D), low),
            pltpu.VMEM((max(1, len(lay.straight())), tokens, D), low),
            pltpu.VMEM((tokens, D), high),
            pltpu.VMEM((n, 2 * tokens, D), low),
            dma((3, 2, lay.hi)),
        ]
        + [dma((2, n))] * 2
        + [dma((n,))] * 2
        + [dma((2, n, 2))] * 4
        + [dma((n, 2))] * 3,
        compiler_params=pltpu.CompilerParams(
            collective_id=collective_id, has_side_effects=True, vmem_limit_bytes=63 * 2**20
        ),
    )(mid, weights, mixed, cotangent, valid, gain)


def norm_scaled(v, gain):
    return v * lax.rsqrt(jnp.mean(v * v, axis=-1, keepdims=True) + EPS) * (1.0 + gain)


def rotate(v, angle):
    half = v.shape[-1] // 2
    cosine = jnp.cos(angle)
    sine = jnp.sin(angle)
    first = v[..., :half]
    second = v[..., half:]
    return jnp.concatenate(
        [first * cosine - second * sine, second * cosine + first * sine], axis=-1
    )


def angles_of(positions):
    inverse = 1.0 / 10000.0 ** (jnp.arange(HD // 2, dtype=jnp.float32) * (2.0 / HD))
    return positions.astype(jnp.float32)[:, None] * inverse[None, :]


def head_inputs(projected, gain_query, gain_key, angle):
    query = projected[..., : HEADS * HD].reshape(projected.shape[:-1] + (HEADS, HD))
    key_rows = projected[..., HEADS * HD : (HEADS + 1) * HD]
    value_rows = projected[..., (HEADS + 1) * HD :]
    query = rotate(norm_scaled(query, gain_query), angle[:, None, :])
    key_rows = rotate(norm_scaled(key_rows, gain_key), angle)
    return (query, key_rows, value_rows)


def contract(left, right, dims_left, dims_right):
    return lax.dot_general(
        left, right, ((dims_left, dims_right), ((), ())), preferred_element_type=jnp.float32
    )


def per_device(lay, tokens, lengths, w_qkv, w_out, w_gate_up, w_down, gains, cotangent):
    seq_count = tokens.shape[0]
    local_len = tokens.shape[1]
    reach = (WINDOW - 1) // local_len + 1
    scale = 1.0 / math.sqrt(HD)
    units = w_down.shape[0]
    per = units // lay.dp
    qkv_rows, out_rows = w_qkv.shape[0], w_out.shape[0]
    cols = w_qkv.shape[1]
    used = qkv_rows + out_rows + 1
    block = 16 * lay.dp
    pack_rows = -(-used // block) * block
    gain_row = jnp.pad(gains, (0, cols - gains.shape[0]))[None]
    pack = jnp.concatenate(
        [w_qkv, w_out, gain_row, jnp.zeros((pack_rows - used, cols), jnp.float32)], axis=0
    ).astype(jnp.bfloat16)
    plane, ffn_rows, earlier_tokens = weights_in(
        lay,
        reach,
        tokens,
        pack.reshape(lay.dp, pack_rows // lay.dp, cols),
        w_gate_up.T,
        w_down.T,
        5,
    )
    ffn_all = lax.all_gather(ffn_rows, "ctx", axis=0, axis_index_groups=lay.hi_groups)
    attn_all = gather_group(
        lay,
        plane,
        (lay.hi, lay.lo, lay.dp, pack_rows // lay.dp, D),
        lambda out, k, chip, core: out.at[
            :, chip // lay.wide, lax.rem(chip, lay.wide) * 2 + core
        ],
        6,
    ).reshape(lay.ctx, pack_rows, D)
    full_qkv = attn_all[:, :qkv_rows].reshape(lay.ctx * qkv_rows, D)
    full_out = attn_all[:, qkv_rows : qkv_rows + out_rows].reshape(lay.ctx * out_rows, D)
    gain_all = (
        attn_all[:, used - 1]
        .reshape(lay.ctx, lay.dp, cols)[:, :, : gains.shape[0]]
        .transpose(1, 0, 2)
        .reshape(-1)
        .astype(jnp.float32)
    )
    gain_in = gain_all[:D]
    gain_attn = gain_all[D : 2 * D]
    gain_pre = gain_all[2 * D : 3 * D]
    gain_post = gain_all[3 * D : 4 * D]
    gain_query = gain_all[4 * D : 4 * D + HD]
    gain_key = gain_all[4 * D + HD :]
    offset = lax.axis_index("ctx") * local_len
    positions = offset + jnp.arange(local_len, dtype=jnp.int32)
    angle = angles_of(positions)
    valid = positions[None, :] < lengths[:, None]
    inputs = tokens.astype(jnp.float32)
    normed_in, pull_in = jax.vjp(norm_scaled, inputs, gain_in)
    normed_low = normed_in.astype(jnp.bfloat16)
    projected = contract(normed_low, full_qkv, (2,), (1,))
    (query, key_rot, value_rows), pull_heads = jax.vjp(
        partial(head_inputs, angle=angle), projected, gain_query, gain_key
    )
    query_low = query.astype(jnp.bfloat16)
    key_pos = offset - reach * local_len + jnp.arange((reach + 1) * local_len, dtype=jnp.int32)
    earlier = earlier_tokens.transpose(1, 0, 2, 3).reshape(seq_count, reach * local_len, D)
    earlier = norm_scaled(earlier.astype(jnp.float32), gain_in).astype(jnp.bfloat16)
    earlier = contract(earlier, full_qkv[HEADS * HD :], (2,), (1,))
    earlier_keys = rotate(
        norm_scaled(earlier[..., :HD], gain_key), angles_of(key_pos[: reach * local_len])
    )
    key_pairs = jnp.concatenate(
        [
            jnp.concatenate([earlier_keys, earlier[..., HD:]], axis=-1).astype(jnp.bfloat16),
            jnp.concatenate([key_rot, value_rows], axis=-1).astype(jnp.bfloat16),
        ],
        axis=1,
    )
    keys_low = key_pairs[..., :HD]
    values_low = key_pairs[..., HD:]
    key_grid = key_pos[None, None, :]
    query_grid = positions[None, :, None]
    allowed = (
        (key_grid >= 0)
        & (key_grid <= query_grid)
        & (query_grid - key_grid < WINDOW)
        & ((key_grid < lengths[:, None, None]) | (key_grid == query_grid))
    )

    def scores_of():
        raw = jnp.einsum("schd,skd->shck", query_low, keys_low, preferred_element_type=jnp.float32)
        return jnp.where(allowed[:, None], raw * scale, -BIG)

    scores = scores_of()
    top = jnp.max(scores, axis=-1, keepdims=True)
    expo = jnp.exp(scores - top)
    total = jnp.sum(expo, axis=-1, keepdims=True)
    probs = expo / total
    log_total = top + jnp.log(total)
    probs_low = probs.astype(jnp.bfloat16)
    attended = jnp.einsum(
        "shck,skd->schd", probs_low, values_low, preferred_element_type=jnp.float32
    )
    attended_low = attended.reshape(seq_count, local_len, HEADS * HD).astype(jnp.bfloat16)
    out_proj = contract(attended_low, full_out, (2,), (0,))
    normed_out, pull_out = jax.vjp(norm_scaled, out_proj, gain_attn)
    mixed = inputs + normed_out
    normed_mid, pull_mid = jax.vjp(norm_scaled, mixed, gain_pre)
    mid_low = normed_mid.astype(jnp.bfloat16)
    token_count = seq_count * local_len
    mid_all = gather_group(
        lay,
        mid_low.reshape(2, token_count // 2, D),
        (lay.chips, 2, 2, token_count // 2, D),
        lambda out, k, chip, core: out.at[lay.position(k), core],
        1,
    ).reshape(lay.chips, 2 * token_count, D)
    result, grad_mid, grad_gain_post, grad_ffn, early_down = feed_forward(
        lay,
        mid_all,
        ffn_all,
        mixed.reshape(token_count, D),
        cotangent.reshape(token_count, D),
        valid.reshape(token_count, 1).astype(jnp.float32),
        gain_post[None],
        2,
    )
    result = result.reshape(mixed.shape)
    grad_mid = grad_mid.reshape(mixed.shape)
    grad_gain_post = jnp.sum(grad_gain_post, axis=0)
    upstream = jnp.where(valid[..., None], cotangent.astype(jnp.float32), 0.0)
    grad_mixed_in, grad_gain_pre = pull_mid(grad_mid)
    grad_mixed = upstream + grad_mixed_in
    grad_proj, grad_gain_attn = pull_out(grad_mixed)
    proj_low = grad_proj.astype(jnp.bfloat16)
    grad_attended = contract(proj_low, full_out, (2,), (1,))
    grad_w_out = contract(attended_low, proj_low, (0, 1), (0, 1))
    attn_low = grad_attended.astype(jnp.bfloat16).reshape(seq_count, local_len, HEADS, HD)
    again_probs = jnp.exp(scores_of() - log_total)
    again_low = again_probs.astype(jnp.bfloat16)
    grad_values = jnp.einsum(
        "shck,schd->skd", again_low, attn_low, preferred_element_type=jnp.float32
    )
    grad_probs = jnp.einsum(
        "schd,skd->shck", attn_low, values_low, preferred_element_type=jnp.float32
    )
    row_dot = jnp.sum(again_probs * grad_probs, axis=-1, keepdims=True)
    grad_scores = (scale * again_probs * (grad_probs - row_dot)).astype(jnp.bfloat16)
    grad_query = jnp.einsum(
        "shck,skd->schd", grad_scores, keys_low, preferred_element_type=jnp.float32
    )
    grad_keys = jnp.einsum(
        "shck,schd->skd", grad_scores, query_low, preferred_element_type=jnp.float32
    )
    grad_pairs = jnp.concatenate([grad_keys, grad_values], axis=-1)
    own_grad = grad_pairs[:, reach * local_len :]
    pieces = grad_pairs[:, : reach * local_len].astype(jnp.bfloat16)
    pieces = pieces.reshape(seq_count, reach, local_len, 2 * HD).transpose(1, 0, 2, 3)

    def blocks_of(grad, rows):
        part = -(-rows // (16 * lay.dp)) * 16
        whole = grad.astype(jnp.bfloat16).reshape(lay.ctx, rows, D)
        if part * lay.dp > rows:
            whole = jnp.pad(whole, ((0, 0), (0, part * lay.dp - rows), (0, 0)))
        return whole.reshape(lay.ctx, lay.dp, part, D)

    later, plane_out = later_sum(lay, reach, pieces, blocks_of(grad_w_out, out_rows), 11)
    own_grad = own_grad + later
    grad_projected, grad_gain_query, grad_gain_key = pull_heads(
        (grad_query, own_grad[..., :HD], own_grad[..., HD:])
    )
    qkv_low = grad_projected.astype(jnp.bfloat16)
    grad_w_qkv = contract(qkv_low, normed_low, (0, 1), (0, 1))
    grad_normed = contract(qkv_low, full_qkv, (2,), (0,))
    grad_in_norm, grad_gain_in = pull_in(grad_normed)
    grad_input = grad_mixed + grad_in_norm
    grad_gain_all = jnp.concatenate(
        [
            grad_gain_in,
            grad_gain_attn,
            grad_gain_pre,
            grad_gain_post,
            grad_gain_query,
            grad_gain_key,
        ]
    )
    plane_qkv, gains_sum = sum_group(
        lay, blocks_of(grad_w_qkv, qkv_rows), grad_gain_all.reshape(-1, 128), 8
    )
    plane_attn = jnp.concatenate([plane_qkv, plane_out], axis=1)
    owned = lax.psum_scatter(grad_ffn, "ctx", scatter_dimension=0, axis_index_groups=lay.hi_groups)
    part_gate_up, part_down, part_attn = grads_out(lay, owned, early_down, plane_attn, per, 9)
    part_attn = part_attn.reshape(lay.dp, -1, cols)
    part_qkv = part_attn[:, : plane_qkv.shape[1]].reshape(-1, cols)[:qkv_rows]
    part_out = part_attn[:, plane_qkv.shape[1] :].reshape(-1, cols)[:out_rows]
    place = (lax.axis_index("dp") * lay.ctx + lax.axis_index("ctx")) * gains.shape[0]
    part_gains = lax.dynamic_slice_in_dim(gains_sum.reshape(-1), place, gains.shape[0])
    part_gate_up = part_gate_up.astype(jnp.float32).T
    part_down = part_down.astype(jnp.float32).T
    return (result, grad_input, part_qkv, part_out, part_gate_up, part_down, part_gains)


def solution(mesh):
    placed = (
        P("dp", "ctx", None),
        P("dp"),
        P("ctx", "dp"),
        P("ctx", "dp"),
        P("ctx", "dp"),
        P("ctx", "dp"),
        P(("dp", "ctx")),
        P("dp", "ctx", None),
    )
    return jax.shard_map(
        partial(per_device, Layout(mesh)),
        mesh=mesh,
        in_specs=placed,
        out_specs=(
            P("dp", "ctx", None),
            P("dp", "ctx", None),
            P("ctx", "dp"),
            P("ctx", "dp"),
            P("ctx", "dp"),
            P("ctx", "dp"),
            P(("dp", "ctx")),
        ),
        check_vma=False,
    )
```

```python
from functools import partial
import math

import jax
import jax.numpy as jnp
from jax import lax
from jax.experimental import pallas as pl
from jax.experimental.pallas import tpu as pltpu
from jax.sharding import PartitionSpec as P

D = 1152
HEADS = 4
HD = 256
WINDOW = 512
GROUP = 8

EPS = 1e-06
BIG = 1e30
MESH = pl.DeviceIdType.MESH
VMEM_LIMIT = 56 * 2**20


class Layout:
    def __init__(self, mesh):
        self.dp = mesh.shape["dp"]
        self.ctx = mesh.shape["ctx"]
        self.lo = max(1, GROUP // self.dp)
        self.hi = self.ctx // self.lo
        self.wide = self.dp // 2
        self.chips = self.wide * self.lo
        self.group = self.dp * self.lo
        self.hi_groups = [
            [h * self.lo + low for h in range(self.hi)] for low in range(self.lo)
        ]

    def place(self):
        dp = lax.axis_index("dp")
        ctx = lax.axis_index("ctx")
        chip = lax.rem(ctx, self.lo) * self.wide + dp // 2
        return chip, lax.rem(dp, 2), ctx // self.lo

    def offset(self, chip, k, sign=1):
        across = lax.rem(chip, self.wide) + self.wide + sign * (k % self.wide)
        low = chip // self.wide + self.lo + sign * (k // self.wide)
        return lax.rem(low, self.lo) * self.wide + lax.rem(across, self.wide)

    def straight(self):
        return list(range(1, self.wide)) + [low * self.wide for low in range(1, self.lo)]

    def bent(self):
        return [k for k in range(1, self.chips) if k not in self.straight()]

    def position(self, k):
        return (self.bent() + self.straight() + [0]).index(k)

    def device(self, chip, core, high):
        return (lax.rem(chip, self.wide) * 2 + core, high * self.lo + chip // self.wide)


def remote(src, dst, send, recv, device):
    return pltpu.make_async_remote_copy(
        src_ref=src, dst_ref=dst, send_sem=send, recv_sem=recv, device_id=device, device_id_type=MESH
    )


def greet(devices):
    barrier = pltpu.get_barrier_semaphore()
    for device in devices:
        pl.semaphore_signal(barrier, inc=1, device_id=device, device_id_type=MESH)
    pl.semaphore_wait(barrier, len(devices))


def gather_group_kernel(lay, slot, own, out, local_sem, send, recv, pass_send, core_send, core_recv):
    chip, core, high = lay.place()
    n = lay.chips
    half = own.shape[0] // 2
    halves = (pl.ds(0, half), pl.ds(half, half))
    peers = [lay.device(lay.offset(chip, k), core, high) for k in range(n)]
    sources = [lay.offset(chip, k, -1) for k in range(n)]
    partner = lay.device(chip, 1 - core, high)
    greet(peers[1:] + [partner])
    mine = [slot(out, k, chip, core) for k in range(n)]
    straight, bent = lay.straight(), lay.bent()
    keep = pltpu.make_async_copy(own, mine[0], local_sem)
    keep.start()
    pushes = []

    def push(k, h, source, target, sem):
        copy = remote(source.at[halves[h]], target.at[halves[h]], sem, recv.at[k, h], peers[k])
        return copy

    ordered = [(k, i if k < lay.wide else 1 - i) for i in range(2) for k in straight]
    for k, h in ordered:
        copy = push(k, h, own, mine[k], send.at[k, h])
        copy.start()
        pushes.append(copy)
    shares = [remote(own, mine[0], core_send.at[0], core_recv.at[0], partner)]
    shares[0].start()

    def arrived(k, h):
        copy = remote(own.at[halves[h]], mine[k].at[halves[h]], send.at[k, h], recv.at[k, h], peers[k])
        copy.wait_recv()

    for k, h in ordered:
        arrived(k, h)
        block = slot(out, k, sources[k], core)
        if k < lay.wide and h == 0:
            onward = [b * lay.wide for b in range(1, lay.lo)]
        elif k >= lay.wide and h == 1:
            onward = list(range(1, lay.wide))
        else:
            onward = []
        for step in onward:
            total = k + step
            there = slot(out, total, sources[k], core)
            copy = remote(
                block.at[halves[h]], there.at[halves[h]], pass_send.at[total, h], recv.at[total, h], peers[step]
            )
            copy.start()
            pushes.append(copy)
    for k in straight + bent:
        if k in bent:
            for h in range(2):
                arrived(k, h)
        block = slot(out, k, sources[k], core)
        share = remote(block, block, core_send.at[k], core_recv.at[k], partner)
        share.start()
        shares.append(share)
    keep.wait()
    for copy in pushes:
        copy.wait_send()
    for share in shares:
        share.wait()


def gather_group(lay, value, out_shape, slot, collective_id):
    n = lay.chips
    dma = pltpu.SemaphoreType.DMA
    return pl.pallas_call(
        partial(gather_group_kernel, lay, slot),
        out_shape=jax.ShapeDtypeStruct(out_shape, value.dtype),
        in_specs=[pl.BlockSpec(memory_space=pl.ANY)],
        out_specs=pl.BlockSpec(memory_space=pl.ANY),
        scratch_shapes=[dma, dma((n, 2)), dma((n, 2)), dma((n, 2)), dma((n,)), dma((n,))],
        compiler_params=pltpu.CompilerParams(
            collective_id=collective_id, has_side_effects=True, vmem_limit_bytes=VMEM_LIMIT
        ),
    )(value)


def weights_in_kernel(
    lay, reach, tokens, qkv, out_t, gains, pairs, lows, attn_out, ffn_out, earlier_out,
    pack, hops_land, attn_land, own, stack, land, keep_sem, hop_send, hop_recv, low_send, low_recv, attn_send, attn_recv, send, recv, chain_send, chain_recv,
):
    n, hi, lo = lay.dp, lay.hi, lay.lo
    dp = lax.axis_index("dp")
    ctx = lax.axis_index("ctx")
    high = ctx // lo
    cols = lows.shape[0]
    per = lows.shape[1] // n
    padded = ffn_out.shape[0] // 3
    targets = [lax.rem(dp + k, n) for k in range(n)]
    right, left = (dp, ctx + lo), (dp, ctx - lo)
    has_right, has_left = high < hi - 1, high > 0
    low = lax.rem(ctx, lo)
    low_peers = [(dp, high * lo + other) for other in range(lo)]
    hops = hops_land.shape[0] - 1
    barrier = pltpu.get_barrier_semaphore()
    for target in targets[1:]:
        pl.semaphore_signal(barrier, inc=1, device_id=(target, ctx), device_id_type=MESH)
    for other in range(lo):
        if lo > 1:
            @pl.when(low != other)
            def _():
                pl.semaphore_signal(barrier, inc=1, device_id=low_peers[other], device_id_type=MESH)
    for there, device in ((has_right, right), (has_left, left)):
        @pl.when(there)
        def _():
            pl.semaphore_signal(barrier, inc=1, device_id=device, device_id_type=MESH)
    sides = jnp.where(has_right, 1, 0) + jnp.where(has_left, 1, 0)
    pl.semaphore_wait(barrier, n - 1 + sides + lo - 1)

    rows = pack.shape[1]
    last = jnp.concatenate([gains[...], jnp.zeros((1, cols - gains.shape[1]), jnp.float32)], axis=1)
    used = qkv.shape[0] + out_t.shape[1]
    first_row = lax.broadcasted_iota(jnp.int32, (n * rows - used, cols), 0) == 0
    block = jnp.concatenate(
        [qkv[...], out_t[...].T, jnp.where(first_row, last, 0.0)], axis=0
    ).astype(jnp.bfloat16)
    pack[...] = block.reshape(n, rows, cols)
    attn_pushes = []
    for k in range(1, n):
        push = remote(
            pack.at[targets[k]], attn_land.at[dp], attn_send.at[k], attn_recv.at[k], (targets[k], ctx)
        )
        push.start()
        attn_pushes.append(push)
    attn_land[dp] = pack[dp]
    wide = land.shape[3]

    def feed_forward_push(q):
        return remote(stack.at[:, q], land.at[:, dp], send.at[q], recv.at[dp], (q, ctx))

    def feed_forward_units(q):
        for i, (ref, first, stride) in enumerate(
            ((pairs, 2 * per * q, 2), (pairs, 2 * per * q + 1, 2), (lows, per * q, 1))
        ):
            begin = first // 128 * 128
            end = min(ref.shape[1], -(-(first + stride * (per - 1) + 1) // 128) * 128)
            column = lax.broadcasted_iota(jnp.int32, (end - begin, wide), 0) + (begin - first)
            unit = lax.broadcasted_iota(jnp.int32, (end - begin, wide), 1)
            pick = jnp.where((column == stride * unit) & (unit < per), 1.0, 0.0).astype(jnp.bfloat16)
            picked = dot_nn(ref[:, begin:end].astype(jnp.bfloat16), pick).astype(jnp.bfloat16)
            stack[i, q] = picked

        @pl.when(dp != q)
        def _():
            feed_forward_push(q).start()

    def chain(source, where, side, step):
        return remote(
            source, attn_out.at[where], chain_send.at[side, step], chain_recv.at[side, step],
            right if side == 0 else left,
        )

    def pass_on(step):
        if step == 0:
            for side, there in ((0, has_right), (1, has_left)):
                @pl.when(there)
                def _():
                    chain(own, high, side, 0).start()
            return
        for side, here, there in (
            (0, high - step >= 0, has_right),
            (1, high + step < hi, has_left),
        ):
            where = high - step if side == 0 else high + step

            @pl.when(here)
            def _():
                chain(own, where, side, step - 1).wait_recv()
                if step < hi - 1:
                    @pl.when(there)
                    def _():
                        chain(attn_out.at[where], where, side, step).start()

    def finish(step):
        for side, here, there in (
            (0, high - step >= 0, has_right),
            (1, high + step < hi, has_left),
        ):
            @pl.when(here & there)
            def _():
                chain(own, high, side, step).wait_send()

    parts = 2
    span = tokens.shape[0] // parts

    def part_of(ref, part):
        return ref.at[pl.ds(part * span, span)]

    def hop(h, part):
        source = tokens if h == 0 else hops_land.at[h]
        return remote(
            part_of(source, part), part_of(hops_land.at[h + 1], part), hop_send.at[h, part], hop_recv.at[h, part], right
        )

    def wanted(h, source, target):
        distance = h * lo + target - source
        return (distance >= 1) & (distance <= reach) & (high >= h)

    def aside(h, source, target, device, part):
        block = tokens if h == 0 else hops_land.at[h]
        return remote(
            part_of(block, part), part_of(earlier_out.at[reach - (h * lo + target - source)], part),
            low_send.at[h, target, part], low_recv.at[h, source, part], device,
        )

    def pass_tokens(h, part):
        if h:
            @pl.when(high >= h)
            def _():
                hop(h - 1, part).wait_recv()
        if h < hops:
            @pl.when((high >= h) & has_right)
            def _():
                hop(h, part).start()
        for other in range(lo):
            if lo > 1:
                @pl.when((low != other) & wanted(h, low, other))
                def _():
                    aside(h, low, other, low_peers[other], part).start()
        if h and h * lo <= reach:
            @pl.when(high >= h)
            def _():
                block = pl.ds(part * span, span)
                earlier_out[reach - h * lo, block] = hops_land[h, block]

    def finish_tokens(h, part):
        if h < hops:
            @pl.when((high >= h) & has_right)
            def _():
                hop(h, part).wait_send()
        for other in range(lo):
            if lo > 1:
                @pl.when((low != other) & wanted(h, other, low))
                def _():
                    aside(h, other, low, low_peers[other], part).wait_recv()

                @pl.when((low != other) & wanted(h, low, other))
                def _():
                    aside(h, low, other, low_peers[other], part).wait_send()

    for part in range(parts):
        pass_tokens(0, part)
    for d in range(1, reach + 1):
        @pl.when(ctx < d)
        def _():
            earlier_out[reach - d] = jnp.zeros(earlier_out.shape[1:], earlier_out.dtype)
    feed_forward_units(0)
    for push in attn_pushes:
        push.wait_recv()
    for q in range(n):
        own[:, q * cols : (q + 1) * cols] = attn_land[q]
    keep = pltpu.make_async_copy(own, attn_out.at[high], keep_sem)
    keep.start()
    pass_on(0)
    events = [partial(feed_forward_units, 1)]
    for step in range(1, max(hi, hops + 1)):
        if step <= hops:
            events += [partial(pass_tokens, step, part) for part in range(parts)]
        if step == 1:
            events.insert(2, partial(feed_forward_units, 2))
        if step < hi:
            events.append(partial(pass_on, step))
        if step == 1:
            events += [partial(feed_forward_units, q) for q in range(3, n)]
    for event in events:
        event()
    for i in range(3):
        land[i, dp] = stack[i, dp]
    for q in range(n):
        @pl.when(dp != q)
        def _():
            remote(stack.at[:, q], land.at[:, q], send.at[q], recv.at[q], (q, ctx)).wait_recv()
    for i in range(3):
        whole = land[i].reshape(n * cols, wide)
        ffn_out[i * padded : (i + 1) * padded] = whole.T[:padded]
    keep.wait()
    for step in range(hi - 1):
        finish(step)
    for h in range(hops + 1):
        for part in range(parts):
            finish_tokens(h, part)
    for push in attn_pushes:
        push.wait_send()
    for q in range(n):
        @pl.when(dp != q)
        def _():
            feed_forward_push(q).wait_send()


def weights_in(lay, reach, tokens, qkv, out_t, gains, pairs, lows, collective_id):
    n = lay.dp
    cols, per = lows.shape[0], lows.shape[1] // n
    block = 16 * n
    rows = -(-(qkv.shape[0] + out_t.shape[1] + 1) // block) * 16
    padded = -(-per // 32) * 32
    vmem = pl.BlockSpec(memory_space=pltpu.VMEM)
    dma = pltpu.SemaphoreType.DMA
    hops = min(lay.hi - 1, (reach + lay.lo - 1) // lay.lo)
    scratch = [
        pltpu.VMEM((n, rows, cols), jnp.bfloat16),
        pltpu.VMEM((hops + 1,) + tokens.shape, tokens.dtype),
        pltpu.VMEM((n, rows, cols), jnp.bfloat16),
        pltpu.VMEM((rows, n * cols), jnp.bfloat16),
        pltpu.VMEM((3, n, cols, -(-padded // 128) * 128), jnp.bfloat16),
        pltpu.VMEM((3, n, cols, -(-padded // 128) * 128), jnp.bfloat16),
        dma,
    ]
    for shape in ((hops + 1, 2), (hops + 1, lay.lo, 2), (n,), (n,), (2, lay.hi)):
        scratch += [dma(shape), dma(shape)]
    return pl.pallas_call(
        partial(weights_in_kernel, lay, reach),
        out_shape=(
            jax.ShapeDtypeStruct((lay.hi, rows, n * cols), jnp.bfloat16),
            jax.ShapeDtypeStruct((3 * padded, n * cols), jnp.bfloat16),
            jax.ShapeDtypeStruct((reach,) + tokens.shape, tokens.dtype),
        ),
        in_specs=[vmem] * 6,
        out_specs=(pl.BlockSpec(memory_space=pl.ANY), vmem, vmem),
        scratch_shapes=scratch,
        compiler_params=pltpu.CompilerParams(
            collective_id=collective_id, has_side_effects=True, vmem_limit_bytes=VMEM_LIMIT
        ),
    )(tokens, qkv, out_t, gains, pairs, lows)


def later_kernel(
    lay, reach, pieces, parts, out, group_out, low_land, moved, arrived, chain_send, chain_recv, low_send, low_recv, *scratch
):
    group = GroupSum(lay, parts, group_out, *scratch)
    hi, lo = lay.hi, lay.lo
    dp = lax.axis_index("dp")
    ctx = lax.axis_index("ctx")
    high, low = ctx // lo, lax.rem(ctx, lo)
    hops = min(hi - 1, (reach + lo - 1) // lo)
    right, left = (dp, ctx + lo), (dp, ctx - lo)
    has_right, has_left = high < hi - 1, high > 0
    low_peers = [(dp, high * lo + other) for other in range(lo)]
    barrier = pltpu.get_barrier_semaphore()
    for device in group.peers:
        pl.semaphore_signal(barrier, inc=1, device_id=device, device_id_type=MESH)
    for there, device in [(has_right, right), (has_left, left)]:
        @pl.when(there)
        def _():
            pl.semaphore_signal(barrier, inc=1, device_id=device, device_id_type=MESH)
    sides = jnp.where(has_right, 1, 0) + jnp.where(has_left, 1, 0)
    pl.semaphore_wait(barrier, sides + len(group.peers))

    def wanted(h, owner, reader):
        distance = h * lo + reader - owner
        return (distance >= 1) & (distance <= reach) & (high >= h)

    def across(h, other):
        return remote(
            pieces.at[reach - (h * lo + low - other)], low_land.at[h, low], low_send.at[h, other],
            low_recv.at[h, low], low_peers[other],
        )

    def from_low(h, other):
        return remote(
            pieces.at[0], low_land.at[h, other], low_send.at[h, other], low_recv.at[h, other], low_peers[other]
        )

    def hop(h):
        return remote(moved.at[h], arrived.at[h - 1], chain_send.at[h], chain_recv.at[h - 1], left)

    for h in range(hops, -1, -1):
        for other in range(lo):
            if lo > 1:
                @pl.when((low != other) & wanted(h, other, low))
                def _():
                    across(h, other).start()
    group.start()
    stages = group.stages()
    bounds = [0, 1] + [1 + (len(stages) - 1) * (i + 1) // hops for i in range(hops)]
    for h in range(hops, -1, -1):
        turn = hops - h
        for calls in stages[bounds[turn] : bounds[turn + 1]]:
            for call in calls:
                call()
        out[...] = jnp.zeros_like(out)
        if h and h * lo <= reach:
            out[...] += pieces[reach - h * lo].astype(jnp.float32)
        for other in range(lo):
            if lo > 1:
                @pl.when((low != other) & wanted(h, low, other))
                def _():
                    from_low(h, other).wait_recv()
                    out[...] += low_land[h, other].astype(jnp.float32)
        if h < hops:
            @pl.when(has_right & (high >= h))
            def _():
                hop(h + 1).wait_recv()
                out[...] += arrived[h].astype(jnp.float32)
        if h:
            @pl.when(high >= h)
            def _():
                moved[h] = out[...].astype(moved.dtype)
                hop(h).start()
    for h in range(hops + 1):
        if h:
            @pl.when(high >= h)
            def _():
                hop(h).wait_send()
        for other in range(lo):
            if lo > 1:
                @pl.when((low != other) & wanted(h, other, low))
                def _():
                    across(h, other).wait_send()
    group.finish()


def later_sum(lay, reach, pieces, parts, collective_id):
    hops = min(lay.hi - 1, (reach + lay.lo - 1) // lay.lo)
    shape = pieces.shape[1:]
    vmem = pl.BlockSpec(memory_space=pltpu.VMEM)
    dma = pltpu.SemaphoreType.DMA
    return pl.pallas_call(
        partial(later_kernel, lay, reach),
        out_shape=(
            jax.ShapeDtypeStruct(shape, jnp.float32),
            jax.ShapeDtypeStruct((lay.hi, parts.shape[2], D), parts.dtype),
        ),
        in_specs=[vmem] * 2,
        out_specs=(vmem,) * 2,
        scratch_shapes=[
            pltpu.VMEM((hops + 1, lay.lo) + shape, pieces.dtype),
            pltpu.VMEM((hops + 1,) + shape, pieces.dtype),
            pltpu.VMEM((hops + 1,) + shape, pieces.dtype),
        ]
        + [dma((hops + 1,))] * 2
        + [dma((hops + 1, lay.lo))] * 2
        + GroupSum.scratch(lay, parts.shape[2]),
        compiler_params=pltpu.CompilerParams(
            collective_id=collective_id, has_side_effects=True, vmem_limit_bytes=VMEM_LIMIT
        ),
    )(pieces, parts)


def flip(index, bit):
    return index + bit * (1 - 2 * lax.rem(index // bit, 2))


class GroupSum:
    @staticmethod
    def scratch(lay, rows):
        dma = pltpu.SemaphoreType.DMA
        blocks = (lay.hi, lay.lo, lay.wide)
        data = [pltpu.VMEM(blocks + (rows, D), jnp.bfloat16)] * 3
        return data + [dma(blocks)] * 6

    def __init__(self, lay, parts, out, land, sums, second_land, core_send, core_recv, send, recv, second_send, second_recv):
        self.lay, self.parts, self.out = lay, parts, out
        self.land, self.sums, self.second_land = land, sums, second_land
        self.core_sems, self.sems, self.second_sems = (core_send, core_recv), (send, recv), (second_send, second_recv)
        dp = lax.axis_index("dp")
        ctx = lax.axis_index("ctx")
        hi, lo, wide = lay.hi, lay.lo, lay.wide
        high, self.low = ctx // lo, lax.rem(ctx, lo)
        self.across, self.core = dp // 2, lax.rem(dp, 2)
        self.partner = (self.across * 2 + 1 - self.core, ctx)
        self.low_peers = [(dp, high * lo + lax.rem(self.low + k, lo)) for k in range(lo)]
        self.wide_peers = [(lax.rem(self.across + k, wide) * 2 + self.core, ctx) for k in range(wide)]
        self.peers = self.low_peers[1:] + self.wide_peers[1:] + [self.partner]
        self.sends = []

    def at(self, h, a, b):
        lay = self.lay
        return h * lay.lo + lax.rem(self.low + a, lay.lo), lax.rem(self.across + b, lay.wide) * 2

    def turned(self, h):
        return h >= self.lay.hi // 2 and self.lay.lo > 1

    def core_copy(self, h, a, b):
        ctx, there = self.at(h, a, b)
        return remote(
            self.parts.at[ctx, there + 1 - self.core], self.land.at[h, a, b], self.core_sems[0].at[h, a, b],
            self.core_sems[1].at[h, a, b], self.partner,
        )

    def blocks(self):
        lay = self.lay
        return [
            (a, b) for a in list(range(1, lay.lo)) + [0] for b in list(range(1, lay.wide)) + [0]
        ]

    def start(self):
        for h in range(self.lay.hi):
            for a, b in self.blocks():
                self.core_copy(h, a, b).start()

    def first_copy(self, h, a, b):
        where = (h, a, b)
        return remote(
            self.sums.at[where], self.land_first(h, a, b), self.sems[0].at[where], self.sems[1].at[where],
            self.low_peers[a] if self.turned(h) else self.wide_peers[b],
        )

    def land_first(self, h, a, b):
        return self.second_land.at[h, a, b]

    def second_copy(self, h, a, b):
        where = (h, a, b)
        return remote(
            self.sums.at[where], self.second_land.at[where], self.second_sems[0].at[where],
            self.second_sems[1].at[where], self.wide_peers[b] if self.turned(h) else self.low_peers[a],
        )

    def moves_first(self, h, a, b):
        return a > 0 if self.turned(h) else b > 0

    def sum_cores(self, h):
        for a, b in self.blocks():
            self.core_copy(h, a, b).wait_recv()
            ctx, there = self.at(h, a, b)
            total = self.parts[ctx, there + self.core].astype(jnp.float32) + self.land[h, a, b].astype(jnp.float32)
            self.sums[h, a, b] = total.astype(jnp.bfloat16)
            if self.moves_first(h, a, b):
                self.first_copy(h, a, b).start()

    def sum_first(self, h):
        lay = self.lay
        for a, b in self.blocks():
            if self.moves_first(h, a, b):
                continue
            total = self.sums[h, a, b].astype(jnp.float32)
            others = [(k, b) for k in range(1, lay.lo)] if self.turned(h) else [(a, k) for k in range(1, lay.wide)]
            for other in others:
                self.first_copy(h, *other).wait_recv()
                total = total + self.second_land[(h,) + other].astype(jnp.float32)
            self.sums[h, a, b] = total.astype(jnp.bfloat16)
            if a or b:
                self.second_copy(h, a, b).start()

    def sum_second(self, h):
        lay = self.lay
        total = self.sums[h, 0, 0].astype(jnp.float32)
        others = [(0, k) for k in range(1, lay.wide)] if self.turned(h) else [(k, 0) for k in range(1, lay.lo)]
        for other in others:
            self.second_copy(h, *other).wait_recv()
            total = total + self.second_land[(h,) + other].astype(jnp.float32)
        self.out[h] = total.astype(jnp.bfloat16)

    def order(self):
        half = self.lay.hi // 2
        pairs = [h for pair in zip(range(half), range(half, 2 * half)) for h in pair]
        return pairs + list(range(2 * half, self.lay.hi))

    def stages(self):
        order = self.order()
        stages = []
        for i in range(len(order) + 4):
            calls = []
            if i < len(order):
                calls.append(partial(self.sum_cores, order[i]))
            if 2 <= i < len(order) + 2:
                calls.append(partial(self.sum_first, order[i - 2]))
            if 4 <= i:
                calls.append(partial(self.sum_second, order[i - 4]))
            stages.append(calls)
        return stages

    def finish(self):
        for h in range(self.lay.hi):
            for a, b in self.blocks():
                self.core_copy(h, a, b).wait_send()
                if self.moves_first(h, a, b):
                    self.first_copy(h, a, b).wait_send()
                elif a or b:
                    self.second_copy(h, a, b).wait_send()


def sum_group_kernel(lay, parts, gains, out, gains_out, gains_sum, gains_land, gains_send, gains_recv, *scratch):
    dp = lax.axis_index("dp")
    ctx = lax.axis_index("ctx")
    group = GroupSum(lay, parts, out, *scratch)
    gain_peers = [(flip(dp, 1 << i), ctx) for i in range((lay.dp - 1).bit_length())]
    gain_peers += [(dp, flip(ctx, 1 << i)) for i in range((lay.ctx - 1).bit_length())]
    greet(group.peers + gain_peers)

    def gains_copy(i):
        return remote(gains_sum.at[i], gains_land.at[i], gains_send.at[i], gains_recv.at[i], gain_peers[i])

    def gains_step(i):
        if i > len(gain_peers):
            return
        if i == 0:
            gains_sum[0] = gains[...]
        else:
            gains_copy(i - 1).wait_recv()
            gains_sum[i] = gains_sum[i - 1] + gains_land[i - 1]
        if i < len(gain_peers):
            gains_copy(i).start()
        else:
            gains_out[...] = gains_sum[i, pl.ds(dp * lay.ctx + ctx, 1)]

    group.start()
    stages = group.stages()
    for i, calls in enumerate(stages):
        gains_step(i)
        for call in calls:
            call()
    for i in range(len(stages), len(gain_peers) + 1):
        gains_step(i)
    group.finish()
    for i in range(len(gain_peers)):
        gains_copy(i).wait_send()


def sum_group(lay, parts, gains, collective_id):
    rows = parts.shape[2]
    vmem = pl.BlockSpec(memory_space=pltpu.VMEM)
    dma = pltpu.SemaphoreType.DMA
    count = (lay.dp - 1).bit_length() + (lay.ctx - 1).bit_length()
    return pl.pallas_call(
        partial(sum_group_kernel, lay),
        out_shape=(
            jax.ShapeDtypeStruct((lay.hi, rows, D), jnp.bfloat16),
            jax.ShapeDtypeStruct((1, gains.shape[1]), jnp.float32),
        ),
        in_specs=[vmem] * 2,
        out_specs=(vmem,) * 2,
        scratch_shapes=[
            pltpu.VMEM((count + 1,) + gains.shape, jnp.float32),
            pltpu.VMEM((count,) + gains.shape, jnp.float32),
            dma((count,)),
            dma((count,)),
        ]
        + GroupSum.scratch(lay, rows),
        compiler_params=pltpu.CompilerParams(
            collective_id=collective_id, has_side_effects=True, vmem_limit_bytes=VMEM_LIMIT
        ),
    )(parts, gains)


def grads_out_kernel(lay, rows, early, plane_qkv, plane_out, pairs_out, lows_out, qkv_out, out_t, attn, stack, land, hi_land, last, last_land,
                     send, recv, hi_send, hi_recv, last_send, last_recv):
    n, hi, lo = lay.dp, lay.hi, lay.lo
    dp = lax.axis_index("dp")
    ctx = lax.axis_index("ctx")
    high, low = ctx // lo, lax.rem(ctx, lo)
    cols = lows_out.shape[0]
    per = lows_out.shape[1] // n
    padded = (rows.shape[0] + early.shape[0]) // 3
    wide = land.shape[3]
    attn_rows = attn.shape[1]
    hi_peers = [(dp, lax.rem(high + k, hi) * lo + low) for k in range(1, hi)]
    greet([(lax.rem(dp + k, n), ctx) for k in range(1, n)] + hi_peers)
    attn[:, : plane_qkv.shape[1]] = plane_qkv[...]
    attn[:, plane_qkv.shape[1] :] = plane_out[...]
    hi_pushes = []
    for k in range(1, hi):
        push = remote(
            attn.at[lax.rem(high + k, hi)], hi_land.at[k - 1], hi_send.at[k], hi_recv.at[k], hi_peers[k - 1]
        )
        push.start()
        hi_pushes.append(push)
    blank = jnp.zeros((wide - padded, n * cols), jnp.bfloat16)
    for i in range(3):
        pieces = [rows[i * padded : (i + 1) * padded if i < 2 else rows.shape[0]]]
        if i == 2:
            pieces.append(early[...])
        if wide > padded:
            pieces.append(blank)
        whole = jnp.concatenate(pieces, axis=0) if len(pieces) > 1 else pieces[0]
        stack[i] = whole.T.reshape(n, cols, wide)
    pushes = []
    for k in range(1, n):
        target = lax.rem(dp + k, n)
        push = remote(stack.at[:, target], land.at[:, dp], send.at[k], recv.at[k], (target, ctx))
        push.start()
        pushes.append(push)
    for i in range(3):
        land[i, dp] = stack[i, dp]
    total = attn[high].astype(jnp.float32)
    for k, push in enumerate(hi_pushes):
        push.wait_recv()
        total = total + hi_land[k].astype(jnp.float32)
    for q in range(n):
        last[q] = total[:, q * cols : (q + 1) * cols].astype(jnp.bfloat16)
    last_pushes = []
    for k in range(1, n):
        target = lax.rem(dp + k, n)
        push = remote(last.at[target], last_land.at[dp], last_send.at[k], last_recv.at[k], (target, ctx))
        push.start()
        last_pushes.append(push)
    last_land[dp] = last[dp]

    unit = lax.broadcasted_iota(jnp.int32, (wide, 2 * per), 0)
    column = lax.broadcasted_iota(jnp.int32, (wide, 2 * per), 1)
    spread = [jnp.where(column == 2 * unit + i, 1.0, 0.0).astype(jnp.bfloat16) for i in range(2)]
    for push in pushes:
        push.wait_recv()
    for q in range(n):
        turns = dot_nn(land[0, q], spread[0]) + dot_nn(land[1, q], spread[1])
        pairs_out[:, 2 * per * q : 2 * per * (q + 1)] = turns.astype(jnp.bfloat16)
        lows_out[:, per * q : per * (q + 1)] = land[2, q, :, :per]
    for push in last_pushes:
        push.wait_recv()
    out_rows = out_t.shape[1]
    out_part, qkv_part = plane_out.shape[1], plane_qkv.shape[1]
    qkv_out[...] = last_land[:, :qkv_part].reshape(n * qkv_part, cols)[: qkv_out.shape[0]].astype(jnp.float32)
    out_t[...] = last_land[:, qkv_part:].reshape(n * out_part, cols)[:out_rows].astype(jnp.float32).T
    for push in hi_pushes + pushes + last_pushes:
        push.wait_send()


def grads_out(lay, rows, early, plane_qkv, plane_out, per, qkv_rows, out_rows, collective_id):
    padded = (rows.shape[0] + early.shape[0]) // 3
    n, cols = lay.dp, rows.shape[1] // lay.dp
    attn_rows = plane_qkv.shape[1] + plane_out.shape[1]
    vmem = pl.BlockSpec(memory_space=pltpu.VMEM)
    dma = pltpu.SemaphoreType.DMA
    return pl.pallas_call(
        partial(grads_out_kernel, lay),
        out_shape=(
            jax.ShapeDtypeStruct((cols, n * 2 * per), jnp.bfloat16),
            jax.ShapeDtypeStruct((cols, n * per), jnp.bfloat16),
            jax.ShapeDtypeStruct((qkv_rows, cols), jnp.float32),
            jax.ShapeDtypeStruct((cols, out_rows), jnp.float32),
        ),
        in_specs=[vmem] * 4,
        out_specs=(vmem,) * 4,
        scratch_shapes=[
            pltpu.VMEM((lay.hi, attn_rows, D), jnp.bfloat16),
            pltpu.VMEM((3, n, cols, -(-padded // 128) * 128), jnp.bfloat16),
            pltpu.VMEM((3, n, cols, -(-padded // 128) * 128), jnp.bfloat16),
            pltpu.VMEM((max(1, lay.hi - 1), attn_rows, D), jnp.bfloat16),
            pltpu.VMEM((n, attn_rows, cols), jnp.bfloat16),
            pltpu.VMEM((n, attn_rows, cols), jnp.bfloat16),
        ]
        + [dma((n,))] * 2
        + [dma((lay.hi,))] * 2
        + [dma((n,))] * 2,
        compiler_params=pltpu.CompilerParams(
            collective_id=collective_id, has_side_effects=True, vmem_limit_bytes=VMEM_LIMIT
        ),
    )(rows, early, plane_qkv, plane_out)


def in_tiles(total, size, body, begin=0):
    whole = total // size

    def step(i, carry):
        body(pl.multiple_of(begin + i * size, math.gcd(begin, size)), size)
        return carry

    if whole:
        lax.fori_loop(0, whole, step, 0)
    if total % size:
        body(begin + whole * size, total % size)


def dot_nt(left, right):
    return lax.dot_general(left, right, (((1,), (1,)), ((), ())), preferred_element_type=jnp.float32)


def dot_nn(left, right):
    return lax.dot_general(left, right, (((1,), (0,)), ((), ())), preferred_element_type=jnp.float32)


ROOT = math.sqrt(2.0 / math.pi)


def feed_forward_kernel(
    lay, mid, weights, mixed, cotangent, valid, gain, result, grad_mid, grad_gain, grad_weights, early_sum,
    late, late_sem, early, early_land, hi_send, hi_recv, w_gate, w_up, w_down, gate_t, up_t, act, slope, hidden, hidden_t, grads, parts, core_land, sums, via, landed,
    total, dy, weight_sem, core_send, core_recv, share_send, share_recv,
    send, recv, via_send, via_recv, dy_send, dy_recv, dy_pass,
):
    chip, core, high = lay.place()
    n, wide = lay.chips, lay.wide
    tokens = mixed.shape[0]
    units = w_gate.shape[0]
    hi = lay.hi
    padded = units // hi
    part_rows = padded // 2
    loads = [
        pltpu.make_async_copy(
            weights.at[h, pl.ds(i * padded + part * part_rows, part_rows)],
            held.at[pl.ds((part * hi + h) * part_rows, part_rows)],
            weight_sem.at[i, part, h],
        )
        for i, held in enumerate((w_gate, w_up, w_down))
        for part in range(2)
        for h in range(hi)
    ]
    for load in loads:
        load.start()
    peers = [lay.device(lay.offset(chip, k), core, high) for k in range(n)]
    owners = [lay.device(lay.offset(chip, k, -1), core, high) for k in range(n)]
    partner = lay.device(chip, 1 - core, high)
    mine = pl.ds(pl.multiple_of(core * tokens, tokens), tokens)
    theirs = pl.ds(pl.multiple_of((1 - core) * tokens, tokens), tokens)
    half = tokens // 2
    halves = (pl.ds(0, half), pl.ds(half, half))
    straight, bent = lay.straight(), lay.bent()
    place = [lay.position(k) for k in range(n)]
    hi_peers = [lay.device(chip, core, lax.rem(high + k, hi)) for k in range(hi)]
    greet(peers[1:] + [partner] + hi_peers[1:])

    def to_partner(phase, k):
        return remote(
            parts.at[place[k], theirs], core_land.at[k], core_send.at[phase, k], core_recv.at[phase, k], partner
        )

    def to_owner(phase, k, h):
        return remote(
            sums.at[k - 1, halves[h]], landed.at[place[k] - len(bent), halves[h]], send.at[phase, k, h],
            recv.at[phase, k, h], owners[k],
        )

    def to_neighbour(phase, k, h):
        step = k % wide if h == 0 else k // wide * wide
        return remote(
            sums.at[k - 1, halves[h]], via.at[place[k], halves[h]], via_send.at[phase, k, h], via_recv.at[phase, k, h],
            owners[step],
        )

    def added(k):
        if k < wide:
            return 1, [k + b * wide for b in range(1, lay.lo)]
        return 0, [k + step for step in range(1, wide)]

    def add_core(phase, k):
        to_partner(phase, k).wait_recv()

        def chunk(first, rows):
            span = pl.ds(first, rows)
            here = pl.ds(pl.multiple_of(core * tokens + first, rows), rows)
            both = parts[place[k], here].astype(jnp.float32) + core_land[k, span].astype(jnp.float32)
            if k:
                sums[k - 1, span] = both.astype(jnp.bfloat16)
            else:
                total[span] = both

        in_tiles(tokens, 32, chunk)
        if k in bent:
            for h in range(2):
                to_neighbour(phase, k, h).start()
        elif k:
            h, others = added(k)
            to_owner(phase, k, 1 - h).start()
            if not others:
                to_owner(phase, k, h).start()

    def add_neighbours(phase, k):
        h, others = added(k)
        if not others:
            return
        for other in others:
            to_neighbour(phase, other, h).wait_recv()

        def chunk(first, rows):
            span = pl.ds(first + h * half, rows)
            value = sums[k - 1, span].astype(jnp.float32)
            for other in others:
                value = value + via[place[other], span].astype(jnp.float32)
            sums[k - 1, span] = value.astype(jnp.bfloat16)

        in_tiles(half, 32, chunk)
        to_owner(phase, k, h).start()

    def add_owners(phase):
        for k in straight:
            for h in range(2):
                to_owner(phase, k, h).wait_recv()

        def chunk(first, rows):
            span = pl.ds(first, rows)
            value = total[span]
            for k in straight:
                value = value + landed[place[k] - len(bent), span].astype(jnp.float32)
            total[span] = value

        in_tiles(tokens, 32, chunk)

    def settle(phase):
        for k in range(n):
            to_partner(phase, k).wait_send()
            for h in range(2):
                if k in bent:
                    to_neighbour(phase, k, h).wait_send()
                elif k:
                    to_owner(phase, k, h).wait_send()

    rows_of = 2 * tokens

    def joined(ref, group, *index):
        value = ref[(pl.ds(*group),) + index]
        return value.reshape((group[1] * rows_of,) + value.shape[2:])

    def forward_units(group, begin, end):
        count = group[1]

        def tile(first, width):
            units_here = pl.ds(first, width)
            weights = jnp.concatenate([w_gate[units_here], w_up[units_here]], axis=0)
            both = dot_nt(joined(mid, group), weights)
            gate, up = both[:, :width], both[:, width:]
            square = gate * gate
            tanh = jnp.tanh(gate * (ROOT + (0.044715 * ROOT) * square))
            half_way = 0.5 + 0.5 * tanh
            active = gate * half_way
            slant = half_way + active * (1.0 - tanh) * (ROOT + (3.0 * 0.044715 * ROOT) * square)
            product = (active * up).astype(jnp.bfloat16)
            shape = (count, rows_of, width)
            act[pl.ds(*group), :, units_here] = active.astype(jnp.bfloat16).reshape(shape)
            slope[pl.ds(*group), :, units_here] = (slant * up).astype(jnp.bfloat16).reshape(shape)
            hidden[: count * rows_of, units_here] = product
            for c in range(count):
                hidden_t[group[0] + c, units_here] = product[c * rows_of : (c + 1) * rows_of].T

        in_tiles(end - begin, 128, tile, begin)

    def forward_down(group):
        count = group[1]

        def tile(first, width):
            lanes = pl.ds(first, width)
            value = dot_nn(hidden[: count * rows_of], w_down[:, lanes]).astype(jnp.bfloat16)
            parts[pl.ds(*group), :, lanes] = value.reshape(count, rows_of, width)

        in_tiles(D, 256, tile)

    def backward_units(group):
        count = group[1]

        def tile(first, width):
            units_here = pl.ds(first, width)
            grad = dot_nt(joined(dy, group), w_down[units_here])
            up_grad = (grad * joined(act, group, slice(None), units_here).astype(jnp.float32)).astype(jnp.bfloat16)
            gate_grad = (grad * joined(slope, group, slice(None), units_here).astype(jnp.float32)).astype(jnp.bfloat16)
            grads[0, : count * rows_of, units_here] = gate_grad
            grads[1, : count * rows_of, units_here] = up_grad
            for c in range(count):
                rows = slice(c * rows_of, (c + 1) * rows_of)
                gate_t[group[0] + c, units_here] = gate_grad[rows].T
                up_t[group[0] + c, units_here] = up_grad[rows].T

        in_tiles(units, 256, tile)

    def backward_in(group):
        count = group[1]

        def tile(first, width):
            lanes = pl.ds(first, width)
            both = dot_nn(grads[0, : count * rows_of], w_gate[:, lanes]) + dot_nn(
                grads[1, : count * rows_of], w_up[:, lanes]
            )
            parts[pl.ds(*group), :, lanes] = both.astype(jnp.bfloat16).reshape(count, rows_of, width)

        in_tiles(D, 256, tile)

    def product_over_tokens(left, begin, end, right, lanes):
        value = dot_nn(left[0, begin:end], right[0, :, lanes])
        for c in range(1, n):
            value = value + dot_nn(left[c, begin:end], right[c, :, lanes])
        return value.astype(jnp.bfloat16)

    far, near, here = (0, len(bent)), (len(bent), len(straight)), (n - 1, 1)
    most = hidden.shape[0] // rows_of

    def runs(group):
        return [(first, min(most, group[0] + group[1] - first)) for first in range(group[0], sum(group), most)]

    quarter = units // 512 * 128
    for load in loads:
        load.wait()
    for run in runs(far):
        forward_units(run, 0, units)
        forward_down(run)
    for k in bent:
        to_partner(0, k).start()
    for i, run in enumerate(runs(near)):
        forward_units(run, 0, 2 * quarter)
        if i == 0:
            for k in bent:
                add_core(0, k)
        forward_units(run, 2 * quarter, units)
        forward_down(run)
    for k in straight:
        to_partner(0, k).start()
    forward_units(here, 0, 2 * quarter)
    for k in straight:
        add_core(0, k)
    for k in straight:
        add_neighbours(0, k)
    forward_units(here, 2 * quarter, units)
    forward_down(here)
    to_partner(0, 0).start()
    add_core(0, 0)
    add_owners(0)

    grad_gain[...] = jnp.zeros_like(grad_gain)
    scale = 1.0 + gain[...]

    def finish(first, rows):
        span = pl.ds(first, rows)
        spot = pl.ds(pl.multiple_of(core * tokens + first, rows), rows)
        y = total[span]
        ok = valid[span]
        rate = lax.rsqrt(jnp.mean(y * y, axis=-1, keepdims=True) + EPS)
        unit = y * rate
        result[span] = ((mixed[span] + unit * scale) * ok).astype(jnp.bfloat16)
        upstream = cotangent[span].astype(jnp.float32) * ok
        down = upstream * unit
        for r in range(0, rows, 8):
            grad_gain[...] += down[r : r + 8]
        scaled = upstream * scale
        inner = jnp.mean(scaled * unit, axis=-1, keepdims=True)
        dy[n - 1, spot] = (rate * (scaled - unit * inner)).astype(jnp.bfloat16)

    in_tiles(tokens, 32, finish)

    def dy_half(k, h):
        return dy.at[place[k], pl.ds(pl.multiple_of(core * tokens + h * half, half), half)]

    def dy_push(k, h):
        return remote(dy_half(0, h), dy_half(k, h), dy_send.at[k, h], dy_recv.at[k, h], peers[k])

    def dy_onward(k, h, step):
        return remote(
            dy_half(k, h), dy_half(k + step, h), dy_pass.at[k + step, h], dy_recv.at[k + step, h], peers[step]
        )

    shares = [
        remote(dy.at[place[k], mine], dy.at[place[k], mine], share_send.at[k], share_recv.at[k], partner)
        for k in range(n)
    ]
    ordered = [(k, i if k < wide else 1 - i) for i in range(2) for k in straight]
    for k, h in ordered:
        dy_push(k, h).start()
    shares[0].start()
    settle(0)
    shares[0].wait_recv()
    backward_units(here)
    backward_in(here)
    to_partner(1, 0).start()
    onward = []
    for k, h in ordered:
        dy_push(k, h).wait_recv()
        if k < wide and h == 0:
            onward += [(k, h, b * wide) for b in range(1, lay.lo)]
        elif k >= wide and h == 1:
            onward += [(k, h, step) for step in range(1, wide)]
        for go in onward:
            if go[:2] == (k, h):
                dy_onward(*go).start()
    for k in straight:
        shares[k].start()
    add_core(1, 0)
    for k in straight:
        shares[k].wait_recv()
    for i, run in enumerate(runs(near)):
        backward_units(run)
        if i == 0:
            for k in bent:
                for h in range(2):
                    dy_push(k, h).wait_recv()
                shares[k].start()
        backward_in(run)
    for k in straight:
        to_partner(1, k).start()
    for k in bent:
        shares[k].wait_recv()
    split = hi * part_rows

    def early_grad(first, width):
        lanes = pl.ds(first, width)
        value = product_over_tokens(hidden_t, split, units, dy, lanes)
        for h in range(hi):
            early[h, :, lanes] = value[h * part_rows : (h + 1) * part_rows]

    in_tiles(D, 256, early_grad)
    hi_pushes = []
    for k in range(1, hi):
        push = remote(
            early.at[lax.rem(high + k, hi)], early_land.at[k - 1], hi_send.at[k], hi_recv.at[k], hi_peers[k]
        )
        push.start()
        hi_pushes.append(push)
    for i, run in enumerate(runs(far)):
        backward_units(run)
        if i == 0:
            for k in straight:
                add_core(1, k)
        backward_in(run)
    if not bent:
        for k in straight:
            add_core(1, k)
    for k in bent:
        to_partner(1, k).start()
    for k in bent:
        add_core(1, k)

    stores = []

    def weight_grad(left, right, i):
        parts_here = (0,) if i == 2 else (0, 1)

        def tile(first, width):
            lanes = pl.ds(first, width)
            value = product_over_tokens(left, 0, split * len(parts_here), right, lanes)
            for part in parts_here:
                for h in range(hi):
                    row = i * padded + part * part_rows
                    start = (part * hi + h) * part_rows
                    late[h, row : row + part_rows, lanes] = value[start : start + part_rows]

        in_tiles(D, 256, tile)
        rows = pl.ds(i * padded, part_rows * len(parts_here))
        store = pltpu.make_async_copy(late.at[:, rows], grad_weights.at[:, rows], late_sem.at[i])
        store.start()
        stores.append(store)

    weight_grad(hidden_t, dy, 2)
    for k in straight:
        add_neighbours(1, k)
    weight_grad(gate_t, mid, 0)
    weight_grad(up_t, mid, 1)
    add_owners(1)
    grad_mid[...] = total[...]
    for push in hi_pushes:
        push.wait_recv()
    early_total = early[high].astype(jnp.float32)
    for k in range(hi - 1):
        early_total = early_total + early_land[k].astype(jnp.float32)
    early_sum[...] = early_total.astype(jnp.bfloat16)
    for push in hi_pushes:
        push.wait_send()
    for store in stores:
        store.wait()
    settle(1)
    for k, h in ordered:
        dy_push(k, h).wait_send()
    for go in onward:
        dy_onward(*go).wait_send()
    for share in shares:
        share.wait_send()


def feed_forward(lay, mid, weights, mixed, cotangent, valid, gain, collective_id):
    n = lay.chips
    tokens = mixed.shape[0]
    units = weights.shape[0] * weights.shape[1] // 3
    early_rows = weights.shape[1] // 6
    late_rows = weights.shape[1] - early_rows
    most = min(n, max(1, 1920 // units))
    low, high = jnp.bfloat16, jnp.float32
    vmem = pl.BlockSpec(memory_space=pltpu.VMEM)
    dma = pltpu.SemaphoreType.DMA
    return pl.pallas_call(
        partial(feed_forward_kernel, lay),
        out_shape=(
            jax.ShapeDtypeStruct((tokens, D), low),
            jax.ShapeDtypeStruct((tokens, D), high),
            jax.ShapeDtypeStruct((8, D), high),
            jax.ShapeDtypeStruct((lay.hi, late_rows, D), low),
            jax.ShapeDtypeStruct((early_rows, D), low),
        ),
        in_specs=[vmem, pl.BlockSpec(memory_space=pl.ANY)] + [vmem] * 4,
        out_specs=(vmem, vmem, vmem, pl.BlockSpec(memory_space=pl.ANY), vmem),
        scratch_shapes=[
            pltpu.VMEM((lay.hi, late_rows, D), low),
            dma((3,)),
            pltpu.VMEM((lay.hi, early_rows, D), low),
            pltpu.VMEM((max(1, lay.hi - 1), early_rows, D), low),
            dma((lay.hi,)),
            dma((lay.hi,)),
            pltpu.VMEM((units, D), low),
            pltpu.VMEM((units, D), low),
            pltpu.VMEM((units, D), low),
            pltpu.VMEM((n, units, 2 * tokens), low),
            pltpu.VMEM((n, units, 2 * tokens), low),
            pltpu.VMEM((n, 2 * tokens, units), low),
            pltpu.VMEM((n, 2 * tokens, units), low),
            pltpu.VMEM((most * 2 * tokens, units), low),
            pltpu.VMEM((n, units, 2 * tokens), low),
            pltpu.VMEM((2, most * 2 * tokens, units), low),
            pltpu.VMEM((n, 2 * tokens, D), low),
            pltpu.VMEM((n, tokens, D), low),
            pltpu.VMEM((max(1, n - 1), tokens, D), low),
            pltpu.VMEM((max(1, len(lay.bent())), tokens if lay.bent() else 16, D), low),
            pltpu.VMEM((max(1, len(lay.straight())), tokens, D), low),
            pltpu.VMEM((tokens, D), high),
            pltpu.VMEM((n, 2 * tokens, D), low),
            dma((3, 2, lay.hi)),
        ]
        + [dma((2, n))] * 2
        + [dma((n,))] * 2
        + [dma((2, n, 2))] * 4
        + [dma((n, 2))] * 3,
        compiler_params=pltpu.CompilerParams(
            collective_id=collective_id, has_side_effects=True, vmem_limit_bytes=63 * 2**20
        ),
    )(mid, weights, mixed, cotangent, valid, gain)


def norm_scaled(v, gain):
    return v * lax.rsqrt(jnp.mean(v * v, axis=-1, keepdims=True) + EPS) * (1.0 + gain)


def rotate(v, angle):
    half = v.shape[-1] // 2
    cosine = jnp.cos(angle)
    sine = jnp.sin(angle)
    first = v[..., :half]
    second = v[..., half:]
    return jnp.concatenate(
        [first * cosine - second * sine, second * cosine + first * sine], axis=-1
    )


def angles_of(positions):
    inverse = 1.0 / 10000.0 ** (jnp.arange(HD // 2, dtype=jnp.float32) * (2.0 / HD))
    return positions.astype(jnp.float32)[:, None] * inverse[None, :]


def head_inputs(projected, gain_query, gain_key, angle):
    query = projected[..., : HEADS * HD].reshape(projected.shape[:-1] + (HEADS, HD))
    key_rows = projected[..., HEADS * HD : (HEADS + 1) * HD]
    value_rows = projected[..., (HEADS + 1) * HD :]
    query = rotate(norm_scaled(query, gain_query), angle[:, None, :])
    key_rows = rotate(norm_scaled(key_rows, gain_key), angle)
    return (query, key_rows, value_rows)


def contract(left, right, dims_left, dims_right):
    return lax.dot_general(
        left, right, ((dims_left, dims_right), ((), ())), preferred_element_type=jnp.float32
    )


def per_device(lay, tokens, lengths, w_qkv, w_out, w_gate_up, w_down, gains, cotangent):
    seq_count = tokens.shape[0]
    local_len = tokens.shape[1]
    reach = (WINDOW - 1) // local_len + 1
    scale = 1.0 / math.sqrt(HD)
    units = w_down.shape[0]
    per = units // lay.dp
    qkv_rows, out_rows = w_qkv.shape[0], w_out.shape[0]
    cols = w_qkv.shape[1]
    used = qkv_rows + out_rows + 1
    block = 16 * lay.dp
    pack_rows = -(-used // block) * block
    plane, ffn_rows, earlier_tokens = weights_in(
        lay,
        reach,
        tokens,
        w_qkv,
        w_out.T,
        gains[None],
        w_gate_up.T,
        w_down.T,
        5,
    )
    ffn_all = lax.all_gather(ffn_rows, "ctx", axis=0, axis_index_groups=lay.hi_groups)
    attn_all = gather_group(
        lay,
        plane,
        (lay.hi, lay.lo, lay.dp, pack_rows // lay.dp, D),
        lambda out, k, chip, core: out.at[
            :, chip // lay.wide, lax.rem(chip, lay.wide) * 2 + core
        ],
        6,
    ).reshape(lay.ctx, pack_rows, D)
    full_qkv = attn_all[:, :qkv_rows].reshape(lay.ctx * qkv_rows, D)
    full_out = attn_all[:, qkv_rows : qkv_rows + out_rows].reshape(lay.ctx * out_rows, D)
    gain_all = (
        attn_all[:, used - 1]
        .reshape(lay.ctx, lay.dp, cols)[:, :, : gains.shape[0]]
        .transpose(1, 0, 2)
        .reshape(-1)
        .astype(jnp.float32)
    )
    gain_in = gain_all[:D]
    gain_attn = gain_all[D : 2 * D]
    gain_pre = gain_all[2 * D : 3 * D]
    gain_post = gain_all[3 * D : 4 * D]
    gain_query = gain_all[4 * D : 4 * D + HD]
    gain_key = gain_all[4 * D + HD :]
    offset = lax.axis_index("ctx") * local_len
    positions = offset + jnp.arange(local_len, dtype=jnp.int32)
    angle = angles_of(positions)
    valid = positions[None, :] < lengths[:, None]
    inputs = tokens.astype(jnp.float32)
    normed_in, pull_in = jax.vjp(norm_scaled, inputs, gain_in)
    normed_low = normed_in.astype(jnp.bfloat16)
    projected = contract(normed_low, full_qkv, (2,), (1,))
    (query, key_rot, value_rows), pull_heads = jax.vjp(
        partial(head_inputs, angle=angle), projected, gain_query, gain_key
    )
    query_low = query.astype(jnp.bfloat16)
    key_pos = offset - reach * local_len + jnp.arange((reach + 1) * local_len, dtype=jnp.int32)
    earlier = earlier_tokens.transpose(1, 0, 2, 3).reshape(seq_count, reach * local_len, D)
    earlier = norm_scaled(earlier.astype(jnp.float32), gain_in).astype(jnp.bfloat16)
    earlier = contract(earlier, full_qkv[HEADS * HD :], (2,), (1,))
    earlier_keys = rotate(
        norm_scaled(earlier[..., :HD], gain_key), angles_of(key_pos[: reach * local_len])
    )
    key_pairs = jnp.concatenate(
        [
            jnp.concatenate([earlier_keys, earlier[..., HD:]], axis=-1).astype(jnp.bfloat16),
            jnp.concatenate([key_rot, value_rows], axis=-1).astype(jnp.bfloat16),
        ],
        axis=1,
    )
    keys_low = key_pairs[..., :HD]
    values_low = key_pairs[..., HD:]
    key_grid = key_pos[None, None, :]
    query_grid = positions[None, :, None]
    allowed = (
        (key_grid >= 0)
        & (key_grid <= query_grid)
        & (query_grid - key_grid < WINDOW)
        & ((key_grid < lengths[:, None, None]) | (key_grid == query_grid))
    )

    def scores_of():
        raw = jnp.einsum("schd,skd->shck", query_low, keys_low, preferred_element_type=jnp.float32)
        return jnp.where(allowed[:, None], raw * scale, -BIG)

    scores = scores_of()
    top = jnp.max(scores, axis=-1, keepdims=True)
    expo = jnp.exp(scores - top)
    total = jnp.sum(expo, axis=-1, keepdims=True)
    probs = expo / total
    log_total = top + jnp.log(total)
    probs_low = probs.astype(jnp.bfloat16)
    attended = jnp.einsum(
        "shck,skd->schd", probs_low, values_low, preferred_element_type=jnp.float32
    )
    attended_low = attended.reshape(seq_count, local_len, HEADS * HD).astype(jnp.bfloat16)
    out_proj = contract(attended_low, full_out, (2,), (0,))
    normed_out, pull_out = jax.vjp(norm_scaled, out_proj, gain_attn)
    mixed = inputs + normed_out
    normed_mid, pull_mid = jax.vjp(norm_scaled, mixed, gain_pre)
    mid_low = normed_mid.astype(jnp.bfloat16)
    token_count = seq_count * local_len
    mid_all = gather_group(
        lay,
        mid_low.reshape(2, token_count // 2, D),
        (lay.chips, 2, 2, token_count // 2, D),
        lambda out, k, chip, core: out.at[lay.position(k), core],
        1,
    ).reshape(lay.chips, 2 * token_count, D)
    result, grad_mid, grad_gain_post, grad_ffn, early_down = feed_forward(
        lay,
        mid_all,
        ffn_all,
        mixed.reshape(token_count, D),
        cotangent.reshape(token_count, D),
        valid.reshape(token_count, 1).astype(jnp.float32),
        gain_post[None],
        2,
    )
    result = result.reshape(mixed.shape)
    grad_mid = grad_mid.reshape(mixed.shape)
    grad_gain_post = jnp.sum(grad_gain_post, axis=0)
    upstream = jnp.where(valid[..., None], cotangent.astype(jnp.float32), 0.0)
    grad_mixed_in, grad_gain_pre = pull_mid(grad_mid)
    grad_mixed = upstream + grad_mixed_in
    grad_proj, grad_gain_attn = pull_out(grad_mixed)
    proj_low = grad_proj.astype(jnp.bfloat16)
    grad_attended = contract(proj_low, full_out, (2,), (1,))
    grad_w_out = contract(attended_low, proj_low, (0, 1), (0, 1))
    attn_low = grad_attended.astype(jnp.bfloat16).reshape(seq_count, local_len, HEADS, HD)
    again_probs = jnp.exp(scores_of() - log_total)
    again_low = again_probs.astype(jnp.bfloat16)
    grad_values = jnp.einsum(
        "shck,schd->skd", again_low, attn_low, preferred_element_type=jnp.float32
    )
    grad_probs = jnp.einsum(
        "schd,skd->shck", attn_low, values_low, preferred_element_type=jnp.float32
    )
    row_dot = jnp.sum(again_probs * grad_probs, axis=-1, keepdims=True)
    grad_scores = (scale * again_probs * (grad_probs - row_dot)).astype(jnp.bfloat16)
    grad_query = jnp.einsum(
        "shck,skd->schd", grad_scores, keys_low, preferred_element_type=jnp.float32
    )
    grad_keys = jnp.einsum(
        "shck,schd->skd", grad_scores, query_low, preferred_element_type=jnp.float32
    )
    grad_pairs = jnp.concatenate([grad_keys, grad_values], axis=-1)
    own_grad = grad_pairs[:, reach * local_len :]
    pieces = grad_pairs[:, : reach * local_len].astype(jnp.bfloat16)
    pieces = pieces.reshape(seq_count, reach, local_len, 2 * HD).transpose(1, 0, 2, 3)

    def blocks_of(grad, rows):
        part = -(-rows // (16 * lay.dp)) * 16
        whole = grad.astype(jnp.bfloat16).reshape(lay.ctx, rows, D)
        if part * lay.dp > rows:
            whole = jnp.pad(whole, ((0, 0), (0, part * lay.dp - rows), (0, 0)))
        return whole.reshape(lay.ctx, lay.dp, part, D)

    later, plane_out = later_sum(lay, reach, pieces, blocks_of(grad_w_out, out_rows), 11)
    own_grad = own_grad + later
    grad_projected, grad_gain_query, grad_gain_key = pull_heads(
        (grad_query, own_grad[..., :HD], own_grad[..., HD:])
    )
    qkv_low = grad_projected.astype(jnp.bfloat16)
    grad_w_qkv = contract(qkv_low, normed_low, (0, 1), (0, 1))
    grad_normed = contract(qkv_low, full_qkv, (2,), (0,))
    grad_in_norm, grad_gain_in = pull_in(grad_normed)
    grad_input = grad_mixed + grad_in_norm
    grad_gain_all = jnp.concatenate(
        [
            grad_gain_in,
            grad_gain_attn,
            grad_gain_pre,
            grad_gain_post,
            grad_gain_query,
            grad_gain_key,
        ]
    )
    plane_qkv, gains_sum = sum_group(
        lay, blocks_of(grad_w_qkv, qkv_rows), grad_gain_all.reshape(-1, gains.shape[0]), 8
    )
    owned = lax.psum_scatter(grad_ffn, "ctx", scatter_dimension=0, axis_index_groups=lay.hi_groups)
    part_gate_up, part_down, part_qkv, part_out = grads_out(
        lay, owned, early_down, plane_qkv, plane_out, per, qkv_rows, out_rows, 9
    )
    part_out = part_out.T
    part_gains = gains_sum[0]
    part_gate_up = part_gate_up.astype(jnp.float32).T
    part_down = part_down.astype(jnp.float32).T
    return (result, grad_input, part_qkv, part_out, part_gate_up, part_down, part_gains)


def solution(mesh):
    placed = (
        P("dp", "ctx", None),
        P("dp"),
        P("ctx", "dp"),
        P("ctx", "dp"),
        P("ctx", "dp"),
        P("ctx", "dp"),
        P(("dp", "ctx")),
        P("dp", "ctx", None),
    )
    return jax.shard_map(
        partial(per_device, Layout(mesh)),
        mesh=mesh,
        in_specs=placed,
        out_specs=(
            P("dp", "ctx", None),
            P("dp", "ctx", None),
            P("ctx", "dp"),
            P("ctx", "dp"),
            P("ctx", "dp"),
            P("ctx", "dp"),
            P(("dp", "ctx")),
        ),
        check_vma=False,
    )
```

```python
from functools import partial
import math

import jax
import jax.numpy as jnp
from jax import lax
from jax.experimental import pallas as pl
from jax.experimental.pallas import tpu as pltpu
from jax.sharding import PartitionSpec as P

D = 1152
HEADS = 4
HD = 256
WINDOW = 512
GROUP = 8

EPS = 1e-06
BIG = 1e30
MESH = pl.DeviceIdType.MESH
VMEM_LIMIT = 56 * 2**20


class Layout:
    def __init__(self, mesh):
        self.dp = mesh.shape["dp"]
        self.ctx = mesh.shape["ctx"]
        self.lo = max(1, GROUP // self.dp)
        self.hi = self.ctx // self.lo
        self.wide = self.dp // 2
        self.chips = self.wide * self.lo
        self.group = self.dp * self.lo
        self.hi_groups = [
            [h * self.lo + low for h in range(self.hi)] for low in range(self.lo)
        ]

    def place(self):
        dp = lax.axis_index("dp")
        ctx = lax.axis_index("ctx")
        chip = lax.rem(ctx, self.lo) * self.wide + dp // 2
        return chip, lax.rem(dp, 2), ctx // self.lo

    def offset(self, chip, k, sign=1):
        across = lax.rem(chip, self.wide) + self.wide + sign * (k % self.wide)
        low = chip // self.wide + self.lo + sign * (k // self.wide)
        return lax.rem(low, self.lo) * self.wide + lax.rem(across, self.wide)

    def straight(self):
        return list(range(1, self.wide)) + [low * self.wide for low in range(1, self.lo)]

    def bent(self):
        return [k for k in range(1, self.chips) if k not in self.straight()]

    def position(self, k):
        return (self.bent() + self.straight() + [0]).index(k)

    def device(self, chip, core, high):
        return (lax.rem(chip, self.wide) * 2 + core, high * self.lo + chip // self.wide)


def remote(src, dst, send, recv, device):
    return pltpu.make_async_remote_copy(
        src_ref=src, dst_ref=dst, send_sem=send, recv_sem=recv, device_id=device, device_id_type=MESH
    )


def greet(devices):
    barrier = pltpu.get_barrier_semaphore()
    for device in devices:
        pl.semaphore_signal(barrier, inc=1, device_id=device, device_id_type=MESH)
    pl.semaphore_wait(barrier, len(devices))


def gather_group_kernel(lay, slot, own, out, local_sem, send, recv, pass_send, core_send, core_recv):
    chip, core, high = lay.place()
    n = lay.chips
    half = own.shape[0] // 2
    halves = (pl.ds(0, half), pl.ds(half, half))
    peers = [lay.device(lay.offset(chip, k), core, high) for k in range(n)]
    sources = [lay.offset(chip, k, -1) for k in range(n)]
    partner = lay.device(chip, 1 - core, high)
    greet(peers[1:] + [partner])
    mine = [slot(out, k, chip, core) for k in range(n)]
    straight, bent = lay.straight(), lay.bent()
    keep = pltpu.make_async_copy(own, mine[0], local_sem)
    keep.start()
    pushes = []

    def push(k, h, source, target, sem):
        copy = remote(source.at[halves[h]], target.at[halves[h]], sem, recv.at[k, h], peers[k])
        return copy

    ordered = [(k, i if k < lay.wide else 1 - i) for i in range(2) for k in straight]
    for k, h in ordered:
        copy = push(k, h, own, mine[k], send.at[k, h])
        copy.start()
        pushes.append(copy)
    shares = [remote(own, mine[0], core_send.at[0], core_recv.at[0], partner)]
    shares[0].start()

    def arrived(k, h):
        copy = remote(own.at[halves[h]], mine[k].at[halves[h]], send.at[k, h], recv.at[k, h], peers[k])
        copy.wait_recv()

    for k, h in ordered:
        arrived(k, h)
        block = slot(out, k, sources[k], core)
        if k < lay.wide and h == 0:
            onward = [b * lay.wide for b in range(1, lay.lo)]
        elif k >= lay.wide and h == 1:
            onward = list(range(1, lay.wide))
        else:
            onward = []
        for step in onward:
            total = k + step
            there = slot(out, total, sources[k], core)
            copy = remote(
                block.at[halves[h]], there.at[halves[h]], pass_send.at[total, h], recv.at[total, h], peers[step]
            )
            copy.start()
            pushes.append(copy)
    for k in straight + bent:
        if k in bent:
            for h in range(2):
                arrived(k, h)
        block = slot(out, k, sources[k], core)
        share = remote(block, block, core_send.at[k], core_recv.at[k], partner)
        share.start()
        shares.append(share)
    keep.wait()
    for copy in pushes:
        copy.wait_send()
    for share in shares:
        share.wait()


def gather_group(lay, value, out_shape, slot, collective_id):
    n = lay.chips
    dma = pltpu.SemaphoreType.DMA
    return pl.pallas_call(
        partial(gather_group_kernel, lay, slot),
        out_shape=jax.ShapeDtypeStruct(out_shape, value.dtype),
        in_specs=[pl.BlockSpec(memory_space=pl.ANY)],
        out_specs=pl.BlockSpec(memory_space=pl.ANY),
        scratch_shapes=[dma, dma((n, 2)), dma((n, 2)), dma((n, 2)), dma((n,)), dma((n,))],
        compiler_params=pltpu.CompilerParams(
            collective_id=collective_id, has_side_effects=True, vmem_limit_bytes=VMEM_LIMIT
        ),
    )(value)


def weights_in_kernel(
    lay, reach, tokens, qkv, out_t, gains, pairs, lows, attn_out, ffn_out, earlier_out,
    pack, hops_land, attn_land, own, stack, land, keep_sem, hop_send, hop_recv, low_send, low_recv, attn_send, attn_recv, send, recv, chain_send, chain_recv,
):
    n, hi, lo = lay.dp, lay.hi, lay.lo
    dp = lax.axis_index("dp")
    ctx = lax.axis_index("ctx")
    high = ctx // lo
    cols = lows.shape[0]
    per = lows.shape[1] // n
    padded = ffn_out.shape[0] // 3
    targets = [lax.rem(dp + k, n) for k in range(n)]
    right, left = (dp, ctx + lo), (dp, ctx - lo)
    has_right, has_left = high < hi - 1, high > 0
    low = lax.rem(ctx, lo)
    low_peers = [(dp, high * lo + other) for other in range(lo)]
    hops = hops_land.shape[0] - 1
    barrier = pltpu.get_barrier_semaphore()
    for target in targets[1:]:
        pl.semaphore_signal(barrier, inc=1, device_id=(target, ctx), device_id_type=MESH)
    for other in range(lo):
        if lo > 1:
            @pl.when(low != other)
            def _():
                pl.semaphore_signal(barrier, inc=1, device_id=low_peers[other], device_id_type=MESH)
    for there, device in ((has_right, right), (has_left, left)):
        @pl.when(there)
        def _():
            pl.semaphore_signal(barrier, inc=1, device_id=device, device_id_type=MESH)
    sides = jnp.where(has_right, 1, 0) + jnp.where(has_left, 1, 0)
    pl.semaphore_wait(barrier, n - 1 + sides + lo - 1)

    rows = pack.shape[1]
    last = jnp.concatenate([gains[...], jnp.zeros((1, cols - gains.shape[1]), jnp.float32)], axis=1)
    used = qkv.shape[0] + out_t.shape[1]
    first_row = lax.broadcasted_iota(jnp.int32, (n * rows - used, cols), 0) == 0
    block = jnp.concatenate(
        [qkv[...], out_t[...].T, jnp.where(first_row, last, 0.0)], axis=0
    ).astype(jnp.bfloat16)
    pack[...] = block.reshape(n, rows, cols)
    attn_pushes = []
    for k in range(1, n):
        push = remote(
            pack.at[targets[k]], attn_land.at[dp], attn_send.at[k], attn_recv.at[k], (targets[k], ctx)
        )
        push.start()
        attn_pushes.append(push)
    attn_land[dp] = pack[dp]
    wide = land.shape[3]

    def feed_forward_push(q):
        return remote(stack.at[:, q], land.at[:, dp], send.at[q], recv.at[dp], (q, ctx))

    def feed_forward_units(q):
        for i, (ref, first, stride) in enumerate(
            ((pairs, 2 * per * q, 2), (pairs, 2 * per * q + 1, 2), (lows, per * q, 1))
        ):
            begin = first // 128 * 128
            end = min(ref.shape[1], -(-(first + stride * (per - 1) + 1) // 128) * 128)
            column = lax.broadcasted_iota(jnp.int32, (end - begin, wide), 0) + (begin - first)
            unit = lax.broadcasted_iota(jnp.int32, (end - begin, wide), 1)
            pick = jnp.where((column == stride * unit) & (unit < per), 1.0, 0.0).astype(jnp.bfloat16)
            picked = dot_nn(ref[:, begin:end].astype(jnp.bfloat16), pick).astype(jnp.bfloat16)
            stack[i, q] = picked

        @pl.when(dp != q)
        def _():
            feed_forward_push(q).start()

    def chain(source, where, side, step):
        return remote(
            source, attn_out.at[where], chain_send.at[side, step], chain_recv.at[side, step],
            right if side == 0 else left,
        )

    def pass_on(step):
        if step == 0:
            for side, there in ((0, has_right), (1, has_left)):
                @pl.when(there)
                def _():
                    chain(own, high, side, 0).start()
            return
        for side, here, there in (
            (0, high - step >= 0, has_right),
            (1, high + step < hi, has_left),
        ):
            where = high - step if side == 0 else high + step

            @pl.when(here)
            def _():
                chain(own, where, side, step - 1).wait_recv()
                if step < hi - 1:
                    @pl.when(there)
                    def _():
                        chain(attn_out.at[where], where, side, step).start()

    def finish(step):
        for side, here, there in (
            (0, high - step >= 0, has_right),
            (1, high + step < hi, has_left),
        ):
            @pl.when(here & there)
            def _():
                chain(own, high, side, step).wait_send()

    parts = 2
    span = tokens.shape[0] // parts

    def part_of(ref, part):
        return ref.at[pl.ds(part * span, span)]

    def hop(h, part):
        source = tokens if h == 0 else hops_land.at[h]
        return remote(
            part_of(source, part), part_of(hops_land.at[h + 1], part), hop_send.at[h, part], hop_recv.at[h, part], right
        )

    def wanted(h, source, target):
        distance = h * lo + target - source
        return (distance >= 1) & (distance <= reach) & (high >= h)

    def aside(h, source, target, device, part):
        block = tokens if h == 0 else hops_land.at[h]
        return remote(
            part_of(block, part), part_of(earlier_out.at[reach - (h * lo + target - source)], part),
            low_send.at[h, target, part], low_recv.at[h, source, part], device,
        )

    def pass_tokens(h, part):
        if h:
            @pl.when(high >= h)
            def _():
                hop(h - 1, part).wait_recv()
        if h < hops:
            @pl.when((high >= h) & has_right)
            def _():
                hop(h, part).start()
        for other in range(lo):
            if lo > 1:
                @pl.when((low != other) & wanted(h, low, other))
                def _():
                    aside(h, low, other, low_peers[other], part).start()
        if h and h * lo <= reach:
            @pl.when(high >= h)
            def _():
                block = pl.ds(part * span, span)
                earlier_out[reach - h * lo, block] = hops_land[h, block]

    def finish_tokens(h, part):
        if h < hops:
            @pl.when((high >= h) & has_right)
            def _():
                hop(h, part).wait_send()
        for other in range(lo):
            if lo > 1:
                @pl.when((low != other) & wanted(h, other, low))
                def _():
                    aside(h, other, low, low_peers[other], part).wait_recv()

                @pl.when((low != other) & wanted(h, low, other))
                def _():
                    aside(h, low, other, low_peers[other], part).wait_send()

    for part in range(parts):
        pass_tokens(0, part)
    for d in range(1, reach + 1):
        @pl.when(ctx < d)
        def _():
            earlier_out[reach - d] = jnp.zeros(earlier_out.shape[1:], earlier_out.dtype)
    feed_forward_units(0)
    for push in attn_pushes:
        push.wait_recv()
    for q in range(n):
        own[:, q * cols : (q + 1) * cols] = attn_land[q]
    keep = pltpu.make_async_copy(own, attn_out.at[high], keep_sem)
    keep.start()
    pass_on(0)
    events = [partial(feed_forward_units, 1)]
    for step in range(1, max(hi, hops + 1)):
        if step <= hops:
            events += [partial(pass_tokens, step, part) for part in range(parts)]
        if step == 1:
            events.insert(2, partial(feed_forward_units, 2))
        if step < hi:
            events.append(partial(pass_on, step))
        if step == 1:
            events += [partial(feed_forward_units, q) for q in range(3, n)]
    for event in events:
        event()
    for i in range(3):
        land[i, dp] = stack[i, dp]
    for q in range(n):
        @pl.when(dp != q)
        def _():
            remote(stack.at[:, q], land.at[:, q], send.at[q], recv.at[q], (q, ctx)).wait_recv()
    for i in range(3):
        whole = land[i].reshape(n * cols, wide)
        ffn_out[i * padded : (i + 1) * padded] = whole.T[:padded]
    keep.wait()
    for step in range(hi - 1):
        finish(step)
    for h in range(hops + 1):
        for part in range(parts):
            finish_tokens(h, part)
    for push in attn_pushes:
        push.wait_send()
    for q in range(n):
        @pl.when(dp != q)
        def _():
            feed_forward_push(q).wait_send()


def weights_in(lay, reach, tokens, qkv, out_t, gains, pairs, lows, collective_id):
    n = lay.dp
    cols, per = lows.shape[0], lows.shape[1] // n
    block = 16 * n
    rows = -(-(qkv.shape[0] + out_t.shape[1] + 1) // block) * 16
    padded = -(-per // 32) * 32
    vmem = pl.BlockSpec(memory_space=pltpu.VMEM)
    dma = pltpu.SemaphoreType.DMA
    hops = min(lay.hi - 1, (reach + lay.lo - 1) // lay.lo)
    scratch = [
        pltpu.VMEM((n, rows, cols), jnp.bfloat16),
        pltpu.VMEM((hops + 1,) + tokens.shape, tokens.dtype),
        pltpu.VMEM((n, rows, cols), jnp.bfloat16),
        pltpu.VMEM((rows, n * cols), jnp.bfloat16),
        pltpu.VMEM((3, n, cols, -(-padded // 128) * 128), jnp.bfloat16),
        pltpu.VMEM((3, n, cols, -(-padded // 128) * 128), jnp.bfloat16),
        dma,
    ]
    for shape in ((hops + 1, 2), (hops + 1, lay.lo, 2), (n,), (n,), (2, lay.hi)):
        scratch += [dma(shape), dma(shape)]
    return pl.pallas_call(
        partial(weights_in_kernel, lay, reach),
        out_shape=(
            jax.ShapeDtypeStruct((lay.hi, rows, n * cols), jnp.bfloat16),
            jax.ShapeDtypeStruct((3 * padded, n * cols), jnp.bfloat16),
            jax.ShapeDtypeStruct((reach,) + tokens.shape, tokens.dtype),
        ),
        in_specs=[vmem] * 6,
        out_specs=(pl.BlockSpec(memory_space=pl.ANY), vmem, vmem),
        scratch_shapes=scratch,
        compiler_params=pltpu.CompilerParams(
            collective_id=collective_id, has_side_effects=True, vmem_limit_bytes=VMEM_LIMIT
        ),
    )(tokens, qkv, out_t, gains, pairs, lows)


def later_kernel(
    lay, reach, pieces, parts, early, out, group_out, early_out, low_land, moved, arrived, early_stack,
    early_send, early_recv, chain_send, chain_recv, low_send, low_recv, *scratch
):
    group = GroupSum(lay, parts, group_out, *scratch)
    groups = [group]
    hi, lo = lay.hi, lay.lo
    dp = lax.axis_index("dp")
    ctx = lax.axis_index("ctx")
    high, low = ctx // lo, lax.rem(ctx, lo)
    hops = min(hi - 1, (reach + lo - 1) // lo)
    right, left = (dp, ctx + lo), (dp, ctx - lo)
    has_right, has_left = high < hi - 1, high > 0
    low_peers = [(dp, high * lo + other) for other in range(lo)]
    barrier = pltpu.get_barrier_semaphore()
    n = lay.dp
    dp_peers = [(lax.rem(dp + k, n), ctx) for k in range(1, n)]
    for device in group.low_peers[1:] + dp_peers:
        pl.semaphore_signal(barrier, inc=1, device_id=device, device_id_type=MESH)
    for there, device in [(has_right, right), (has_left, left)]:
        @pl.when(there)
        def _():
            pl.semaphore_signal(barrier, inc=1, device_id=device, device_id_type=MESH)
    sides = jnp.where(has_right, 1, 0) + jnp.where(has_left, 1, 0)
    pl.semaphore_wait(barrier, sides + lo - 1 + n - 1)

    def wanted(h, owner, reader):
        distance = h * lo + reader - owner
        return (distance >= 1) & (distance <= reach) & (high >= h)

    span = out.shape[0] // 2

    def part_of(ref, part):
        return ref.at[pl.ds(part * span, span)]

    def across(h, other, part):
        return remote(
            part_of(pieces.at[reach - (h * lo + low - other)], part), part_of(low_land.at[h, low], part),
            low_send.at[h, other, part], low_recv.at[h, low, part], low_peers[other],
        )

    def from_low(h, other, part):
        return remote(
            part_of(pieces.at[0], part), part_of(low_land.at[h, other], part), low_send.at[h, other, part],
            low_recv.at[h, other, part], low_peers[other],
        )

    def hop(h, part):
        return remote(
            part_of(moved.at[h], part), part_of(arrived.at[h - 1], part), chain_send.at[h, part],
            chain_recv.at[h - 1, part], left,
        )

    def pass_on(h, part):
        block = pl.ds(part * span, span)
        out[block] = jnp.zeros((span,) + out.shape[1:], out.dtype)
        if h and h * lo <= reach:
            out[block] += pieces[reach - h * lo, block].astype(jnp.float32)
        for other in range(lo):
            if lo > 1:
                @pl.when((low != other) & wanted(h, low, other))
                def _():
                    from_low(h, other, part).wait_recv()
                    out[block] += low_land[h, other, block].astype(jnp.float32)
        if h < hops:
            @pl.when(has_right & (high >= h))
            def _():
                hop(h + 1, part).wait_recv()
                out[block] += arrived[h, block].astype(jnp.float32)
        if h:
            @pl.when(high >= h)
            def _():
                moved[h, block] = out[block].astype(moved.dtype)
                hop(h, part).start()

    for h in range(hops, -1, -1):
        for part in range(2):
            for other in range(lo):
                if lo > 1:
                    @pl.when((low != other) & wanted(h, other, low))
                    def _():
                        across(h, other, part).start()
    for each in groups:
        each.start()
    cols, wide = early_stack.shape[1:]
    whole = early[...]
    if wide > early.shape[0]:
        blank = jnp.zeros((wide - early.shape[0], n * cols), early.dtype)
        whole = jnp.concatenate([whole, blank], axis=0)
    early_stack[...] = whole.T.reshape(n, cols, wide)
    early_pushes = []
    for k in range(1, n):
        push = remote(
            early_stack.at[lax.rem(dp + k, n)], early_out.at[dp], early_send.at[k], early_recv.at[k], dp_peers[k - 1]
        )
        push.start()
        early_pushes.append(push)
    early_out[dp] = early_stack[dp]
    stages = groups[0].stages()
    bounds = [0, 1] + [1 + (len(stages) - 1) * (i + 1) // hops for i in range(hops)]
    for h in range(hops, -1, -1):
        turn = hops - h
        for calls in stages[bounds[turn] : bounds[turn + 1]]:
            for call in calls:
                call()
        for part in range(2):
            pass_on(h, part)
    for h in range(hops + 1):
        for part in range(2):
            if h:
                @pl.when(high >= h)
                def _():
                    hop(h, part).wait_send()
            for other in range(lo):
                if lo > 1:
                    @pl.when((low != other) & wanted(h, other, low))
                    def _():
                        across(h, other, part).wait_send()
    for each in groups:
        each.finish()
    for push in early_pushes:
        push.wait()


def later_sum(lay, reach, pieces, parts, early, collective_id):
    n = lay.dp
    early_shape = (n, early.shape[1] // n, -(-early.shape[0] // 128) * 128)
    hops = min(lay.hi - 1, (reach + lay.lo - 1) // lay.lo)
    shape = pieces.shape[1:]
    vmem = pl.BlockSpec(memory_space=pltpu.VMEM)
    dma = pltpu.SemaphoreType.DMA
    return pl.pallas_call(
        partial(later_kernel, lay, reach),
        out_shape=(
            jax.ShapeDtypeStruct(shape, jnp.float32),
            jax.ShapeDtypeStruct((lay.hi, parts.shape[2], D), parts.dtype),
            jax.ShapeDtypeStruct(early_shape, early.dtype),
        ),
        in_specs=[vmem] * 3,
        out_specs=(vmem,) * 3,
        scratch_shapes=[
            pltpu.VMEM((hops + 1, lay.lo) + shape, pieces.dtype),
            pltpu.VMEM((hops + 1,) + shape, pieces.dtype),
            pltpu.VMEM((hops + 1,) + shape, pieces.dtype),
        ]
        + [pltpu.VMEM(early_shape, early.dtype), dma((n,)), dma((n,))]
        + [dma((hops + 1, 2))] * 2
        + [dma((hops + 1, lay.lo, 2))] * 2
        + GroupSum.scratch(lay, parts.shape[2]),
        compiler_params=pltpu.CompilerParams(
            collective_id=collective_id, has_side_effects=True, vmem_limit_bytes=VMEM_LIMIT
        ),
    )(pieces, parts, early)


def flip(index, bit):
    return index + bit * (1 - 2 * lax.rem(index // bit, 2))


class GroupSum:
    @staticmethod
    def scratch(lay, rows):
        dma = pltpu.SemaphoreType.DMA
        blocks = (lay.hi, lay.lo, lay.wide)
        data = [pltpu.VMEM(blocks + (rows, D), jnp.bfloat16)] * 3
        return data + [dma(blocks)] * 6

    def __init__(self, lay, parts, out, land, sums, second_land, core_send, core_recv, send, recv, second_send, second_recv):
        self.lay, self.parts, self.out = lay, parts, out
        self.land, self.sums, self.second_land = land, sums, second_land
        self.core_sems, self.sems, self.second_sems = (core_send, core_recv), (send, recv), (second_send, second_recv)
        dp = lax.axis_index("dp")
        ctx = lax.axis_index("ctx")
        hi, lo, wide = lay.hi, lay.lo, lay.wide
        high, self.low = ctx // lo, lax.rem(ctx, lo)
        self.across, self.core = dp // 2, lax.rem(dp, 2)
        self.partner = (self.across * 2 + 1 - self.core, ctx)
        self.low_peers = [(dp, high * lo + lax.rem(self.low + k, lo)) for k in range(lo)]
        self.wide_peers = [(lax.rem(self.across + k, wide) * 2 + self.core, ctx) for k in range(wide)]
        self.peers = self.low_peers[1:] + self.wide_peers[1:] + [self.partner]
        self.sends = []

    def at(self, h, a, b):
        lay = self.lay
        return h * lay.lo + lax.rem(self.low + a, lay.lo), lax.rem(self.across + b, lay.wide) * 2

    def turned(self, h):
        return h >= self.lay.hi // 2 and self.lay.lo > 1

    def core_copy(self, h, a, b):
        ctx, there = self.at(h, a, b)
        return remote(
            self.parts.at[ctx, there + 1 - self.core], self.land.at[h, a, b], self.core_sems[0].at[h, a, b],
            self.core_sems[1].at[h, a, b], self.partner,
        )

    def blocks(self):
        lay = self.lay
        return [
            (a, b) for a in list(range(1, lay.lo)) + [0] for b in list(range(1, lay.wide)) + [0]
        ]

    def start(self):
        for h in range(self.lay.hi):
            for a, b in self.blocks():
                self.core_copy(h, a, b).start()

    def first_copy(self, h, a, b):
        where = (h, a, b)
        return remote(
            self.sums.at[where], self.land_first(h, a, b), self.sems[0].at[where], self.sems[1].at[where],
            self.low_peers[a] if self.turned(h) else self.wide_peers[b],
        )

    def land_first(self, h, a, b):
        return self.second_land.at[h, a, b]

    def second_copy(self, h, a, b):
        where = (h, a, b)
        return remote(
            self.sums.at[where], self.second_land.at[where], self.second_sems[0].at[where],
            self.second_sems[1].at[where], self.wide_peers[b] if self.turned(h) else self.low_peers[a],
        )

    def moves_first(self, h, a, b):
        return a > 0 if self.turned(h) else b > 0

    def sum_cores(self, h):
        for a, b in self.blocks():
            self.core_copy(h, a, b).wait_recv()
            ctx, there = self.at(h, a, b)
            total = self.parts[ctx, there + self.core].astype(jnp.float32) + self.land[h, a, b].astype(jnp.float32)
            self.sums[h, a, b] = total.astype(jnp.bfloat16)
            if self.moves_first(h, a, b):
                self.first_copy(h, a, b).start()

    def sum_first(self, h):
        lay = self.lay
        for a, b in self.blocks():
            if self.moves_first(h, a, b):
                continue
            total = self.sums[h, a, b].astype(jnp.float32)
            others = [(k, b) for k in range(1, lay.lo)] if self.turned(h) else [(a, k) for k in range(1, lay.wide)]
            for other in others:
                self.first_copy(h, *other).wait_recv()
                total = total + self.second_land[(h,) + other].astype(jnp.float32)
            self.sums[h, a, b] = total.astype(jnp.bfloat16)
            if a or b:
                self.second_copy(h, a, b).start()

    def sum_second(self, h):
        lay = self.lay
        total = self.sums[h, 0, 0].astype(jnp.float32)
        others = [(0, k) for k in range(1, lay.wide)] if self.turned(h) else [(k, 0) for k in range(1, lay.lo)]
        for other in others:
            self.second_copy(h, *other).wait_recv()
            total = total + self.second_land[(h,) + other].astype(jnp.float32)
        self.out[h] = total.astype(jnp.bfloat16)

    def order(self):
        half = self.lay.hi // 2
        pairs = [h for pair in zip(range(half), range(half, 2 * half)) for h in pair]
        return pairs + list(range(2 * half, self.lay.hi))

    def stages(self):
        order = self.order()
        stages = []
        for i in range(len(order) + 4):
            calls = []
            if i < len(order):
                calls.append(partial(self.sum_cores, order[i]))
            if 2 <= i < len(order) + 2:
                calls.append(partial(self.sum_first, order[i - 2]))
            if 4 <= i:
                calls.append(partial(self.sum_second, order[i - 4]))
            stages.append(calls)
        return stages

    def finish(self):
        for h in range(self.lay.hi):
            for a, b in self.blocks():
                self.core_copy(h, a, b).wait_send()
                if self.moves_first(h, a, b):
                    self.first_copy(h, a, b).wait_send()
                elif a or b:
                    self.second_copy(h, a, b).wait_send()


def sum_group_kernel(lay, parts, gains, out, gains_out, gains_sum, gains_land, gains_send, gains_recv, *scratch):
    dp = lax.axis_index("dp")
    ctx = lax.axis_index("ctx")
    group = GroupSum(lay, parts, out, *scratch)
    gain_peers = [(flip(dp, 1 << i), ctx) for i in range((lay.dp - 1).bit_length())]
    gain_peers += [(dp, flip(ctx, 1 << i)) for i in range((lay.ctx - 1).bit_length())]
    greet(group.peers + gain_peers)

    def gains_copy(i):
        return remote(gains_sum.at[i], gains_land.at[i], gains_send.at[i], gains_recv.at[i], gain_peers[i])

    def gains_step(i):
        if i > len(gain_peers):
            return
        if i == 0:
            gains_sum[0] = gains[...]
        else:
            gains_copy(i - 1).wait_recv()
            gains_sum[i] = gains_sum[i - 1] + gains_land[i - 1]
        if i < len(gain_peers):
            gains_copy(i).start()
        else:
            gains_out[...] = gains_sum[i, pl.ds(dp * lay.ctx + ctx, 1)]

    group.start()
    stages = group.stages()
    for i, calls in enumerate(stages):
        gains_step(i)
        for call in calls:
            call()
    for i in range(len(stages), len(gain_peers) + 1):
        gains_step(i)
    group.finish()
    for i in range(len(gain_peers)):
        gains_copy(i).wait_send()


def sum_group(lay, parts, gains, collective_id):
    rows = parts.shape[2]
    vmem = pl.BlockSpec(memory_space=pltpu.VMEM)
    dma = pltpu.SemaphoreType.DMA
    count = (lay.dp - 1).bit_length() + (lay.ctx - 1).bit_length()
    return pl.pallas_call(
        partial(sum_group_kernel, lay),
        out_shape=(
            jax.ShapeDtypeStruct((lay.hi, rows, D), jnp.bfloat16),
            jax.ShapeDtypeStruct((1, gains.shape[1]), jnp.float32),
        ),
        in_specs=[vmem] * 2,
        out_specs=(vmem,) * 2,
        scratch_shapes=[
            pltpu.VMEM((count + 1,) + gains.shape, jnp.float32),
            pltpu.VMEM((count,) + gains.shape, jnp.float32),
            dma((count,)),
            dma((count,)),
        ]
        + GroupSum.scratch(lay, rows),
        compiler_params=pltpu.CompilerParams(
            collective_id=collective_id, has_side_effects=True, vmem_limit_bytes=VMEM_LIMIT
        ),
    )(parts, gains)


def grads_out_kernel(lay, rows, early, plane_qkv, plane_out, pairs_out, lows_out, qkv_out, out_t, attn, stack, land, low_stack, low_land, hi_land, last, last_land,
                     send, recv, hi_send, hi_recv, last_send, last_recv):
    n, hi, lo = lay.dp, lay.hi, lay.lo
    dp = lax.axis_index("dp")
    ctx = lax.axis_index("ctx")
    high, low = ctx // lo, lax.rem(ctx, lo)
    cols = lows_out.shape[0]
    per = lows_out.shape[1] // n
    half = rows.shape[0] // 5
    padded = 2 * half
    wide = land.shape[3]
    attn_rows = attn.shape[1]
    hi_peers = [(dp, lax.rem(high + k, hi) * lo + low) for k in range(1, hi)]
    greet([(lax.rem(dp + k, n), ctx) for k in range(1, n)] + hi_peers)
    attn[:, : plane_qkv.shape[1]] = plane_qkv[...]
    attn[:, plane_qkv.shape[1] :] = plane_out[...]
    hi_pushes = []
    for k in range(1, hi):
        push = remote(
            attn.at[lax.rem(high + k, hi)], hi_land.at[k - 1], hi_send.at[k], hi_recv.at[k], hi_peers[k - 1]
        )
        push.start()
        hi_pushes.append(push)
    pushes = []
    for i in range(3):
        held, arriving = (stack.at[i], land.at[i]) if i < 2 else (low_stack, low_land)
        lanes = held.shape[2]
        whole = rows[i * padded : min((i + 1) * padded, rows.shape[0])]
        if lanes > whole.shape[0]:
            blank = jnp.zeros((lanes - whole.shape[0], n * cols), jnp.bfloat16)
            whole = jnp.concatenate([whole, blank], axis=0)
        held[...] = whole.T.reshape(n, cols, lanes)
        for k in range(1, n):
            target = lax.rem(dp + k, n)
            push = remote(held.at[target], arriving.at[dp], send.at[i, k], recv.at[i, k], (target, ctx))
            push.start()
            pushes.append(push)
        arriving[dp] = held[dp]
    total = attn[high].astype(jnp.float32)
    for k, push in enumerate(hi_pushes):
        push.wait_recv()
        total = total + hi_land[k].astype(jnp.float32)
    for q in range(n):
        last[q] = total[:, q * cols : (q + 1) * cols].astype(jnp.bfloat16)
    last_pushes = []
    for k in range(1, n):
        target = lax.rem(dp + k, n)
        push = remote(last.at[target], last_land.at[dp], last_send.at[k], last_recv.at[k], (target, ctx))
        push.start()
        last_pushes.append(push)
    last_land[dp] = last[dp]

    unit = lax.broadcasted_iota(jnp.int32, (wide, 2 * per), 0)
    column = lax.broadcasted_iota(jnp.int32, (wide, 2 * per), 1)
    spread = [jnp.where(column == 2 * unit + i, 1.0, 0.0).astype(jnp.bfloat16) for i in range(2)]
    for push in pushes:
        push.wait_recv()
    for q in range(n):
        turns = dot_nn(land[0, q], spread[0]) + dot_nn(land[1, q], spread[1])
        pairs_out[:, 2 * per * q : 2 * per * (q + 1)] = turns.astype(jnp.bfloat16)
        lows_out[:, per * q : per * q + half] = low_land[q, :, :half]
        lows_out[:, per * q + half : per * (q + 1)] = early[q, :, : per - half]
    for push in last_pushes:
        push.wait_recv()
    out_rows = out_t.shape[1]
    out_part, qkv_part = plane_out.shape[1], plane_qkv.shape[1]
    qkv_out[...] = last_land[:, :qkv_part].reshape(n * qkv_part, cols)[: qkv_out.shape[0]].astype(jnp.float32)
    out_t[...] = last_land[:, qkv_part:].reshape(n * out_part, cols)[:out_rows].astype(jnp.float32).T
    for push in hi_pushes + pushes + last_pushes:
        push.wait_send()


def grads_out(lay, rows, early, plane_qkv, plane_out, per, qkv_rows, out_rows, collective_id):
    padded = 2 * rows.shape[0] // 5
    n, cols = lay.dp, rows.shape[1] // lay.dp
    attn_rows = plane_qkv.shape[1] + plane_out.shape[1]
    vmem = pl.BlockSpec(memory_space=pltpu.VMEM)
    dma = pltpu.SemaphoreType.DMA
    return pl.pallas_call(
        partial(grads_out_kernel, lay),
        out_shape=(
            jax.ShapeDtypeStruct((cols, n * 2 * per), jnp.bfloat16),
            jax.ShapeDtypeStruct((cols, n * per), jnp.bfloat16),
            jax.ShapeDtypeStruct((qkv_rows, cols), jnp.float32),
            jax.ShapeDtypeStruct((cols, out_rows), jnp.float32),
        ),
        in_specs=[vmem] * 4,
        out_specs=(vmem,) * 4,
        scratch_shapes=[
            pltpu.VMEM((lay.hi, attn_rows, D), jnp.bfloat16),
            pltpu.VMEM((2, n, cols, -(-padded // 128) * 128), jnp.bfloat16),
            pltpu.VMEM((2, n, cols, -(-padded // 128) * 128), jnp.bfloat16),
            pltpu.VMEM(early.shape, jnp.bfloat16),
            pltpu.VMEM(early.shape, jnp.bfloat16),
            pltpu.VMEM((max(1, lay.hi - 1), attn_rows, D), jnp.bfloat16),
            pltpu.VMEM((n, attn_rows, cols), jnp.bfloat16),
            pltpu.VMEM((n, attn_rows, cols), jnp.bfloat16),
        ]
        + [dma((3, n))] * 2
        + [dma((lay.hi,))] * 2
        + [dma((n,))] * 2,
        compiler_params=pltpu.CompilerParams(
            collective_id=collective_id, has_side_effects=True, vmem_limit_bytes=VMEM_LIMIT
        ),
    )(rows, early, plane_qkv, plane_out)


def in_tiles(total, size, body, begin=0):
    whole = total // size

    def step(i, carry):
        body(pl.multiple_of(begin + i * size, math.gcd(begin, size)), size)
        return carry

    if whole:
        lax.fori_loop(0, whole, step, 0)
    if total % size:
        body(begin + whole * size, total % size)


def dot_nt(left, right):
    return lax.dot_general(left, right, (((1,), (1,)), ((), ())), preferred_element_type=jnp.float32)


def dot_nn(left, right):
    return lax.dot_general(left, right, (((1,), (0,)), ((), ())), preferred_element_type=jnp.float32)


ROOT = math.sqrt(2.0 / math.pi)


def feed_forward_kernel(
    lay, mid_in, weights, mixed, cotangent, valid, gain, result, grad_mid, grad_gain, grad_weights, early_sum,
    mid, mid_sem, late, late_sem, early, early_land, hi_send, hi_recv, w_gate, w_up, w_down, gate_t, up_t, act, slope, hidden, hidden_t, grads, parts, core_land, sums, via, landed,
    total, dy, weight_sem, core_send, core_recv, share_send, share_recv,
    send, recv, via_send, via_recv, dy_send, dy_recv, dy_pass,
):
    chip, core, high = lay.place()
    n, wide = lay.chips, lay.wide
    tokens = mixed.shape[0]
    units = w_gate.shape[0]
    hi = lay.hi
    padded = units // hi
    part_rows = padded // 2
    loads = [
        pltpu.make_async_copy(
            weights.at[h, pl.ds(i * padded + part * part_rows, part_rows)],
            held.at[pl.ds((part * hi + h) * part_rows, part_rows)],
            weight_sem.at[i, part, h],
        )
        for i, held in enumerate((w_gate, w_up, w_down))
        for part in range(2)
        for h in range(hi)
    ]
    mid_loads = [
        pltpu.make_async_copy(mid_in.at[p], mid.at[p], mid_sem.at[p]) for p in range(lay.chips)
    ]
    gates = len(loads) * 2 // 3
    for load in mid_loads[:1] + loads[:gates] + mid_loads[1:] + loads[gates:]:
        load.start()
    peers = [lay.device(lay.offset(chip, k), core, high) for k in range(n)]
    owners = [lay.device(lay.offset(chip, k, -1), core, high) for k in range(n)]
    partner = lay.device(chip, 1 - core, high)
    mine = pl.ds(pl.multiple_of(core * tokens, tokens), tokens)
    theirs = pl.ds(pl.multiple_of((1 - core) * tokens, tokens), tokens)
    half = tokens // 2
    halves = (pl.ds(0, half), pl.ds(half, half))
    straight, bent = lay.straight(), lay.bent()
    place = [lay.position(k) for k in range(n)]
    hi_peers = [lay.device(chip, core, lax.rem(high + k, hi)) for k in range(hi)]
    greet(peers[1:] + [partner] + hi_peers[1:])

    def to_partner(phase, k):
        return remote(
            parts.at[place[k], theirs], core_land.at[k], core_send.at[phase, k], core_recv.at[phase, k], partner
        )

    def to_owner(phase, k, h):
        return remote(
            sums.at[k - 1, halves[h]], landed.at[place[k] - len(bent), halves[h]], send.at[phase, k, h],
            recv.at[phase, k, h], owners[k],
        )

    def to_neighbour(phase, k, h):
        step = k % wide if h == 0 else k // wide * wide
        return remote(
            sums.at[k - 1, halves[h]], via.at[place[k], halves[h]], via_send.at[phase, k, h], via_recv.at[phase, k, h],
            owners[step],
        )

    def added(k):
        if k < wide:
            return 1, [k + b * wide for b in range(1, lay.lo)]
        return 0, [k + step for step in range(1, wide)]

    def add_core(phase, k):
        to_partner(phase, k).wait_recv()

        def chunk(first, rows):
            span = pl.ds(first, rows)
            here = pl.ds(pl.multiple_of(core * tokens + first, rows), rows)
            both = parts[place[k], here].astype(jnp.float32) + core_land[k, span].astype(jnp.float32)
            if k:
                sums[k - 1, span] = both.astype(jnp.bfloat16)
            else:
                total[span] = both

        in_tiles(tokens, 32, chunk)
        if k in bent:
            for h in range(2):
                to_neighbour(phase, k, h).start()
        elif k:
            h, others = added(k)
            to_owner(phase, k, 1 - h).start()
            if not others:
                to_owner(phase, k, h).start()

    def add_neighbours(phase, k):
        h, others = added(k)
        if not others:
            return
        for other in others:
            to_neighbour(phase, other, h).wait_recv()

        def chunk(first, rows):
            span = pl.ds(first + h * half, rows)
            value = sums[k - 1, span].astype(jnp.float32)
            for other in others:
                value = value + via[place[other], span].astype(jnp.float32)
            sums[k - 1, span] = value.astype(jnp.bfloat16)

        in_tiles(half, 32, chunk)
        to_owner(phase, k, h).start()

    def add_owners(phase):
        for k in straight:
            for h in range(2):
                to_owner(phase, k, h).wait_recv()

        def chunk(first, rows):
            span = pl.ds(first, rows)
            value = total[span]
            for k in straight:
                value = value + landed[place[k] - len(bent), span].astype(jnp.float32)
            total[span] = value

        in_tiles(tokens, 32, chunk)

    def settle(phase):
        for k in range(n):
            to_partner(phase, k).wait_send()
            for h in range(2):
                if k in bent:
                    to_neighbour(phase, k, h).wait_send()
                elif k:
                    to_owner(phase, k, h).wait_send()

    rows_of = 2 * tokens

    def joined(ref, group, *index):
        value = ref[(pl.ds(*group),) + index]
        return value.reshape((group[1] * rows_of,) + value.shape[2:])

    def forward_units(group, begin, end):
        count = group[1]

        def tile(first, width):
            units_here = pl.ds(first, width)
            weights = jnp.concatenate([w_gate[units_here], w_up[units_here]], axis=0)
            both = dot_nt(joined(mid, group), weights)
            gate, up = both[:, :width], both[:, width:]
            square = gate * gate
            tanh = jnp.tanh(gate * (ROOT + (0.044715 * ROOT) * square))
            half_way = 0.5 + 0.5 * tanh
            active = gate * half_way
            slant = half_way + active * (1.0 - tanh) * (ROOT + (3.0 * 0.044715 * ROOT) * square)
            product = (active * up).astype(jnp.bfloat16)
            shape = (count, rows_of, width)
            act[pl.ds(*group), :, units_here] = active.astype(jnp.bfloat16).reshape(shape)
            slope[pl.ds(*group), :, units_here] = (slant * up).astype(jnp.bfloat16).reshape(shape)
            hidden[: count * rows_of, units_here] = product
            for c in range(count):
                hidden_t[group[0] + c, units_here] = product[c * rows_of : (c + 1) * rows_of].T

        in_tiles(end - begin, 128, tile, begin)

    def forward_down(group):
        count = group[1]

        def tile(first, width):
            lanes = pl.ds(first, width)
            value = dot_nn(hidden[: count * rows_of], w_down[:, lanes]).astype(jnp.bfloat16)
            parts[pl.ds(*group), :, lanes] = value.reshape(count, rows_of, width)

        in_tiles(D, 256, tile)

    def backward_units(group):
        count = group[1]

        def tile(first, width):
            units_here = pl.ds(first, width)
            grad = dot_nt(joined(dy, group), w_down[units_here])
            up_grad = (grad * joined(act, group, slice(None), units_here).astype(jnp.float32)).astype(jnp.bfloat16)
            gate_grad = (grad * joined(slope, group, slice(None), units_here).astype(jnp.float32)).astype(jnp.bfloat16)
            grads[0, : count * rows_of, units_here] = gate_grad
            grads[1, : count * rows_of, units_here] = up_grad
            for c in range(count):
                rows = slice(c * rows_of, (c + 1) * rows_of)
                gate_t[group[0] + c, units_here] = gate_grad[rows].T
                up_t[group[0] + c, units_here] = up_grad[rows].T

        in_tiles(units, 256, tile)

    def backward_in(group):
        count = group[1]

        def tile(first, width):
            lanes = pl.ds(first, width)
            both = dot_nn(grads[0, : count * rows_of], w_gate[:, lanes]) + dot_nn(
                grads[1, : count * rows_of], w_up[:, lanes]
            )
            parts[pl.ds(*group), :, lanes] = both.astype(jnp.bfloat16).reshape(count, rows_of, width)

        in_tiles(D, 256, tile)

    def product_over_tokens(left, begin, end, right, lanes):
        value = dot_nn(left[0, begin:end], right[0, :, lanes])
        for c in range(1, n):
            value = value + dot_nn(left[c, begin:end], right[c, :, lanes])
        return value.astype(jnp.bfloat16)

    far, near, here = (0, len(bent)), (len(bent), len(straight)), (n - 1, 1)
    most = hidden.shape[0] // rows_of

    def runs(group):
        return [(first, min(most, group[0] + group[1] - first)) for first in range(group[0], sum(group), most)]

    quarter = units // 512 * 128
    for load in mid_loads[:1] + loads[:gates]:
        load.wait()
    waiting = [mid_loads[1:], loads[gates:]]

    def arrive(which):
        while waiting[which]:
            waiting[which].pop(0).wait()

    for run in runs(far):
        if run[0] + run[1] > 1:
            arrive(0)
        forward_units(run, 0, units)
        arrive(1)
        forward_down(run)
    for k in bent:
        to_partner(0, k).start()
    arrive(0)
    for i, run in enumerate(runs(near)):
        forward_units(run, 0, 2 * quarter)
        if i == 0:
            for k in bent:
                add_core(0, k)
        forward_units(run, 2 * quarter, units)
        arrive(1)
        forward_down(run)
    for k in straight:
        to_partner(0, k).start()
    forward_units(here, 0, 2 * quarter)
    for k in straight:
        add_core(0, k)
    for k in straight:
        add_neighbours(0, k)
    forward_units(here, 2 * quarter, units)
    forward_down(here)
    to_partner(0, 0).start()
    add_core(0, 0)
    add_owners(0)

    grad_gain[...] = jnp.zeros_like(grad_gain)
    scale = 1.0 + gain[...]

    def finish(first, rows):
        span = pl.ds(first, rows)
        spot = pl.ds(pl.multiple_of(core * tokens + first, rows), rows)
        y = total[span]
        ok = valid[span]
        rate = lax.rsqrt(jnp.mean(y * y, axis=-1, keepdims=True) + EPS)
        unit = y * rate
        result[span] = ((mixed[span] + unit * scale) * ok).astype(jnp.bfloat16)
        upstream = cotangent[span].astype(jnp.float32) * ok
        down = upstream * unit
        for r in range(0, rows, 8):
            grad_gain[...] += down[r : r + 8]
        scaled = upstream * scale
        inner = jnp.mean(scaled * unit, axis=-1, keepdims=True)
        dy[n - 1, spot] = (rate * (scaled - unit * inner)).astype(jnp.bfloat16)

    in_tiles(tokens, 32, finish)

    def dy_half(k, h):
        return dy.at[place[k], pl.ds(pl.multiple_of(core * tokens + h * half, half), half)]

    def dy_push(k, h):
        return remote(dy_half(0, h), dy_half(k, h), dy_send.at[k, h], dy_recv.at[k, h], peers[k])

    def dy_onward(k, h, step):
        return remote(
            dy_half(k, h), dy_half(k + step, h), dy_pass.at[k + step, h], dy_recv.at[k + step, h], peers[step]
        )

    shares = [
        remote(dy.at[place[k], mine], dy.at[place[k], mine], share_send.at[k], share_recv.at[k], partner)
        for k in range(n)
    ]
    ordered = [(k, i if k < wide else 1 - i) for i in range(2) for k in straight]
    for k, h in ordered:
        dy_push(k, h).start()
    shares[0].start()
    settle(0)
    shares[0].wait_recv()
    backward_units(here)
    backward_in(here)
    to_partner(1, 0).start()
    onward = []
    for k, h in ordered:
        dy_push(k, h).wait_recv()
        if k < wide and h == 0:
            onward += [(k, h, b * wide) for b in range(1, lay.lo)]
        elif k >= wide and h == 1:
            onward += [(k, h, step) for step in range(1, wide)]
        for go in onward:
            if go[:2] == (k, h):
                dy_onward(*go).start()
    for k in straight:
        shares[k].start()
    add_core(1, 0)
    for k in straight:
        shares[k].wait_recv()
    for i, run in enumerate(runs(near)):
        backward_units(run)
        if i == 0:
            for k in bent:
                for h in range(2):
                    dy_push(k, h).wait_recv()
                shares[k].start()
        backward_in(run)
    for k in straight:
        to_partner(1, k).start()
    for k in bent:
        shares[k].wait_recv()
    split = hi * part_rows

    def early_grad(first, width):
        lanes = pl.ds(first, width)
        value = product_over_tokens(hidden_t, split, units, dy, lanes)
        for h in range(hi):
            early[h, :, lanes] = value[h * part_rows : (h + 1) * part_rows]

    in_tiles(D, 256, early_grad)
    hi_pushes = []
    for k in range(1, hi):
        push = remote(
            early.at[lax.rem(high + k, hi)], early_land.at[k - 1], hi_send.at[k], hi_recv.at[k], hi_peers[k]
        )
        push.start()
        hi_pushes.append(push)
    for i, run in enumerate(runs(far)):
        backward_units(run)
        if i == 0:
            for k in straight:
                add_core(1, k)
        backward_in(run)
    if not bent:
        for k in straight:
            add_core(1, k)
    for k in bent:
        to_partner(1, k).start()
    for k in bent:
        add_core(1, k)

    stores = []

    def weight_grad(left, right, i):
        parts_here = (0,) if i == 2 else (0, 1)

        def tile(first, width):
            lanes = pl.ds(first, width)
            value = product_over_tokens(left, 0, split * len(parts_here), right, lanes)
            for part in parts_here:
                for h in range(hi):
                    row = i * padded + part * part_rows
                    start = (part * hi + h) * part_rows
                    late[h, row : row + part_rows, lanes] = value[start : start + part_rows]

        in_tiles(D, 256, tile)
        rows = pl.ds(i * padded, part_rows * len(parts_here))
        store = pltpu.make_async_copy(late.at[:, rows], grad_weights.at[:, rows], late_sem.at[i])
        store.start()
        stores.append(store)

    weight_grad(hidden_t, dy, 2)
    for k in straight:
        add_neighbours(1, k)
    weight_grad(gate_t, mid, 0)
    weight_grad(up_t, mid, 1)
    add_owners(1)
    grad_mid[...] = total[...]
    for push in hi_pushes:
        push.wait_recv()
    early_total = early[high].astype(jnp.float32)
    for k in range(hi - 1):
        early_total = early_total + early_land[k].astype(jnp.float32)
    early_sum[...] = early_total.astype(jnp.bfloat16)
    for push in hi_pushes:
        push.wait_send()
    for store in stores:
        store.wait()
    settle(1)
    for k, h in ordered:
        dy_push(k, h).wait_send()
    for go in onward:
        dy_onward(*go).wait_send()
    for share in shares:
        share.wait_send()


def feed_forward(lay, mid, weights, mixed, cotangent, valid, gain, collective_id):
    n = lay.chips
    tokens = mixed.shape[0]
    units = weights.shape[0] * weights.shape[1] // 3
    early_rows = weights.shape[1] // 6
    late_rows = weights.shape[1] - early_rows
    most = min(n, max(1, 1920 // units))
    low, high = jnp.bfloat16, jnp.float32
    vmem = pl.BlockSpec(memory_space=pltpu.VMEM)
    dma = pltpu.SemaphoreType.DMA
    return pl.pallas_call(
        partial(feed_forward_kernel, lay),
        out_shape=(
            jax.ShapeDtypeStruct((tokens, D), low),
            jax.ShapeDtypeStruct((tokens, D), high),
            jax.ShapeDtypeStruct((8, D), high),
            jax.ShapeDtypeStruct((lay.hi, late_rows, D), low),
            jax.ShapeDtypeStruct((early_rows, D), low),
        ),
        in_specs=[pl.BlockSpec(memory_space=pl.ANY)] * 2 + [vmem] * 4,
        out_specs=(vmem, vmem, vmem, pl.BlockSpec(memory_space=pl.ANY), vmem),
        scratch_shapes=[
            pltpu.VMEM((n, 2 * tokens, D), low),
            dma((n,)),
            pltpu.VMEM((lay.hi, late_rows, D), low),
            dma((3,)),
            pltpu.VMEM((lay.hi, early_rows, D), low),
            pltpu.VMEM((max(1, lay.hi - 1), early_rows, D), low),
            dma((lay.hi,)),
            dma((lay.hi,)),
            pltpu.VMEM((units, D), low),
            pltpu.VMEM((units, D), low),
            pltpu.VMEM((units, D), low),
            pltpu.VMEM((n, units, 2 * tokens), low),
            pltpu.VMEM((n, units, 2 * tokens), low),
            pltpu.VMEM((n, 2 * tokens, units), low),
            pltpu.VMEM((n, 2 * tokens, units), low),
            pltpu.VMEM((most * 2 * tokens, units), low),
            pltpu.VMEM((n, units, 2 * tokens), low),
            pltpu.VMEM((2, most * 2 * tokens, units), low),
            pltpu.VMEM((n, 2 * tokens, D), low),
            pltpu.VMEM((n, tokens, D), low),
            pltpu.VMEM((max(1, n - 1), tokens, D), low),
            pltpu.VMEM((max(1, len(lay.bent())), tokens if lay.bent() else 16, D), low),
            pltpu.VMEM((max(1, len(lay.straight())), tokens, D), low),
            pltpu.VMEM((tokens, D), high),
            pltpu.VMEM((n, 2 * tokens, D), low),
            dma((3, 2, lay.hi)),
        ]
        + [dma((2, n))] * 2
        + [dma((n,))] * 2
        + [dma((2, n, 2))] * 4
        + [dma((n, 2))] * 3,
        compiler_params=pltpu.CompilerParams(
            collective_id=collective_id, has_side_effects=True, vmem_limit_bytes=63 * 2**20
        ),
    )(mid, weights, mixed, cotangent, valid, gain)


def norm_scaled(v, gain):
    return v * lax.rsqrt(jnp.mean(v * v, axis=-1, keepdims=True) + EPS) * (1.0 + gain)


def rotate(v, angle):
    half = v.shape[-1] // 2
    cosine = jnp.cos(angle)
    sine = jnp.sin(angle)
    first = v[..., :half]
    second = v[..., half:]
    return jnp.concatenate(
        [first * cosine - second * sine, second * cosine + first * sine], axis=-1
    )


def angles_of(positions):
    inverse = 1.0 / 10000.0 ** (jnp.arange(HD // 2, dtype=jnp.float32) * (2.0 / HD))
    return positions.astype(jnp.float32)[:, None] * inverse[None, :]


def head_inputs(projected, gain_query, gain_key, angle):
    query = projected[..., : HEADS * HD].reshape(projected.shape[:-1] + (HEADS, HD))
    key_rows = projected[..., HEADS * HD : (HEADS + 1) * HD]
    value_rows = projected[..., (HEADS + 1) * HD :]
    query = rotate(norm_scaled(query, gain_query), angle[:, None, :])
    key_rows = rotate(norm_scaled(key_rows, gain_key), angle)
    return (query, key_rows, value_rows)


def contract(left, right, dims_left, dims_right):
    return lax.dot_general(
        left, right, ((dims_left, dims_right), ((), ())), preferred_element_type=jnp.float32
    )


def per_device(lay, tokens, lengths, w_qkv, w_out, w_gate_up, w_down, gains, cotangent):
    seq_count = tokens.shape[0]
    local_len = tokens.shape[1]
    reach = (WINDOW - 1) // local_len + 1
    scale = 1.0 / math.sqrt(HD)
    units = w_down.shape[0]
    per = units // lay.dp
    qkv_rows, out_rows = w_qkv.shape[0], w_out.shape[0]
    cols = w_qkv.shape[1]
    used = qkv_rows + out_rows + 1
    block = 16 * lay.dp
    pack_rows = -(-used // block) * block
    plane, ffn_rows, earlier_tokens = weights_in(
        lay,
        reach,
        tokens,
        w_qkv,
        w_out.T,
        gains[None],
        w_gate_up.T,
        w_down.T,
        5,
    )
    ffn_all = lax.all_gather(ffn_rows, "ctx", axis=0, axis_index_groups=lay.hi_groups)
    attn_all = gather_group(
        lay,
        plane,
        (lay.hi, lay.lo, lay.dp, pack_rows // lay.dp, D),
        lambda out, k, chip, core: out.at[
            :, chip // lay.wide, lax.rem(chip, lay.wide) * 2 + core
        ],
        6,
    ).reshape(lay.ctx, pack_rows, D)
    full_qkv = attn_all[:, :qkv_rows].reshape(lay.ctx * qkv_rows, D)
    full_out = attn_all[:, qkv_rows : qkv_rows + out_rows].reshape(lay.ctx * out_rows, D)
    gain_all = (
        attn_all[:, used - 1]
        .reshape(lay.ctx, lay.dp, cols)[:, :, : gains.shape[0]]
        .transpose(1, 0, 2)
        .reshape(-1)
        .astype(jnp.float32)
    )
    gain_in = gain_all[:D]
    gain_attn = gain_all[D : 2 * D]
    gain_pre = gain_all[2 * D : 3 * D]
    gain_post = gain_all[3 * D : 4 * D]
    gain_query = gain_all[4 * D : 4 * D + HD]
    gain_key = gain_all[4 * D + HD :]
    offset = lax.axis_index("ctx") * local_len
    positions = offset + jnp.arange(local_len, dtype=jnp.int32)
    angle = angles_of(positions)
    valid = positions[None, :] < lengths[:, None]
    inputs = tokens.astype(jnp.float32)
    normed_in, pull_in = jax.vjp(norm_scaled, inputs, gain_in)
    normed_low = normed_in.astype(jnp.bfloat16)
    projected = contract(normed_low, full_qkv, (2,), (1,))
    (query, key_rot, value_rows), pull_heads = jax.vjp(
        partial(head_inputs, angle=angle), projected, gain_query, gain_key
    )
    query_low = query.astype(jnp.bfloat16)
    key_pos = offset - reach * local_len + jnp.arange((reach + 1) * local_len, dtype=jnp.int32)
    earlier = earlier_tokens.transpose(1, 0, 2, 3).reshape(seq_count, reach * local_len, D)
    earlier = norm_scaled(earlier.astype(jnp.float32), gain_in).astype(jnp.bfloat16)
    earlier = contract(earlier, full_qkv[HEADS * HD :], (2,), (1,))
    earlier_keys = rotate(
        norm_scaled(earlier[..., :HD], gain_key), angles_of(key_pos[: reach * local_len])
    )
    key_pairs = jnp.concatenate(
        [
            jnp.concatenate([earlier_keys, earlier[..., HD:]], axis=-1).astype(jnp.bfloat16),
            jnp.concatenate([key_rot, value_rows], axis=-1).astype(jnp.bfloat16),
        ],
        axis=1,
    )
    keys_low = key_pairs[..., :HD]
    values_low = key_pairs[..., HD:]
    key_grid = key_pos[None, None, :]
    query_grid = positions[None, :, None]
    allowed = (
        (key_grid >= 0)
        & (key_grid <= query_grid)
        & (query_grid - key_grid < WINDOW)
        & ((key_grid < lengths[:, None, None]) | (key_grid == query_grid))
    )

    def scores_of():
        raw = jnp.einsum("schd,skd->shck", query_low, keys_low, preferred_element_type=jnp.float32)
        return jnp.where(allowed[:, None], raw * scale, -BIG)

    scores = scores_of()
    top = jnp.max(scores, axis=-1, keepdims=True)
    expo = jnp.exp(scores - top)
    total = jnp.sum(expo, axis=-1, keepdims=True)
    probs = expo / total
    log_total = top + jnp.log(total)
    probs_low = probs.astype(jnp.bfloat16)
    attended = jnp.einsum(
        "shck,skd->schd", probs_low, values_low, preferred_element_type=jnp.float32
    )
    attended_low = attended.reshape(seq_count, local_len, HEADS * HD).astype(jnp.bfloat16)
    out_proj = contract(attended_low, full_out, (2,), (0,))
    normed_out, pull_out = jax.vjp(norm_scaled, out_proj, gain_attn)
    mixed = inputs + normed_out
    normed_mid, pull_mid = jax.vjp(norm_scaled, mixed, gain_pre)
    mid_low = normed_mid.astype(jnp.bfloat16)
    token_count = seq_count * local_len
    mid_all = gather_group(
        lay,
        mid_low.reshape(2, token_count // 2, D),
        (lay.chips, 2, 2, token_count // 2, D),
        lambda out, k, chip, core: out.at[lay.position(k), core],
        1,
    ).reshape(lay.chips, 2 * token_count, D)
    result, grad_mid, grad_gain_post, grad_ffn, early_down = feed_forward(
        lay,
        mid_all,
        ffn_all,
        mixed.reshape(token_count, D),
        cotangent.reshape(token_count, D),
        valid.reshape(token_count, 1).astype(jnp.float32),
        gain_post[None],
        2,
    )
    result = result.reshape(mixed.shape)
    grad_mid = grad_mid.reshape(mixed.shape)
    grad_gain_post = jnp.sum(grad_gain_post, axis=0)
    upstream = jnp.where(valid[..., None], cotangent.astype(jnp.float32), 0.0)
    grad_mixed_in, grad_gain_pre = pull_mid(grad_mid)
    grad_mixed = upstream + grad_mixed_in
    grad_proj, grad_gain_attn = pull_out(grad_mixed)
    proj_low = grad_proj.astype(jnp.bfloat16)
    grad_attended = contract(proj_low, full_out, (2,), (1,))
    grad_w_out = contract(attended_low, proj_low, (0, 1), (0, 1))
    attn_low = grad_attended.astype(jnp.bfloat16).reshape(seq_count, local_len, HEADS, HD)
    again_probs = jnp.exp(scores_of() - log_total)
    again_low = again_probs.astype(jnp.bfloat16)
    grad_values = jnp.einsum(
        "shck,schd->skd", again_low, attn_low, preferred_element_type=jnp.float32
    )
    grad_probs = jnp.einsum(
        "schd,skd->shck", attn_low, values_low, preferred_element_type=jnp.float32
    )
    row_dot = jnp.sum(again_probs * grad_probs, axis=-1, keepdims=True)
    grad_scores = (scale * again_probs * (grad_probs - row_dot)).astype(jnp.bfloat16)
    grad_query = jnp.einsum(
        "shck,skd->schd", grad_scores, keys_low, preferred_element_type=jnp.float32
    )
    grad_keys = jnp.einsum(
        "shck,schd->skd", grad_scores, query_low, preferred_element_type=jnp.float32
    )
    grad_pairs = jnp.concatenate([grad_keys, grad_values], axis=-1)
    own_grad = grad_pairs[:, reach * local_len :]
    pieces = grad_pairs[:, : reach * local_len].astype(jnp.bfloat16)
    pieces = pieces.reshape(seq_count, reach, local_len, 2 * HD).transpose(1, 0, 2, 3)

    def blocks_of(grad, rows):
        part = -(-rows // (16 * lay.dp)) * 16
        whole = grad.astype(jnp.bfloat16).reshape(lay.ctx, rows, D)
        if part * lay.dp > rows:
            whole = jnp.pad(whole, ((0, 0), (0, part * lay.dp - rows), (0, 0)))
        return whole.reshape(lay.ctx, lay.dp, part, D)

    later, plane_out, early_units = later_sum(
        lay, reach, pieces, blocks_of(grad_w_out, out_rows), early_down, 11
    )
    own_grad = own_grad + later
    grad_projected, grad_gain_query, grad_gain_key = pull_heads(
        (grad_query, own_grad[..., :HD], own_grad[..., HD:])
    )
    qkv_low = grad_projected.astype(jnp.bfloat16)
    grad_w_qkv = contract(qkv_low, normed_low, (0, 1), (0, 1))
    grad_normed = contract(qkv_low, full_qkv, (2,), (0,))
    grad_in_norm, grad_gain_in = pull_in(grad_normed)
    grad_input = grad_mixed + grad_in_norm
    grad_gain_all = jnp.concatenate(
        [
            grad_gain_in,
            grad_gain_attn,
            grad_gain_pre,
            grad_gain_post,
            grad_gain_query,
            grad_gain_key,
        ]
    )
    plane_qkv, gains_sum = sum_group(
        lay, blocks_of(grad_w_qkv, qkv_rows), grad_gain_all.reshape(-1, gains.shape[0]), 8
    )
    owned = lax.psum_scatter(grad_ffn, "ctx", scatter_dimension=0, axis_index_groups=lay.hi_groups)
    part_gate_up, part_down, part_qkv, part_out = grads_out(
        lay, owned, early_units, plane_qkv, plane_out, per, qkv_rows, out_rows, 9
    )
    part_out = part_out.T
    part_gains = gains_sum[0]
    part_gate_up = part_gate_up.astype(jnp.float32).T
    part_down = part_down.astype(jnp.float32).T
    return (result, grad_input, part_qkv, part_out, part_gate_up, part_down, part_gains)


def solution(mesh):
    placed = (
        P("dp", "ctx", None),
        P("dp"),
        P("ctx", "dp"),
        P("ctx", "dp"),
        P("ctx", "dp"),
        P("ctx", "dp"),
        P(("dp", "ctx")),
        P("dp", "ctx", None),
    )
    return jax.shard_map(
        partial(per_device, Layout(mesh)),
        mesh=mesh,
        in_specs=placed,
        out_specs=(
            P("dp", "ctx", None),
            P("dp", "ctx", None),
            P("ctx", "dp"),
            P("ctx", "dp"),
            P("ctx", "dp"),
            P("ctx", "dp"),
            P(("dp", "ctx")),
        ),
        check_vma=False,
    )
```

```python
from functools import partial
import math

import jax
import jax.numpy as jnp
from jax import lax
from jax.experimental import pallas as pl
from jax.experimental.pallas import tpu as pltpu
from jax.sharding import PartitionSpec as P

D = 1152
HEADS = 4
HD = 256
WINDOW = 512
GROUP = 8

EPS = 1e-06
BIG = 1e30
MESH = pl.DeviceIdType.MESH
VMEM_LIMIT = 56 * 2**20


class Layout:
    def __init__(self, mesh):
        self.dp = mesh.shape["dp"]
        self.ctx = mesh.shape["ctx"]
        self.lo = max(1, GROUP // self.dp)
        self.hi = self.ctx // self.lo
        self.wide = self.dp // 2
        self.chips = self.wide * self.lo
        self.group = self.dp * self.lo
        self.hi_groups = [
            [h * self.lo + low for h in range(self.hi)] for low in range(self.lo)
        ]

    def place(self):
        dp = lax.axis_index("dp")
        ctx = lax.axis_index("ctx")
        chip = lax.rem(ctx, self.lo) * self.wide + dp // 2
        return chip, lax.rem(dp, 2), ctx // self.lo

    def offset(self, chip, k, sign=1):
        across = lax.rem(chip, self.wide) + self.wide + sign * (k % self.wide)
        low = chip // self.wide + self.lo + sign * (k // self.wide)
        return lax.rem(low, self.lo) * self.wide + lax.rem(across, self.wide)

    def straight(self):
        return list(range(1, self.wide)) + [low * self.wide for low in range(1, self.lo)]

    def bent(self):
        return [k for k in range(1, self.chips) if k not in self.straight()]

    def position(self, k):
        return (self.bent() + self.straight() + [0]).index(k)

    def device(self, chip, core, high):
        return (lax.rem(chip, self.wide) * 2 + core, high * self.lo + chip // self.wide)


def remote(src, dst, send, recv, device):
    return pltpu.make_async_remote_copy(
        src_ref=src, dst_ref=dst, send_sem=send, recv_sem=recv, device_id=device, device_id_type=MESH
    )


def greet(devices):
    barrier = pltpu.get_barrier_semaphore()
    for device in devices:
        pl.semaphore_signal(barrier, inc=1, device_id=device, device_id_type=MESH)
    pl.semaphore_wait(barrier, len(devices))


def gather_group_kernel(lay, slot, own, out, local_sem, send, recv, pass_send, core_send, core_recv):
    chip, core, high = lay.place()
    n = lay.chips
    half = own.shape[0] // 2
    halves = (pl.ds(0, half), pl.ds(half, half))
    peers = [lay.device(lay.offset(chip, k), core, high) for k in range(n)]
    sources = [lay.offset(chip, k, -1) for k in range(n)]
    partner = lay.device(chip, 1 - core, high)
    greet(peers[1:] + [partner])
    mine = [slot(out, k, chip, core) for k in range(n)]
    straight, bent = lay.straight(), lay.bent()
    keep = pltpu.make_async_copy(own, mine[0], local_sem)
    keep.start()
    pushes = []

    def push(k, h, source, target, sem):
        copy = remote(source.at[halves[h]], target.at[halves[h]], sem, recv.at[k, h], peers[k])
        return copy

    ordered = [(k, i if k < lay.wide else 1 - i) for i in range(2) for k in straight]
    for k, h in ordered:
        copy = push(k, h, own, mine[k], send.at[k, h])
        copy.start()
        pushes.append(copy)
    shares = [remote(own, mine[0], core_send.at[0], core_recv.at[0], partner)]
    shares[0].start()

    def arrived(k, h):
        copy = remote(own.at[halves[h]], mine[k].at[halves[h]], send.at[k, h], recv.at[k, h], peers[k])
        copy.wait_recv()

    for k, h in ordered:
        arrived(k, h)
        block = slot(out, k, sources[k], core)
        if k < lay.wide and h == 0:
            onward = [b * lay.wide for b in range(1, lay.lo)]
        elif k >= lay.wide and h == 1:
            onward = list(range(1, lay.wide))
        else:
            onward = []
        for step in onward:
            total = k + step
            there = slot(out, total, sources[k], core)
            copy = remote(
                block.at[halves[h]], there.at[halves[h]], pass_send.at[total, h], recv.at[total, h], peers[step]
            )
            copy.start()
            pushes.append(copy)
    for k in straight + bent:
        if k in bent:
            for h in range(2):
                arrived(k, h)
        block = slot(out, k, sources[k], core)
        share = remote(block, block, core_send.at[k], core_recv.at[k], partner)
        share.start()
        shares.append(share)
    keep.wait()
    for copy in pushes:
        copy.wait_send()
    for share in shares:
        share.wait()


def gather_group(lay, value, out_shape, slot, collective_id):
    n = lay.chips
    dma = pltpu.SemaphoreType.DMA
    return pl.pallas_call(
        partial(gather_group_kernel, lay, slot),
        out_shape=jax.ShapeDtypeStruct(out_shape, value.dtype),
        in_specs=[pl.BlockSpec(memory_space=pl.ANY)],
        out_specs=pl.BlockSpec(memory_space=pl.ANY),
        scratch_shapes=[dma, dma((n, 2)), dma((n, 2)), dma((n, 2)), dma((n,)), dma((n,))],
        compiler_params=pltpu.CompilerParams(
            collective_id=collective_id, has_side_effects=True, vmem_limit_bytes=VMEM_LIMIT
        ),
    )(value)


def weights_in_kernel(
    lay, reach, tokens, qkv, out_t, gains, pairs, lows, attn_out, ffn_out, earlier_out,
    pack, hops_land, attn_land, own, stack, land, keep_sem, hop_send, hop_recv, low_send, low_recv, attn_send, attn_recv, send, recv, chain_send, chain_recv,
):
    n, hi, lo = lay.dp, lay.hi, lay.lo
    dp = lax.axis_index("dp")
    ctx = lax.axis_index("ctx")
    high = ctx // lo
    cols = lows.shape[0]
    per = lows.shape[1] // n
    padded = ffn_out.shape[0] // 3
    targets = [lax.rem(dp + k, n) for k in range(n)]
    right, left = (dp, ctx + lo), (dp, ctx - lo)
    has_right, has_left = high < hi - 1, high > 0
    low = lax.rem(ctx, lo)
    low_peers = [(dp, high * lo + other) for other in range(lo)]
    hops = hops_land.shape[0] - 1
    barrier = pltpu.get_barrier_semaphore()
    for target in targets[1:]:
        pl.semaphore_signal(barrier, inc=1, device_id=(target, ctx), device_id_type=MESH)
    for other in range(lo):
        if lo > 1:
            @pl.when(low != other)
            def _():
                pl.semaphore_signal(barrier, inc=1, device_id=low_peers[other], device_id_type=MESH)
    for there, device in ((has_right, right), (has_left, left)):
        @pl.when(there)
        def _():
            pl.semaphore_signal(barrier, inc=1, device_id=device, device_id_type=MESH)
    sides = jnp.where(has_right, 1, 0) + jnp.where(has_left, 1, 0)
    pl.semaphore_wait(barrier, n - 1 + sides + lo - 1)

    rows = pack.shape[1]
    last = jnp.concatenate([gains[...], jnp.zeros((1, cols - gains.shape[1]), jnp.float32)], axis=1)
    used = qkv.shape[0] + out_t.shape[1]
    first_row = lax.broadcasted_iota(jnp.int32, (n * rows - used, cols), 0) == 0
    block = jnp.concatenate(
        [qkv[...], out_t[...].T, jnp.where(first_row, last, 0.0)], axis=0
    ).astype(jnp.bfloat16)
    pack[...] = block.reshape(n, rows, cols)
    attn_pushes = []
    for k in range(1, n):
        push = remote(
            pack.at[targets[k]], attn_land.at[dp], attn_send.at[k], attn_recv.at[k], (targets[k], ctx)
        )
        push.start()
        attn_pushes.append(push)
    attn_land[dp] = pack[dp]
    wide = land.shape[3]

    def feed_forward_push(q):
        return remote(stack.at[:, q], land.at[:, dp], send.at[q], recv.at[dp], (q, ctx))

    def feed_forward_units(q):
        for i, (ref, first, stride) in enumerate(
            ((pairs, 2 * per * q, 2), (pairs, 2 * per * q + 1, 2), (lows, per * q, 1))
        ):
            begin = first // 128 * 128
            end = min(ref.shape[1], -(-(first + stride * (per - 1) + 1) // 128) * 128)
            column = lax.broadcasted_iota(jnp.int32, (end - begin, wide), 0) + (begin - first)
            unit = lax.broadcasted_iota(jnp.int32, (end - begin, wide), 1)
            pick = jnp.where((column == stride * unit) & (unit < per), 1.0, 0.0).astype(jnp.bfloat16)
            picked = dot_nn(ref[:, begin:end].astype(jnp.bfloat16), pick).astype(jnp.bfloat16)
            stack[i, q] = picked

        @pl.when(dp != q)
        def _():
            feed_forward_push(q).start()

    def chain(source, where, side, step):
        return remote(
            source, attn_out.at[where], chain_send.at[side, step], chain_recv.at[side, step],
            right if side == 0 else left,
        )

    def pass_on(step):
        if step == 0:
            for side, there in ((0, has_right), (1, has_left)):
                @pl.when(there)
                def _():
                    chain(own, high, side, 0).start()
            return
        for side, here, there in (
            (0, high - step >= 0, has_right),
            (1, high + step < hi, has_left),
        ):
            where = high - step if side == 0 else high + step

            @pl.when(here)
            def _():
                chain(own, where, side, step - 1).wait_recv()
                if step < hi - 1:
                    @pl.when(there)
                    def _():
                        chain(attn_out.at[where], where, side, step).start()

    def finish(step):
        for side, here, there in (
            (0, high - step >= 0, has_right),
            (1, high + step < hi, has_left),
        ):
            @pl.when(here & there)
            def _():
                chain(own, high, side, step).wait_send()

    parts = 2
    span = tokens.shape[0] // parts

    def part_of(ref, part):
        return ref.at[pl.ds(part * span, span)]

    def hop(h, part):
        source = tokens if h == 0 else hops_land.at[h]
        return remote(
            part_of(source, part), part_of(hops_land.at[h + 1], part), hop_send.at[h, part], hop_recv.at[h, part], right
        )

    def wanted(h, source, target):
        distance = h * lo + target - source
        return (distance >= 1) & (distance <= reach) & (high >= h)

    def aside(h, source, target, device, part):
        block = tokens if h == 0 else hops_land.at[h]
        return remote(
            part_of(block, part), part_of(earlier_out.at[reach - (h * lo + target - source)], part),
            low_send.at[h, target, part], low_recv.at[h, source, part], device,
        )

    def pass_tokens(h, part):
        if h:
            @pl.when(high >= h)
            def _():
                hop(h - 1, part).wait_recv()
        if h < hops:
            @pl.when((high >= h) & has_right)
            def _():
                hop(h, part).start()
        for other in range(lo):
            if lo > 1:
                @pl.when((low != other) & wanted(h, low, other))
                def _():
                    aside(h, low, other, low_peers[other], part).start()
        if h and h * lo <= reach:
            @pl.when(high >= h)
            def _():
                block = pl.ds(part * span, span)
                earlier_out[reach - h * lo, block] = hops_land[h, block]

    def finish_tokens(h, part):
        if h < hops:
            @pl.when((high >= h) & has_right)
            def _():
                hop(h, part).wait_send()
        for other in range(lo):
            if lo > 1:
                @pl.when((low != other) & wanted(h, other, low))
                def _():
                    aside(h, other, low, low_peers[other], part).wait_recv()

                @pl.when((low != other) & wanted(h, low, other))
                def _():
                    aside(h, low, other, low_peers[other], part).wait_send()

    for part in range(parts):
        pass_tokens(0, part)
    for d in range(1, reach + 1):
        @pl.when(ctx < d)
        def _():
            earlier_out[reach - d] = jnp.zeros(earlier_out.shape[1:], earlier_out.dtype)
    feed_forward_units(0)
    for push in attn_pushes:
        push.wait_recv()
    for q in range(n):
        own[:, q * cols : (q + 1) * cols] = attn_land[q]
    keep = pltpu.make_async_copy(own, attn_out.at[high], keep_sem)
    keep.start()
    pass_on(0)
    events = [partial(feed_forward_units, 1)]
    for step in range(1, max(hi, hops + 1)):
        if step <= hops:
            events += [partial(pass_tokens, step, part) for part in range(parts)]
        if step == 1:
            events.insert(2, partial(feed_forward_units, 2))
        if step < hi:
            events.append(partial(pass_on, step))
        if step == 1:
            events += [partial(feed_forward_units, q) for q in range(3, n)]
    for event in events:
        event()
    for i in range(3):
        land[i, dp] = stack[i, dp]
    for q in range(n):
        @pl.when(dp != q)
        def _():
            remote(stack.at[:, q], land.at[:, q], send.at[q], recv.at[q], (q, ctx)).wait_recv()
    for i in range(3):
        whole = land[i].reshape(n * cols, wide)
        ffn_out[i * padded : (i + 1) * padded] = whole.T[:padded]
    keep.wait()
    for step in range(hi - 1):
        finish(step)
    for h in range(hops + 1):
        for part in range(parts):
            finish_tokens(h, part)
    for push in attn_pushes:
        push.wait_send()
    for q in range(n):
        @pl.when(dp != q)
        def _():
            feed_forward_push(q).wait_send()


def weights_in(lay, reach, tokens, qkv, out_t, gains, pairs, lows, collective_id):
    n = lay.dp
    cols, per = lows.shape[0], lows.shape[1] // n
    block = 16 * n
    rows = -(-(qkv.shape[0] + out_t.shape[1] + 1) // block) * 16
    padded = -(-per // 32) * 32
    vmem = pl.BlockSpec(memory_space=pltpu.VMEM)
    dma = pltpu.SemaphoreType.DMA
    hops = min(lay.hi - 1, (reach + lay.lo - 1) // lay.lo)
    scratch = [
        pltpu.VMEM((n, rows, cols), jnp.bfloat16),
        pltpu.VMEM((hops + 1,) + tokens.shape, tokens.dtype),
        pltpu.VMEM((n, rows, cols), jnp.bfloat16),
        pltpu.VMEM((rows, n * cols), jnp.bfloat16),
        pltpu.VMEM((3, n, cols, -(-padded // 128) * 128), jnp.bfloat16),
        pltpu.VMEM((3, n, cols, -(-padded // 128) * 128), jnp.bfloat16),
        dma,
    ]
    for shape in ((hops + 1, 2), (hops + 1, lay.lo, 2), (n,), (n,), (2, lay.hi)):
        scratch += [dma(shape), dma(shape)]
    return pl.pallas_call(
        partial(weights_in_kernel, lay, reach),
        out_shape=(
            jax.ShapeDtypeStruct((lay.hi, rows, n * cols), jnp.bfloat16),
            jax.ShapeDtypeStruct((3 * padded, n * cols), jnp.bfloat16),
            jax.ShapeDtypeStruct((reach,) + tokens.shape, tokens.dtype),
        ),
        in_specs=[vmem] * 6,
        out_specs=(pl.BlockSpec(memory_space=pl.ANY), vmem, vmem),
        scratch_shapes=scratch,
        compiler_params=pltpu.CompilerParams(
            collective_id=collective_id, has_side_effects=True, vmem_limit_bytes=VMEM_LIMIT
        ),
    )(tokens, qkv, out_t, gains, pairs, lows)


def later_kernel(
    lay, reach, pieces, parts, early, out, group_out, early_out, low_land, moved, arrived, early_stack,
    early_send, early_recv, chain_send, chain_recv, low_send, low_recv, *scratch
):
    group = GroupSum(lay, parts, group_out, *scratch)
    groups = [group]
    hi, lo = lay.hi, lay.lo
    dp = lax.axis_index("dp")
    ctx = lax.axis_index("ctx")
    high, low = ctx // lo, lax.rem(ctx, lo)
    hops = min(hi - 1, (reach + lo - 1) // lo)
    right, left = (dp, ctx + lo), (dp, ctx - lo)
    has_right, has_left = high < hi - 1, high > 0
    low_peers = [(dp, high * lo + other) for other in range(lo)]
    barrier = pltpu.get_barrier_semaphore()
    n = lay.dp
    dp_peers = [(lax.rem(dp + k, n), ctx) for k in range(1, n)]
    for device in group.low_peers[1:] + dp_peers:
        pl.semaphore_signal(barrier, inc=1, device_id=device, device_id_type=MESH)
    for there, device in [(has_right, right), (has_left, left)]:
        @pl.when(there)
        def _():
            pl.semaphore_signal(barrier, inc=1, device_id=device, device_id_type=MESH)
    sides = jnp.where(has_right, 1, 0) + jnp.where(has_left, 1, 0)
    pl.semaphore_wait(barrier, sides + lo - 1 + n - 1)

    def wanted(h, owner, reader):
        distance = h * lo + reader - owner
        return (distance >= 1) & (distance <= reach) & (high >= h)

    span = out.shape[0] // 2

    def part_of(ref, part):
        return ref.at[pl.ds(part * span, span)]

    def across(h, other, part):
        return remote(
            part_of(pieces.at[reach - (h * lo + low - other)], part), part_of(low_land.at[h, low], part),
            low_send.at[h, other, part], low_recv.at[h, low, part], low_peers[other],
        )

    def from_low(h, other, part):
        return remote(
            part_of(pieces.at[0], part), part_of(low_land.at[h, other], part), low_send.at[h, other, part],
            low_recv.at[h, other, part], low_peers[other],
        )

    def hop(h, part):
        return remote(
            part_of(moved.at[h], part), part_of(arrived.at[h - 1], part), chain_send.at[h, part],
            chain_recv.at[h - 1, part], left,
        )

    def pass_on(h, part):
        block = pl.ds(part * span, span)
        out[block] = jnp.zeros((span,) + out.shape[1:], out.dtype)
        if h and h * lo <= reach:
            out[block] += pieces[reach - h * lo, block].astype(jnp.float32)
        for other in range(lo):
            if lo > 1:
                @pl.when((low != other) & wanted(h, low, other))
                def _():
                    from_low(h, other, part).wait_recv()
                    out[block] += low_land[h, other, block].astype(jnp.float32)
        if h < hops:
            @pl.when(has_right & (high >= h))
            def _():
                hop(h + 1, part).wait_recv()
                out[block] += arrived[h, block].astype(jnp.float32)
        if h:
            @pl.when(high >= h)
            def _():
                moved[h, block] = out[block].astype(moved.dtype)
                hop(h, part).start()

    for h in range(hops, -1, -1):
        for part in range(2):
            for other in range(lo):
                if lo > 1:
                    @pl.when((low != other) & wanted(h, other, low))
                    def _():
                        across(h, other, part).start()
    for each in groups:
        each.start()
    cols, wide = early_stack.shape[1:]
    whole = early[...]
    if wide > early.shape[0]:
        blank = jnp.zeros((wide - early.shape[0], n * cols), early.dtype)
        whole = jnp.concatenate([whole, blank], axis=0)
    early_stack[...] = whole.T.reshape(n, cols, wide)
    early_pushes = []
    for k in range(1, n):
        push = remote(
            early_stack.at[lax.rem(dp + k, n)], early_out.at[dp], early_send.at[k], early_recv.at[k], dp_peers[k - 1]
        )
        push.start()
        early_pushes.append(push)
    early_out[dp] = early_stack[dp]
    stages = groups[0].stages()
    bounds = [0, 1] + [1 + (len(stages) - 1) * (i + 1) // hops for i in range(hops)]
    for h in range(hops, -1, -1):
        turn = hops - h
        for calls in stages[bounds[turn] : bounds[turn + 1]]:
            for call in calls:
                call()
        for part in range(2):
            pass_on(h, part)
    for h in range(hops + 1):
        for part in range(2):
            if h:
                @pl.when(high >= h)
                def _():
                    hop(h, part).wait_send()
            for other in range(lo):
                if lo > 1:
                    @pl.when((low != other) & wanted(h, other, low))
                    def _():
                        across(h, other, part).wait_send()
    for each in groups:
        each.finish()
    for push in early_pushes:
        push.wait()


def later_sum(lay, reach, pieces, parts, early, collective_id):
    n = lay.dp
    early_shape = (n, early.shape[1] // n, -(-early.shape[0] // 128) * 128)
    hops = min(lay.hi - 1, (reach + lay.lo - 1) // lay.lo)
    shape = pieces.shape[1:]
    vmem = pl.BlockSpec(memory_space=pltpu.VMEM)
    dma = pltpu.SemaphoreType.DMA
    return pl.pallas_call(
        partial(later_kernel, lay, reach),
        out_shape=(
            jax.ShapeDtypeStruct(shape, jnp.float32),
            jax.ShapeDtypeStruct((lay.hi, parts.shape[2], D), parts.dtype),
            jax.ShapeDtypeStruct(early_shape, early.dtype),
        ),
        in_specs=[vmem] * 3,
        out_specs=(vmem,) * 3,
        scratch_shapes=[
            pltpu.VMEM((hops + 1, lay.lo) + shape, pieces.dtype),
            pltpu.VMEM((hops + 1,) + shape, pieces.dtype),
            pltpu.VMEM((hops + 1,) + shape, pieces.dtype),
        ]
        + [pltpu.VMEM(early_shape, early.dtype), dma((n,)), dma((n,))]
        + [dma((hops + 1, 2))] * 2
        + [dma((hops + 1, lay.lo, 2))] * 2
        + GroupSum.scratch(lay, parts.shape[2]),
        compiler_params=pltpu.CompilerParams(
            collective_id=collective_id, has_side_effects=True, vmem_limit_bytes=VMEM_LIMIT
        ),
    )(pieces, parts, early)


def flip(index, bit):
    return index + bit * (1 - 2 * lax.rem(index // bit, 2))


class GroupSum:
    @staticmethod
    def scratch(lay, rows):
        dma = pltpu.SemaphoreType.DMA
        blocks = (lay.hi, lay.lo, lay.wide)
        data = [pltpu.VMEM(blocks + (rows, D), jnp.bfloat16)] * 3
        return data + [dma(blocks)] * 6

    def __init__(self, lay, parts, out, land, sums, second_land, core_send, core_recv, send, recv, second_send, second_recv):
        self.lay, self.parts, self.out = lay, parts, out
        self.land, self.sums, self.second_land = land, sums, second_land
        self.core_sems, self.sems, self.second_sems = (core_send, core_recv), (send, recv), (second_send, second_recv)
        dp = lax.axis_index("dp")
        ctx = lax.axis_index("ctx")
        hi, lo, wide = lay.hi, lay.lo, lay.wide
        high, self.low = ctx // lo, lax.rem(ctx, lo)
        self.across, self.core = dp // 2, lax.rem(dp, 2)
        self.partner = (self.across * 2 + 1 - self.core, ctx)
        self.low_peers = [(dp, high * lo + lax.rem(self.low + k, lo)) for k in range(lo)]
        self.wide_peers = [(lax.rem(self.across + k, wide) * 2 + self.core, ctx) for k in range(wide)]
        self.peers = self.low_peers[1:] + self.wide_peers[1:] + [self.partner]
        self.sends = []

    def at(self, h, a, b):
        lay = self.lay
        return h * lay.lo + lax.rem(self.low + a, lay.lo), lax.rem(self.across + b, lay.wide) * 2

    def turned(self, h):
        return h >= self.lay.hi // 2 and self.lay.lo > 1

    def core_copy(self, h, a, b):
        ctx, there = self.at(h, a, b)
        return remote(
            self.parts.at[ctx, there + 1 - self.core], self.land.at[h, a, b], self.core_sems[0].at[h, a, b],
            self.core_sems[1].at[h, a, b], self.partner,
        )

    def blocks(self):
        lay = self.lay
        return [
            (a, b) for a in list(range(1, lay.lo)) + [0] for b in list(range(1, lay.wide)) + [0]
        ]

    def start(self):
        for h in range(self.lay.hi):
            for a, b in self.blocks():
                self.core_copy(h, a, b).start()

    def first_copy(self, h, a, b):
        where = (h, a, b)
        return remote(
            self.sums.at[where], self.land_first(h, a, b), self.sems[0].at[where], self.sems[1].at[where],
            self.low_peers[a] if self.turned(h) else self.wide_peers[b],
        )

    def land_first(self, h, a, b):
        return self.second_land.at[h, a, b]

    def second_copy(self, h, a, b):
        where = (h, a, b)
        return remote(
            self.sums.at[where], self.second_land.at[where], self.second_sems[0].at[where],
            self.second_sems[1].at[where], self.wide_peers[b] if self.turned(h) else self.low_peers[a],
        )

    def moves_first(self, h, a, b):
        return a > 0 if self.turned(h) else b > 0

    def sum_cores(self, h):
        for a, b in self.blocks():
            self.core_copy(h, a, b).wait_recv()
            ctx, there = self.at(h, a, b)
            total = self.parts[ctx, there + self.core].astype(jnp.float32) + self.land[h, a, b].astype(jnp.float32)
            self.sums[h, a, b] = total.astype(jnp.bfloat16)
            if self.moves_first(h, a, b):
                self.first_copy(h, a, b).start()

    def sum_first(self, h):
        lay = self.lay
        for a, b in self.blocks():
            if self.moves_first(h, a, b):
                continue
            total = self.sums[h, a, b].astype(jnp.float32)
            others = [(k, b) for k in range(1, lay.lo)] if self.turned(h) else [(a, k) for k in range(1, lay.wide)]
            for other in others:
                self.first_copy(h, *other).wait_recv()
                total = total + self.second_land[(h,) + other].astype(jnp.float32)
            self.sums[h, a, b] = total.astype(jnp.bfloat16)
            if a or b:
                self.second_copy(h, a, b).start()

    def sum_second(self, h):
        lay = self.lay
        total = self.sums[h, 0, 0].astype(jnp.float32)
        others = [(0, k) for k in range(1, lay.wide)] if self.turned(h) else [(k, 0) for k in range(1, lay.lo)]
        for other in others:
            self.second_copy(h, *other).wait_recv()
            total = total + self.second_land[(h,) + other].astype(jnp.float32)
        self.out[h] = total.astype(jnp.bfloat16)

    def order(self):
        half = self.lay.hi // 2
        pairs = [h for pair in zip(range(half), range(half, 2 * half)) for h in pair]
        return pairs + list(range(2 * half, self.lay.hi))

    def stages(self):
        order = self.order()
        stages = []
        for i in range(len(order) + 4):
            calls = []
            if i < len(order):
                calls.append(partial(self.sum_cores, order[i]))
            if 2 <= i < len(order) + 2:
                calls.append(partial(self.sum_first, order[i - 2]))
            if 4 <= i:
                calls.append(partial(self.sum_second, order[i - 4]))
            stages.append(calls)
        return stages

    def finish(self):
        for h in range(self.lay.hi):
            for a, b in self.blocks():
                self.core_copy(h, a, b).wait_send()
                if self.moves_first(h, a, b):
                    self.first_copy(h, a, b).wait_send()
                elif a or b:
                    self.second_copy(h, a, b).wait_send()


def near_bits(lay, dp, ctx):
    peers = [(flip(dp, 1 << i), ctx) for i in range((lay.dp - 1).bit_length())]
    return peers + [(dp, flip(ctx, 1 << i)) for i in range((lay.lo - 1).bit_length())]


def far_bits(lay, dp, ctx):
    return [
        (dp, flip(ctx, 1 << i)) for i in range((lay.lo - 1).bit_length(), (lay.ctx - 1).bit_length())
    ]


def sum_group_kernel(lay, parts, gains, out, gains_out, gains_sum, gains_land, gains_send, gains_recv, *scratch):
    dp = lax.axis_index("dp")
    ctx = lax.axis_index("ctx")
    group = GroupSum(lay, parts, out, *scratch)
    gain_peers = near_bits(lay, dp, ctx)
    greet(group.peers + gain_peers)

    def gains_copy(i):
        return remote(gains_sum.at[i], gains_land.at[i], gains_send.at[i], gains_recv.at[i], gain_peers[i])

    def gains_step(i):
        if i > len(gain_peers):
            return
        if i == 0:
            gains_sum[0] = gains[...]
        else:
            gains_copy(i - 1).wait_recv()
            gains_sum[i] = gains_sum[i - 1] + gains_land[i - 1]
        if i < len(gain_peers):
            gains_copy(i).start()
        else:
            gains_out[...] = gains_sum[i]

    group.start()
    stages = group.stages()
    for i, calls in enumerate(stages):
        gains_step(i)
        for call in calls:
            call()
    for i in range(len(stages), len(gain_peers) + 1):
        gains_step(i)
    group.finish()
    for i in range(len(gain_peers)):
        gains_copy(i).wait_send()


def sum_group(lay, parts, gains, collective_id):
    rows = parts.shape[2]
    vmem = pl.BlockSpec(memory_space=pltpu.VMEM)
    dma = pltpu.SemaphoreType.DMA
    count = len(near_bits(lay, 0, 0))
    return pl.pallas_call(
        partial(sum_group_kernel, lay),
        out_shape=(
            jax.ShapeDtypeStruct((lay.hi, rows, D), jnp.bfloat16),
            jax.ShapeDtypeStruct(gains.shape, jnp.float32),
        ),
        in_specs=[vmem] * 2,
        out_specs=(vmem,) * 2,
        scratch_shapes=[
            pltpu.VMEM((count + 1,) + gains.shape, jnp.float32),
            pltpu.VMEM((count,) + gains.shape, jnp.float32),
            dma((count,)),
            dma((count,)),
        ]
        + GroupSum.scratch(lay, rows),
        compiler_params=pltpu.CompilerParams(
            collective_id=collective_id, has_side_effects=True, vmem_limit_bytes=VMEM_LIMIT
        ),
    )(parts, gains)


def grads_out_kernel(lay, rows, early, plane_qkv, plane_out, gains, pairs_out, lows_out, qkv_out, out_t, gains_out,
                     gains_sum, gains_land, gains_send, gains_recv, attn, stack, land, low_stack, low_land, hi_land, last, last_land,
                     send, recv, hi_send, hi_recv, last_send, last_recv):
    n, hi, lo = lay.dp, lay.hi, lay.lo
    dp = lax.axis_index("dp")
    ctx = lax.axis_index("ctx")
    high, low = ctx // lo, lax.rem(ctx, lo)
    cols = lows_out.shape[0]
    per = lows_out.shape[1] // n
    half = rows.shape[0] // 5
    padded = 2 * half
    wide = land.shape[3]
    attn_rows = attn.shape[1]
    hi_peers = [(dp, lax.rem(high + k, hi) * lo + low) for k in range(1, hi)]
    gain_peers = far_bits(lay, dp, ctx)
    greet([(lax.rem(dp + k, n), ctx) for k in range(1, n)] + hi_peers + gain_peers)

    def gains_copy(i):
        return remote(gains_sum.at[i], gains_land.at[i], gains_send.at[i], gains_recv.at[i], gain_peers[i])

    gains_sum[0] = gains[...]
    gains_copy(0).start()
    attn[:, : plane_qkv.shape[1]] = plane_qkv[...]
    attn[:, plane_qkv.shape[1] :] = plane_out[...]
    hi_pushes = []
    for k in range(1, hi):
        push = remote(
            attn.at[lax.rem(high + k, hi)], hi_land.at[k - 1], hi_send.at[k], hi_recv.at[k], hi_peers[k - 1]
        )
        push.start()
        hi_pushes.append(push)
    pushes = []
    for i in range(3):
        held, arriving = (stack.at[i], land.at[i]) if i < 2 else (low_stack, low_land)
        lanes = held.shape[2]
        whole = rows[i * padded : min((i + 1) * padded, rows.shape[0])]
        if lanes > whole.shape[0]:
            blank = jnp.zeros((lanes - whole.shape[0], n * cols), jnp.bfloat16)
            whole = jnp.concatenate([whole, blank], axis=0)
        held[...] = whole.T.reshape(n, cols, lanes)
        for k in range(1, n):
            target = lax.rem(dp + k, n)
            push = remote(held.at[target], arriving.at[dp], send.at[i, k], recv.at[i, k], (target, ctx))
            push.start()
            pushes.append(push)
        arriving[dp] = held[dp]

    def gains_step(i):
        gains_copy(i).wait_recv()
        gains_sum[i + 1] = gains_sum[i] + gains_land[i]
        if i + 1 < len(gain_peers):
            gains_copy(i + 1).start()

    gains_step(0)
    total = attn[high].astype(jnp.float32)
    for k, push in enumerate(hi_pushes):
        push.wait_recv()
        total = total + hi_land[k].astype(jnp.float32)
    for q in range(n):
        last[q] = total[:, q * cols : (q + 1) * cols].astype(jnp.bfloat16)
    last_pushes = []
    for k in range(1, n):
        target = lax.rem(dp + k, n)
        push = remote(last.at[target], last_land.at[dp], last_send.at[k], last_recv.at[k], (target, ctx))
        push.start()
        last_pushes.append(push)
    last_land[dp] = last[dp]

    unit = lax.broadcasted_iota(jnp.int32, (wide, 2 * per), 0)
    column = lax.broadcasted_iota(jnp.int32, (wide, 2 * per), 1)
    spread = [jnp.where(column == 2 * unit + i, 1.0, 0.0).astype(jnp.bfloat16) for i in range(2)]
    for push in pushes:
        push.wait_recv()
    for q in range(n):
        turns = dot_nn(land[0, q], spread[0]) + dot_nn(land[1, q], spread[1])
        pairs_out[:, 2 * per * q : 2 * per * (q + 1)] = turns.astype(jnp.bfloat16)
        lows_out[:, per * q : per * q + half] = low_land[q, :, :half]
        lows_out[:, per * q + half : per * (q + 1)] = early[q, :, : per - half]
    for i in range(1, len(gain_peers)):
        gains_step(i)
    gains_out[...] = gains_sum[len(gain_peers), pl.ds(dp * lay.ctx + ctx, 1)]
    for push in last_pushes:
        push.wait_recv()
    out_rows = out_t.shape[1]
    out_part, qkv_part = plane_out.shape[1], plane_qkv.shape[1]
    qkv_out[...] = last_land[:, :qkv_part].reshape(n * qkv_part, cols)[: qkv_out.shape[0]].astype(jnp.float32)
    out_t[...] = last_land[:, qkv_part:].reshape(n * out_part, cols)[:out_rows].astype(jnp.float32).T
    for push in hi_pushes + pushes + last_pushes:
        push.wait_send()
    for i in range(len(gain_peers)):
        gains_copy(i).wait_send()


def grads_out(lay, rows, early, plane_qkv, plane_out, gains, per, qkv_rows, out_rows, collective_id):
    count = len(far_bits(lay, 0, 0))
    padded = 2 * rows.shape[0] // 5
    n, cols = lay.dp, rows.shape[1] // lay.dp
    attn_rows = plane_qkv.shape[1] + plane_out.shape[1]
    vmem = pl.BlockSpec(memory_space=pltpu.VMEM)
    dma = pltpu.SemaphoreType.DMA
    return pl.pallas_call(
        partial(grads_out_kernel, lay),
        out_shape=(
            jax.ShapeDtypeStruct((cols, n * 2 * per), jnp.bfloat16),
            jax.ShapeDtypeStruct((cols, n * per), jnp.bfloat16),
            jax.ShapeDtypeStruct((qkv_rows, cols), jnp.float32),
            jax.ShapeDtypeStruct((cols, out_rows), jnp.float32),
            jax.ShapeDtypeStruct((1, gains.shape[1]), jnp.float32),
        ),
        in_specs=[vmem] * 5,
        out_specs=(vmem,) * 5,
        scratch_shapes=[
            pltpu.VMEM((count + 1,) + gains.shape, jnp.float32),
            pltpu.VMEM((count,) + gains.shape, jnp.float32),
            dma((count,)),
            dma((count,)),
            pltpu.VMEM((lay.hi, attn_rows, D), jnp.bfloat16),
            pltpu.VMEM((2, n, cols, -(-padded // 128) * 128), jnp.bfloat16),
            pltpu.VMEM((2, n, cols, -(-padded // 128) * 128), jnp.bfloat16),
            pltpu.VMEM(early.shape, jnp.bfloat16),
            pltpu.VMEM(early.shape, jnp.bfloat16),
            pltpu.VMEM((max(1, lay.hi - 1), attn_rows, D), jnp.bfloat16),
            pltpu.VMEM((n, attn_rows, cols), jnp.bfloat16),
            pltpu.VMEM((n, attn_rows, cols), jnp.bfloat16),
        ]
        + [dma((3, n))] * 2
        + [dma((lay.hi,))] * 2
        + [dma((n,))] * 2,
        compiler_params=pltpu.CompilerParams(
            collective_id=collective_id, has_side_effects=True, vmem_limit_bytes=VMEM_LIMIT
        ),
    )(rows, early, plane_qkv, plane_out, gains)


def in_tiles(total, size, body, begin=0):
    whole = total // size

    def step(i, carry):
        body(pl.multiple_of(begin + i * size, math.gcd(begin, size)), size)
        return carry

    if whole:
        lax.fori_loop(0, whole, step, 0)
    if total % size:
        body(begin + whole * size, total % size)


def dot_nt(left, right):
    return lax.dot_general(left, right, (((1,), (1,)), ((), ())), preferred_element_type=jnp.float32)


def dot_nn(left, right):
    return lax.dot_general(left, right, (((1,), (0,)), ((), ())), preferred_element_type=jnp.float32)


ROOT = math.sqrt(2.0 / math.pi)


def feed_forward_kernel(
    lay, mid_in, weights, mixed, cotangent, valid, gain, result, grad_mid, grad_gain, grad_weights, early_sum,
    mid, mid_sem, late, late_sem, early, early_land, hi_send, hi_recv, w_gate, w_up, w_down, gate_t, up_t, act, slope, hidden, hidden_t, grads, parts, core_land, sums, via, landed,
    total, dy, weight_sem, core_send, core_recv, share_send, share_recv,
    send, recv, via_send, via_recv, dy_send, dy_recv, dy_pass,
):
    chip, core, high = lay.place()
    n, wide = lay.chips, lay.wide
    tokens = mixed.shape[0]
    units = w_gate.shape[0]
    hi = lay.hi
    padded = units // hi
    part_rows = padded // 2
    loads = [
        pltpu.make_async_copy(
            weights.at[h, pl.ds(i * padded + part * part_rows, part_rows)],
            held.at[pl.ds((part * hi + h) * part_rows, part_rows)],
            weight_sem.at[i, part, h],
        )
        for i, held in enumerate((w_gate, w_up, w_down))
        for part in range(2)
        for h in range(hi)
    ]
    mid_loads = [
        pltpu.make_async_copy(mid_in.at[p], mid.at[p], mid_sem.at[p]) for p in range(lay.chips)
    ]
    gates = len(loads) * 2 // 3
    for load in mid_loads[:1] + loads[:gates] + mid_loads[1:] + loads[gates:]:
        load.start()
    peers = [lay.device(lay.offset(chip, k), core, high) for k in range(n)]
    owners = [lay.device(lay.offset(chip, k, -1), core, high) for k in range(n)]
    partner = lay.device(chip, 1 - core, high)
    mine = pl.ds(pl.multiple_of(core * tokens, tokens), tokens)
    theirs = pl.ds(pl.multiple_of((1 - core) * tokens, tokens), tokens)
    half = tokens // 2
    halves = (pl.ds(0, half), pl.ds(half, half))
    straight, bent = lay.straight(), lay.bent()
    place = [lay.position(k) for k in range(n)]
    hi_peers = [lay.device(chip, core, lax.rem(high + k, hi)) for k in range(hi)]
    greet(peers[1:] + [partner] + hi_peers[1:])

    def to_partner(phase, k):
        return remote(
            parts.at[place[k], theirs], core_land.at[k], core_send.at[phase, k], core_recv.at[phase, k], partner
        )

    def to_owner(phase, k, h):
        return remote(
            sums.at[k - 1, halves[h]], landed.at[place[k] - len(bent), halves[h]], send.at[phase, k, h],
            recv.at[phase, k, h], owners[k],
        )

    def to_neighbour(phase, k, h):
        step = k % wide if h == 0 else k // wide * wide
        return remote(
            sums.at[k - 1, halves[h]], via.at[place[k], halves[h]], via_send.at[phase, k, h], via_recv.at[phase, k, h],
            owners[step],
        )

    def added(k):
        if k < wide:
            return 1, [k + b * wide for b in range(1, lay.lo)]
        return 0, [k + step for step in range(1, wide)]

    def add_core(phase, k):
        to_partner(phase, k).wait_recv()

        def chunk(first, rows):
            span = pl.ds(first, rows)
            here = pl.ds(pl.multiple_of(core * tokens + first, rows), rows)
            both = parts[place[k], here].astype(jnp.float32) + core_land[k, span].astype(jnp.float32)
            if k:
                sums[k - 1, span] = both.astype(jnp.bfloat16)
            else:
                total[span] = both

        in_tiles(tokens, 32, chunk)
        if k in bent:
            for h in range(2):
                to_neighbour(phase, k, h).start()
        elif k:
            h, others = added(k)
            to_owner(phase, k, 1 - h).start()
            if not others:
                to_owner(phase, k, h).start()

    def add_neighbours(phase, k):
        h, others = added(k)
        if not others:
            return
        for other in others:
            to_neighbour(phase, other, h).wait_recv()

        def chunk(first, rows):
            span = pl.ds(first + h * half, rows)
            value = sums[k - 1, span].astype(jnp.float32)
            for other in others:
                value = value + via[place[other], span].astype(jnp.float32)
            sums[k - 1, span] = value.astype(jnp.bfloat16)

        in_tiles(half, 32, chunk)
        to_owner(phase, k, h).start()

    def add_owners(phase):
        for k in straight:
            for h in range(2):
                to_owner(phase, k, h).wait_recv()

        def chunk(first, rows):
            span = pl.ds(first, rows)
            value = total[span]
            for k in straight:
                value = value + landed[place[k] - len(bent), span].astype(jnp.float32)
            total[span] = value

        in_tiles(tokens, 32, chunk)

    def settle(phase):
        for k in range(n):
            to_partner(phase, k).wait_send()
            for h in range(2):
                if k in bent:
                    to_neighbour(phase, k, h).wait_send()
                elif k:
                    to_owner(phase, k, h).wait_send()

    rows_of = 2 * tokens

    def joined(ref, group, *index):
        value = ref[(pl.ds(*group),) + index]
        return value.reshape((group[1] * rows_of,) + value.shape[2:])

    def forward_units(group, begin, end):
        count = group[1]

        def tile(first, width):
            units_here = pl.ds(first, width)
            weights = jnp.concatenate([w_gate[units_here], w_up[units_here]], axis=0)
            both = dot_nt(joined(mid, group), weights)
            gate, up = both[:, :width], both[:, width:]
            square = gate * gate
            tanh = jnp.tanh(gate * (ROOT + (0.044715 * ROOT) * square))
            half_way = 0.5 + 0.5 * tanh
            active = gate * half_way
            slant = half_way + active * (1.0 - tanh) * (ROOT + (3.0 * 0.044715 * ROOT) * square)
            product = (active * up).astype(jnp.bfloat16)
            shape = (count, rows_of, width)
            act[pl.ds(*group), :, units_here] = active.astype(jnp.bfloat16).reshape(shape)
            slope[pl.ds(*group), :, units_here] = (slant * up).astype(jnp.bfloat16).reshape(shape)
            hidden[: count * rows_of, units_here] = product
            for c in range(count):
                hidden_t[group[0] + c, units_here] = product[c * rows_of : (c + 1) * rows_of].T

        in_tiles(end - begin, 128, tile, begin)

    def forward_down(group):
        count = group[1]

        def tile(first, width):
            lanes = pl.ds(first, width)
            value = dot_nn(hidden[: count * rows_of], w_down[:, lanes]).astype(jnp.bfloat16)
            parts[pl.ds(*group), :, lanes] = value.reshape(count, rows_of, width)

        in_tiles(D, 256, tile)

    def backward_units(group):
        count = group[1]

        def tile(first, width):
            units_here = pl.ds(first, width)
            grad = dot_nt(joined(dy, group), w_down[units_here])
            up_grad = (grad * joined(act, group, slice(None), units_here).astype(jnp.float32)).astype(jnp.bfloat16)
            gate_grad = (grad * joined(slope, group, slice(None), units_here).astype(jnp.float32)).astype(jnp.bfloat16)
            grads[0, : count * rows_of, units_here] = gate_grad
            grads[1, : count * rows_of, units_here] = up_grad
            for c in range(count):
                rows = slice(c * rows_of, (c + 1) * rows_of)
                gate_t[group[0] + c, units_here] = gate_grad[rows].T
                up_t[group[0] + c, units_here] = up_grad[rows].T

        in_tiles(units, 256, tile)

    def backward_in(group):
        count = group[1]

        def tile(first, width):
            lanes = pl.ds(first, width)
            both = dot_nn(grads[0, : count * rows_of], w_gate[:, lanes]) + dot_nn(
                grads[1, : count * rows_of], w_up[:, lanes]
            )
            parts[pl.ds(*group), :, lanes] = both.astype(jnp.bfloat16).reshape(count, rows_of, width)

        in_tiles(D, 256, tile)

    def product_over_tokens(left, begin, end, right, lanes):
        value = dot_nn(left[0, begin:end], right[0, :, lanes])
        for c in range(1, n):
            value = value + dot_nn(left[c, begin:end], right[c, :, lanes])
        return value.astype(jnp.bfloat16)

    far, near, here = (0, len(bent)), (len(bent), len(straight)), (n - 1, 1)
    most = hidden.shape[0] // rows_of

    def runs(group):
        return [(first, min(most, group[0] + group[1] - first)) for first in range(group[0], sum(group), most)]

    quarter = units // 512 * 128
    for load in mid_loads[:1] + loads[:gates]:
        load.wait()
    waiting = [mid_loads[1:], loads[gates:]]

    def arrive(which):
        while waiting[which]:
            waiting[which].pop(0).wait()

    for run in runs(far):
        if run[0] + run[1] > 1:
            arrive(0)
        forward_units(run, 0, units)
        arrive(1)
        forward_down(run)
    for k in bent:
        to_partner(0, k).start()
    arrive(0)
    for i, run in enumerate(runs(near)):
        forward_units(run, 0, 2 * quarter)
        if i == 0:
            for k in bent:
                add_core(0, k)
        forward_units(run, 2 * quarter, units)
        arrive(1)
        forward_down(run)
    for k in straight:
        to_partner(0, k).start()
    forward_units(here, 0, 2 * quarter)
    for k in straight:
        add_core(0, k)
    for k in straight:
        add_neighbours(0, k)
    forward_units(here, 2 * quarter, units)
    forward_down(here)
    to_partner(0, 0).start()
    add_core(0, 0)
    add_owners(0)

    grad_gain[...] = jnp.zeros_like(grad_gain)
    scale = 1.0 + gain[...]

    def finish(first, rows):
        span = pl.ds(first, rows)
        spot = pl.ds(pl.multiple_of(core * tokens + first, rows), rows)
        y = total[span]
        ok = valid[span]
        rate = lax.rsqrt(jnp.mean(y * y, axis=-1, keepdims=True) + EPS)
        unit = y * rate
        result[span] = ((mixed[span] + unit * scale) * ok).astype(jnp.bfloat16)
        upstream = cotangent[span].astype(jnp.float32) * ok
        down = upstream * unit
        for r in range(0, rows, 8):
            grad_gain[...] += down[r : r + 8]
        scaled = upstream * scale
        inner = jnp.mean(scaled * unit, axis=-1, keepdims=True)
        dy[n - 1, spot] = (rate * (scaled - unit * inner)).astype(jnp.bfloat16)

    in_tiles(tokens, 32, finish)

    def dy_half(k, h):
        return dy.at[place[k], pl.ds(pl.multiple_of(core * tokens + h * half, half), half)]

    def dy_push(k, h):
        return remote(dy_half(0, h), dy_half(k, h), dy_send.at[k, h], dy_recv.at[k, h], peers[k])

    def dy_onward(k, h, step):
        return remote(
            dy_half(k, h), dy_half(k + step, h), dy_pass.at[k + step, h], dy_recv.at[k + step, h], peers[step]
        )

    shares = [
        remote(dy.at[place[k], mine], dy.at[place[k], mine], share_send.at[k], share_recv.at[k], partner)
        for k in range(n)
    ]
    ordered = [(k, i if k < wide else 1 - i) for i in range(2) for k in straight]
    for k, h in ordered:
        dy_push(k, h).start()
    shares[0].start()
    settle(0)
    shares[0].wait_recv()
    backward_units(here)
    backward_in(here)
    to_partner(1, 0).start()
    onward = []
    for k, h in ordered:
        dy_push(k, h).wait_recv()
        if k < wide and h == 0:
            onward += [(k, h, b * wide) for b in range(1, lay.lo)]
        elif k >= wide and h == 1:
            onward += [(k, h, step) for step in range(1, wide)]
        for go in onward:
            if go[:2] == (k, h):
                dy_onward(*go).start()
    for k in straight:
        shares[k].start()
    add_core(1, 0)
    for k in straight:
        shares[k].wait_recv()
    for i, run in enumerate(runs(near)):
        backward_units(run)
        if i == 0:
            for k in bent:
                for h in range(2):
                    dy_push(k, h).wait_recv()
                shares[k].start()
        backward_in(run)
    for k in straight:
        to_partner(1, k).start()
    for k in bent:
        shares[k].wait_recv()
    split = hi * part_rows

    def early_grad(first, width):
        lanes = pl.ds(first, width)
        value = product_over_tokens(hidden_t, split, units, dy, lanes)
        for h in range(hi):
            early[h, :, lanes] = value[h * part_rows : (h + 1) * part_rows]

    in_tiles(D, 256, early_grad)
    hi_pushes = []
    for k in range(1, hi):
        push = remote(
            early.at[lax.rem(high + k, hi)], early_land.at[k - 1], hi_send.at[k], hi_recv.at[k], hi_peers[k]
        )
        push.start()
        hi_pushes.append(push)
    for i, run in enumerate(runs(far)):
        backward_units(run)
        if i == 0:
            for k in straight:
                add_core(1, k)
        backward_in(run)
    if not bent:
        for k in straight:
            add_core(1, k)
    for k in bent:
        to_partner(1, k).start()
    for k in bent:
        add_core(1, k)

    stores = []

    def weight_grad(left, right, i):
        parts_here = (0,) if i == 2 else (0, 1)

        def tile(first, width):
            lanes = pl.ds(first, width)
            value = product_over_tokens(left, 0, split * len(parts_here), right, lanes)
            for part in parts_here:
                for h in range(hi):
                    row = i * padded + part * part_rows
                    start = (part * hi + h) * part_rows
                    late[h, row : row + part_rows, lanes] = value[start : start + part_rows]

        in_tiles(D, 256, tile)
        rows = pl.ds(i * padded, part_rows * len(parts_here))
        store = pltpu.make_async_copy(late.at[:, rows], grad_weights.at[:, rows], late_sem.at[i])
        store.start()
        stores.append(store)

    weight_grad(hidden_t, dy, 2)
    for k in straight:
        add_neighbours(1, k)
    weight_grad(gate_t, mid, 0)
    weight_grad(up_t, mid, 1)
    add_owners(1)
    grad_mid[...] = total[...]
    for push in hi_pushes:
        push.wait_recv()
    early_total = early[high].astype(jnp.float32)
    for k in range(hi - 1):
        early_total = early_total + early_land[k].astype(jnp.float32)
    early_sum[...] = early_total.astype(jnp.bfloat16)
    for push in hi_pushes:
        push.wait_send()
    for store in stores:
        store.wait()
    settle(1)
    for k, h in ordered:
        dy_push(k, h).wait_send()
    for go in onward:
        dy_onward(*go).wait_send()
    for share in shares:
        share.wait_send()


def feed_forward(lay, mid, weights, mixed, cotangent, valid, gain, collective_id):
    n = lay.chips
    tokens = mixed.shape[0]
    units = weights.shape[0] * weights.shape[1] // 3
    early_rows = weights.shape[1] // 6
    late_rows = weights.shape[1] - early_rows
    most = min(n, max(1, 1920 // units))
    low, high = jnp.bfloat16, jnp.float32
    vmem = pl.BlockSpec(memory_space=pltpu.VMEM)
    dma = pltpu.SemaphoreType.DMA
    return pl.pallas_call(
        partial(feed_forward_kernel, lay),
        out_shape=(
            jax.ShapeDtypeStruct((tokens, D), low),
            jax.ShapeDtypeStruct((tokens, D), high),
            jax.ShapeDtypeStruct((8, D), high),
            jax.ShapeDtypeStruct((lay.hi, late_rows, D), low),
            jax.ShapeDtypeStruct((early_rows, D), low),
        ),
        in_specs=[pl.BlockSpec(memory_space=pl.ANY)] * 2 + [vmem] * 4,
        out_specs=(vmem, vmem, vmem, pl.BlockSpec(memory_space=pl.ANY), vmem),
        scratch_shapes=[
            pltpu.VMEM((n, 2 * tokens, D), low),
            dma((n,)),
            pltpu.VMEM((lay.hi, late_rows, D), low),
            dma((3,)),
            pltpu.VMEM((lay.hi, early_rows, D), low),
            pltpu.VMEM((max(1, lay.hi - 1), early_rows, D), low),
            dma((lay.hi,)),
            dma((lay.hi,)),
            pltpu.VMEM((units, D), low),
            pltpu.VMEM((units, D), low),
            pltpu.VMEM((units, D), low),
            pltpu.VMEM((n, units, 2 * tokens), low),
            pltpu.VMEM((n, units, 2 * tokens), low),
            pltpu.VMEM((n, 2 * tokens, units), low),
            pltpu.VMEM((n, 2 * tokens, units), low),
            pltpu.VMEM((most * 2 * tokens, units), low),
            pltpu.VMEM((n, units, 2 * tokens), low),
            pltpu.VMEM((2, most * 2 * tokens, units), low),
            pltpu.VMEM((n, 2 * tokens, D), low),
            pltpu.VMEM((n, tokens, D), low),
            pltpu.VMEM((max(1, n - 1), tokens, D), low),
            pltpu.VMEM((max(1, len(lay.bent())), tokens if lay.bent() else 16, D), low),
            pltpu.VMEM((max(1, len(lay.straight())), tokens, D), low),
            pltpu.VMEM((tokens, D), high),
            pltpu.VMEM((n, 2 * tokens, D), low),
            dma((3, 2, lay.hi)),
        ]
        + [dma((2, n))] * 2
        + [dma((n,))] * 2
        + [dma((2, n, 2))] * 4
        + [dma((n, 2))] * 3,
        compiler_params=pltpu.CompilerParams(
            collective_id=collective_id, has_side_effects=True, vmem_limit_bytes=63 * 2**20
        ),
    )(mid, weights, mixed, cotangent, valid, gain)


def norm_scaled(v, gain):
    return v * lax.rsqrt(jnp.mean(v * v, axis=-1, keepdims=True) + EPS) * (1.0 + gain)


def rotate(v, angle):
    half = v.shape[-1] // 2
    cosine = jnp.cos(angle)
    sine = jnp.sin(angle)
    first = v[..., :half]
    second = v[..., half:]
    return jnp.concatenate(
        [first * cosine - second * sine, second * cosine + first * sine], axis=-1
    )


def angles_of(positions):
    inverse = 1.0 / 10000.0 ** (jnp.arange(HD // 2, dtype=jnp.float32) * (2.0 / HD))
    return positions.astype(jnp.float32)[:, None] * inverse[None, :]


def head_inputs(projected, gain_query, gain_key, angle):
    query = projected[..., : HEADS * HD].reshape(projected.shape[:-1] + (HEADS, HD))
    key_rows = projected[..., HEADS * HD : (HEADS + 1) * HD]
    value_rows = projected[..., (HEADS + 1) * HD :]
    query = rotate(norm_scaled(query, gain_query), angle[:, None, :])
    key_rows = rotate(norm_scaled(key_rows, gain_key), angle)
    return (query, key_rows, value_rows)


def contract(left, right, dims_left, dims_right):
    return lax.dot_general(
        left, right, ((dims_left, dims_right), ((), ())), preferred_element_type=jnp.float32
    )


def per_device(lay, tokens, lengths, w_qkv, w_out, w_gate_up, w_down, gains, cotangent):
    seq_count = tokens.shape[0]
    local_len = tokens.shape[1]
    reach = (WINDOW - 1) // local_len + 1
    scale = 1.0 / math.sqrt(HD)
    units = w_down.shape[0]
    per = units // lay.dp
    qkv_rows, out_rows = w_qkv.shape[0], w_out.shape[0]
    cols = w_qkv.shape[1]
    used = qkv_rows + out_rows + 1
    block = 16 * lay.dp
    pack_rows = -(-used // block) * block
    plane, ffn_rows, earlier_tokens = weights_in(
        lay,
        reach,
        tokens,
        w_qkv,
        w_out.T,
        gains[None],
        w_gate_up.T,
        w_down.T,
        5,
    )
    ffn_all = lax.all_gather(ffn_rows, "ctx", axis=0, axis_index_groups=lay.hi_groups)
    attn_all = gather_group(
        lay,
        plane,
        (lay.hi, lay.lo, lay.dp, pack_rows // lay.dp, D),
        lambda out, k, chip, core: out.at[
            :, chip // lay.wide, lax.rem(chip, lay.wide) * 2 + core
        ],
        6,
    ).reshape(lay.ctx, pack_rows, D)
    full_qkv = attn_all[:, :qkv_rows].reshape(lay.ctx * qkv_rows, D)
    full_out = attn_all[:, qkv_rows : qkv_rows + out_rows].reshape(lay.ctx * out_rows, D)
    gain_all = (
        attn_all[:, used - 1]
        .reshape(lay.ctx, lay.dp, cols)[:, :, : gains.shape[0]]
        .transpose(1, 0, 2)
        .reshape(-1)
        .astype(jnp.float32)
    )
    gain_in = gain_all[:D]
    gain_attn = gain_all[D : 2 * D]
    gain_pre = gain_all[2 * D : 3 * D]
    gain_post = gain_all[3 * D : 4 * D]
    gain_query = gain_all[4 * D : 4 * D + HD]
    gain_key = gain_all[4 * D + HD :]
    offset = lax.axis_index("ctx") * local_len
    positions = offset + jnp.arange(local_len, dtype=jnp.int32)
    angle = angles_of(positions)
    valid = positions[None, :] < lengths[:, None]
    inputs = tokens.astype(jnp.float32)
    normed_in, pull_in = jax.vjp(norm_scaled, inputs, gain_in)
    normed_low = normed_in.astype(jnp.bfloat16)
    projected = contract(normed_low, full_qkv, (2,), (1,))
    (query, key_rot, value_rows), pull_heads = jax.vjp(
        partial(head_inputs, angle=angle), projected, gain_query, gain_key
    )
    query_low = query.astype(jnp.bfloat16)
    key_pos = offset - reach * local_len + jnp.arange((reach + 1) * local_len, dtype=jnp.int32)
    earlier = earlier_tokens.transpose(1, 0, 2, 3).reshape(seq_count, reach * local_len, D)
    earlier = norm_scaled(earlier.astype(jnp.float32), gain_in).astype(jnp.bfloat16)
    earlier = contract(earlier, full_qkv[HEADS * HD :], (2,), (1,))
    earlier_keys = rotate(
        norm_scaled(earlier[..., :HD], gain_key), angles_of(key_pos[: reach * local_len])
    )
    key_pairs = jnp.concatenate(
        [
            jnp.concatenate([earlier_keys, earlier[..., HD:]], axis=-1).astype(jnp.bfloat16),
            jnp.concatenate([key_rot, value_rows], axis=-1).astype(jnp.bfloat16),
        ],
        axis=1,
    )
    keys_low = key_pairs[..., :HD]
    values_low = key_pairs[..., HD:]
    key_grid = key_pos[None, None, :]
    query_grid = positions[None, :, None]
    allowed = (
        (key_grid >= 0)
        & (key_grid <= query_grid)
        & (query_grid - key_grid < WINDOW)
        & ((key_grid < lengths[:, None, None]) | (key_grid == query_grid))
    )

    def scores_of():
        raw = jnp.einsum("schd,skd->shck", query_low, keys_low, preferred_element_type=jnp.float32)
        return jnp.where(allowed[:, None], raw * scale, -BIG)

    scores = scores_of()
    top = jnp.max(scores, axis=-1, keepdims=True)
    expo = jnp.exp(scores - top)
    total = jnp.sum(expo, axis=-1, keepdims=True)
    probs = expo / total
    log_total = top + jnp.log(total)
    probs_low = probs.astype(jnp.bfloat16)
    attended = jnp.einsum(
        "shck,skd->schd", probs_low, values_low, preferred_element_type=jnp.float32
    )
    attended_low = attended.reshape(seq_count, local_len, HEADS * HD).astype(jnp.bfloat16)
    out_proj = contract(attended_low, full_out, (2,), (0,))
    normed_out, pull_out = jax.vjp(norm_scaled, out_proj, gain_attn)
    mixed = inputs + normed_out
    normed_mid, pull_mid = jax.vjp(norm_scaled, mixed, gain_pre)
    mid_low = normed_mid.astype(jnp.bfloat16)
    token_count = seq_count * local_len
    mid_all = gather_group(
        lay,
        mid_low.reshape(2, token_count // 2, D),
        (lay.chips, 2, 2, token_count // 2, D),
        lambda out, k, chip, core: out.at[lay.position(k), core],
        1,
    ).reshape(lay.chips, 2 * token_count, D)
    result, grad_mid, grad_gain_post, grad_ffn, early_down = feed_forward(
        lay,
        mid_all,
        ffn_all,
        mixed.reshape(token_count, D),
        cotangent.reshape(token_count, D),
        valid.reshape(token_count, 1).astype(jnp.float32),
        gain_post[None],
        2,
    )
    result = result.reshape(mixed.shape)
    grad_mid = grad_mid.reshape(mixed.shape)
    grad_gain_post = jnp.sum(grad_gain_post, axis=0)
    upstream = jnp.where(valid[..., None], cotangent.astype(jnp.float32), 0.0)
    grad_mixed_in, grad_gain_pre = pull_mid(grad_mid)
    grad_mixed = upstream + grad_mixed_in
    grad_proj, grad_gain_attn = pull_out(grad_mixed)
    proj_low = grad_proj.astype(jnp.bfloat16)
    grad_attended = contract(proj_low, full_out, (2,), (1,))
    grad_w_out = contract(attended_low, proj_low, (0, 1), (0, 1))
    attn_low = grad_attended.astype(jnp.bfloat16).reshape(seq_count, local_len, HEADS, HD)
    again_probs = jnp.exp(scores_of() - log_total)
    again_low = again_probs.astype(jnp.bfloat16)
    grad_values = jnp.einsum(
        "shck,schd->skd", again_low, attn_low, preferred_element_type=jnp.float32
    )
    grad_probs = jnp.einsum(
        "schd,skd->shck", attn_low, values_low, preferred_element_type=jnp.float32
    )
    row_dot = jnp.sum(again_probs * grad_probs, axis=-1, keepdims=True)
    grad_scores = (scale * again_probs * (grad_probs - row_dot)).astype(jnp.bfloat16)
    grad_query = jnp.einsum(
        "shck,skd->schd", grad_scores, keys_low, preferred_element_type=jnp.float32
    )
    grad_keys = jnp.einsum(
        "shck,schd->skd", grad_scores, query_low, preferred_element_type=jnp.float32
    )
    grad_pairs = jnp.concatenate([grad_keys, grad_values], axis=-1)
    own_grad = grad_pairs[:, reach * local_len :]
    pieces = grad_pairs[:, : reach * local_len].astype(jnp.bfloat16)
    pieces = pieces.reshape(seq_count, reach, local_len, 2 * HD).transpose(1, 0, 2, 3)

    def blocks_of(grad, rows):
        part = -(-rows // (16 * lay.dp)) * 16
        whole = grad.astype(jnp.bfloat16).reshape(lay.ctx, rows, D)
        if part * lay.dp > rows:
            whole = jnp.pad(whole, ((0, 0), (0, part * lay.dp - rows), (0, 0)))
        return whole.reshape(lay.ctx, lay.dp, part, D)

    later, plane_out, early_units = later_sum(
        lay, reach, pieces, blocks_of(grad_w_out, out_rows), early_down, 11
    )
    own_grad = own_grad + later
    grad_projected, grad_gain_query, grad_gain_key = pull_heads(
        (grad_query, own_grad[..., :HD], own_grad[..., HD:])
    )
    qkv_low = grad_projected.astype(jnp.bfloat16)
    grad_w_qkv = contract(qkv_low, normed_low, (0, 1), (0, 1))
    grad_normed = contract(qkv_low, full_qkv, (2,), (0,))
    grad_in_norm, grad_gain_in = pull_in(grad_normed)
    grad_input = grad_mixed + grad_in_norm
    grad_gain_all = jnp.concatenate(
        [
            grad_gain_in,
            grad_gain_attn,
            grad_gain_pre,
            grad_gain_post,
            grad_gain_query,
            grad_gain_key,
        ]
    )
    plane_qkv, gains_sum = sum_group(
        lay, blocks_of(grad_w_qkv, qkv_rows), grad_gain_all.reshape(-1, gains.shape[0]), 8
    )
    owned = lax.psum_scatter(grad_ffn, "ctx", scatter_dimension=0, axis_index_groups=lay.hi_groups)
    part_gate_up, part_down, part_qkv, part_out, part_gains = grads_out(
        lay, owned, early_units, plane_qkv, plane_out, gains_sum,
        per, qkv_rows, out_rows, 9,
    )
    part_out = part_out.T
    part_gains = part_gains[0]
    part_gate_up = part_gate_up.astype(jnp.float32).T
    part_down = part_down.astype(jnp.float32).T
    return (result, grad_input, part_qkv, part_out, part_gate_up, part_down, part_gains)


def solution(mesh):
    placed = (
        P("dp", "ctx", None),
        P("dp"),
        P("ctx", "dp"),
        P("ctx", "dp"),
        P("ctx", "dp"),
        P("ctx", "dp"),
        P(("dp", "ctx")),
        P("dp", "ctx", None),
    )
    return jax.shard_map(
        partial(per_device, Layout(mesh)),
        mesh=mesh,
        in_specs=placed,
        out_specs=(
            P("dp", "ctx", None),
            P("dp", "ctx", None),
            P("ctx", "dp"),
            P("ctx", "dp"),
            P("ctx", "dp"),
            P("ctx", "dp"),
            P(("dp", "ctx")),
        ),
        check_vma=False,
    )
```

```python
from functools import partial
import math

import jax
import jax.numpy as jnp
from jax import lax
from jax.experimental import pallas as pl
from jax.experimental.pallas import tpu as pltpu
from jax.sharding import PartitionSpec as P

D = 1152
HEADS = 4
HD = 256
WINDOW = 512
GROUP = 8

EPS = 1e-06
BIG = 1e30
MESH = pl.DeviceIdType.MESH
VMEM_LIMIT = 56 * 2**20


class Layout:
    def __init__(self, mesh):
        self.dp = mesh.shape["dp"]
        self.ctx = mesh.shape["ctx"]
        self.lo = max(1, GROUP // self.dp)
        self.hi = self.ctx // self.lo
        self.wide = self.dp // 2
        self.chips = self.wide * self.lo
        self.group = self.dp * self.lo
        self.hi_groups = [
            [h * self.lo + low for h in range(self.hi)] for low in range(self.lo)
        ]

    def place(self):
        dp = lax.axis_index("dp")
        ctx = lax.axis_index("ctx")
        chip = lax.rem(ctx, self.lo) * self.wide + dp // 2
        return chip, lax.rem(dp, 2), ctx // self.lo

    def offset(self, chip, k, sign=1):
        across = lax.rem(chip, self.wide) + self.wide + sign * (k % self.wide)
        low = chip // self.wide + self.lo + sign * (k // self.wide)
        return lax.rem(low, self.lo) * self.wide + lax.rem(across, self.wide)

    def straight(self):
        return list(range(1, self.wide)) + [low * self.wide for low in range(1, self.lo)]

    def bent(self):
        return [k for k in range(1, self.chips) if k not in self.straight()]

    def position(self, k):
        return (self.bent() + self.straight() + [0]).index(k)

    def device(self, chip, core, high):
        return (lax.rem(chip, self.wide) * 2 + core, high * self.lo + chip // self.wide)


def remote(src, dst, send, recv, device):
    return pltpu.make_async_remote_copy(
        src_ref=src, dst_ref=dst, send_sem=send, recv_sem=recv, device_id=device, device_id_type=MESH
    )


def greet(devices):
    barrier = pltpu.get_barrier_semaphore()
    for device in devices:
        pl.semaphore_signal(barrier, inc=1, device_id=device, device_id_type=MESH)
    pl.semaphore_wait(barrier, len(devices))


def gather_group_kernel(lay, slot, own, out, local_sem, send, recv, pass_send, core_send, core_recv):
    chip, core, high = lay.place()
    n = lay.chips
    half = own.shape[0] // 2
    halves = (pl.ds(0, half), pl.ds(half, half))
    peers = [lay.device(lay.offset(chip, k), core, high) for k in range(n)]
    sources = [lay.offset(chip, k, -1) for k in range(n)]
    partner = lay.device(chip, 1 - core, high)
    greet(peers[1:] + [partner])
    mine = [slot(out, k, chip, core) for k in range(n)]
    straight, bent = lay.straight(), lay.bent()
    keep = pltpu.make_async_copy(own, mine[0], local_sem)
    keep.start()
    pushes = []

    def push(k, h, source, target, sem):
        copy = remote(source.at[halves[h]], target.at[halves[h]], sem, recv.at[k, h], peers[k])
        return copy

    ordered = [(k, i if k < lay.wide else 1 - i) for i in range(2) for k in straight]
    for k, h in ordered:
        copy = push(k, h, own, mine[k], send.at[k, h])
        copy.start()
        pushes.append(copy)
    shares = [remote(own, mine[0], core_send.at[0], core_recv.at[0], partner)]
    shares[0].start()

    def arrived(k, h):
        copy = remote(own.at[halves[h]], mine[k].at[halves[h]], send.at[k, h], recv.at[k, h], peers[k])
        copy.wait_recv()

    for k, h in ordered:
        arrived(k, h)
        block = slot(out, k, sources[k], core)
        if k < lay.wide and h == 0:
            onward = [b * lay.wide for b in range(1, lay.lo)]
        elif k >= lay.wide and h == 1:
            onward = list(range(1, lay.wide))
        else:
            onward = []
        for step in onward:
            total = k + step
            there = slot(out, total, sources[k], core)
            copy = remote(
                block.at[halves[h]], there.at[halves[h]], pass_send.at[total, h], recv.at[total, h], peers[step]
            )
            copy.start()
            pushes.append(copy)
    for k in straight + bent:
        if k in bent:
            for h in range(2):
                arrived(k, h)
        block = slot(out, k, sources[k], core)
        share = remote(block, block, core_send.at[k], core_recv.at[k], partner)
        share.start()
        shares.append(share)
    keep.wait()
    for copy in pushes:
        copy.wait_send()
    for share in shares:
        share.wait()


def gather_group(lay, value, out_shape, slot, collective_id):
    n = lay.chips
    dma = pltpu.SemaphoreType.DMA
    return pl.pallas_call(
        partial(gather_group_kernel, lay, slot),
        out_shape=jax.ShapeDtypeStruct(out_shape, value.dtype),
        in_specs=[pl.BlockSpec(memory_space=pl.ANY)],
        out_specs=pl.BlockSpec(memory_space=pl.ANY),
        scratch_shapes=[dma, dma((n, 2)), dma((n, 2)), dma((n, 2)), dma((n,)), dma((n,))],
        compiler_params=pltpu.CompilerParams(
            collective_id=collective_id, has_side_effects=True, vmem_limit_bytes=VMEM_LIMIT
        ),
    )(value)


def weights_in_kernel(
    lay, reach, tokens, qkv, out_t, gains, pairs, lows, attn_out, ffn_out, earlier_out,
    pack, hops_land, attn_land, own, stack, land, keep_sem, hop_send, hop_recv, low_send, low_recv, attn_send, attn_recv, send, recv, chain_send, chain_recv,
):
    n, hi, lo = lay.dp, lay.hi, lay.lo
    dp = lax.axis_index("dp")
    ctx = lax.axis_index("ctx")
    high = ctx // lo
    cols = lows.shape[0]
    per = lows.shape[1] // n
    padded = ffn_out.shape[0] // 3
    targets = [lax.rem(dp + k, n) for k in range(n)]
    right, left = (dp, ctx + lo), (dp, ctx - lo)
    has_right, has_left = high < hi - 1, high > 0
    low = lax.rem(ctx, lo)
    low_peers = [(dp, high * lo + other) for other in range(lo)]
    hops = hops_land.shape[0] - 1
    barrier = pltpu.get_barrier_semaphore()
    for target in targets[1:]:
        pl.semaphore_signal(barrier, inc=1, device_id=(target, ctx), device_id_type=MESH)
    for other in range(lo):
        if lo > 1:
            @pl.when(low != other)
            def _():
                pl.semaphore_signal(barrier, inc=1, device_id=low_peers[other], device_id_type=MESH)
    for there, device in ((has_right, right), (has_left, left)):
        @pl.when(there)
        def _():
            pl.semaphore_signal(barrier, inc=1, device_id=device, device_id_type=MESH)
    sides = jnp.where(has_right, 1, 0) + jnp.where(has_left, 1, 0)
    pl.semaphore_wait(barrier, n - 1 + sides + lo - 1)

    rows = pack.shape[1]
    last = jnp.concatenate([gains[...], jnp.zeros((1, cols - gains.shape[1]), jnp.float32)], axis=1)
    used = qkv.shape[0] + out_t.shape[1]
    first_row = lax.broadcasted_iota(jnp.int32, (n * rows - used, cols), 0) == 0
    block = jnp.concatenate(
        [qkv[...], out_t[...].T, jnp.where(first_row, last, 0.0)], axis=0
    ).astype(jnp.bfloat16)
    pack[...] = block.reshape(n, rows, cols)
    attn_pushes = []
    for k in range(1, n):
        push = remote(
            pack.at[targets[k]], attn_land.at[dp], attn_send.at[k], attn_recv.at[k], (targets[k], ctx)
        )
        push.start()
        attn_pushes.append(push)
    attn_land[dp] = pack[dp]
    wide = land.shape[3]

    def feed_forward_push(q):
        return remote(stack.at[:, q], land.at[:, dp], send.at[q], recv.at[dp], (q, ctx))

    def feed_forward_units(q):
        for i, (ref, first, stride) in enumerate(
            ((pairs, 2 * per * q, 2), (pairs, 2 * per * q + 1, 2), (lows, per * q, 1))
        ):
            begin = first // 128 * 128
            end = min(ref.shape[1], -(-(first + stride * (per - 1) + 1) // 128) * 128)
            column = lax.broadcasted_iota(jnp.int32, (end - begin, wide), 0) + (begin - first)
            unit = lax.broadcasted_iota(jnp.int32, (end - begin, wide), 1)
            pick = jnp.where((column == stride * unit) & (unit < per), 1.0, 0.0).astype(jnp.bfloat16)
            picked = dot_nn(ref[:, begin:end].astype(jnp.bfloat16), pick).astype(jnp.bfloat16)
            stack[i, q] = picked

        @pl.when(dp != q)
        def _():
            feed_forward_push(q).start()

    def chain(source, where, side, step):
        return remote(
            source, attn_out.at[where], chain_send.at[side, step], chain_recv.at[side, step],
            right if side == 0 else left,
        )

    def pass_on(step):
        if step == 0:
            for side, there in ((0, has_right), (1, has_left)):
                @pl.when(there)
                def _():
                    chain(own, high, side, 0).start()
            return
        for side, here, there in (
            (0, high - step >= 0, has_right),
            (1, high + step < hi, has_left),
        ):
            where = high - step if side == 0 else high + step

            @pl.when(here)
            def _():
                chain(own, where, side, step - 1).wait_recv()
                if step < hi - 1:
                    @pl.when(there)
                    def _():
                        chain(attn_out.at[where], where, side, step).start()

    def finish(step):
        for side, here, there in (
            (0, high - step >= 0, has_right),
            (1, high + step < hi, has_left),
        ):
            @pl.when(here & there)
            def _():
                chain(own, high, side, step).wait_send()

    parts = 2
    span = tokens.shape[0] // parts

    def part_of(ref, part):
        return ref.at[pl.ds(part * span, span)]

    def hop(h, part):
        source = tokens if h == 0 else hops_land.at[h]
        return remote(
            part_of(source, part), part_of(hops_land.at[h + 1], part), hop_send.at[h, part], hop_recv.at[h, part], right
        )

    def wanted(h, source, target):
        distance = h * lo + target - source
        return (distance >= 1) & (distance <= reach) & (high >= h)

    def aside(h, source, target, device, part):
        block = tokens if h == 0 else hops_land.at[h]
        return remote(
            part_of(block, part), part_of(earlier_out.at[reach - (h * lo + target - source)], part),
            low_send.at[h, target, part], low_recv.at[h, source, part], device,
        )

    def pass_tokens(h, part):
        if h:
            @pl.when(high >= h)
            def _():
                hop(h - 1, part).wait_recv()
        if h < hops:
            @pl.when((high >= h) & has_right)
            def _():
                hop(h, part).start()
        for other in range(lo):
            if lo > 1:
                @pl.when((low != other) & wanted(h, low, other))
                def _():
                    aside(h, low, other, low_peers[other], part).start()
        if h and h * lo <= reach:
            @pl.when(high >= h)
            def _():
                block = pl.ds(part * span, span)
                earlier_out[reach - h * lo, block] = hops_land[h, block]

    def finish_tokens(h, part):
        if h < hops:
            @pl.when((high >= h) & has_right)
            def _():
                hop(h, part).wait_send()
        for other in range(lo):
            if lo > 1:
                @pl.when((low != other) & wanted(h, other, low))
                def _():
                    aside(h, other, low, low_peers[other], part).wait_recv()

                @pl.when((low != other) & wanted(h, low, other))
                def _():
                    aside(h, low, other, low_peers[other], part).wait_send()

    for part in range(parts):
        pass_tokens(0, part)
    for d in range(1, reach + 1):
        @pl.when(ctx < d)
        def _():
            earlier_out[reach - d] = jnp.zeros(earlier_out.shape[1:], earlier_out.dtype)
    feed_forward_units(0)
    for push in attn_pushes:
        push.wait_recv()
    for q in range(n):
        own[:, q * cols : (q + 1) * cols] = attn_land[q]
    keep = pltpu.make_async_copy(own, attn_out.at[high], keep_sem)
    keep.start()
    pass_on(0)
    events = [partial(feed_forward_units, 1)]
    for step in range(1, max(hi, hops + 1)):
        if step <= hops:
            events += [partial(pass_tokens, step, part) for part in range(parts)]
        if step == 1:
            events.insert(2, partial(feed_forward_units, 2))
        if step < hi:
            events.append(partial(pass_on, step))
        if step == 1:
            events += [partial(feed_forward_units, q) for q in range(3, n)]
    for event in events:
        event()
    for i in range(3):
        land[i, dp] = stack[i, dp]
    for q in range(n):
        @pl.when(dp != q)
        def _():
            remote(stack.at[:, q], land.at[:, q], send.at[q], recv.at[q], (q, ctx)).wait_recv()
    for i in range(3):
        whole = land[i].reshape(n * cols, wide)
        ffn_out[i * padded : (i + 1) * padded] = whole.T[:padded]
    keep.wait()
    for step in range(hi - 1):
        finish(step)
    for h in range(hops + 1):
        for part in range(parts):
            finish_tokens(h, part)
    for push in attn_pushes:
        push.wait_send()
    for q in range(n):
        @pl.when(dp != q)
        def _():
            feed_forward_push(q).wait_send()


def weights_in(lay, reach, tokens, qkv, out_t, gains, pairs, lows, collective_id):
    n = lay.dp
    cols, per = lows.shape[0], lows.shape[1] // n
    block = 16 * n
    rows = -(-(qkv.shape[0] + out_t.shape[1] + 1) // block) * 16
    padded = -(-per // 32) * 32
    vmem = pl.BlockSpec(memory_space=pltpu.VMEM)
    dma = pltpu.SemaphoreType.DMA
    hops = min(lay.hi - 1, (reach + lay.lo - 1) // lay.lo)
    scratch = [
        pltpu.VMEM((n, rows, cols), jnp.bfloat16),
        pltpu.VMEM((hops + 1,) + tokens.shape, tokens.dtype),
        pltpu.VMEM((n, rows, cols), jnp.bfloat16),
        pltpu.VMEM((rows, n * cols), jnp.bfloat16),
        pltpu.VMEM((3, n, cols, -(-padded // 128) * 128), jnp.bfloat16),
        pltpu.VMEM((3, n, cols, -(-padded // 128) * 128), jnp.bfloat16),
        dma,
    ]
    for shape in ((hops + 1, 2), (hops + 1, lay.lo, 2), (n,), (n,), (2, lay.hi)):
        scratch += [dma(shape), dma(shape)]
    return pl.pallas_call(
        partial(weights_in_kernel, lay, reach),
        out_shape=(
            jax.ShapeDtypeStruct((lay.hi, rows, n * cols), jnp.bfloat16),
            jax.ShapeDtypeStruct((3 * padded, n * cols), jnp.bfloat16),
            jax.ShapeDtypeStruct((reach,) + tokens.shape, tokens.dtype),
        ),
        in_specs=[vmem] * 6,
        out_specs=(pl.BlockSpec(memory_space=pl.ANY), vmem, vmem),
        scratch_shapes=scratch,
        compiler_params=pltpu.CompilerParams(
            collective_id=collective_id, has_side_effects=True, vmem_limit_bytes=VMEM_LIMIT
        ),
    )(tokens, qkv, out_t, gains, pairs, lows)


def later_kernel(
    lay, reach, pieces, parts, early, out, group_out, early_out, low_land, moved, arrived, early_stack,
    early_send, early_recv, chain_send, chain_recv, low_send, low_recv, *scratch
):
    group = GroupSum(lay, parts, group_out, *scratch)
    groups = [group]
    hi, lo = lay.hi, lay.lo
    dp = lax.axis_index("dp")
    ctx = lax.axis_index("ctx")
    high, low = ctx // lo, lax.rem(ctx, lo)
    hops = min(hi - 1, (reach + lo - 1) // lo)
    right, left = (dp, ctx + lo), (dp, ctx - lo)
    has_right, has_left = high < hi - 1, high > 0
    low_peers = [(dp, high * lo + other) for other in range(lo)]
    barrier = pltpu.get_barrier_semaphore()
    n = lay.dp
    dp_peers = [(lax.rem(dp + k, n), ctx) for k in range(1, n)]
    for device in group.low_peers[1:] + dp_peers:
        pl.semaphore_signal(barrier, inc=1, device_id=device, device_id_type=MESH)
    for there, device in [(has_right, right), (has_left, left)]:
        @pl.when(there)
        def _():
            pl.semaphore_signal(barrier, inc=1, device_id=device, device_id_type=MESH)
    sides = jnp.where(has_right, 1, 0) + jnp.where(has_left, 1, 0)
    pl.semaphore_wait(barrier, sides + lo - 1 + n - 1)

    def wanted(h, owner, reader):
        distance = h * lo + reader - owner
        return (distance >= 1) & (distance <= reach) & (high >= h)

    span = out.shape[0] // 2

    def part_of(ref, part):
        return ref.at[pl.ds(part * span, span)]

    def across(h, other, part):
        return remote(
            part_of(pieces.at[reach - (h * lo + low - other)], part), part_of(low_land.at[h, low], part),
            low_send.at[h, other, part], low_recv.at[h, low, part], low_peers[other],
        )

    def from_low(h, other, part):
        return remote(
            part_of(pieces.at[0], part), part_of(low_land.at[h, other], part), low_send.at[h, other, part],
            low_recv.at[h, other, part], low_peers[other],
        )

    def hop(h, part):
        return remote(
            part_of(moved.at[h], part), part_of(arrived.at[h - 1], part), chain_send.at[h, part],
            chain_recv.at[h - 1, part], left,
        )

    def pass_on(h, part):
        block = pl.ds(part * span, span)
        out[block] = jnp.zeros((span,) + out.shape[1:], out.dtype)
        if h and h * lo <= reach:
            out[block] += pieces[reach - h * lo, block].astype(jnp.float32)
        for other in range(lo):
            if lo > 1:
                @pl.when((low != other) & wanted(h, low, other))
                def _():
                    from_low(h, other, part).wait_recv()
                    out[block] += low_land[h, other, block].astype(jnp.float32)
        if h < hops:
            @pl.when(has_right & (high >= h))
            def _():
                hop(h + 1, part).wait_recv()
                out[block] += arrived[h, block].astype(jnp.float32)
        if h:
            @pl.when(high >= h)
            def _():
                moved[h, block] = out[block].astype(moved.dtype)
                hop(h, part).start()

    for h in range(hops, -1, -1):
        for part in range(2):
            for other in range(lo):
                if lo > 1:
                    @pl.when((low != other) & wanted(h, other, low))
                    def _():
                        across(h, other, part).start()
    for each in groups:
        each.start()
    cols, wide = early_stack.shape[1:]
    whole = early[...]
    if wide > early.shape[0]:
        blank = jnp.zeros((wide - early.shape[0], n * cols), early.dtype)
        whole = jnp.concatenate([whole, blank], axis=0)
    early_stack[...] = whole.T.reshape(n, cols, wide)
    early_pushes = []
    for k in range(1, n):
        push = remote(
            early_stack.at[lax.rem(dp + k, n)], early_out.at[dp], early_send.at[k], early_recv.at[k], dp_peers[k - 1]
        )
        push.start()
        early_pushes.append(push)
    early_out[dp] = early_stack[dp]
    stages = groups[0].stages()
    bounds = [0, 1] + [1 + (len(stages) - 1) * (i + 1) // hops for i in range(hops)]
    for h in range(hops, -1, -1):
        turn = hops - h
        for calls in stages[bounds[turn] : bounds[turn + 1]]:
            for call in calls:
                call()
        for part in range(2):
            pass_on(h, part)
    for h in range(hops + 1):
        for part in range(2):
            if h:
                @pl.when(high >= h)
                def _():
                    hop(h, part).wait_send()
            for other in range(lo):
                if lo > 1:
                    @pl.when((low != other) & wanted(h, other, low))
                    def _():
                        across(h, other, part).wait_send()
    for each in groups:
        each.finish()
    for push in early_pushes:
        push.wait()


def later_sum(lay, reach, pieces, parts, early, collective_id):
    n = lay.dp
    early_shape = (n, early.shape[1] // n, -(-early.shape[0] // 128) * 128)
    hops = min(lay.hi - 1, (reach + lay.lo - 1) // lay.lo)
    shape = pieces.shape[1:]
    vmem = pl.BlockSpec(memory_space=pltpu.VMEM)
    dma = pltpu.SemaphoreType.DMA
    return pl.pallas_call(
        partial(later_kernel, lay, reach),
        out_shape=(
            jax.ShapeDtypeStruct(shape, jnp.float32),
            jax.ShapeDtypeStruct((lay.hi, parts.shape[2], D), parts.dtype),
            jax.ShapeDtypeStruct(early_shape, early.dtype),
        ),
        in_specs=[vmem] * 3,
        out_specs=(vmem,) * 3,
        scratch_shapes=[
            pltpu.VMEM((hops + 1, lay.lo) + shape, pieces.dtype),
            pltpu.VMEM((hops + 1,) + shape, pieces.dtype),
            pltpu.VMEM((hops + 1,) + shape, pieces.dtype),
        ]
        + [pltpu.VMEM(early_shape, early.dtype), dma((n,)), dma((n,))]
        + [dma((hops + 1, 2))] * 2
        + [dma((hops + 1, lay.lo, 2))] * 2
        + GroupSum.scratch(lay, parts.shape[2]),
        compiler_params=pltpu.CompilerParams(
            collective_id=collective_id, has_side_effects=True, vmem_limit_bytes=VMEM_LIMIT
        ),
    )(pieces, parts, early)


def flip(index, bit):
    return index + bit * (1 - 2 * lax.rem(index // bit, 2))


class GroupSum:
    @staticmethod
    def scratch(lay, rows):
        dma = pltpu.SemaphoreType.DMA
        blocks = (lay.hi, lay.lo, lay.wide)
        data = [pltpu.VMEM(blocks + (rows, D), jnp.bfloat16)] * 3
        return data + [dma(blocks)] * 6

    def __init__(self, lay, parts, out, land, sums, second_land, core_send, core_recv, send, recv, second_send, second_recv):
        self.lay, self.parts, self.out = lay, parts, out
        self.land, self.sums, self.second_land = land, sums, second_land
        self.core_sems, self.sems, self.second_sems = (core_send, core_recv), (send, recv), (second_send, second_recv)
        dp = lax.axis_index("dp")
        ctx = lax.axis_index("ctx")
        hi, lo, wide = lay.hi, lay.lo, lay.wide
        high, self.low = ctx // lo, lax.rem(ctx, lo)
        self.across, self.core = dp // 2, lax.rem(dp, 2)
        self.partner = (self.across * 2 + 1 - self.core, ctx)
        self.low_peers = [(dp, high * lo + lax.rem(self.low + k, lo)) for k in range(lo)]
        self.wide_peers = [(lax.rem(self.across + k, wide) * 2 + self.core, ctx) for k in range(wide)]
        self.peers = self.low_peers[1:] + self.wide_peers[1:] + [self.partner]
        self.sends = []

    def at(self, h, a, b):
        lay = self.lay
        return h * lay.lo + lax.rem(self.low + a, lay.lo), lax.rem(self.across + b, lay.wide) * 2

    def turned(self, h):
        return h >= self.lay.hi // 2 and self.lay.lo > 1

    def core_copy(self, h, a, b):
        ctx, there = self.at(h, a, b)
        return remote(
            self.parts.at[ctx, there + 1 - self.core], self.land.at[h, a, b], self.core_sems[0].at[h, a, b],
            self.core_sems[1].at[h, a, b], self.partner,
        )

    def blocks(self):
        lay = self.lay
        return [
            (a, b) for a in list(range(1, lay.lo)) + [0] for b in list(range(1, lay.wide)) + [0]
        ]

    def start(self):
        for h in range(self.lay.hi):
            for a, b in self.blocks():
                self.core_copy(h, a, b).start()

    def first_copy(self, h, a, b):
        where = (h, a, b)
        return remote(
            self.sums.at[where], self.land_first(h, a, b), self.sems[0].at[where], self.sems[1].at[where],
            self.low_peers[a] if self.turned(h) else self.wide_peers[b],
        )

    def land_first(self, h, a, b):
        return self.second_land.at[h, a, b]

    def second_copy(self, h, a, b):
        where = (h, a, b)
        return remote(
            self.sums.at[where], self.second_land.at[where], self.second_sems[0].at[where],
            self.second_sems[1].at[where], self.wide_peers[b] if self.turned(h) else self.low_peers[a],
        )

    def moves_first(self, h, a, b):
        return a > 0 if self.turned(h) else b > 0

    def sum_cores(self, h):
        for a, b in self.blocks():
            self.core_copy(h, a, b).wait_recv()
            ctx, there = self.at(h, a, b)
            total = self.parts[ctx, there + self.core].astype(jnp.float32) + self.land[h, a, b].astype(jnp.float32)
            self.sums[h, a, b] = total.astype(jnp.bfloat16)
            if self.moves_first(h, a, b):
                self.first_copy(h, a, b).start()

    def sum_first(self, h):
        lay = self.lay
        for a, b in self.blocks():
            if self.moves_first(h, a, b):
                continue
            total = self.sums[h, a, b].astype(jnp.float32)
            others = [(k, b) for k in range(1, lay.lo)] if self.turned(h) else [(a, k) for k in range(1, lay.wide)]
            for other in others:
                self.first_copy(h, *other).wait_recv()
                total = total + self.second_land[(h,) + other].astype(jnp.float32)
            self.sums[h, a, b] = total.astype(jnp.bfloat16)
            if a or b:
                self.second_copy(h, a, b).start()

    def sum_second(self, h):
        lay = self.lay
        total = self.sums[h, 0, 0].astype(jnp.float32)
        others = [(0, k) for k in range(1, lay.wide)] if self.turned(h) else [(k, 0) for k in range(1, lay.lo)]
        for other in others:
            self.second_copy(h, *other).wait_recv()
            total = total + self.second_land[(h,) + other].astype(jnp.float32)
        self.out[h] = total.astype(jnp.bfloat16)

    def order(self):
        half = self.lay.hi // 2
        pairs = [h for pair in zip(range(half), range(half, 2 * half)) for h in pair]
        return pairs + list(range(2 * half, self.lay.hi))

    def stages(self):
        order = self.order()
        stages = []
        for i in range(len(order) + 4):
            calls = []
            if i < len(order):
                calls.append(partial(self.sum_cores, order[i]))
            if 2 <= i < len(order) + 2:
                calls.append(partial(self.sum_first, order[i - 2]))
            if 4 <= i:
                calls.append(partial(self.sum_second, order[i - 4]))
            stages.append(calls)
        return stages

    def finish(self):
        for h in range(self.lay.hi):
            for a, b in self.blocks():
                self.core_copy(h, a, b).wait_send()
                if self.moves_first(h, a, b):
                    self.first_copy(h, a, b).wait_send()
                elif a or b:
                    self.second_copy(h, a, b).wait_send()


def near_bits(lay, dp, ctx):
    peers = [(flip(dp, 1 << i), ctx) for i in range((lay.dp - 1).bit_length())]
    return peers + [(dp, flip(ctx, 1 << i)) for i in range((lay.lo - 1).bit_length())]


def far_bits(lay, dp, ctx):
    return [
        (dp, flip(ctx, 1 << i)) for i in range((lay.lo - 1).bit_length(), (lay.ctx - 1).bit_length())
    ]


def sum_group_kernel(lay, parts, gains, out, gains_out, gains_sum, gains_land, gains_send, gains_recv, *scratch):
    dp = lax.axis_index("dp")
    ctx = lax.axis_index("ctx")
    group = GroupSum(lay, parts, out, *scratch)
    gain_peers = near_bits(lay, dp, ctx)
    greet(group.peers + gain_peers)

    def gains_copy(i):
        return remote(gains_sum.at[i], gains_land.at[i], gains_send.at[i], gains_recv.at[i], gain_peers[i])

    def gains_step(i):
        if i > len(gain_peers):
            return
        if i == 0:
            gains_sum[0] = gains[...]
        else:
            gains_copy(i - 1).wait_recv()
            gains_sum[i] = gains_sum[i - 1] + gains_land[i - 1]
        if i < len(gain_peers):
            gains_copy(i).start()
        else:
            gains_out[...] = gains_sum[i]

    group.start()
    stages = group.stages()
    for i, calls in enumerate(stages):
        gains_step(i)
        for call in calls:
            call()
    for i in range(len(stages), len(gain_peers) + 1):
        gains_step(i)
    group.finish()
    for i in range(len(gain_peers)):
        gains_copy(i).wait_send()


def sum_group(lay, parts, gains, collective_id):
    rows = parts.shape[2]
    vmem = pl.BlockSpec(memory_space=pltpu.VMEM)
    dma = pltpu.SemaphoreType.DMA
    count = len(near_bits(lay, 0, 0))
    return pl.pallas_call(
        partial(sum_group_kernel, lay),
        out_shape=(
            jax.ShapeDtypeStruct((lay.hi, rows, D), jnp.bfloat16),
            jax.ShapeDtypeStruct(gains.shape, jnp.float32),
        ),
        in_specs=[vmem] * 2,
        out_specs=(vmem,) * 2,
        scratch_shapes=[
            pltpu.VMEM((count + 1,) + gains.shape, jnp.float32),
            pltpu.VMEM((count,) + gains.shape, jnp.float32),
            dma((count,)),
            dma((count,)),
        ]
        + GroupSum.scratch(lay, rows),
        compiler_params=pltpu.CompilerParams(
            collective_id=collective_id, has_side_effects=True, vmem_limit_bytes=VMEM_LIMIT
        ),
    )(parts, gains)


def grads_out_kernel(lay, rows, early, plane_qkv, plane_out, gains, pairs_out, lows_out, qkv_out, out_t, gains_out,
                     gains_sum, gains_land, gains_send, gains_recv, attn, stack, land, low_stack, low_land, hi_land, last, last_land,
                     send, recv, hi_send, hi_recv, last_send, last_recv):
    n, hi, lo = lay.dp, lay.hi, lay.lo
    dp = lax.axis_index("dp")
    ctx = lax.axis_index("ctx")
    high, low = ctx // lo, lax.rem(ctx, lo)
    cols = lows_out.shape[0]
    per = lows_out.shape[1] // n
    half = rows.shape[0] // 5
    padded = 2 * half
    wide = land.shape[3]
    attn_rows = attn.shape[1]
    hi_peers = [(dp, lax.rem(high + k, hi) * lo + low) for k in range(1, hi)]
    gain_peers = far_bits(lay, dp, ctx)
    greet([(lax.rem(dp + k, n), ctx) for k in range(1, n)] + hi_peers + gain_peers)

    def gains_copy(i):
        return remote(gains_sum.at[i], gains_land.at[i], gains_send.at[i], gains_recv.at[i], gain_peers[i])

    gains_sum[0] = gains[...]
    gains_copy(0).start()
    attn[:, : plane_qkv.shape[1]] = plane_qkv[...]
    attn[:, plane_qkv.shape[1] :] = plane_out[...]
    hi_pushes = []
    for k in range(1, hi):
        push = remote(
            attn.at[lax.rem(high + k, hi)], hi_land.at[k - 1], hi_send.at[k], hi_recv.at[k], hi_peers[k - 1]
        )
        push.start()
        hi_pushes.append(push)
    pushes = []
    for i in range(3):
        held, arriving = (stack.at[i], land.at[i]) if i < 2 else (low_stack, low_land)
        lanes = held.shape[2]
        whole = rows[i * padded : min((i + 1) * padded, rows.shape[0])]
        if lanes > whole.shape[0]:
            blank = jnp.zeros((lanes - whole.shape[0], n * cols), jnp.bfloat16)
            whole = jnp.concatenate([whole, blank], axis=0)
        held[...] = whole.T.reshape(n, cols, lanes)
        for k in range(1, n):
            target = lax.rem(dp + k, n)
            push = remote(held.at[target], arriving.at[dp], send.at[i, k], recv.at[i, k], (target, ctx))
            push.start()
            pushes.append(push)
        arriving[dp] = held[dp]

    def gains_step(i):
        gains_copy(i).wait_recv()
        gains_sum[i + 1] = gains_sum[i] + gains_land[i]
        if i + 1 < len(gain_peers):
            gains_copy(i + 1).start()

    gains_step(0)
    total = attn[high].astype(jnp.float32)
    for k, push in enumerate(hi_pushes):
        push.wait_recv()
        total = total + hi_land[k].astype(jnp.float32)
    for q in range(n):
        last[q] = total[:, q * cols : (q + 1) * cols].astype(jnp.bfloat16)
    last_pushes = []
    for k in range(1, n):
        target = lax.rem(dp + k, n)
        push = remote(last.at[target], last_land.at[dp], last_send.at[k], last_recv.at[k], (target, ctx))
        push.start()
        last_pushes.append(push)
    last_land[dp] = last[dp]

    unit = lax.broadcasted_iota(jnp.int32, (wide, 2 * per), 0)
    column = lax.broadcasted_iota(jnp.int32, (wide, 2 * per), 1)
    spread = [jnp.where(column == 2 * unit + i, 1.0, 0.0).astype(jnp.bfloat16) for i in range(2)]
    for push in pushes[: 2 * (n - 1)]:
        push.wait_recv()
    for q in range(n):
        turns = dot_nn(land[0, q], spread[0]) + dot_nn(land[1, q], spread[1])
        pairs_out[:, 2 * per * q : 2 * per * (q + 1)] = turns.astype(jnp.bfloat16)
    for push in pushes[2 * (n - 1) :]:
        push.wait_recv()
    for q in range(n):
        lows_out[:, per * q : per * q + half] = low_land[q, :, :half]
        lows_out[:, per * q + half : per * (q + 1)] = early[q, :, : per - half]
    for i in range(1, len(gain_peers)):
        gains_step(i)
    gains_out[...] = gains_sum[len(gain_peers), pl.ds(dp * lay.ctx + ctx, 1)]
    for push in last_pushes:
        push.wait_recv()
    out_rows = out_t.shape[1]
    out_part, qkv_part = plane_out.shape[1], plane_qkv.shape[1]
    qkv_out[...] = last_land[:, :qkv_part].reshape(n * qkv_part, cols)[: qkv_out.shape[0]].astype(jnp.float32)
    out_t[...] = last_land[:, qkv_part:].reshape(n * out_part, cols)[:out_rows].astype(jnp.float32).T
    for push in hi_pushes + pushes + last_pushes:
        push.wait_send()
    for i in range(len(gain_peers)):
        gains_copy(i).wait_send()


def grads_out(lay, rows, early, plane_qkv, plane_out, gains, per, qkv_rows, out_rows, collective_id):
    count = len(far_bits(lay, 0, 0))
    padded = 2 * rows.shape[0] // 5
    n, cols = lay.dp, rows.shape[1] // lay.dp
    attn_rows = plane_qkv.shape[1] + plane_out.shape[1]
    vmem = pl.BlockSpec(memory_space=pltpu.VMEM)
    dma = pltpu.SemaphoreType.DMA
    return pl.pallas_call(
        partial(grads_out_kernel, lay),
        out_shape=(
            jax.ShapeDtypeStruct((cols, n * 2 * per), jnp.bfloat16),
            jax.ShapeDtypeStruct((cols, n * per), jnp.bfloat16),
            jax.ShapeDtypeStruct((qkv_rows, cols), jnp.float32),
            jax.ShapeDtypeStruct((cols, out_rows), jnp.float32),
            jax.ShapeDtypeStruct((1, gains.shape[1]), jnp.float32),
        ),
        in_specs=[vmem] * 5,
        out_specs=(vmem,) * 5,
        scratch_shapes=[
            pltpu.VMEM((count + 1,) + gains.shape, jnp.float32),
            pltpu.VMEM((count,) + gains.shape, jnp.float32),
            dma((count,)),
            dma((count,)),
            pltpu.VMEM((lay.hi, attn_rows, D), jnp.bfloat16),
            pltpu.VMEM((2, n, cols, -(-padded // 128) * 128), jnp.bfloat16),
            pltpu.VMEM((2, n, cols, -(-padded // 128) * 128), jnp.bfloat16),
            pltpu.VMEM(early.shape, jnp.bfloat16),
            pltpu.VMEM(early.shape, jnp.bfloat16),
            pltpu.VMEM((max(1, lay.hi - 1), attn_rows, D), jnp.bfloat16),
            pltpu.VMEM((n, attn_rows, cols), jnp.bfloat16),
            pltpu.VMEM((n, attn_rows, cols), jnp.bfloat16),
        ]
        + [dma((3, n))] * 2
        + [dma((lay.hi,))] * 2
        + [dma((n,))] * 2,
        compiler_params=pltpu.CompilerParams(
            collective_id=collective_id, has_side_effects=True, vmem_limit_bytes=VMEM_LIMIT
        ),
    )(rows, early, plane_qkv, plane_out, gains)


def in_tiles(total, size, body, begin=0):
    whole = total // size

    def step(i, carry):
        body(pl.multiple_of(begin + i * size, math.gcd(begin, size)), size)
        return carry

    if whole:
        lax.fori_loop(0, whole, step, 0)
    if total % size:
        body(begin + whole * size, total % size)


def dot_nt(left, right):
    return lax.dot_general(left, right, (((1,), (1,)), ((), ())), preferred_element_type=jnp.float32)


def dot_nn(left, right):
    return lax.dot_general(left, right, (((1,), (0,)), ((), ())), preferred_element_type=jnp.float32)


ROOT = math.sqrt(2.0 / math.pi)


def feed_forward_kernel(
    lay, mid_in, weights, mixed, cotangent, valid, gain, result, grad_mid, grad_gain, grad_weights, early_sum,
    mid, mid_sem, late, late_sem, early, early_land, hi_send, hi_recv, w_gate, w_up, w_down, gate_t, up_t, act, slope, hidden, hidden_t, grads, parts, core_land, sums, via, landed,
    total, dy, weight_sem, core_send, core_recv, share_send, share_recv,
    send, recv, via_send, via_recv, dy_send, dy_recv, dy_pass,
):
    chip, core, high = lay.place()
    n, wide = lay.chips, lay.wide
    tokens = mixed.shape[0]
    units = w_gate.shape[0]
    hi = lay.hi
    padded = units // hi
    part_rows = padded // 2
    loads = [
        pltpu.make_async_copy(
            weights.at[h, pl.ds(i * padded + part * part_rows, part_rows)],
            held.at[pl.ds((part * hi + h) * part_rows, part_rows)],
            weight_sem.at[i, part, h],
        )
        for i, held in enumerate((w_gate, w_up, w_down))
        for part in range(2)
        for h in range(hi)
    ]
    mid_loads = [
        pltpu.make_async_copy(mid_in.at[p], mid.at[p], mid_sem.at[p]) for p in range(lay.chips)
    ]
    gates = len(loads) * 2 // 3
    for load in mid_loads[:1] + loads[:gates] + mid_loads[1:] + loads[gates:]:
        load.start()
    peers = [lay.device(lay.offset(chip, k), core, high) for k in range(n)]
    owners = [lay.device(lay.offset(chip, k, -1), core, high) for k in range(n)]
    partner = lay.device(chip, 1 - core, high)
    mine = pl.ds(pl.multiple_of(core * tokens, tokens), tokens)
    theirs = pl.ds(pl.multiple_of((1 - core) * tokens, tokens), tokens)
    half = tokens // 2
    halves = (pl.ds(0, half), pl.ds(half, half))
    straight, bent = lay.straight(), lay.bent()
    place = [lay.position(k) for k in range(n)]
    hi_peers = [lay.device(chip, core, lax.rem(high + k, hi)) for k in range(hi)]
    greet(peers[1:] + [partner] + hi_peers[1:])

    def to_partner(phase, k):
        return remote(
            parts.at[place[k], theirs], core_land.at[k], core_send.at[phase, k], core_recv.at[phase, k], partner
        )

    def to_owner(phase, k, h):
        return remote(
            sums.at[k - 1, halves[h]], landed.at[place[k] - len(bent), halves[h]], send.at[phase, k, h],
            recv.at[phase, k, h], owners[k],
        )

    def to_neighbour(phase, k, h):
        step = k % wide if h == 0 else k // wide * wide
        return remote(
            sums.at[k - 1, halves[h]], via.at[place[k], halves[h]], via_send.at[phase, k, h], via_recv.at[phase, k, h],
            owners[step],
        )

    def added(k):
        if k < wide:
            return 1, [k + b * wide for b in range(1, lay.lo)]
        return 0, [k + step for step in range(1, wide)]

    def add_core(phase, k):
        to_partner(phase, k).wait_recv()

        def chunk(first, rows):
            span = pl.ds(first, rows)
            here = pl.ds(pl.multiple_of(core * tokens + first, rows), rows)
            both = parts[place[k], here].astype(jnp.float32) + core_land[k, span].astype(jnp.float32)
            if k:
                sums[k - 1, span] = both.astype(jnp.bfloat16)
            else:
                total[span] = both

        in_tiles(tokens, 32, chunk)
        if k in bent:
            for h in range(2):
                to_neighbour(phase, k, h).start()
        elif k:
            h, others = added(k)
            to_owner(phase, k, 1 - h).start()
            if not others:
                to_owner(phase, k, h).start()

    def add_neighbours(phase, k):
        h, others = added(k)
        if not others:
            return
        for other in others:
            to_neighbour(phase, other, h).wait_recv()

        def chunk(first, rows):
            span = pl.ds(first + h * half, rows)
            value = sums[k - 1, span].astype(jnp.float32)
            for other in others:
                value = value + via[place[other], span].astype(jnp.float32)
            sums[k - 1, span] = value.astype(jnp.bfloat16)

        in_tiles(half, 32, chunk)
        to_owner(phase, k, h).start()

    def add_owners(phase):
        for k in straight:
            for h in range(2):
                to_owner(phase, k, h).wait_recv()

        def chunk(first, rows):
            span = pl.ds(first, rows)
            value = total[span]
            for k in straight:
                value = value + landed[place[k] - len(bent), span].astype(jnp.float32)
            total[span] = value

        in_tiles(tokens, 32, chunk)

    def settle(phase):
        for k in range(n):
            to_partner(phase, k).wait_send()
            for h in range(2):
                if k in bent:
                    to_neighbour(phase, k, h).wait_send()
                elif k:
                    to_owner(phase, k, h).wait_send()

    rows_of = 2 * tokens

    def joined(ref, group, *index):
        value = ref[(pl.ds(*group),) + index]
        return value.reshape((group[1] * rows_of,) + value.shape[2:])

    def forward_units(group, begin, end):
        count = group[1]

        def tile(first, width):
            units_here = pl.ds(first, width)
            weights = jnp.concatenate([w_gate[units_here], w_up[units_here]], axis=0)
            both = dot_nt(joined(mid, group), weights)
            gate, up = both[:, :width], both[:, width:]
            square = gate * gate
            tanh = jnp.tanh(gate * (ROOT + (0.044715 * ROOT) * square))
            half_way = 0.5 + 0.5 * tanh
            active = gate * half_way
            slant = half_way + active * (1.0 - tanh) * (ROOT + (3.0 * 0.044715 * ROOT) * square)
            product = (active * up).astype(jnp.bfloat16)
            shape = (count, rows_of, width)
            act[pl.ds(*group), :, units_here] = active.astype(jnp.bfloat16).reshape(shape)
            slope[pl.ds(*group), :, units_here] = (slant * up).astype(jnp.bfloat16).reshape(shape)
            hidden[: count * rows_of, units_here] = product
            for c in range(count):
                hidden_t[group[0] + c, units_here] = product[c * rows_of : (c + 1) * rows_of].T

        in_tiles(end - begin, 128, tile, begin)

    def forward_down(group):
        count = group[1]

        def tile(first, width):
            lanes = pl.ds(first, width)
            value = dot_nn(hidden[: count * rows_of], w_down[:, lanes]).astype(jnp.bfloat16)
            parts[pl.ds(*group), :, lanes] = value.reshape(count, rows_of, width)

        in_tiles(D, 256, tile)

    def backward_units(group):
        count = group[1]

        def tile(first, width):
            units_here = pl.ds(first, width)
            grad = dot_nt(joined(dy, group), w_down[units_here])
            up_grad = (grad * joined(act, group, slice(None), units_here).astype(jnp.float32)).astype(jnp.bfloat16)
            gate_grad = (grad * joined(slope, group, slice(None), units_here).astype(jnp.float32)).astype(jnp.bfloat16)
            grads[0, : count * rows_of, units_here] = gate_grad
            grads[1, : count * rows_of, units_here] = up_grad
            for c in range(count):
                rows = slice(c * rows_of, (c + 1) * rows_of)
                gate_t[group[0] + c, units_here] = gate_grad[rows].T
                up_t[group[0] + c, units_here] = up_grad[rows].T

        in_tiles(units, 256, tile)

    def backward_in(group):
        count = group[1]

        def tile(first, width):
            lanes = pl.ds(first, width)
            both = dot_nn(grads[0, : count * rows_of], w_gate[:, lanes]) + dot_nn(
                grads[1, : count * rows_of], w_up[:, lanes]
            )
            parts[pl.ds(*group), :, lanes] = both.astype(jnp.bfloat16).reshape(count, rows_of, width)

        in_tiles(D, 256, tile)

    def product_over_tokens(left, begin, end, right, lanes):
        value = dot_nn(left[0, begin:end], right[0, :, lanes])
        for c in range(1, n):
            value = value + dot_nn(left[c, begin:end], right[c, :, lanes])
        return value.astype(jnp.bfloat16)

    far, near, here = (0, len(bent)), (len(bent), len(straight)), (n - 1, 1)
    most = hidden.shape[0] // rows_of

    def runs(group):
        return [(first, min(most, group[0] + group[1] - first)) for first in range(group[0], sum(group), most)]

    quarter = units // 512 * 128
    for load in mid_loads[:1] + loads[:gates]:
        load.wait()
    waiting = [mid_loads[1:], loads[gates:]]

    def arrive(which):
        while waiting[which]:
            waiting[which].pop(0).wait()

    for run in runs(far):
        if run[0] + run[1] > 1:
            arrive(0)
        forward_units(run, 0, units)
        arrive(1)
        forward_down(run)
    for k in bent:
        to_partner(0, k).start()
    arrive(0)
    for i, run in enumerate(runs(near)):
        forward_units(run, 0, 2 * quarter)
        if i == 0:
            for k in bent:
                add_core(0, k)
        forward_units(run, 2 * quarter, units)
        arrive(1)
        forward_down(run)
    for k in straight:
        to_partner(0, k).start()
    forward_units(here, 0, 2 * quarter)
    for k in straight:
        add_core(0, k)
    for k in straight:
        add_neighbours(0, k)
    forward_units(here, 2 * quarter, units)
    forward_down(here)
    to_partner(0, 0).start()
    add_core(0, 0)
    add_owners(0)

    grad_gain[...] = jnp.zeros_like(grad_gain)
    scale = 1.0 + gain[...]

    def finish(first, rows):
        span = pl.ds(first, rows)
        spot = pl.ds(pl.multiple_of(core * tokens + first, rows), rows)
        y = total[span]
        ok = valid[span]
        rate = lax.rsqrt(jnp.mean(y * y, axis=-1, keepdims=True) + EPS)
        unit = y * rate
        result[span] = ((mixed[span] + unit * scale) * ok).astype(jnp.bfloat16)
        upstream = cotangent[span].astype(jnp.float32) * ok
        down = upstream * unit
        for r in range(0, rows, 8):
            grad_gain[...] += down[r : r + 8]
        scaled = upstream * scale
        inner = jnp.mean(scaled * unit, axis=-1, keepdims=True)
        dy[n - 1, spot] = (rate * (scaled - unit * inner)).astype(jnp.bfloat16)

    in_tiles(tokens, 32, finish)

    def dy_half(k, h):
        return dy.at[place[k], pl.ds(pl.multiple_of(core * tokens + h * half, half), half)]

    def dy_push(k, h):
        return remote(dy_half(0, h), dy_half(k, h), dy_send.at[k, h], dy_recv.at[k, h], peers[k])

    def dy_onward(k, h, step):
        return remote(
            dy_half(k, h), dy_half(k + step, h), dy_pass.at[k + step, h], dy_recv.at[k + step, h], peers[step]
        )

    shares = [
        remote(dy.at[place[k], mine], dy.at[place[k], mine], share_send.at[k], share_recv.at[k], partner)
        for k in range(n)
    ]
    ordered = [(k, i if k < wide else 1 - i) for i in range(2) for k in straight]
    for k, h in ordered:
        dy_push(k, h).start()
    shares[0].start()
    settle(0)
    shares[0].wait_recv()
    backward_units(here)
    backward_in(here)
    to_partner(1, 0).start()
    onward = []
    for k, h in ordered:
        dy_push(k, h).wait_recv()
        if k < wide and h == 0:
            onward += [(k, h, b * wide) for b in range(1, lay.lo)]
        elif k >= wide and h == 1:
            onward += [(k, h, step) for step in range(1, wide)]
        for go in onward:
            if go[:2] == (k, h):
                dy_onward(*go).start()
    for k in straight:
        shares[k].start()
    add_core(1, 0)
    for k in straight:
        shares[k].wait_recv()
    for i, run in enumerate(runs(near)):
        backward_units(run)
        if i == 0:
            for k in bent:
                for h in range(2):
                    dy_push(k, h).wait_recv()
                shares[k].start()
        backward_in(run)
    for k in straight:
        to_partner(1, k).start()
    for k in bent:
        shares[k].wait_recv()
    split = hi * part_rows

    def early_grad(first, width):
        lanes = pl.ds(first, width)
        value = product_over_tokens(hidden_t, split, units, dy, lanes)
        for h in range(hi):
            early[h, :, lanes] = value[h * part_rows : (h + 1) * part_rows]

    in_tiles(D, 256, early_grad)
    hi_pushes = []
    for k in range(1, hi):
        push = remote(
            early.at[lax.rem(high + k, hi)], early_land.at[k - 1], hi_send.at[k], hi_recv.at[k], hi_peers[k]
        )
        push.start()
        hi_pushes.append(push)
    for i, run in enumerate(runs(far)):
        backward_units(run)
        if i == 0:
            for k in straight:
                add_core(1, k)
        backward_in(run)
    if not bent:
        for k in straight:
            add_core(1, k)
    for k in bent:
        to_partner(1, k).start()
    for k in bent:
        add_core(1, k)

    stores = []

    def weight_grad(left, right, i):
        parts_here = (0,) if i == 2 else (0, 1)

        def tile(first, width):
            lanes = pl.ds(first, width)
            value = product_over_tokens(left, 0, split * len(parts_here), right, lanes)
            for part in parts_here:
                for h in range(hi):
                    row = i * padded + part * part_rows
                    start = (part * hi + h) * part_rows
                    late[h, row : row + part_rows, lanes] = value[start : start + part_rows]

        in_tiles(D, 256, tile)
        rows = pl.ds(i * padded, part_rows * len(parts_here))
        store = pltpu.make_async_copy(late.at[:, rows], grad_weights.at[:, rows], late_sem.at[i])
        store.start()
        stores.append(store)

    weight_grad(hidden_t, dy, 2)
    for k in straight:
        add_neighbours(1, k)
    weight_grad(gate_t, mid, 0)
    weight_grad(up_t, mid, 1)
    add_owners(1)
    grad_mid[...] = total[...]
    for push in hi_pushes:
        push.wait_recv()
    early_total = early[high].astype(jnp.float32)
    for k in range(hi - 1):
        early_total = early_total + early_land[k].astype(jnp.float32)
    early_sum[...] = early_total.astype(jnp.bfloat16)
    for push in hi_pushes:
        push.wait_send()
    for store in stores:
        store.wait()
    settle(1)
    for k, h in ordered:
        dy_push(k, h).wait_send()
    for go in onward:
        dy_onward(*go).wait_send()
    for share in shares:
        share.wait_send()


def feed_forward(lay, mid, weights, mixed, cotangent, valid, gain, collective_id):
    n = lay.chips
    tokens = mixed.shape[0]
    units = weights.shape[0] * weights.shape[1] // 3
    early_rows = weights.shape[1] // 6
    late_rows = weights.shape[1] - early_rows
    most = min(n, max(1, 1920 // units))
    low, high = jnp.bfloat16, jnp.float32
    vmem = pl.BlockSpec(memory_space=pltpu.VMEM)
    dma = pltpu.SemaphoreType.DMA
    return pl.pallas_call(
        partial(feed_forward_kernel, lay),
        out_shape=(
            jax.ShapeDtypeStruct((tokens, D), low),
            jax.ShapeDtypeStruct((tokens, D), high),
            jax.ShapeDtypeStruct((8, D), high),
            jax.ShapeDtypeStruct((lay.hi, late_rows, D), low),
            jax.ShapeDtypeStruct((early_rows, D), low),
        ),
        in_specs=[pl.BlockSpec(memory_space=pl.ANY)] * 2 + [vmem] * 4,
        out_specs=(vmem, vmem, vmem, pl.BlockSpec(memory_space=pl.ANY), vmem),
        scratch_shapes=[
            pltpu.VMEM((n, 2 * tokens, D), low),
            dma((n,)),
            pltpu.VMEM((lay.hi, late_rows, D), low),
            dma((3,)),
            pltpu.VMEM((lay.hi, early_rows, D), low),
            pltpu.VMEM((max(1, lay.hi - 1), early_rows, D), low),
            dma((lay.hi,)),
            dma((lay.hi,)),
            pltpu.VMEM((units, D), low),
            pltpu.VMEM((units, D), low),
            pltpu.VMEM((units, D), low),
            pltpu.VMEM((n, units, 2 * tokens), low),
            pltpu.VMEM((n, units, 2 * tokens), low),
            pltpu.VMEM((n, 2 * tokens, units), low),
            pltpu.VMEM((n, 2 * tokens, units), low),
            pltpu.VMEM((most * 2 * tokens, units), low),
            pltpu.VMEM((n, units, 2 * tokens), low),
            pltpu.VMEM((2, most * 2 * tokens, units), low),
            pltpu.VMEM((n, 2 * tokens, D), low),
            pltpu.VMEM((n, tokens, D), low),
            pltpu.VMEM((max(1, n - 1), tokens, D), low),
            pltpu.VMEM((max(1, len(lay.bent())), tokens if lay.bent() else 16, D), low),
            pltpu.VMEM((max(1, len(lay.straight())), tokens, D), low),
            pltpu.VMEM((tokens, D), high),
            pltpu.VMEM((n, 2 * tokens, D), low),
            dma((3, 2, lay.hi)),
        ]
        + [dma((2, n))] * 2
        + [dma((n,))] * 2
        + [dma((2, n, 2))] * 4
        + [dma((n, 2))] * 3,
        compiler_params=pltpu.CompilerParams(
            collective_id=collective_id, has_side_effects=True, vmem_limit_bytes=63 * 2**20
        ),
    )(mid, weights, mixed, cotangent, valid, gain)


def norm_scaled(v, gain):
    return v * lax.rsqrt(jnp.mean(v * v, axis=-1, keepdims=True) + EPS) * (1.0 + gain)


def rotate(v, angle):
    half = v.shape[-1] // 2
    cosine = jnp.cos(angle)
    sine = jnp.sin(angle)
    first = v[..., :half]
    second = v[..., half:]
    return jnp.concatenate(
        [first * cosine - second * sine, second * cosine + first * sine], axis=-1
    )


def angles_of(positions):
    inverse = 1.0 / 10000.0 ** (jnp.arange(HD // 2, dtype=jnp.float32) * (2.0 / HD))
    return positions.astype(jnp.float32)[:, None] * inverse[None, :]


def head_inputs(projected, gain_query, gain_key, angle):
    query = projected[..., : HEADS * HD].reshape(projected.shape[:-1] + (HEADS, HD))
    key_rows = projected[..., HEADS * HD : (HEADS + 1) * HD]
    value_rows = projected[..., (HEADS + 1) * HD :]
    query = rotate(norm_scaled(query, gain_query), angle[:, None, :])
    key_rows = rotate(norm_scaled(key_rows, gain_key), angle)
    return (query, key_rows, value_rows)


def contract(left, right, dims_left, dims_right):
    return lax.dot_general(
        left, right, ((dims_left, dims_right), ((), ())), preferred_element_type=jnp.float32
    )


def per_device(lay, tokens, lengths, w_qkv, w_out, w_gate_up, w_down, gains, cotangent):
    seq_count = tokens.shape[0]
    local_len = tokens.shape[1]
    reach = (WINDOW - 1) // local_len + 1
    scale = 1.0 / math.sqrt(HD)
    units = w_down.shape[0]
    per = units // lay.dp
    qkv_rows, out_rows = w_qkv.shape[0], w_out.shape[0]
    cols = w_qkv.shape[1]
    used = qkv_rows + out_rows + 1
    block = 16 * lay.dp
    pack_rows = -(-used // block) * block
    plane, ffn_rows, earlier_tokens = weights_in(
        lay,
        reach,
        tokens,
        w_qkv,
        w_out.T,
        gains[None],
        w_gate_up.T,
        w_down.T,
        5,
    )
    ffn_all = lax.all_gather(ffn_rows, "ctx", axis=0, axis_index_groups=lay.hi_groups)
    attn_all = gather_group(
        lay,
        plane,
        (lay.hi, lay.lo, lay.dp, pack_rows // lay.dp, D),
        lambda out, k, chip, core: out.at[
            :, chip // lay.wide, lax.rem(chip, lay.wide) * 2 + core
        ],
        6,
    ).reshape(lay.ctx, pack_rows, D)
    full_qkv = attn_all[:, :qkv_rows].reshape(lay.ctx * qkv_rows, D)
    full_out = attn_all[:, qkv_rows : qkv_rows + out_rows].reshape(lay.ctx * out_rows, D)
    gain_all = (
        attn_all[:, used - 1]
        .reshape(lay.ctx, lay.dp, cols)[:, :, : gains.shape[0]]
        .transpose(1, 0, 2)
        .reshape(-1)
        .astype(jnp.float32)
    )
    gain_in = gain_all[:D]
    gain_attn = gain_all[D : 2 * D]
    gain_pre = gain_all[2 * D : 3 * D]
    gain_post = gain_all[3 * D : 4 * D]
    gain_query = gain_all[4 * D : 4 * D + HD]
    gain_key = gain_all[4 * D + HD :]
    offset = lax.axis_index("ctx") * local_len
    positions = offset + jnp.arange(local_len, dtype=jnp.int32)
    angle = angles_of(positions)
    valid = positions[None, :] < lengths[:, None]
    inputs = tokens.astype(jnp.float32)
    normed_in, pull_in = jax.vjp(norm_scaled, inputs, gain_in)
    normed_low = normed_in.astype(jnp.bfloat16)
    projected = contract(normed_low, full_qkv, (2,), (1,))
    (query, key_rot, value_rows), pull_heads = jax.vjp(
        partial(head_inputs, angle=angle), projected, gain_query, gain_key
    )
    query_low = query.astype(jnp.bfloat16)
    key_pos = offset - reach * local_len + jnp.arange((reach + 1) * local_len, dtype=jnp.int32)
    earlier = earlier_tokens.transpose(1, 0, 2, 3).reshape(seq_count, reach * local_len, D)
    earlier = norm_scaled(earlier.astype(jnp.float32), gain_in).astype(jnp.bfloat16)
    earlier = contract(earlier, full_qkv[HEADS * HD :], (2,), (1,))
    earlier_keys = rotate(
        norm_scaled(earlier[..., :HD], gain_key), angles_of(key_pos[: reach * local_len])
    )
    key_pairs = jnp.concatenate(
        [
            jnp.concatenate([earlier_keys, earlier[..., HD:]], axis=-1).astype(jnp.bfloat16),
            jnp.concatenate([key_rot, value_rows], axis=-1).astype(jnp.bfloat16),
        ],
        axis=1,
    )
    keys_low = key_pairs[..., :HD]
    values_low = key_pairs[..., HD:]
    key_grid = key_pos[None, None, :]
    query_grid = positions[None, :, None]
    allowed = (
        (key_grid >= 0)
        & (key_grid <= query_grid)
        & (query_grid - key_grid < WINDOW)
        & ((key_grid < lengths[:, None, None]) | (key_grid == query_grid))
    )

    def scores_of():
        raw = jnp.einsum("schd,skd->shck", query_low, keys_low, preferred_element_type=jnp.float32)
        return jnp.where(allowed[:, None], raw * scale, -BIG)

    scores = scores_of()
    top = jnp.max(scores, axis=-1, keepdims=True)
    expo = jnp.exp(scores - top)
    total = jnp.sum(expo, axis=-1, keepdims=True)
    probs = expo / total
    log_total = top + jnp.log(total)
    probs_low = probs.astype(jnp.bfloat16)
    attended = jnp.einsum(
        "shck,skd->schd", probs_low, values_low, preferred_element_type=jnp.float32
    )
    attended_low = attended.reshape(seq_count, local_len, HEADS * HD).astype(jnp.bfloat16)
    out_proj = contract(attended_low, full_out, (2,), (0,))
    normed_out, pull_out = jax.vjp(norm_scaled, out_proj, gain_attn)
    mixed = inputs + normed_out
    normed_mid, pull_mid = jax.vjp(norm_scaled, mixed, gain_pre)
    mid_low = normed_mid.astype(jnp.bfloat16)
    token_count = seq_count * local_len
    mid_all = gather_group(
        lay,
        mid_low.reshape(2, token_count // 2, D),
        (lay.chips, 2, 2, token_count // 2, D),
        lambda out, k, chip, core: out.at[lay.position(k), core],
        1,
    ).reshape(lay.chips, 2 * token_count, D)
    result, grad_mid, grad_gain_post, grad_ffn, early_down = feed_forward(
        lay,
        mid_all,
        ffn_all,
        mixed.reshape(token_count, D),
        cotangent.reshape(token_count, D),
        valid.reshape(token_count, 1).astype(jnp.float32),
        gain_post[None],
        2,
    )
    result = result.reshape(mixed.shape)
    grad_mid = grad_mid.reshape(mixed.shape)
    grad_gain_post = jnp.sum(grad_gain_post, axis=0)
    upstream = jnp.where(valid[..., None], cotangent.astype(jnp.float32), 0.0)
    grad_mixed_in, grad_gain_pre = pull_mid(grad_mid)
    grad_mixed = upstream + grad_mixed_in
    grad_proj, grad_gain_attn = pull_out(grad_mixed)
    proj_low = grad_proj.astype(jnp.bfloat16)
    grad_attended = contract(proj_low, full_out, (2,), (1,))
    grad_w_out = contract(attended_low, proj_low, (0, 1), (0, 1))
    attn_low = grad_attended.astype(jnp.bfloat16).reshape(seq_count, local_len, HEADS, HD)
    again_probs = jnp.exp(scores_of() - log_total)
    again_low = again_probs.astype(jnp.bfloat16)
    grad_values = jnp.einsum(
        "shck,schd->skd", again_low, attn_low, preferred_element_type=jnp.float32
    )
    grad_probs = jnp.einsum(
        "schd,skd->shck", attn_low, values_low, preferred_element_type=jnp.float32
    )
    row_dot = jnp.sum(again_probs * grad_probs, axis=-1, keepdims=True)
    grad_scores = (scale * again_probs * (grad_probs - row_dot)).astype(jnp.bfloat16)
    grad_query = jnp.einsum(
        "shck,skd->schd", grad_scores, keys_low, preferred_element_type=jnp.float32
    )
    grad_keys = jnp.einsum(
        "shck,schd->skd", grad_scores, query_low, preferred_element_type=jnp.float32
    )
    grad_pairs = jnp.concatenate([grad_keys, grad_values], axis=-1)
    own_grad = grad_pairs[:, reach * local_len :]
    pieces = grad_pairs[:, : reach * local_len].astype(jnp.bfloat16)
    pieces = pieces.reshape(seq_count, reach, local_len, 2 * HD).transpose(1, 0, 2, 3)

    def blocks_of(grad, rows):
        part = -(-rows // (16 * lay.dp)) * 16
        whole = grad.astype(jnp.bfloat16).reshape(lay.ctx, rows, D)
        if part * lay.dp > rows:
            whole = jnp.pad(whole, ((0, 0), (0, part * lay.dp - rows), (0, 0)))
        return whole.reshape(lay.ctx, lay.dp, part, D)

    later, plane_out, early_units = later_sum(
        lay, reach, pieces, blocks_of(grad_w_out, out_rows), early_down, 11
    )
    own_grad = own_grad + later
    grad_projected, grad_gain_query, grad_gain_key = pull_heads(
        (grad_query, own_grad[..., :HD], own_grad[..., HD:])
    )
    qkv_low = grad_projected.astype(jnp.bfloat16)
    grad_w_qkv = contract(qkv_low, normed_low, (0, 1), (0, 1))
    grad_normed = contract(qkv_low, full_qkv, (2,), (0,))
    grad_in_norm, grad_gain_in = pull_in(grad_normed)
    grad_input = grad_mixed + grad_in_norm
    grad_gain_all = jnp.concatenate(
        [
            grad_gain_in,
            grad_gain_attn,
            grad_gain_pre,
            grad_gain_post,
            grad_gain_query,
            grad_gain_key,
        ]
    )
    plane_qkv, gains_sum = sum_group(
        lay, blocks_of(grad_w_qkv, qkv_rows), grad_gain_all.reshape(-1, gains.shape[0]), 8
    )
    owned = lax.psum_scatter(grad_ffn, "ctx", scatter_dimension=0, axis_index_groups=lay.hi_groups)
    part_gate_up, part_down, part_qkv, part_out, part_gains = grads_out(
        lay, owned, early_units, plane_qkv, plane_out, gains_sum,
        per, qkv_rows, out_rows, 9,
    )
    part_out = part_out.T
    part_gains = part_gains[0]
    part_gate_up = part_gate_up.astype(jnp.float32).T
    part_down = part_down.astype(jnp.float32).T
    return (result, grad_input, part_qkv, part_out, part_gate_up, part_down, part_gains)


def solution(mesh):
    placed = (
        P("dp", "ctx", None),
        P("dp"),
        P("ctx", "dp"),
        P("ctx", "dp"),
        P("ctx", "dp"),
        P("ctx", "dp"),
        P(("dp", "ctx")),
        P("dp", "ctx", None),
    )
    return jax.shard_map(
        partial(per_device, Layout(mesh)),
        mesh=mesh,
        in_specs=placed,
        out_specs=(
            P("dp", "ctx", None),
            P("dp", "ctx", None),
            P("ctx", "dp"),
            P("ctx", "dp"),
            P("ctx", "dp"),
            P("ctx", "dp"),
            P(("dp", "ctx")),
        ),
        check_vma=False,
    )
```
